32 devices in a mesh: psg: 4 (over z), exp: 8 (over y, x, core).
Axes of the slice: x: 2, y: 2, z: 4, core: 2. Of those that a mesh axis runs over, the one named last changes fastest.
Arguments:
- hidden: bfloat16 [8, 4, 128, 2048], P('exp', 'psg')
- norm_gain: float32 [2048], replicated, may hold values from 0.5 to 2
- router: bfloat16 [2048, 8], replicated, may hold values from -0.125 to 0.125
- gate_proj: bfloat16 [8, 2048, 768], P('exp'), may hold values from -0.125 to 0.125
- up_proj: bfloat16 [8, 2048, 768], P('exp'), may hold values from -0.125 to 0.125
- down_proj: bfloat16 [8, 768, 2048], P('exp'), may hold values from -0.21875 to 0.21875
- final_gain: float32 [2048], replicated, may hold values from 0.5 to 2
- score_vector: bfloat16 [2048], replicated, may hold values from -0.125 to 0.125
- expert_ids: int32 [8, 4, 128, 8], P('exp', 'psg'), may hold values from 0 to 7, as said below
- grades: int32 [8, 4], P('exp'), may hold values from 0 to 4, as said below
- passage_ranks: int32 [8, 4], P('exp'), may hold values from 0 to 3, each once within a row
Outputs:
- loss: float32 [8], P('exp')
- scores: float32 [8, 4], P('exp', 'psg')
- grad_hidden: bfloat16 [8, 4, 128, 2048], P('exp', 'psg')
The draws below stay inside these ranges and needn't reach their ends.
Inputs may be any that keep to these rules, and one draw needn't show every extreme that they name: `expert_ids`: each token names 8 different experts. Among the tokens of one device each expert is named at most 128 times, and one expert, the same on every device, is named exactly 128 times on every device. `grades`: every query has some passage of grade 4. `passage_ranks`: each rank appears once in each query.
All inputs are finite; a program needn't handle non-finite values.
Results may differ from the reference program's by a relative error of at most 0.0067.
Values may be sent and summed in bfloat16 or wider, within the bound.
No kernel may reach another device: no remote copies, remote signals or barrier semaphores. Data moves between devices by JAX's collectives and lax.ppermute only.
A program may use at most 128 MiB of HBM per device.

```python
import math
import jax
import jax.numpy as jnp
from jax import lax

D = 2048
FF = 768
TOP = 8
PSG_DEV = 1
PLEN = 128
TOK_DEV = 128
PASSAGES = 4
QUERIES = 8
EXPERTS = 8
CAP = 128


def draw_hidden(key, part):
    scale_key, channel_key, noise_key = jax.random.split(key, 3)
    token_scale = jnp.exp(jax.random.uniform(scale_key, (QUERIES, PASSAGES, PLEN, 1), jnp.float32, math.log(0.25), math.log(2.5)))
    channel_scale = jnp.exp(jax.random.uniform(channel_key, (1, 1, 1, D), jnp.float32, -0.5 * math.log(10.0), 0.5 * math.log(10.0)))
    noise = jax.random.normal(noise_key, (QUERIES, PASSAGES, PLEN, D), jnp.float32)
    return (noise * token_scale * channel_scale).astype(jnp.bfloat16)


def draw_grades(key, part):
    grade_key, best_key = jax.random.split(key)
    values = jax.random.randint(grade_key, (QUERIES, PASSAGES), 0, 5, jnp.int32)
    best_index = jax.random.randint(best_key, (QUERIES, 1), 0, PASSAGES, jnp.int32)
    return jnp.where(jnp.arange(PASSAGES, dtype=jnp.int32)[None, :] == best_index, 4, values).astype(jnp.int32)


def route_block(block_key, hot_expert, base_load, extra_load, spread_most):
    order_key, move_key, token_key, column_key = jax.random.split(block_key, 4)
    expert_range = jnp.arange(EXPERTS, dtype=jnp.int32)
    shuffled = jax.random.permutation(order_key, EXPERTS).astype(jnp.int32)
    priority = jnp.where(shuffled == hot_expert, -1, expert_range)
    ordering = shuffled[jnp.argsort(priority)]
    loads = jnp.where(expert_range == 0, CAP, base_load + (expert_range - 1 < extra_load).astype(jnp.int32))
    pair_count = min(8, (EXPERTS - 1) // 2)
    moves = jax.random.randint(move_key, (EXPERTS,), 0, spread_most + 1, jnp.int32)
    raise_mask = jnp.logical_and(expert_range >= 1, expert_range <= pair_count)
    moves_up = jnp.where(raise_mask, moves, 0)
    loads = loads + moves_up - jnp.roll(moves_up, pair_count)
    bounds = jnp.cumsum(loads)
    slot_index = jnp.arange(TOK_DEV * TOP, dtype=jnp.int32)
    label_rank = jnp.sum((bounds[None, :] <= slot_index[:, None]).astype(jnp.int32), axis=1)
    labels = ordering[label_rank].reshape(TOP, TOK_DEV).T
    token_order = jax.random.permutation(token_key, TOK_DEV)
    labels = labels[token_order]
    column_score = jax.random.randint(column_key, (TOK_DEV, TOP), 0, 1 << 20, jnp.int32) * TOP + jnp.arange(TOP, dtype=jnp.int32)[None, :]
    return jnp.take_along_axis(labels, jnp.argsort(column_score, axis=1), axis=1).astype(jnp.int32)


def draw_expert_ids(key, part):
    slot_total = TOK_DEV * TOP
    base_load = (slot_total - CAP) // (EXPERTS - 1)
    extra_load = (slot_total - CAP) % (EXPERTS - 1)
    spread_most = max(0, min(CAP - base_load - 1, base_load // 2))
    hot_key, block_key = jax.random.split(key)
    hot_expert = jax.random.randint(hot_key, (), 0, EXPERTS, jnp.int32)
    group_count = PASSAGES // PSG_DEV
    block_keys = jax.random.split(block_key, QUERIES * group_count)
    blocks = jax.vmap(lambda one_key: route_block(one_key, hot_expert, base_load, extra_load, spread_most))(block_keys)
    return blocks.reshape(QUERIES, PASSAGES, PLEN, TOP)


def shard_levels(own_key, shape, shards, smallest, top_value):
    loudness = 1.0
    for dim, parts in shards:
        steps = jax.random.uniform(jax.random.fold_in(jax.random.fold_in(own_key, 6), dim), (parts,), jnp.float32, smallest / len(shards), top_value / len(shards))
        loudness = loudness * jnp.repeat(jnp.exp(steps), shape[dim] // parts).reshape((-1,) + (1,) * (len(shape) - 1 - dim))
    return loudness


def centred(rng, dims, spread, reach, cuts=(), kind=jnp.bfloat16):
    factor_of = shard_levels(rng, dims, cuts, -0.22, 0.18) if cuts else 1.0
    drawn = jax.random.normal(rng, dims, jnp.float32) * spread * factor_of
    return jnp.minimum(jnp.maximum(drawn, -reach), reach).astype(kind)


def setup_inputs(seed: int = 0) -> dict:
    arg_keys = jax.random.split(jax.random.key(seed), 12)
    return {
        "hidden": draw_hidden(jax.random.fold_in(arg_keys[11], 71), 0),
        "norm_gain": jnp.clip(jnp.exp(jax.random.uniform(arg_keys[1], (D,), jnp.float32, math.log(0.5), math.log(2.0))), 0.5, 2.0),
        "router": centred(arg_keys[2], (D, EXPERTS), D ** -0.5, 0.125),
        "gate_proj": centred(arg_keys[3], (EXPERTS, D, FF), D ** -0.5, 0.125, ((0, 8),)),
        "up_proj": centred(arg_keys[4], (EXPERTS, D, FF), D ** -0.5, 0.125, ((0, 8),)),
        "down_proj": centred(arg_keys[5], (EXPERTS, FF, D), FF ** -0.5, 0.21875, ((0, 8),)),
        "final_gain": jnp.clip(jnp.exp(jax.random.uniform(arg_keys[6], (D,), jnp.float32, math.log(0.5), math.log(2.0))), 0.5, 2.0),
        "score_vector": centred(arg_keys[7], (D,), D ** -0.5, 0.125),
        "expert_ids": draw_expert_ids(jax.random.fold_in(arg_keys[11], 71), 0),
        "grades": draw_grades(jax.random.fold_in(arg_keys[11], 71), 0),
        "passage_ranks": jax.vmap(lambda own: jax.random.permutation(own, PASSAGES))(jax.random.split(arg_keys[10], QUERIES)).reshape((QUERIES, PASSAGES)).astype(jnp.int32),
    }


epsilon = 1e-06
loss_scale = 256.0
highest = lax.Precision.HIGHEST

def rms_scale(values):
    return lax.rsqrt(lax.optimization_barrier(jnp.mean(values * values, axis=-1, keepdims=True)) + epsilon)

def head_score(pooled, final_gain, score_vector):
    scaled = pooled * rms_scale(pooled) * final_gain
    return jnp.dot(scaled, score_vector.astype(jnp.float32), precision=highest)

def rank_loss(scores, grades, passage_ranks):
    grade_value = grades.astype(jnp.float32)
    worth_gain = jnp.exp2(grade_value)
    discount = 1.0 / jnp.log2(2.0 + passage_ranks.astype(jnp.float32))
    better_than = grades[None, :] > grades[:, None]
    equal_grade = grades[None, :] == grades[:, None]
    position = jnp.arange(grades.shape[0], dtype=jnp.int32)
    earlier = position[None, :] < position[:, None]
    ideal_rank = lax.optimization_barrier(jnp.sum(jnp.logical_or(better_than, jnp.logical_and(equal_grade, earlier)).astype(jnp.float32), axis=1))
    ideal_gain = jnp.sum((worth_gain - 1.0) / jnp.log2(2.0 + ideal_rank))
    ordered = (grades[:, None] > grades[None, :]).astype(jnp.float32)
    swap_gain = jnp.abs((worth_gain[:, None] - worth_gain[None, :]) * (discount[:, None] - discount[None, :])) / ideal_gain
    margin = scores[:, None] - scores[None, :]
    return jnp.sum(ordered * swap_gain * jax.nn.softplus(-margin))

def total_loss(scores, grades, passage_ranks):
    every = jax.vmap(rank_loss)(scores, grades, passage_ranks)
    return (jnp.sum(every), every)

def pick_gates(normed, router, picked_ids):
    expert_total = router.shape[1]
    logits = jnp.dot(normed, router, preferred_element_type=jnp.float32)
    onehot = (picked_ids[:, :, None] == jnp.arange(expert_total, dtype=jnp.int32)[None, None, :]).astype(jnp.float32)
    chosen = jnp.einsum('nke,ne->nk', onehot, logits, precision=highest)
    weights = jnp.exp(chosen)
    return (weights / lax.optimization_barrier(jnp.sum(weights, axis=1, keepdims=True)), onehot)

def gate_parts(pre_gate):
    sigmoid_gate = jax.nn.sigmoid(pre_gate)
    return (pre_gate * sigmoid_gate, sigmoid_gate * (1.0 + pre_gate * (1.0 - sigmoid_gate)))

def norm_back(flat_rows, inverse, norm_gain, d_normed):
    scaled = d_normed * norm_gain
    return inverse * scaled - flat_rows * inverse * inverse * inverse * lax.optimization_barrier(jnp.mean(flat_rows * scaled, axis=-1, keepdims=True))

def to_low(values):
    return lax.optimization_barrier(values.astype(jnp.bfloat16)).astype(jnp.float32)

def reference(hidden, norm_gain, router, gate_proj, up_proj, down_proj, final_gain, score_vector, expert_ids, grades, passage_ranks):
    passage_total = QUERIES * PASSAGES
    token_count = passage_total * PLEN
    slot_count = token_count * TOP
    row_limit = CAP * (token_count // TOK_DEV)
    flat_rows = hidden.reshape(token_count, D).astype(jnp.float32)
    inverse = rms_scale(flat_rows)
    normed = (flat_rows * inverse * norm_gain).astype(jnp.bfloat16)
    picked_ids = expert_ids.reshape(token_count, TOP)
    gate_values, onehot = pick_gates(normed, router, picked_ids)
    gate_low = to_low(gate_values).reshape(slot_count)
    slot_ids = picked_ids.reshape(slot_count)
    slot_hits = onehot.reshape(slot_count, EXPERTS).astype(jnp.int32)
    slot_rank = lax.optimization_barrier(jnp.sum((jnp.cumsum(slot_hits, axis=0) - slot_hits) * slot_hits, axis=1))
    table = jnp.full((EXPERTS, row_limit), slot_count, jnp.int32)
    table = table.at[slot_ids, slot_rank].set(jnp.arange(slot_count, dtype=jnp.int32))
    passage_ids = jnp.arange(passage_total, dtype=jnp.int32)

    def expert_rows(slot_row):
        valid = slot_row < slot_count
        safe_slot = jnp.where(valid, slot_row, 0)
        token_row = safe_slot // TOP
        weight = jnp.where(valid, gate_low[safe_slot], 0.0)
        belongs = (token_row[:, None] // PLEN == passage_ids[None, :]).astype(jnp.float32)
        return (token_row, weight, belongs)

    def expert_front(gate_one, up_one, token_row):
        inputs = normed[token_row].astype(jnp.float32)
        pre_gate = jnp.dot(inputs, gate_one.astype(jnp.float32), precision=highest)
        pre_up = jnp.dot(inputs, up_one.astype(jnp.float32), precision=highest)
        silu_gate, slope = gate_parts(pre_gate)
        act_low = to_low(silu_gate * pre_up)
        return (pre_up, silu_gate, slope, act_low)

    def forward_one(operands):
        gate_one, up_one, down_one, slot_row = operands
        token_row, weight, belongs = expert_rows(slot_row)
        unused_up, silu_gate, slope, act_low = expert_front(gate_one, up_one, token_row)
        passage_part = jnp.dot((belongs * weight[:, None]).T, act_low, precision=highest)
        return jnp.dot(passage_part, down_one.astype(jnp.float32), precision=highest)
    moe_terms = lax.map(forward_one, (gate_proj, up_proj, down_proj, table))
    pooled = (lax.optimization_barrier(jnp.sum(flat_rows.reshape(passage_total, PLEN, D), axis=1)) + lax.optimization_barrier(jnp.sum(moe_terms, axis=0))) / PLEN
    scores = head_score(pooled, final_gain, score_vector).reshape(QUERIES, PASSAGES)
    (unused_total, losses), loss_grad = jax.value_and_grad(total_loss, has_aux=True)(scores, grades, passage_ranks)
    unused_score, head_back = jax.vjp(lambda values: head_score(values, final_gain, score_vector), pooled)
    d_vector = head_back(loss_grad.reshape(passage_total) * loss_scale)[0] / PLEN

    def backward_one(carry, operands):
        d_normed, slot_grad = carry
        gate_one, up_one, down_one, slot_row = operands
        token_row, weight, belongs = expert_rows(slot_row)
        pre_up, silu_gate, slope, act_low = expert_front(gate_one, up_one, token_row)
        near_table = jnp.dot(d_vector, down_one.astype(jnp.float32).T, precision=highest)
        near_rows = jnp.dot(belongs, near_table, precision=highest)
        d_act = weight[:, None] * near_rows
        d_gate = to_low(d_act * pre_up * slope)
        d_up = to_low(d_act * silu_gate)
        pick_grad = jnp.dot(d_gate, gate_one.astype(jnp.float32).T, precision=highest) + jnp.dot(d_up, up_one.astype(jnp.float32).T, precision=highest)
        pick_grad = to_low(pick_grad)
        gate_grad = to_low(lax.optimization_barrier(jnp.sum(act_low * near_rows, axis=1)))
        valid = slot_row < slot_count
        d_normed = d_normed.at[token_row].add(jnp.where(valid[:, None], pick_grad, 0.0))
        slot_grad = slot_grad.at[slot_row].set(gate_grad, mode='drop')
        return ((d_normed, slot_grad), None)
    start = (jnp.zeros((token_count, D), jnp.float32), jnp.zeros((slot_count,), jnp.float32))
    (d_normed, slot_grad), unused_rest = lax.scan(backward_one, start, (gate_proj, up_proj, down_proj, table))
    slot_gate = slot_grad.reshape(token_count, TOP)
    d_logit = gate_values * (slot_gate - lax.optimization_barrier(jnp.sum(gate_values * slot_gate, axis=1, keepdims=True)))
    dense_logit = jnp.einsum('nk,nke->ne', d_logit, onehot, precision=highest)
    d_normed = d_normed + jnp.dot(dense_logit, router.astype(jnp.float32).T, precision=highest)
    grad_flat = norm_back(flat_rows, inverse, norm_gain, d_normed)
    grad_hidden = grad_flat.reshape(passage_total, PLEN, D) + d_vector[:, None, :]
    return (losses, scores, grad_hidden.reshape(QUERIES, PASSAGES, PLEN, D).astype(jnp.bfloat16))
```

```python
import jax
import jax.numpy as jnp
from jax import lax
from jax.sharding import PartitionSpec as P

epsilon = 1e-06
loss_scale = 256.0
highest = lax.Precision.HIGHEST


def rms_scale(values):
    return lax.rsqrt(jnp.mean(values * values, axis=-1, keepdims=True) + epsilon)


def head_score(pooled, final_gain, score_vector):
    scaled = pooled * rms_scale(pooled) * final_gain
    return jnp.dot(scaled, score_vector.astype(jnp.float32), precision=highest)


def rank_loss(scores, grades, passage_ranks):
    grade_value = grades.astype(jnp.float32)
    worth_gain = jnp.exp2(grade_value)
    discount = 1.0 / jnp.log2(2.0 + passage_ranks.astype(jnp.float32))
    better_than = grades[None, :] > grades[:, None]
    equal_grade = grades[None, :] == grades[:, None]
    position = jnp.arange(grades.shape[0], dtype=jnp.int32)
    earlier = position[None, :] < position[:, None]
    ideal_rank = jnp.sum(
        jnp.logical_or(better_than, jnp.logical_and(equal_grade, earlier)).astype(jnp.float32),
        axis=1,
    )
    ideal_gain = jnp.sum((worth_gain - 1.0) / jnp.log2(2.0 + ideal_rank))
    ordered = (grades[:, None] > grades[None, :]).astype(jnp.float32)
    swap_gain = (
        jnp.abs(
            (worth_gain[:, None] - worth_gain[None, :]) * (discount[:, None] - discount[None, :])
        )
        / ideal_gain
    )
    margin = scores[:, None] - scores[None, :]
    return jnp.sum(ordered * swap_gain * jax.nn.softplus(-margin))


def pick_gates(normed, router, picked_ids):
    expert_total = router.shape[1]
    logits = jnp.dot(normed, router, preferred_element_type=jnp.float32)
    onehot = (
        picked_ids[:, :, None] == jnp.arange(expert_total, dtype=jnp.int32)[None, None, :]
    ).astype(jnp.float32)
    chosen = jnp.einsum("nke,ne->nk", onehot, logits, precision=highest)
    weights = jnp.exp(chosen)
    return (weights / jnp.sum(weights, axis=1, keepdims=True), onehot)


def gate_parts(pre_gate):
    sigmoid_gate = jax.nn.sigmoid(pre_gate)
    return (pre_gate * sigmoid_gate, sigmoid_gate * (1.0 + pre_gate * (1.0 - sigmoid_gate)))


def norm_back(flat_rows, inverse, norm_gain, d_normed):
    scaled = d_normed * norm_gain
    return inverse * scaled - flat_rows * inverse * inverse * inverse * jnp.mean(
        flat_rows * scaled, axis=-1, keepdims=True
    )


def unpack_front(front_out, buffer_rows):
    pre_gate, pre_up, received = front_out
    hidden_units = pre_gate.shape[2]
    pre_gate = pre_gate.reshape(buffer_rows, hidden_units)
    pre_up = pre_up.reshape(buffer_rows, hidden_units)
    silu_gate, slope = gate_parts(pre_gate)
    activation = (silu_gate * pre_up).astype(jnp.bfloat16)
    return (pre_up, received, silu_gate, slope, activation)


def local(
    hidden,
    norm_gain,
    router,
    gate_proj,
    up_proj,
    down_proj,
    final_gain,
    score_vector,
    expert_ids,
    grades,
    passage_ranks,
):
    unused_query, local_passages, local_positions, model_width = hidden.shape
    top_count = expert_ids.shape[3]
    expert_count = lax.axis_size("exp")
    token_count = local_passages * local_positions
    slot_count = token_count * top_count
    capacity = min(token_count, 9 * token_count * top_count // (8 * expert_count))
    buffer_rows = expert_count * capacity
    flat_rows = hidden.reshape(token_count, model_width).astype(jnp.float32)
    inverse = rms_scale(flat_rows)
    normed = (flat_rows * inverse * norm_gain).astype(jnp.bfloat16)
    picked_ids = expert_ids.reshape(token_count, top_count)
    gate_values, onehot = pick_gates(normed, router, picked_ids)
    slot_hits = onehot.reshape(slot_count, expert_count).astype(jnp.int32)
    slot_rank = jnp.sum((jnp.cumsum(slot_hits, axis=0) - slot_hits) * slot_hits, axis=1)
    target = picked_ids.reshape(slot_count) * capacity + slot_rank
    source_token = jnp.arange(slot_count, dtype=jnp.int32) // top_count
    passage_onehot = (
        source_token[:, None] // local_positions
        == jnp.arange(local_passages, dtype=jnp.int32)[None, :]
    ).astype(jnp.float32)
    weighted = (passage_onehot * gate_values.reshape(slot_count, 1)).astype(jnp.bfloat16)
    send_rows = (
        jnp.zeros((buffer_rows, model_width), jnp.bfloat16).at[target].set(normed[source_token])
    )
    send_weights = jnp.zeros((buffer_rows, local_passages), jnp.bfloat16).at[target].set(weighted)
    outgoing = (
        send_rows.reshape(expert_count, capacity, model_width),
        send_weights.reshape(expert_count, capacity, local_passages),
    )
    gate_matrix = gate_proj[0]
    up_matrix = up_proj[0]
    down_matrix = down_proj[0]
    rows_in = lax.all_to_all(outgoing[0], "exp", split_axis=0, concat_axis=0, tiled=True)
    weights_in = lax.all_to_all(outgoing[1], "exp", split_axis=0, concat_axis=0, tiled=True)
    pre_gate = jnp.einsum("end,df->enf", rows_in, gate_matrix, preferred_element_type=jnp.float32)
    pre_up = jnp.einsum("end,df->enf", rows_in, up_matrix, preferred_element_type=jnp.float32)
    front_out = (pre_gate, pre_up, weights_in)
    pre_up, received, silu_gate, slope, activation = unpack_front(front_out, buffer_rows)
    hidden_units = activation.shape[1]
    passage_part = jnp.einsum(
        "scp,scf->spf",
        received,
        activation.reshape(expert_count, capacity, hidden_units),
        preferred_element_type=jnp.float32,
    )
    down_wide = down_matrix.astype(jnp.float32)
    expert_terms = jnp.einsum("spf,fd->spd", passage_part, down_wide, precision=highest)
    came_back = lax.all_to_all(expert_terms, "exp", split_axis=0, concat_axis=0, tiled=True)
    token_sums = jnp.sum(flat_rows.reshape(local_passages, local_positions, model_width), axis=1)
    pooled = (token_sums + jnp.sum(came_back, axis=0)) / local_positions
    first_row = lax.axis_index("psg") * local_passages
    own_score = head_score(pooled, final_gain, score_vector)
    every_score = lax.all_gather(own_score, "psg", axis=0, tiled=True)
    loss_value, loss_grad = jax.value_and_grad(rank_loss)(every_score, grades[0], passage_ranks[0])
    d_own = lax.dynamic_slice_in_dim(loss_grad, first_row, local_passages, 0) * loss_scale
    unused_score, head_back = jax.vjp(
        lambda values: head_score(values, final_gain, score_vector), pooled
    )
    d_vector = head_back(d_own)[0] / local_positions
    every_vector = lax.all_gather(d_vector[None], "exp", axis=0, tiled=True)
    near_table = jnp.einsum("spd,fd->spf", every_vector, down_wide, precision=highest)
    present = (received != 0).astype(jnp.float32)
    near_rows = jnp.einsum("scp,spf->scf", present, near_table, precision=highest).reshape(
        buffer_rows, hidden_units
    )
    gate_weight = jnp.sum(received.astype(jnp.float32), axis=2).reshape(buffer_rows, 1)
    d_act = gate_weight * near_rows
    d_gate = (d_act * pre_up * slope).astype(jnp.bfloat16)
    d_up = (d_act * silu_gate).astype(jnp.bfloat16)
    contract = (((1,), (1,)), ((), ()))
    pick_grad = lax.dot_general(d_gate, gate_matrix, contract, preferred_element_type=jnp.float32)
    pick_grad = (
        pick_grad + lax.dot_general(d_up, up_matrix, contract, preferred_element_type=jnp.float32)
    ).astype(jnp.bfloat16)
    gate_grad = jnp.sum(activation.astype(jnp.float32) * near_rows, axis=1).astype(jnp.bfloat16)
    back_rows, back_gate = (
        lax.all_to_all(
            pick_grad.reshape(expert_count, capacity, model_width),
            "exp",
            split_axis=0,
            concat_axis=0,
            tiled=True,
        ),
        lax.all_to_all(
            gate_grad.reshape(expert_count, capacity),
            "exp",
            split_axis=0,
            concat_axis=0,
            tiled=True,
        ),
    )
    picked_rows = back_rows.reshape(buffer_rows, model_width)[target]
    d_normed = jnp.sum(
        picked_rows.reshape(token_count, top_count, model_width).astype(jnp.float32), axis=1
    )
    picked_gate = (
        back_gate.reshape(buffer_rows)[target].astype(jnp.float32).reshape(token_count, top_count)
    )
    d_logit = gate_values * (
        picked_gate - jnp.sum(gate_values * picked_gate, axis=1, keepdims=True)
    )
    dense_logit = jnp.einsum("nk,nke->ne", d_logit, onehot, precision=highest)
    d_normed = d_normed + jnp.einsum(
        "ne,de->nd", dense_logit, router.astype(jnp.float32), precision=highest
    )
    grad_flat = norm_back(flat_rows, inverse, norm_gain, d_normed)
    grad_hidden = (
        grad_flat.reshape(1, local_passages, local_positions, model_width)
        + d_vector[None, :, None, :]
    )
    return (
        loss_value.reshape(1),
        own_score.reshape(1, local_passages),
        grad_hidden.astype(jnp.bfloat16),
    )


def split_low(values):
    high = values.astype(jnp.bfloat16)
    rest = values - high.astype(jnp.float32)
    middle = rest.astype(jnp.bfloat16)
    low = (rest - middle.astype(jnp.float32)).astype(jnp.bfloat16)
    return jnp.concatenate([high, middle, low], axis=0)


def exact_dot(values, low_matrix, contract):
    parts = lax.dot_general(
        split_low(values), low_matrix, contract, preferred_element_type=jnp.float32
    )
    return jnp.sum(parts.reshape(3, values.shape[0], parts.shape[1]), axis=0)


def every_expert(
    hidden,
    norm_gain,
    router,
    gate_proj,
    up_proj,
    down_proj,
    final_gain,
    score_vector,
    expert_ids,
    grades,
    passage_ranks,
):
    unused_query, local_passages, token_count, model_width = hidden.shape
    expert_count = lax.axis_size("exp")
    expert = lax.axis_index("exp")
    flat_rows = hidden.reshape(token_count, model_width).astype(jnp.float32)
    inverse = rms_scale(flat_rows)
    normed = (flat_rows * inverse * norm_gain).astype(jnp.bfloat16)
    gate_matrix, up_matrix, down_matrix = gate_proj[0], up_proj[0], down_proj[0]
    hidden_units = gate_matrix.shape[1]

    rows = lax.all_gather(normed, "exp", axis=0, tiled=True)
    weights = jnp.exp(jnp.dot(rows, router, preferred_element_type=jnp.float32))
    gates = weights / jnp.sum(weights, axis=1, keepdims=True)
    own_column = lax.dynamic_slice_in_dim(gates, expert, 1, axis=1)
    gate_low = own_column.astype(jnp.bfloat16)
    pre_gate = jnp.dot(rows, gate_matrix, preferred_element_type=jnp.float32)
    pre_up = jnp.dot(rows, up_matrix, preferred_element_type=jnp.float32)
    silu_gate, slope = gate_parts(pre_gate)
    activation = (silu_gate * pre_up).astype(jnp.bfloat16)
    passage_part = jnp.einsum(
        "sc,scf->sf",
        gate_low.reshape(expert_count, token_count),
        activation.reshape(expert_count, token_count, hidden_units),
        preferred_element_type=jnp.float32,
    )
    forward = (((1,), (0,)), ((), ()))
    across = (((1,), (1,)), ((), ()))
    terms = exact_dot(passage_part, down_matrix, forward)
    own_passage = (jnp.arange(expert_count) == expert).astype(jnp.float32)[:, None]
    terms = terms + own_passage * jnp.sum(flat_rows, axis=0)[None, :]
    pooled = lax.psum(terms, "exp") / token_count

    head = final_gain * score_vector.astype(jnp.float32)
    pooled_scale = rms_scale(pooled)
    along = jnp.sum(pooled * head[None, :], axis=1, keepdims=True)
    every_query = pooled_scale * along
    own_score = lax.dynamic_slice_in_dim(every_query, expert, 1, axis=0).reshape(1)
    unit_vector = (
        pooled_scale * head[None, :]
        - pooled_scale * pooled_scale * pooled_scale * (along / model_width) * pooled
    ) / token_count
    near_table = exact_dot(unit_vector, down_matrix, across)
    near_rows = jnp.repeat(near_table, token_count, axis=0)

    every_score = lax.all_gather(own_score, "psg", axis=0, tiled=True)
    loss_value, loss_grad = jax.value_and_grad(rank_loss)(every_score, grades[0], passage_ranks[0])
    d_own = lax.dynamic_slice_in_dim(loss_grad, lax.axis_index("psg"), 1, 0) * loss_scale

    d_act = gate_low.astype(jnp.float32) * near_rows
    d_gate = (d_act * pre_up * slope).astype(jnp.bfloat16)
    d_up = (d_act * silu_gate).astype(jnp.bfloat16)
    gate_grad = jnp.sum(activation.astype(jnp.float32) * near_rows, axis=1).astype(jnp.bfloat16)
    back_gate = lax.all_to_all(
        gate_grad.reshape(expert_count, token_count), "exp", split_axis=0, concat_axis=0, tiled=True
    )
    pick_grad = lax.dot_general(
        d_gate, gate_matrix, across, preferred_element_type=jnp.float32
    ) + lax.dot_general(d_up, up_matrix, across, preferred_element_type=jnp.float32)
    d_normed = lax.psum_scatter(
        pick_grad.astype(jnp.bfloat16), "exp", scatter_dimension=0, tiled=True
    ).astype(jnp.float32)

    own_gates = lax.dynamic_slice_in_dim(gates, expert * token_count, token_count, axis=0)
    slot_grad = back_gate.astype(jnp.float32).T
    d_logit = own_gates * (slot_grad - jnp.sum(own_gates * slot_grad, axis=1, keepdims=True))
    d_normed = d_normed + lax.dot_general(
        d_logit, router.astype(jnp.float32), across, precision=highest
    )
    own_vector = lax.dynamic_slice_in_dim(unit_vector, expert, 1, axis=0)
    grad = (norm_back(flat_rows, inverse, norm_gain, d_normed) + own_vector) * d_own
    return (
        loss_value.reshape(1),
        own_score.reshape(1, 1),
        grad.reshape(hidden.shape).astype(jnp.bfloat16),
    )


def block(*arrays):
    hidden, router, expert_ids = arrays[0], arrays[2], arrays[8]
    if hidden.shape[1] == 1 and router.shape[1] == expert_ids.shape[3]:
        return every_expert(*arrays)
    return local(*arrays)


def solution(mesh):
    placed = (
        P("exp", "psg", None, None),
        P(),
        P(),
        P("exp", None, None),
        P("exp", None, None),
        P("exp", None, None),
        P(),
        P(),
        P("exp", "psg", None, None),
        P("exp", None),
        P("exp", None),
    )
    return jax.shard_map(
        block,
        mesh=mesh,
        in_specs=placed,
        out_specs=(P("exp"), P("exp", "psg"), P("exp", "psg", None, None)),
        check_vma=False,
    )
```

```python
import functools
import math

import jax
import jax.numpy as jnp
from jax import lax
from jax.experimental import pallas as pl
from jax.experimental.pallas import tpu as pltpu
from jax.sharding import PartitionSpec as P

epsilon = 1e-06
loss_scale = 256.0
highest = lax.Precision.HIGHEST


def rms_scale(values):
    return lax.rsqrt(jnp.mean(values * values, axis=-1, keepdims=True) + epsilon)


def head_score(pooled, final_gain, score_vector):
    scaled = pooled * rms_scale(pooled) * final_gain
    return jnp.dot(scaled, score_vector.astype(jnp.float32), precision=highest)


def rank_loss(scores, grades, passage_ranks):
    grade_value = grades.astype(jnp.float32)
    worth_gain = jnp.exp2(grade_value)
    discount = 1.0 / jnp.log2(2.0 + passage_ranks.astype(jnp.float32))
    better_than = grades[None, :] > grades[:, None]
    equal_grade = grades[None, :] == grades[:, None]
    position = jnp.arange(grades.shape[0], dtype=jnp.int32)
    earlier = position[None, :] < position[:, None]
    ideal_rank = jnp.sum(
        jnp.logical_or(better_than, jnp.logical_and(equal_grade, earlier)).astype(jnp.float32),
        axis=1,
    )
    ideal_gain = jnp.sum((worth_gain - 1.0) / jnp.log2(2.0 + ideal_rank))
    ordered = (grades[:, None] > grades[None, :]).astype(jnp.float32)
    swap_gain = (
        jnp.abs(
            (worth_gain[:, None] - worth_gain[None, :]) * (discount[:, None] - discount[None, :])
        )
        / ideal_gain
    )
    margin = scores[:, None] - scores[None, :]
    return jnp.sum(ordered * swap_gain * jax.nn.softplus(-margin))


def pick_gates(normed, router, picked_ids):
    expert_total = router.shape[1]
    logits = jnp.dot(normed, router, preferred_element_type=jnp.float32)
    onehot = (
        picked_ids[:, :, None] == jnp.arange(expert_total, dtype=jnp.int32)[None, None, :]
    ).astype(jnp.float32)
    chosen = jnp.einsum("nke,ne->nk", onehot, logits, precision=highest)
    weights = jnp.exp(chosen)
    return (weights / jnp.sum(weights, axis=1, keepdims=True), onehot)


def gate_parts(pre_gate):
    sigmoid_gate = jax.nn.sigmoid(pre_gate)
    return (pre_gate * sigmoid_gate, sigmoid_gate * (1.0 + pre_gate * (1.0 - sigmoid_gate)))


def norm_back(flat_rows, inverse, norm_gain, d_normed):
    scaled = d_normed * norm_gain
    return inverse * scaled - flat_rows * inverse * inverse * inverse * jnp.mean(
        flat_rows * scaled, axis=-1, keepdims=True
    )


def unpack_front(front_out, buffer_rows):
    pre_gate, pre_up, received = front_out
    hidden_units = pre_gate.shape[2]
    pre_gate = pre_gate.reshape(buffer_rows, hidden_units)
    pre_up = pre_up.reshape(buffer_rows, hidden_units)
    silu_gate, slope = gate_parts(pre_gate)
    activation = (silu_gate * pre_up).astype(jnp.bfloat16)
    return (pre_up, received, silu_gate, slope, activation)


def local(
    hidden,
    norm_gain,
    router,
    gate_proj,
    up_proj,
    down_proj,
    final_gain,
    score_vector,
    expert_ids,
    grades,
    passage_ranks,
):
    unused_query, local_passages, local_positions, model_width = hidden.shape
    top_count = expert_ids.shape[3]
    expert_count = lax.axis_size("exp")
    token_count = local_passages * local_positions
    slot_count = token_count * top_count
    capacity = min(token_count, 9 * token_count * top_count // (8 * expert_count))
    buffer_rows = expert_count * capacity
    flat_rows = hidden.reshape(token_count, model_width).astype(jnp.float32)
    inverse = rms_scale(flat_rows)
    normed = (flat_rows * inverse * norm_gain).astype(jnp.bfloat16)
    picked_ids = expert_ids.reshape(token_count, top_count)
    gate_values, onehot = pick_gates(normed, router, picked_ids)
    slot_hits = onehot.reshape(slot_count, expert_count).astype(jnp.int32)
    slot_rank = jnp.sum((jnp.cumsum(slot_hits, axis=0) - slot_hits) * slot_hits, axis=1)
    target = picked_ids.reshape(slot_count) * capacity + slot_rank
    source_token = jnp.arange(slot_count, dtype=jnp.int32) // top_count
    passage_onehot = (
        source_token[:, None] // local_positions
        == jnp.arange(local_passages, dtype=jnp.int32)[None, :]
    ).astype(jnp.float32)
    weighted = (passage_onehot * gate_values.reshape(slot_count, 1)).astype(jnp.bfloat16)
    send_rows = (
        jnp.zeros((buffer_rows, model_width), jnp.bfloat16).at[target].set(normed[source_token])
    )
    send_weights = jnp.zeros((buffer_rows, local_passages), jnp.bfloat16).at[target].set(weighted)
    outgoing = (
        send_rows.reshape(expert_count, capacity, model_width),
        send_weights.reshape(expert_count, capacity, local_passages),
    )
    gate_matrix = gate_proj[0]
    up_matrix = up_proj[0]
    down_matrix = down_proj[0]
    rows_in = lax.all_to_all(outgoing[0], "exp", split_axis=0, concat_axis=0, tiled=True)
    weights_in = lax.all_to_all(outgoing[1], "exp", split_axis=0, concat_axis=0, tiled=True)
    pre_gate = jnp.einsum("end,df->enf", rows_in, gate_matrix, preferred_element_type=jnp.float32)
    pre_up = jnp.einsum("end,df->enf", rows_in, up_matrix, preferred_element_type=jnp.float32)
    front_out = (pre_gate, pre_up, weights_in)
    pre_up, received, silu_gate, slope, activation = unpack_front(front_out, buffer_rows)
    hidden_units = activation.shape[1]
    passage_part = jnp.einsum(
        "scp,scf->spf",
        received,
        activation.reshape(expert_count, capacity, hidden_units),
        preferred_element_type=jnp.float32,
    )
    down_wide = down_matrix.astype(jnp.float32)
    expert_terms = jnp.einsum("spf,fd->spd", passage_part, down_wide, precision=highest)
    came_back = lax.all_to_all(expert_terms, "exp", split_axis=0, concat_axis=0, tiled=True)
    token_sums = jnp.sum(flat_rows.reshape(local_passages, local_positions, model_width), axis=1)
    pooled = (token_sums + jnp.sum(came_back, axis=0)) / local_positions
    first_row = lax.axis_index("psg") * local_passages
    own_score = head_score(pooled, final_gain, score_vector)
    every_score = lax.all_gather(own_score, "psg", axis=0, tiled=True)
    loss_value, loss_grad = jax.value_and_grad(rank_loss)(every_score, grades[0], passage_ranks[0])
    d_own = lax.dynamic_slice_in_dim(loss_grad, first_row, local_passages, 0) * loss_scale
    unused_score, head_back = jax.vjp(
        lambda values: head_score(values, final_gain, score_vector), pooled
    )
    d_vector = head_back(d_own)[0] / local_positions
    every_vector = lax.all_gather(d_vector[None], "exp", axis=0, tiled=True)
    near_table = jnp.einsum("spd,fd->spf", every_vector, down_wide, precision=highest)
    present = (received != 0).astype(jnp.float32)
    near_rows = jnp.einsum("scp,spf->scf", present, near_table, precision=highest).reshape(
        buffer_rows, hidden_units
    )
    gate_weight = jnp.sum(received.astype(jnp.float32), axis=2).reshape(buffer_rows, 1)
    d_act = gate_weight * near_rows
    d_gate = (d_act * pre_up * slope).astype(jnp.bfloat16)
    d_up = (d_act * silu_gate).astype(jnp.bfloat16)
    contract = (((1,), (1,)), ((), ()))
    pick_grad = lax.dot_general(d_gate, gate_matrix, contract, preferred_element_type=jnp.float32)
    pick_grad = (
        pick_grad + lax.dot_general(d_up, up_matrix, contract, preferred_element_type=jnp.float32)
    ).astype(jnp.bfloat16)
    gate_grad = jnp.sum(activation.astype(jnp.float32) * near_rows, axis=1).astype(jnp.bfloat16)
    back_rows, back_gate = (
        lax.all_to_all(
            pick_grad.reshape(expert_count, capacity, model_width),
            "exp",
            split_axis=0,
            concat_axis=0,
            tiled=True,
        ),
        lax.all_to_all(
            gate_grad.reshape(expert_count, capacity),
            "exp",
            split_axis=0,
            concat_axis=0,
            tiled=True,
        ),
    )
    picked_rows = back_rows.reshape(buffer_rows, model_width)[target]
    d_normed = jnp.sum(
        picked_rows.reshape(token_count, top_count, model_width).astype(jnp.float32), axis=1
    )
    picked_gate = (
        back_gate.reshape(buffer_rows)[target].astype(jnp.float32).reshape(token_count, top_count)
    )
    d_logit = gate_values * (
        picked_gate - jnp.sum(gate_values * picked_gate, axis=1, keepdims=True)
    )
    dense_logit = jnp.einsum("nk,nke->ne", d_logit, onehot, precision=highest)
    d_normed = d_normed + jnp.einsum(
        "ne,de->nd", dense_logit, router.astype(jnp.float32), precision=highest
    )
    grad_flat = norm_back(flat_rows, inverse, norm_gain, d_normed)
    grad_hidden = (
        grad_flat.reshape(1, local_passages, local_positions, model_width)
        + d_vector[None, :, None, :]
    )
    return (
        loss_value.reshape(1),
        own_score.reshape(1, local_passages),
        grad_hidden.astype(jnp.bfloat16),
    )


CORE, ACROSS_X, ACROSS_Y = 1, 2, 4
forward = (((1,), (0,)), ((), ()))
across = (((1,), (1,)), ((), ()))
MIB = 1 << 20


def swap(value, bit, size=8):
    return lax.ppermute(value, "exp", [(index, index ^ bit) for index in range(size)])


def whole_spec(array):
    zeros = (0,) * len(array.shape)
    return pl.BlockSpec(array.shape, lambda *step: zeros)


def scalar_spec():
    return pl.BlockSpec(memory_space=pltpu.SMEM)


def shape_of(shape, dtype):
    return jax.ShapeDtypeStruct(shape, dtype)


def kernel_call(body, name, outs, ins, in_specs=None, out_specs=None, grid=(1,), scratch=(), flops=0):
    moved = sum(math.prod(array.shape) * array.dtype.itemsize for array in tuple(ins) + tuple(outs))
    return pl.pallas_call(
        body,
        name=name,
        out_shape=outs,
        grid=grid,
        in_specs=in_specs or [whole_spec(array) for array in ins],
        out_specs=out_specs or [whole_spec(array) for array in outs],
        scratch_shapes=scratch,
        compiler_params=pltpu.CompilerParams(vmem_limit_bytes=32 * MIB),
        cost_estimate=pl.CostEstimate(flops=flops, bytes_accessed=moved, transcendentals=0),
    )(*ins)


def split_low(values):
    high = values.astype(jnp.bfloat16)
    rest = values - high.astype(jnp.float32)
    middle = rest.astype(jnp.bfloat16)
    low = (rest - middle.astype(jnp.float32)).astype(jnp.bfloat16)
    return high, middle, low


def exact_dot(values, low_matrix, contract):
    parts = lax.dot_general(
        jnp.concatenate(split_low(values), axis=0),
        low_matrix,
        contract,
        preferred_element_type=jnp.float32,
    )
    return parts[0:8] + parts[8:16] + parts[16:24]


def other_order(values, bits):
    row = lax.broadcasted_iota(jnp.int32, values.shape, 0)
    for bit in (1, 2, 4):
        if bits & bit:
            values = jnp.where(
                (row & bit) == 0, pltpu.roll(values, 8 - bit, 0), pltpu.roll(values, bit, 0)
            )
    return values


def norm_kernel(hidden_ref, gain_ref, whole_ref, low_ref, high_ref, sums_ref):
    rows = hidden_ref[...].astype(jnp.float32)
    normed = (rows * rms_scale(rows) * gain_ref[...]).astype(jnp.bfloat16)
    half = low_ref.shape[0]
    whole_ref[...] = normed
    low_ref[...] = normed[:half]
    high_ref[...] = normed[half:]
    sums_ref[...] = jnp.sum(rows, axis=0, keepdims=True)


def front_kernel(owners, last, expert_ref, router_ref, gate_ref, up_ref, *refs):
    count = len(owners)
    pieces, refs = refs[:count], refs[count:]
    if last:
        (sums_ref, down_ref, *earlier), refs = refs[:5], refs[5:]
    slope_ref, silu_ref, act_ref, gates_ref, part_ref, rows_ref, low_ref = refs[:7]
    step = pl.program_id(0)
    steps = pl.num_programs(0)
    size = pieces[0].shape[0]
    if last:
        down_full, part_full, copy_sem = refs[7:]
        copy = pltpu.make_async_copy(down_ref, down_full, copy_sem)

    @pl.when(step == 0)
    def start():
        if last:
            copy.start()
        for index, piece in enumerate(pieces):
            rows_ref[index * size : (index + 1) * size, :] = piece[...]
        logits = lax.dot_general(
            rows_ref[...], router_ref[...], across, preferred_element_type=jnp.float32
        )
        weights = jnp.exp(logits)
        gates = weights / jnp.sum(weights, axis=1, keepdims=True)
        gates_ref[...] = gates
        lane = lax.broadcasted_iota(jnp.int32, gates.shape, 1)
        own = jnp.sum(jnp.where(lane == expert_ref[0, 0], gates, 0.0), axis=1, keepdims=True)
        low_ref[...] = own.astype(jnp.bfloat16).astype(jnp.float32)

    rows = rows_ref[...]
    pre_gate = jnp.dot(rows, gate_ref[...], preferred_element_type=jnp.float32)
    pre_up = jnp.dot(rows, up_ref[...], preferred_element_type=jnp.float32)
    silu_gate, slope = gate_parts(pre_gate)
    activation = (silu_gate * pre_up).astype(jnp.bfloat16)
    slope_ref[...] = slope * pre_up
    silu_ref[...] = silu_gate
    act_ref[...] = activation
    weighted = activation.astype(jnp.float32) * low_ref[...]
    found = {}
    for index, owner in enumerate(owners):
        piece = jnp.sum(weighted[index * size : (index + 1) * size], axis=0, keepdims=True)
        found[owner] = found[owner] + piece if owner in found else piece
    nothing = jnp.zeros_like(weighted[:1])
    part = jnp.concatenate([found.get(owner, nothing) for owner in range(8)], axis=0)
    if not last:
        part_ref[...] = part
        return
    tile = part.shape[1]
    part_full[:, pl.ds(pl.multiple_of(step * tile, tile), tile)] = part

    @pl.when(step == steps - 1)
    def finish():
        copy.wait()
        total = part_full[...]
        for ref in earlier:
            total = total + ref[...]
        terms = exact_dot(total, down_full[...], forward)
        row = lax.broadcasted_iota(jnp.int32, terms.shape, 0)
        part_ref[...] = terms + jnp.where(row == 0, sums_ref[...], 0.0)


def front(owners, pieces, expert, router_rows, gate_matrix, up_matrix, last=()):
    size, model_width = pieces[0].shape
    row_total = size * len(pieces)
    hidden_units = gate_matrix.shape[1]
    tile = 256
    column = pl.BlockSpec((model_width, tile), lambda step: (0, step))
    saved = pl.BlockSpec((row_total, tile), lambda step: (0, step))
    ins = [expert, router_rows, gate_matrix, up_matrix, *pieces]
    in_specs = [scalar_spec(), whole_spec(router_rows), column, column]
    in_specs += [whole_spec(piece) for piece in pieces]
    outs = [
        shape_of((row_total, hidden_units), jnp.float32),
        shape_of((row_total, hidden_units), jnp.float32),
        shape_of((row_total, hidden_units), jnp.bfloat16),
        shape_of((row_total, 8), jnp.float32),
        shape_of((8, model_width if last else hidden_units), jnp.float32),
    ]
    out_specs = [saved, saved, saved, whole_spec(outs[3])]
    out_specs.append(
        whole_spec(outs[4]) if last else pl.BlockSpec((8, tile), lambda step: (0, step))
    )
    scratch = [
        pltpu.VMEM((row_total, model_width), jnp.bfloat16),
        pltpu.VMEM((row_total, 1), jnp.float32),
    ]
    if last:
        token_sums, down_matrix, *earlier = last
        ins += [token_sums, down_matrix, *earlier]
        in_specs += [whole_spec(token_sums), pl.BlockSpec(memory_space=pl.ANY)]
        in_specs += [whole_spec(part) for part in earlier]
        scratch += [
            pltpu.VMEM(down_matrix.shape, jnp.bfloat16),
            pltpu.VMEM((8, hidden_units), jnp.float32),
            pltpu.SemaphoreType.DMA,
        ]
    slope, silu, act, gates, part = kernel_call(
        functools.partial(front_kernel, owners, bool(last)),
        "front",
        outs,
        ins,
        in_specs,
        out_specs,
        (hidden_units // tile,),
        scratch,
        4 * row_total * hidden_units * model_width,
    )
    return (slope, silu, act, gates), part


def core_sum_kernel(own_ref, other_ref, out_ref):
    out_ref[...] = own_ref[...] + other_order(other_ref[...], CORE)


def near_kernel(
    own_ref, x_ref, y_ref, far_ref, gain_ref, vector_ref, down_ref,
    near_ref, unit_ref, score_ref, down_full, copy_sem, *, token_count,
):
    copy = pltpu.make_async_copy(down_ref, down_full, copy_sem)
    copy.start()
    pooled = (
        (own_ref[...] + other_order(x_ref[...], ACROSS_X))
        + (other_order(y_ref[...], ACROSS_Y) + other_order(far_ref[...], ACROSS_X | ACROSS_Y))
    ) / token_count
    head = gain_ref[...] * vector_ref[...].astype(jnp.float32)
    scale = rms_scale(pooled)
    along = jnp.sum(pooled * head, axis=1, keepdims=True)
    score_ref[...] = jnp.broadcast_to((scale * along)[:1], score_ref.shape)
    unit = (
        scale * head - scale * scale * scale * (along / pooled.shape[1]) * pooled
    ) / token_count
    unit_ref[...] = unit[:1]
    copy.wait()
    near_ref[...] = exact_dot(unit, down_full[...], across)


def back_kernel(
    owners, expert_ref, near_ref, gates_ref, slope_ref, silu_ref, act_ref, gate_ref, up_ref, *refs
):
    count = len(owners)
    pieces, (d_gate_ref, d_up_ref) = refs[:count], refs[count:]
    step = pl.program_id(0)
    size, wide = pieces[0].shape
    tile = gate_ref.shape[0]
    model_width = wide - 128

    @pl.when(step == 0)
    def start():
        for index, owner in enumerate(owners):
            rows = slice(index * size, (index + 1) * size)
            near = near_ref[owner : owner + 1, :]
            gates = gates_ref[rows, :]
            lane = lax.broadcasted_iota(jnp.int32, gates.shape, 1)
            own = jnp.sum(jnp.where(lane == expert_ref[0, 0], gates, 0.0), axis=1, keepdims=True)
            d_act = own.astype(jnp.bfloat16).astype(jnp.float32) * near
            d_gate_ref[rows, :] = (d_act * slope_ref[rows, :]).astype(jnp.bfloat16)
            d_up_ref[rows, :] = (d_act * silu_ref[rows, :]).astype(jnp.bfloat16)
            gate_grad = jnp.sum(act_ref[rows, :].astype(jnp.float32) * near, axis=1, keepdims=True)
            lane = lax.broadcasted_iota(jnp.int32, (size, 128), 1)
            pieces[index][:, model_width:] = jnp.where(
                lane == expert_ref[0, 0], gate_grad, 0.0
            ).astype(jnp.bfloat16)

    pick_grad = lax.dot_general(
        d_gate_ref[...], gate_ref[...], across, preferred_element_type=jnp.float32
    ) + lax.dot_general(d_up_ref[...], up_ref[...], across, preferred_element_type=jnp.float32)
    pick_grad = pick_grad.astype(jnp.bfloat16)
    columns = pl.ds(pl.multiple_of(step * tile, tile), tile)
    for index in range(count):
        pieces[index][:, columns] = pick_grad[index * size : (index + 1) * size]


def back(owners, saved, expert, near, gate_matrix, up_matrix):
    slope, silu, act, gates = saved
    row_total, hidden_units = slope.shape
    model_width = gate_matrix.shape[0]
    size = row_total // len(owners)
    tile = 512
    ins = [expert, near, gates, slope, silu, act, gate_matrix, up_matrix]
    weight = pl.BlockSpec((tile, hidden_units), lambda step: (step, 0))
    in_specs = [scalar_spec()] + [whole_spec(array) for array in ins[1:6]] + [weight, weight]
    return kernel_call(
        functools.partial(back_kernel, owners),
        "back",
        [shape_of((size, model_width + 128), jnp.bfloat16)] * len(owners),
        ins,
        in_specs,
        None,
        (model_width // tile,),
        [pltpu.VMEM((row_total, hidden_units), jnp.bfloat16)] * 2,
        4 * row_total * hidden_units * model_width,
    )


def end_kernel(
    factor_ref, own_ref, core_ref, x_low_ref, x_high_ref, y_low_ref, y_high_ref,
    hidden_ref, gain_ref, gates_ref, router_ref, unit_ref, grad_ref,
):
    half = x_low_ref.shape[0]
    model_width = hidden_ref.shape[1]
    router_rows = router_ref[...]
    for part, x_ref, y_ref in ((0, x_low_ref, y_low_ref), (1, x_high_ref, y_high_ref)):
        rows = slice(part * half, (part + 1) * half)
        total = (own_ref[rows, :].astype(jnp.float32) + core_ref[rows, :].astype(jnp.float32)) + (
            x_ref[...].astype(jnp.float32) + y_ref[...].astype(jnp.float32)
        )
        gates = gates_ref[rows, :]
        slot_grad = total[:, model_width : model_width + 8]
        d_logit = gates * (slot_grad - jnp.sum(gates * slot_grad, axis=1, keepdims=True))
        d_normed = total[:, :model_width]
        for share in split_low(d_logit):
            d_normed = d_normed + jnp.dot(
                share, router_rows, preferred_element_type=jnp.float32
            )
        flat_rows = hidden_ref[rows, :].astype(jnp.float32)
        grad = norm_back(flat_rows, rms_scale(flat_rows), gain_ref[...], d_normed) + unit_ref[...]
        grad_ref[rows, :] = (grad * factor_ref[0, 0]).astype(jnp.bfloat16)


def every_expert(
    hidden,
    norm_gain,
    router,
    gate_proj,
    up_proj,
    down_proj,
    final_gain,
    score_vector,
    expert_ids,
    grades,
    passage_ranks,
):
    unused_query, unused_passage, token_count, model_width = hidden.shape
    half = token_count // 2
    flat = hidden.reshape(token_count, model_width)
    gate_matrix, up_matrix, down_matrix = gate_proj[0], up_proj[0], down_proj[0]
    gain = norm_gain.reshape(1, model_width)
    router_rows = router.T
    expert = lax.axis_index("exp").astype(jnp.int32).reshape(1, 1)

    normed, low, high, token_sums = kernel_call(
        norm_kernel,
        "norm",
        [
            shape_of((token_count, model_width), jnp.bfloat16),
            shape_of((half, model_width), jnp.bfloat16),
            shape_of((half, model_width), jnp.bfloat16),
            shape_of((1, model_width), jnp.float32),
        ],
        [flat, gain],
    )
    x_low = swap(low, ACROSS_X)
    y_high = swap(high, ACROSS_Y)
    core = swap(normed, CORE)
    x_high = swap(high, ACROSS_X)
    y_low = swap(low, ACROSS_Y)
    far_low = swap(x_low, ACROSS_Y)
    far_high = swap(y_high, ACROSS_X)

    groups = [
        ((0, 1), [normed, core]),
        ((2, 4, 3, 5), [x_low, y_high, swap(x_low, CORE), swap(y_high, CORE)]),
        ((2, 4, 3, 5), [x_high, y_low, swap(x_high, CORE), swap(y_low, CORE)]),
        ((6, 6, 7, 7), [far_low, far_high, swap(far_low, CORE), swap(far_high, CORE)]),
    ]
    saved, parts = [], []
    for index, (owners, pieces) in enumerate(groups):
        last = (token_sums, down_matrix, *parts) if index == len(groups) - 1 else ()
        kept, part = front(owners, pieces, expert, router_rows, gate_matrix, up_matrix, last)
        saved.append(kept)
        parts.append(part)

    terms = parts[-1]
    (chip_terms,) = kernel_call(
        core_sum_kernel, "core_sum", [shape_of(terms.shape, jnp.float32)], [terms, swap(terms, CORE)]
    )
    ins = [
        chip_terms,
        swap(chip_terms, ACROSS_X),
        swap(chip_terms, ACROSS_Y),
        swap(chip_terms, ACROSS_X | ACROSS_Y),
        final_gain.reshape(1, model_width),
        score_vector.reshape(1, model_width),
        down_matrix,
    ]
    near, unit_vector, own_score = kernel_call(
        functools.partial(near_kernel, token_count=token_count),
        "near",
        [
            shape_of((8, down_matrix.shape[0]), jnp.float32),
            shape_of((1, model_width), jnp.float32),
            shape_of((1, 128), jnp.float32),
        ],
        ins,
        [whole_spec(array) for array in ins[:-1]] + [pl.BlockSpec(memory_space=pl.ANY)],
        scratch=[pltpu.VMEM(down_matrix.shape, jnp.bfloat16), pltpu.SemaphoreType.DMA],
    )

    def go_back(index):
        return back(groups[index][0], saved[index], expert, near, gate_matrix, up_matrix)

    def add(*arrays):
        total = sum(array.astype(jnp.float32) for array in arrays)
        return total.astype(jnp.bfloat16)

    far_low, far_high, other_low, other_high = go_back(3)
    far_low = swap(add(far_low, swap(other_low, CORE)), ACROSS_X)
    far_high = swap(add(far_high, swap(other_high, CORE)), ACROSS_Y)
    x_low, y_high, other_x, other_y = go_back(1)
    x_low = swap(add(x_low, swap(other_x, CORE)), ACROSS_X)
    y_high = swap(add(y_high, swap(other_y, CORE)), ACROSS_Y)
    x_high, y_low, other_x, other_y = go_back(2)
    x_high = swap(add(x_high, swap(other_x, CORE), far_high), ACROSS_X)
    y_low = swap(add(y_low, swap(other_y, CORE), far_low), ACROSS_Y)
    own, other = go_back(0)
    core = swap(other, CORE)

    place = lax.axis_index("psg")
    passages = grades.shape[1]
    every_score = own_score[0, :1] * (jnp.arange(passages) == place)
    for hop in range(1, passages):
        travelled = lax.ppermute(
            own_score, "psg", [(index, (index + hop) % passages) for index in range(passages)]
        )
        origin = (place - hop) % passages
        every_score = every_score + travelled[0, :1] * (jnp.arange(passages) == origin)
    loss_value, loss_grad = jax.value_and_grad(rank_loss)(every_score, grades[0], passage_ranks[0])
    factor = lax.dynamic_slice_in_dim(loss_grad, place, 1, 0) * loss_scale

    ins = [
        factor.reshape(1, 1), own, core, x_low, x_high, y_low, y_high,
        flat, gain, saved[0][3][:token_count], router_rows, unit_vector,
    ]
    (grad,) = kernel_call(
        end_kernel,
        "end",
        [shape_of((token_count, model_width), jnp.bfloat16)],
        ins,
        [scalar_spec()] + [whole_spec(array) for array in ins[1:]],
    )
    return (loss_value.reshape(1), own_score[:, :1], grad.reshape(hidden.shape))


def block(*arrays):
    hidden, router, expert_ids = arrays[0], arrays[2], arrays[8]
    if hidden.shape[1] == 1 and router.shape[1] == expert_ids.shape[3] == 8:
        return every_expert(*arrays)
    return local(*arrays)


def solution(mesh):
    placed = (
        P("exp", "psg", None, None),
        P(),
        P(),
        P("exp", None, None),
        P("exp", None, None),
        P("exp", None, None),
        P(),
        P(),
        P("exp", "psg", None, None),
        P("exp", None),
        P("exp", None),
    )
    return jax.shard_map(
        block,
        mesh=mesh,
        in_specs=placed,
        out_specs=(P("exp"), P("exp", "psg"), P("exp", "psg", None, None)),
        check_vma=False,
    )
```

```python
import functools
import math

import jax
import jax.numpy as jnp
from jax import lax
from jax.experimental import pallas as pl
from jax.experimental.pallas import tpu as pltpu
from jax.sharding import PartitionSpec as P

epsilon = 1e-06
loss_scale = 256.0
highest = lax.Precision.HIGHEST


def rms_scale(values):
    return lax.rsqrt(jnp.mean(values * values, axis=-1, keepdims=True) + epsilon)


def head_score(pooled, final_gain, score_vector):
    scaled = pooled * rms_scale(pooled) * final_gain
    return jnp.dot(scaled, score_vector.astype(jnp.float32), precision=highest)


def rank_loss(scores, grades, passage_ranks):
    grade_value = grades.astype(jnp.float32)
    worth_gain = jnp.exp2(grade_value)
    discount = 1.0 / jnp.log2(2.0 + passage_ranks.astype(jnp.float32))
    better_than = grades[None, :] > grades[:, None]
    equal_grade = grades[None, :] == grades[:, None]
    position = jnp.arange(grades.shape[0], dtype=jnp.int32)
    earlier = position[None, :] < position[:, None]
    ideal_rank = jnp.sum(
        jnp.logical_or(better_than, jnp.logical_and(equal_grade, earlier)).astype(jnp.float32),
        axis=1,
    )
    ideal_gain = jnp.sum((worth_gain - 1.0) / jnp.log2(2.0 + ideal_rank))
    ordered = (grades[:, None] > grades[None, :]).astype(jnp.float32)
    swap_gain = (
        jnp.abs(
            (worth_gain[:, None] - worth_gain[None, :]) * (discount[:, None] - discount[None, :])
        )
        / ideal_gain
    )
    margin = scores[:, None] - scores[None, :]
    return jnp.sum(ordered * swap_gain * jax.nn.softplus(-margin))


def pick_gates(normed, router, picked_ids):
    expert_total = router.shape[1]
    logits = jnp.dot(normed, router, preferred_element_type=jnp.float32)
    onehot = (
        picked_ids[:, :, None] == jnp.arange(expert_total, dtype=jnp.int32)[None, None, :]
    ).astype(jnp.float32)
    chosen = jnp.einsum("nke,ne->nk", onehot, logits, precision=highest)
    weights = jnp.exp(chosen)
    return (weights / jnp.sum(weights, axis=1, keepdims=True), onehot)


def gate_parts(pre_gate):
    sigmoid_gate = jax.nn.sigmoid(pre_gate)
    return (pre_gate * sigmoid_gate, sigmoid_gate * (1.0 + pre_gate * (1.0 - sigmoid_gate)))


def norm_back(flat_rows, inverse, norm_gain, d_normed):
    scaled = d_normed * norm_gain
    return inverse * scaled - flat_rows * inverse * inverse * inverse * jnp.mean(
        flat_rows * scaled, axis=-1, keepdims=True
    )


def unpack_front(front_out, buffer_rows):
    pre_gate, pre_up, received = front_out
    hidden_units = pre_gate.shape[2]
    pre_gate = pre_gate.reshape(buffer_rows, hidden_units)
    pre_up = pre_up.reshape(buffer_rows, hidden_units)
    silu_gate, slope = gate_parts(pre_gate)
    activation = (silu_gate * pre_up).astype(jnp.bfloat16)
    return (pre_up, received, silu_gate, slope, activation)


def local(
    hidden,
    norm_gain,
    router,
    gate_proj,
    up_proj,
    down_proj,
    final_gain,
    score_vector,
    expert_ids,
    grades,
    passage_ranks,
):
    unused_query, local_passages, local_positions, model_width = hidden.shape
    top_count = expert_ids.shape[3]
    expert_count = lax.axis_size("exp")
    token_count = local_passages * local_positions
    slot_count = token_count * top_count
    capacity = min(token_count, 9 * token_count * top_count // (8 * expert_count))
    buffer_rows = expert_count * capacity
    flat_rows = hidden.reshape(token_count, model_width).astype(jnp.float32)
    inverse = rms_scale(flat_rows)
    normed = (flat_rows * inverse * norm_gain).astype(jnp.bfloat16)
    picked_ids = expert_ids.reshape(token_count, top_count)
    gate_values, onehot = pick_gates(normed, router, picked_ids)
    slot_hits = onehot.reshape(slot_count, expert_count).astype(jnp.int32)
    slot_rank = jnp.sum((jnp.cumsum(slot_hits, axis=0) - slot_hits) * slot_hits, axis=1)
    target = picked_ids.reshape(slot_count) * capacity + slot_rank
    source_token = jnp.arange(slot_count, dtype=jnp.int32) // top_count
    passage_onehot = (
        source_token[:, None] // local_positions
        == jnp.arange(local_passages, dtype=jnp.int32)[None, :]
    ).astype(jnp.float32)
    weighted = (passage_onehot * gate_values.reshape(slot_count, 1)).astype(jnp.bfloat16)
    send_rows = (
        jnp.zeros((buffer_rows, model_width), jnp.bfloat16).at[target].set(normed[source_token])
    )
    send_weights = jnp.zeros((buffer_rows, local_passages), jnp.bfloat16).at[target].set(weighted)
    outgoing = (
        send_rows.reshape(expert_count, capacity, model_width),
        send_weights.reshape(expert_count, capacity, local_passages),
    )
    gate_matrix = gate_proj[0]
    up_matrix = up_proj[0]
    down_matrix = down_proj[0]
    rows_in = lax.all_to_all(outgoing[0], "exp", split_axis=0, concat_axis=0, tiled=True)
    weights_in = lax.all_to_all(outgoing[1], "exp", split_axis=0, concat_axis=0, tiled=True)
    pre_gate = jnp.einsum("end,df->enf", rows_in, gate_matrix, preferred_element_type=jnp.float32)
    pre_up = jnp.einsum("end,df->enf", rows_in, up_matrix, preferred_element_type=jnp.float32)
    front_out = (pre_gate, pre_up, weights_in)
    pre_up, received, silu_gate, slope, activation = unpack_front(front_out, buffer_rows)
    hidden_units = activation.shape[1]
    passage_part = jnp.einsum(
        "scp,scf->spf",
        received,
        activation.reshape(expert_count, capacity, hidden_units),
        preferred_element_type=jnp.float32,
    )
    down_wide = down_matrix.astype(jnp.float32)
    expert_terms = jnp.einsum("spf,fd->spd", passage_part, down_wide, precision=highest)
    came_back = lax.all_to_all(expert_terms, "exp", split_axis=0, concat_axis=0, tiled=True)
    token_sums = jnp.sum(flat_rows.reshape(local_passages, local_positions, model_width), axis=1)
    pooled = (token_sums + jnp.sum(came_back, axis=0)) / local_positions
    first_row = lax.axis_index("psg") * local_passages
    own_score = head_score(pooled, final_gain, score_vector)
    every_score = lax.all_gather(own_score, "psg", axis=0, tiled=True)
    loss_value, loss_grad = jax.value_and_grad(rank_loss)(every_score, grades[0], passage_ranks[0])
    d_own = lax.dynamic_slice_in_dim(loss_grad, first_row, local_passages, 0) * loss_scale
    unused_score, head_back = jax.vjp(
        lambda values: head_score(values, final_gain, score_vector), pooled
    )
    d_vector = head_back(d_own)[0] / local_positions
    every_vector = lax.all_gather(d_vector[None], "exp", axis=0, tiled=True)
    near_table = jnp.einsum("spd,fd->spf", every_vector, down_wide, precision=highest)
    present = (received != 0).astype(jnp.float32)
    near_rows = jnp.einsum("scp,spf->scf", present, near_table, precision=highest).reshape(
        buffer_rows, hidden_units
    )
    gate_weight = jnp.sum(received.astype(jnp.float32), axis=2).reshape(buffer_rows, 1)
    d_act = gate_weight * near_rows
    d_gate = (d_act * pre_up * slope).astype(jnp.bfloat16)
    d_up = (d_act * silu_gate).astype(jnp.bfloat16)
    contract = (((1,), (1,)), ((), ()))
    pick_grad = lax.dot_general(d_gate, gate_matrix, contract, preferred_element_type=jnp.float32)
    pick_grad = (
        pick_grad + lax.dot_general(d_up, up_matrix, contract, preferred_element_type=jnp.float32)
    ).astype(jnp.bfloat16)
    gate_grad = jnp.sum(activation.astype(jnp.float32) * near_rows, axis=1).astype(jnp.bfloat16)
    back_rows, back_gate = (
        lax.all_to_all(
            pick_grad.reshape(expert_count, capacity, model_width),
            "exp",
            split_axis=0,
            concat_axis=0,
            tiled=True,
        ),
        lax.all_to_all(
            gate_grad.reshape(expert_count, capacity),
            "exp",
            split_axis=0,
            concat_axis=0,
            tiled=True,
        ),
    )
    picked_rows = back_rows.reshape(buffer_rows, model_width)[target]
    d_normed = jnp.sum(
        picked_rows.reshape(token_count, top_count, model_width).astype(jnp.float32), axis=1
    )
    picked_gate = (
        back_gate.reshape(buffer_rows)[target].astype(jnp.float32).reshape(token_count, top_count)
    )
    d_logit = gate_values * (
        picked_gate - jnp.sum(gate_values * picked_gate, axis=1, keepdims=True)
    )
    dense_logit = jnp.einsum("nk,nke->ne", d_logit, onehot, precision=highest)
    d_normed = d_normed + jnp.einsum(
        "ne,de->nd", dense_logit, router.astype(jnp.float32), precision=highest
    )
    grad_flat = norm_back(flat_rows, inverse, norm_gain, d_normed)
    grad_hidden = (
        grad_flat.reshape(1, local_passages, local_positions, model_width)
        + d_vector[None, :, None, :]
    )
    return (
        loss_value.reshape(1),
        own_score.reshape(1, local_passages),
        grad_hidden.astype(jnp.bfloat16),
    )


CORE, ACROSS_X, ACROSS_Y = 1, 2, 4
forward = (((1,), (0,)), ((), ()))
across = (((1,), (1,)), ((), ()))
MIB = 1 << 20


def swap(value, bit, size=8):
    return lax.ppermute(value, "exp", [(index, index ^ bit) for index in range(size)])


def shape_of(shape, dtype):
    return jax.ShapeDtypeStruct(shape, dtype)


def after(value, *others):
    return lax.optimization_barrier((value, *others))[0]


def kernel_call(body, name, outs, ins, scalars=0, scratch=(), flops=0):
    moved = sum(math.prod(array.shape) * array.dtype.itemsize for array in tuple(ins) + tuple(outs))
    spaces = [pltpu.SMEM] * scalars + [pltpu.VMEM] * (len(ins) - scalars)
    return pl.pallas_call(
        body,
        name=name,
        out_shape=outs,
        in_specs=[pl.BlockSpec(memory_space=space) for space in spaces],
        out_specs=[pl.BlockSpec(memory_space=pltpu.VMEM)] * len(outs),
        scratch_shapes=scratch,
        compiler_params=pltpu.CompilerParams(vmem_limit_bytes=12 * MIB),
        cost_estimate=pl.CostEstimate(flops=flops, bytes_accessed=moved, transcendentals=0),
    )(*ins)


def split_low(values):
    high = values.astype(jnp.bfloat16)
    rest = values - high.astype(jnp.float32)
    middle = rest.astype(jnp.bfloat16)
    low = (rest - middle.astype(jnp.float32)).astype(jnp.bfloat16)
    return high, middle, low


def exact_dot(values, low_matrix, contract):
    parts = lax.dot_general(
        jnp.concatenate(split_low(values), axis=0),
        low_matrix,
        contract,
        preferred_element_type=jnp.float32,
    )
    return parts[0:8] + parts[8:16] + parts[16:24]


def other_order(values, bits):
    row = lax.broadcasted_iota(jnp.int32, values.shape, 0)
    for bit in (1, 2, 4):
        if bits & bit:
            values = jnp.where(
                (row & bit) == 0, pltpu.roll(values, 8 - bit, 0), pltpu.roll(values, bit, 0)
            )
    return values


def norm_kernel(hidden_ref, gain_ref, whole_ref, low_ref, high_ref, sums_ref):
    rows = hidden_ref[...].astype(jnp.float32)
    normed = (rows * rms_scale(rows) * gain_ref[...]).astype(jnp.bfloat16)
    half = low_ref.shape[0]
    whole_ref[...] = normed
    low_ref[...] = normed[:half]
    high_ref[...] = normed[half:]
    sums_ref[...] = jnp.sum(rows, axis=0, keepdims=True)


def front_kernel(owners, last, expert_ref, router_ref, gate_ref, up_ref, *refs):
    count = len(owners)
    pieces, refs = refs[:count], refs[count:]
    if last:
        (sums_ref, down_ref, *earlier), refs = refs[:5], refs[5:]
    slope_ref, silu_ref, act_ref, gates_ref, part_ref, rows_ref = refs
    size = pieces[0].shape[0]
    hidden_units = gate_ref.shape[1]
    for index, piece in enumerate(pieces):
        rows_ref[index * size : (index + 1) * size, :] = piece[...]
    logits = lax.dot_general(
        rows_ref[...], router_ref[...], across, preferred_element_type=jnp.float32
    )
    weights = jnp.exp(logits)
    gates = weights / jnp.sum(weights, axis=1, keepdims=True)
    gates_ref[...] = gates
    lane = lax.broadcasted_iota(jnp.int32, gates.shape, 1)
    own = jnp.sum(jnp.where(lane == expert_ref[0, 0], gates, 0.0), axis=1, keepdims=True)
    low = own.astype(jnp.bfloat16).astype(jnp.float32)

    parts = []
    for first in range(0, hidden_units, 256):
        columns = slice(first, first + 256)
        pre_gate = jnp.dot(rows_ref[...], gate_ref[:, columns], preferred_element_type=jnp.float32)
        pre_up = jnp.dot(rows_ref[...], up_ref[:, columns], preferred_element_type=jnp.float32)
        silu_gate, slope = gate_parts(pre_gate)
        activation = (silu_gate * pre_up).astype(jnp.bfloat16)
        slope_ref[:, columns] = slope * pre_up
        silu_ref[:, columns] = silu_gate
        act_ref[:, columns] = activation
        weighted = activation.astype(jnp.float32) * low
        found = {}
        for index, owner in enumerate(owners):
            piece = jnp.sum(weighted[index * size : (index + 1) * size], axis=0, keepdims=True)
            found[owner] = found[owner] + piece if owner in found else piece
        nothing = jnp.zeros_like(weighted[:1])
        parts.append(jnp.concatenate([found.get(owner, nothing) for owner in range(8)], axis=0))
    part = jnp.concatenate(parts, axis=1)
    if not last:
        part_ref[...] = part
        return
    for ref in earlier:
        part = part + ref[...]
    terms = exact_dot(part, down_ref[...], forward)
    row = lax.broadcasted_iota(jnp.int32, terms.shape, 0)
    part_ref[...] = terms + jnp.where(row == 0, sums_ref[...], 0.0)


def front(owners, pieces, expert, router_rows, gate_matrix, up_matrix, last=()):
    size, model_width = pieces[0].shape
    row_total = size * len(pieces)
    hidden_units = gate_matrix.shape[1]
    slope, silu, act, gates, part = kernel_call(
        functools.partial(front_kernel, owners, bool(last)),
        "front",
        [
            shape_of((row_total, hidden_units), jnp.float32),
            shape_of((row_total, hidden_units), jnp.float32),
            shape_of((row_total, hidden_units), jnp.bfloat16),
            shape_of((row_total, 8), jnp.float32),
            shape_of((8, model_width if last else hidden_units), jnp.float32),
        ],
        [expert, router_rows, gate_matrix, up_matrix, *pieces, *last],
        1,
        [pltpu.VMEM((row_total, model_width), jnp.bfloat16)],
        4 * row_total * hidden_units * model_width,
    )
    return (slope, silu, act, gates), part


def core_sum_kernel(own_ref, other_ref, out_ref):
    out_ref[...] = own_ref[...] + other_order(other_ref[...], CORE)


def near_kernel(
    own_ref, x_ref, y_ref, far_ref, gain_ref, vector_ref, down_ref,
    near_ref, unit_ref, score_ref, *, token_count,
):
    pooled = (
        (own_ref[...] + other_order(x_ref[...], ACROSS_X))
        + (other_order(y_ref[...], ACROSS_Y) + other_order(far_ref[...], ACROSS_X | ACROSS_Y))
    ) / token_count
    head = gain_ref[...] * vector_ref[...].astype(jnp.float32)
    scale = rms_scale(pooled)
    along = jnp.sum(pooled * head, axis=1, keepdims=True)
    score_ref[...] = jnp.broadcast_to((scale * along)[:1], score_ref.shape)
    unit = (
        scale * head - scale * scale * scale * (along / pooled.shape[1]) * pooled
    ) / token_count
    unit_ref[...] = unit[:1]
    near_ref[...] = exact_dot(unit, down_ref[...], across)


def back_kernel(
    owners, expert_ref, near_ref, gates_ref, slope_ref, silu_ref, act_ref, gate_ref, up_ref, *refs
):
    count = len(owners)
    pieces, (d_gate_ref, d_up_ref) = refs[:count], refs[count:]
    size, wide = pieces[0].shape
    model_width = wide - 128
    for index, owner in enumerate(owners):
        rows = slice(index * size, (index + 1) * size)
        near = near_ref[owner : owner + 1, :]
        gates = gates_ref[rows, :]
        lane = lax.broadcasted_iota(jnp.int32, gates.shape, 1)
        own = jnp.sum(jnp.where(lane == expert_ref[0, 0], gates, 0.0), axis=1, keepdims=True)
        d_act = own.astype(jnp.bfloat16).astype(jnp.float32) * near
        d_gate_ref[rows, :] = (d_act * slope_ref[rows, :]).astype(jnp.bfloat16)
        d_up_ref[rows, :] = (d_act * silu_ref[rows, :]).astype(jnp.bfloat16)
        gate_grad = jnp.sum(act_ref[rows, :].astype(jnp.float32) * near, axis=1, keepdims=True)
        lane = lax.broadcasted_iota(jnp.int32, (size, 128), 1)
        pieces[index][:, model_width:] = jnp.where(
            lane == expert_ref[0, 0], gate_grad, 0.0
        ).astype(jnp.bfloat16)

    for first in range(0, model_width, 256):
        columns = slice(first, first + 256)
        pick_grad = lax.dot_general(
            d_gate_ref[...], gate_ref[columns, :], across, preferred_element_type=jnp.float32
        ) + lax.dot_general(
            d_up_ref[...], up_ref[columns, :], across, preferred_element_type=jnp.float32
        )
        pick_grad = pick_grad.astype(jnp.bfloat16)
        for index in range(count):
            pieces[index][:, columns] = pick_grad[index * size : (index + 1) * size]


def back(owners, saved, expert, near, gate_matrix, up_matrix):
    slope, silu, act, gates = saved
    row_total, hidden_units = slope.shape
    model_width = gate_matrix.shape[0]
    size = row_total // len(owners)
    return kernel_call(
        functools.partial(back_kernel, owners),
        "back",
        [shape_of((size, model_width + 128), jnp.bfloat16)] * len(owners),
        [expert, near, gates, slope, silu, act, gate_matrix, up_matrix],
        1,
        [pltpu.VMEM((row_total, hidden_units), jnp.bfloat16)] * 2,
        4 * row_total * hidden_units * model_width,
    )


def end_kernel(
    factor_ref, own_ref, core_ref, x_low_ref, x_high_ref, y_low_ref, y_high_ref,
    hidden_ref, gain_ref, gates_ref, router_ref, unit_ref, grad_ref,
):
    half = x_low_ref.shape[0]
    model_width = hidden_ref.shape[1]
    router_rows = router_ref[...]
    for part, x_ref, y_ref in ((0, x_low_ref, y_low_ref), (1, x_high_ref, y_high_ref)):
        rows = slice(part * half, (part + 1) * half)
        total = (own_ref[rows, :].astype(jnp.float32) + core_ref[rows, :].astype(jnp.float32)) + (
            x_ref[...].astype(jnp.float32) + y_ref[...].astype(jnp.float32)
        )
        gates = gates_ref[rows, :]
        slot_grad = total[:, model_width : model_width + 8]
        d_logit = gates * (slot_grad - jnp.sum(gates * slot_grad, axis=1, keepdims=True))
        d_normed = total[:, :model_width]
        for share in split_low(d_logit):
            d_normed = d_normed + jnp.dot(
                share, router_rows, preferred_element_type=jnp.float32
            )
        flat_rows = hidden_ref[rows, :].astype(jnp.float32)
        grad = norm_back(flat_rows, rms_scale(flat_rows), gain_ref[...], d_normed) + unit_ref[...]
        grad_ref[rows, :] = (grad * factor_ref[0, 0]).astype(jnp.bfloat16)


def every_expert(
    hidden,
    norm_gain,
    router,
    gate_proj,
    up_proj,
    down_proj,
    final_gain,
    score_vector,
    expert_ids,
    grades,
    passage_ranks,
):
    unused_query, unused_passage, token_count, model_width = hidden.shape
    half = token_count // 2
    flat = hidden.reshape(token_count, model_width)
    gate_matrix, up_matrix, down_matrix = gate_proj[0], up_proj[0], down_proj[0]
    gain = norm_gain.reshape(1, model_width)
    router_rows = router.T
    expert = lax.axis_index("exp").astype(jnp.int32).reshape(1, 1)

    normed, low, high, token_sums = kernel_call(
        norm_kernel,
        "norm",
        [
            shape_of((token_count, model_width), jnp.bfloat16),
            shape_of((half, model_width), jnp.bfloat16),
            shape_of((half, model_width), jnp.bfloat16),
            shape_of((1, model_width), jnp.float32),
        ],
        [flat, gain],
    )
    x_low = swap(low, ACROSS_X)
    y_high = swap(high, ACROSS_Y)
    core = swap(normed, CORE)
    x_high = swap(high, ACROSS_X)
    y_low = swap(low, ACROSS_Y)

    saved, parts = [], []
    owners_of = ((0, 1), (2, 4, 3, 5), (2, 4, 3, 5), (6, 6, 7, 7))

    def go_on(*pieces):
        index = len(parts)
        last = (token_sums, down_matrix, *parts) if index == 3 else ()
        kept, part = front(
            owners_of[index], pieces, expert, router_rows, gate_matrix, up_matrix, last
        )
        saved.append(kept)
        parts.append(part)

    go_on(normed, core)
    x_low, y_high = after(x_low, parts[0]), after(y_high, parts[0])
    far_low = swap(x_low, ACROSS_Y)
    far_high = swap(y_high, ACROSS_X)
    go_on(x_low, y_high, swap(x_low, CORE), swap(y_high, CORE))
    x_high, y_low = after(x_high, parts[1]), after(y_low, parts[1])
    go_on(x_high, y_low, swap(x_high, CORE), swap(y_low, CORE))
    far_low, far_high = after(far_low, parts[2]), after(far_high, parts[2])
    go_on(far_low, far_high, swap(far_low, CORE), swap(far_high, CORE))

    terms = parts[-1]
    (chip_terms,) = kernel_call(
        core_sum_kernel, "core_sum", [shape_of(terms.shape, jnp.float32)], [terms, swap(terms, CORE)]
    )
    near, unit_vector, own_score = kernel_call(
        functools.partial(near_kernel, token_count=token_count),
        "near",
        [
            shape_of((8, down_matrix.shape[0]), jnp.float32),
            shape_of((1, model_width), jnp.float32),
            shape_of((1, 128), jnp.float32),
        ],
        [
            chip_terms,
            swap(chip_terms, ACROSS_X),
            swap(chip_terms, ACROSS_Y),
            swap(chip_terms, ACROSS_X | ACROSS_Y),
            final_gain.reshape(1, model_width),
            score_vector.reshape(1, model_width),
            down_matrix,
        ],
    )

    def go_back(index, *earlier):
        return back(
            owners_of[index], saved[index], expert, after(near, *earlier), gate_matrix, up_matrix
        )

    def add(*arrays):
        total = sum(array.astype(jnp.float32) for array in arrays)
        return total.astype(jnp.bfloat16)

    far_low, far_high, other_low, other_high = go_back(3)
    x_low, y_high, other_x, other_y = go_back(1, far_low)
    far_low = add(far_low, swap(other_low, CORE))
    far_high = add(far_high, swap(other_high, CORE))
    x_high, y_low, next_x, next_y = go_back(2, far_low, far_high)
    far_low = swap(far_low, ACROSS_X)
    far_high = swap(far_high, ACROSS_Y)
    x_low = add(x_low, swap(other_x, CORE))
    y_high = add(y_high, swap(other_y, CORE))
    own, other = go_back(0, x_low, y_high)
    x_low = swap(x_low, ACROSS_X)
    y_high = swap(y_high, ACROSS_Y)
    core = swap(other, CORE)
    x_high = add(x_high, swap(next_x, CORE), far_high)
    y_low = add(y_low, swap(next_y, CORE), far_low)
    own_score = after(own_score, own)
    x_high = swap(x_high, ACROSS_X)
    y_low = swap(y_low, ACROSS_Y)

    place = lax.axis_index("psg")
    passages = grades.shape[1]
    every_score = own_score[0, :1] * (jnp.arange(passages) == place)
    for hop in range(1, passages):
        travelled = lax.ppermute(
            own_score, "psg", [(index, (index + hop) % passages) for index in range(passages)]
        )
        origin = (place - hop) % passages
        every_score = every_score + travelled[0, :1] * (jnp.arange(passages) == origin)
    loss_value, loss_grad = jax.value_and_grad(rank_loss)(every_score, grades[0], passage_ranks[0])
    factor = lax.dynamic_slice_in_dim(loss_grad, place, 1, 0) * loss_scale

    (grad,) = kernel_call(
        end_kernel,
        "end",
        [shape_of((token_count, model_width), jnp.bfloat16)],
        [
            factor.reshape(1, 1), own, core, x_low, x_high, y_low, y_high,
            flat, gain, saved[0][3][:token_count], router_rows, unit_vector,
        ],
        1,
    )
    return (loss_value.reshape(1), own_score[:, :1], grad.reshape(hidden.shape))


def block(*arrays):
    hidden, router, expert_ids = arrays[0], arrays[2], arrays[8]
    if hidden.shape[1] == 1 and router.shape[1] == expert_ids.shape[3] == 8:
        return every_expert(*arrays)
    return local(*arrays)


def solution(mesh):
    placed = (
        P("exp", "psg", None, None),
        P(),
        P(),
        P("exp", None, None),
        P("exp", None, None),
        P("exp", None, None),
        P(),
        P(),
        P("exp", "psg", None, None),
        P("exp", None),
        P("exp", None),
    )
    return jax.shard_map(
        block,
        mesh=mesh,
        in_specs=placed,
        out_specs=(P("exp"), P("exp", "psg"), P("exp", "psg", None, None)),
        check_vma=False,
    )
```

```python
import functools
import math

import jax
import jax.numpy as jnp
from jax import lax
from jax.experimental import pallas as pl
from jax.experimental.pallas import tpu as pltpu
from jax.sharding import PartitionSpec as P

epsilon = 1e-06
loss_scale = 256.0
highest = lax.Precision.HIGHEST


def rms_scale(values):
    return lax.rsqrt(jnp.mean(values * values, axis=-1, keepdims=True) + epsilon)


def head_score(pooled, final_gain, score_vector):
    scaled = pooled * rms_scale(pooled) * final_gain
    return jnp.dot(scaled, score_vector.astype(jnp.float32), precision=highest)


def rank_loss(scores, grades, passage_ranks):
    grade_value = grades.astype(jnp.float32)
    worth_gain = jnp.exp2(grade_value)
    discount = 1.0 / jnp.log2(2.0 + passage_ranks.astype(jnp.float32))
    better_than = grades[None, :] > grades[:, None]
    equal_grade = grades[None, :] == grades[:, None]
    position = jnp.arange(grades.shape[0], dtype=jnp.int32)
    earlier = position[None, :] < position[:, None]
    ideal_rank = jnp.sum(
        jnp.logical_or(better_than, jnp.logical_and(equal_grade, earlier)).astype(jnp.float32),
        axis=1,
    )
    ideal_gain = jnp.sum((worth_gain - 1.0) / jnp.log2(2.0 + ideal_rank))
    ordered = (grades[:, None] > grades[None, :]).astype(jnp.float32)
    swap_gain = (
        jnp.abs(
            (worth_gain[:, None] - worth_gain[None, :]) * (discount[:, None] - discount[None, :])
        )
        / ideal_gain
    )
    margin = scores[:, None] - scores[None, :]
    return jnp.sum(ordered * swap_gain * jax.nn.softplus(-margin))


def pick_gates(normed, router, picked_ids):
    expert_total = router.shape[1]
    logits = jnp.dot(normed, router, preferred_element_type=jnp.float32)
    onehot = (
        picked_ids[:, :, None] == jnp.arange(expert_total, dtype=jnp.int32)[None, None, :]
    ).astype(jnp.float32)
    chosen = jnp.einsum("nke,ne->nk", onehot, logits, precision=highest)
    weights = jnp.exp(chosen)
    return (weights / jnp.sum(weights, axis=1, keepdims=True), onehot)


def gate_parts(pre_gate):
    sigmoid_gate = jax.nn.sigmoid(pre_gate)
    return (pre_gate * sigmoid_gate, sigmoid_gate * (1.0 + pre_gate * (1.0 - sigmoid_gate)))


def norm_back(flat_rows, inverse, norm_gain, d_normed):
    scaled = d_normed * norm_gain
    return inverse * scaled - flat_rows * inverse * inverse * inverse * jnp.mean(
        flat_rows * scaled, axis=-1, keepdims=True
    )


def unpack_front(front_out, buffer_rows):
    pre_gate, pre_up, received = front_out
    hidden_units = pre_gate.shape[2]
    pre_gate = pre_gate.reshape(buffer_rows, hidden_units)
    pre_up = pre_up.reshape(buffer_rows, hidden_units)
    silu_gate, slope = gate_parts(pre_gate)
    activation = (silu_gate * pre_up).astype(jnp.bfloat16)
    return (pre_up, received, silu_gate, slope, activation)


def local(
    hidden,
    norm_gain,
    router,
    gate_proj,
    up_proj,
    down_proj,
    final_gain,
    score_vector,
    expert_ids,
    grades,
    passage_ranks,
):
    unused_query, local_passages, local_positions, model_width = hidden.shape
    top_count = expert_ids.shape[3]
    expert_count = lax.axis_size("exp")
    token_count = local_passages * local_positions
    slot_count = token_count * top_count
    capacity = min(token_count, 9 * token_count * top_count // (8 * expert_count))
    buffer_rows = expert_count * capacity
    flat_rows = hidden.reshape(token_count, model_width).astype(jnp.float32)
    inverse = rms_scale(flat_rows)
    normed = (flat_rows * inverse * norm_gain).astype(jnp.bfloat16)
    picked_ids = expert_ids.reshape(token_count, top_count)
    gate_values, onehot = pick_gates(normed, router, picked_ids)
    slot_hits = onehot.reshape(slot_count, expert_count).astype(jnp.int32)
    slot_rank = jnp.sum((jnp.cumsum(slot_hits, axis=0) - slot_hits) * slot_hits, axis=1)
    target = picked_ids.reshape(slot_count) * capacity + slot_rank
    source_token = jnp.arange(slot_count, dtype=jnp.int32) // top_count
    passage_onehot = (
        source_token[:, None] // local_positions
        == jnp.arange(local_passages, dtype=jnp.int32)[None, :]
    ).astype(jnp.float32)
    weighted = (passage_onehot * gate_values.reshape(slot_count, 1)).astype(jnp.bfloat16)
    send_rows = (
        jnp.zeros((buffer_rows, model_width), jnp.bfloat16).at[target].set(normed[source_token])
    )
    send_weights = jnp.zeros((buffer_rows, local_passages), jnp.bfloat16).at[target].set(weighted)
    outgoing = (
        send_rows.reshape(expert_count, capacity, model_width),
        send_weights.reshape(expert_count, capacity, local_passages),
    )
    gate_matrix = gate_proj[0]
    up_matrix = up_proj[0]
    down_matrix = down_proj[0]
    rows_in = lax.all_to_all(outgoing[0], "exp", split_axis=0, concat_axis=0, tiled=True)
    weights_in = lax.all_to_all(outgoing[1], "exp", split_axis=0, concat_axis=0, tiled=True)
    pre_gate = jnp.einsum("end,df->enf", rows_in, gate_matrix, preferred_element_type=jnp.float32)
    pre_up = jnp.einsum("end,df->enf", rows_in, up_matrix, preferred_element_type=jnp.float32)
    front_out = (pre_gate, pre_up, weights_in)
    pre_up, received, silu_gate, slope, activation = unpack_front(front_out, buffer_rows)
    hidden_units = activation.shape[1]
    passage_part = jnp.einsum(
        "scp,scf->spf",
        received,
        activation.reshape(expert_count, capacity, hidden_units),
        preferred_element_type=jnp.float32,
    )
    down_wide = down_matrix.astype(jnp.float32)
    expert_terms = jnp.einsum("spf,fd->spd", passage_part, down_wide, precision=highest)
    came_back = lax.all_to_all(expert_terms, "exp", split_axis=0, concat_axis=0, tiled=True)
    token_sums = jnp.sum(flat_rows.reshape(local_passages, local_positions, model_width), axis=1)
    pooled = (token_sums + jnp.sum(came_back, axis=0)) / local_positions
    first_row = lax.axis_index("psg") * local_passages
    own_score = head_score(pooled, final_gain, score_vector)
    every_score = lax.all_gather(own_score, "psg", axis=0, tiled=True)
    loss_value, loss_grad = jax.value_and_grad(rank_loss)(every_score, grades[0], passage_ranks[0])
    d_own = lax.dynamic_slice_in_dim(loss_grad, first_row, local_passages, 0) * loss_scale
    unused_score, head_back = jax.vjp(
        lambda values: head_score(values, final_gain, score_vector), pooled
    )
    d_vector = head_back(d_own)[0] / local_positions
    every_vector = lax.all_gather(d_vector[None], "exp", axis=0, tiled=True)
    near_table = jnp.einsum("spd,fd->spf", every_vector, down_wide, precision=highest)
    present = (received != 0).astype(jnp.float32)
    near_rows = jnp.einsum("scp,spf->scf", present, near_table, precision=highest).reshape(
        buffer_rows, hidden_units
    )
    gate_weight = jnp.sum(received.astype(jnp.float32), axis=2).reshape(buffer_rows, 1)
    d_act = gate_weight * near_rows
    d_gate = (d_act * pre_up * slope).astype(jnp.bfloat16)
    d_up = (d_act * silu_gate).astype(jnp.bfloat16)
    contract = (((1,), (1,)), ((), ()))
    pick_grad = lax.dot_general(d_gate, gate_matrix, contract, preferred_element_type=jnp.float32)
    pick_grad = (
        pick_grad + lax.dot_general(d_up, up_matrix, contract, preferred_element_type=jnp.float32)
    ).astype(jnp.bfloat16)
    gate_grad = jnp.sum(activation.astype(jnp.float32) * near_rows, axis=1).astype(jnp.bfloat16)
    back_rows, back_gate = (
        lax.all_to_all(
            pick_grad.reshape(expert_count, capacity, model_width),
            "exp",
            split_axis=0,
            concat_axis=0,
            tiled=True,
        ),
        lax.all_to_all(
            gate_grad.reshape(expert_count, capacity),
            "exp",
            split_axis=0,
            concat_axis=0,
            tiled=True,
        ),
    )
    picked_rows = back_rows.reshape(buffer_rows, model_width)[target]
    d_normed = jnp.sum(
        picked_rows.reshape(token_count, top_count, model_width).astype(jnp.float32), axis=1
    )
    picked_gate = (
        back_gate.reshape(buffer_rows)[target].astype(jnp.float32).reshape(token_count, top_count)
    )
    d_logit = gate_values * (
        picked_gate - jnp.sum(gate_values * picked_gate, axis=1, keepdims=True)
    )
    dense_logit = jnp.einsum("nk,nke->ne", d_logit, onehot, precision=highest)
    d_normed = d_normed + jnp.einsum(
        "ne,de->nd", dense_logit, router.astype(jnp.float32), precision=highest
    )
    grad_flat = norm_back(flat_rows, inverse, norm_gain, d_normed)
    grad_hidden = (
        grad_flat.reshape(1, local_passages, local_positions, model_width)
        + d_vector[None, :, None, :]
    )
    return (
        loss_value.reshape(1),
        own_score.reshape(1, local_passages),
        grad_hidden.astype(jnp.bfloat16),
    )


CORE, ACROSS_X, ACROSS_Y = 1, 2, 4
forward = (((1,), (0,)), ((), ()))
across = (((1,), (1,)), ((), ()))
MIB = 1 << 20


def swap(value, bit, size=8):
    return lax.ppermute(value, "exp", [(index, index ^ bit) for index in range(size)])


def shape_of(shape, dtype):
    return jax.ShapeDtypeStruct(shape, dtype)


def after(value, *others):
    return lax.optimization_barrier((value, *others))[0]


def kept(shape, dtype):
    return pltpu.VMEM(shape, dtype)


def pinned(array):
    return pltpu.with_memory_space_constraint(array, pltpu.VMEM)


def kernel_call(body, name, outs, ins, scalars=0, far=(), scratch=(), flops=0):
    spaces = [pltpu.SMEM] * scalars + [pltpu.VMEM] * (len(ins) - scalars)
    ins = list(ins)
    for index in far:
        spaces[index] = pl.ANY
        ins[index] = pltpu.with_memory_space_constraint(ins[index], pltpu.HBM)
    return pl.pallas_call(
        body,
        name=name,
        out_shape=outs,
        in_specs=[pl.BlockSpec(memory_space=space) for space in spaces],
        out_specs=[pl.BlockSpec(memory_space=pltpu.VMEM)] * len(outs),
        scratch_shapes=scratch,
        compiler_params=pltpu.CompilerParams(vmem_limit_bytes=12 * MIB),
        cost_estimate=pl.CostEstimate(flops=flops, bytes_accessed=4 * MIB, transcendentals=0),
    )(*ins)


def split_low(values):
    high = values.astype(jnp.bfloat16)
    rest = values - high.astype(jnp.float32)
    middle = rest.astype(jnp.bfloat16)
    low = (rest - middle.astype(jnp.float32)).astype(jnp.bfloat16)
    return high, middle, low


def exact_dot(values, low_matrix, contract):
    parts = lax.dot_general(
        jnp.concatenate(split_low(values), axis=0),
        low_matrix,
        contract,
        preferred_element_type=jnp.float32,
    )
    return parts[0:8] + parts[8:16] + parts[16:24]


def other_order(values, bits):
    row = lax.broadcasted_iota(jnp.int32, values.shape, 0)
    for bit in (1, 2, 4):
        if bits & bit:
            values = jnp.where(
                (row & bit) == 0, pltpu.roll(values, 8 - bit, 0), pltpu.roll(values, bit, 0)
            )
    return values


def norm_kernel(
    hidden_far, gain_far, router_far,
    hidden_ref, gain_ref, router_ref, low_ref, high_ref, sums_ref, copy_sems,
):
    pairs = ((hidden_far, hidden_ref), (gain_far, gain_ref), (router_far, router_ref))
    copies = [
        pltpu.make_async_copy(source, target, copy_sems.at[index])
        for index, (source, target) in enumerate(pairs)
    ]
    for copy in copies:
        copy.start()
    for copy in copies:
        copy.wait()
    rows = hidden_ref[...].astype(jnp.float32)
    normed = (rows * rms_scale(rows) * gain_ref[...]).astype(jnp.bfloat16)
    half = low_ref.shape[0]
    low_ref[...] = normed[:half]
    high_ref[...] = normed[half:]
    sums_ref[...] = jnp.sum(rows, axis=0, keepdims=True)


def front_kernel(stage, owners, expert_ref, router_ref, gate_ref, up_ref, *refs):
    count = len(owners)
    pieces, refs = refs[:count], refs[count:]
    size = pieces[0].shape[0]
    hidden_units = gate_ref.shape[1]
    tile = 256
    firsts = range(0, hidden_units, tile)
    if stage == 0:
        gate_far, up_far = gate_ref, up_ref
        *refs, gate_ref, up_ref, rows_ref, copy_sems = refs
        copies = [
            pltpu.make_async_copy(
                source.at[:, first : first + tile],
                target.at[:, first : first + tile],
                copy_sems.at[which, number],
            )
            for number, first in enumerate(firsts)
            for which, (source, target) in enumerate(((gate_far, gate_ref), (up_far, up_ref)))
        ]
        for copy in copies:
            copy.start()
    elif stage == 1:
        down_far, *refs, down_ref, rows_ref, copy_sem = refs
        down_copy = pltpu.make_async_copy(down_far, down_ref, copy_sem)
        down_copy.start()
    elif stage == 3:
        sums_ref, down_ref, *earlier = refs[:5]
        *refs, rows_ref = refs[5:]
    else:
        *refs, rows_ref = refs
    slope_ref, silu_ref, act_ref, gates_ref, part_ref = refs
    for index, piece in enumerate(pieces):
        rows_ref[index * size : (index + 1) * size, :] = piece[...]
    logits = lax.dot_general(
        rows_ref[...], router_ref[...], across, preferred_element_type=jnp.float32
    )
    weights = jnp.exp(logits)
    gates = weights / jnp.sum(weights, axis=1, keepdims=True)
    gates_ref[...] = gates
    lane = lax.broadcasted_iota(jnp.int32, gates.shape, 1)
    own = jnp.sum(jnp.where(lane == expert_ref[0, 0], gates, 0.0), axis=1, keepdims=True)
    low = own.astype(jnp.bfloat16).astype(jnp.float32)

    parts = []
    for number, first in enumerate(firsts):
        columns = slice(first, first + tile)
        if stage == 0:
            copies[2 * number].wait()
            copies[2 * number + 1].wait()
        pre_gate = jnp.dot(rows_ref[...], gate_ref[:, columns], preferred_element_type=jnp.float32)
        pre_up = jnp.dot(rows_ref[...], up_ref[:, columns], preferred_element_type=jnp.float32)
        silu_gate, slope = gate_parts(pre_gate)
        activation = (silu_gate * pre_up).astype(jnp.bfloat16)
        slope_ref[:, columns] = slope * pre_up
        silu_ref[:, columns] = silu_gate
        act_ref[:, columns] = activation
        weighted = activation.astype(jnp.float32) * low
        found = {}
        for index, owner in enumerate(owners):
            piece = jnp.sum(weighted[index * size : (index + 1) * size], axis=0, keepdims=True)
            found[owner] = found[owner] + piece if owner in found else piece
        nothing = jnp.zeros_like(weighted[:1])
        parts.append(jnp.concatenate([found.get(owner, nothing) for owner in range(8)], axis=0))
    part = jnp.concatenate(parts, axis=1)
    if stage == 1:
        down_copy.wait()
    if stage < 3:
        part_ref[...] = part
        return
    for ref in earlier:
        part = part + ref[...]
    terms = exact_dot(part, down_ref[...], forward)
    row = lax.broadcasted_iota(jnp.int32, terms.shape, 0)
    part_ref[...] = terms + jnp.where(row == 0, sums_ref[...], 0.0)


def front(stage, owners, pieces, expert, router_rows, gate_matrix, up_matrix, more=()):
    size, model_width = pieces[0].shape
    row_total = size * len(pieces)
    hidden_units = gate_matrix.shape[1]
    outs = [
        kept((row_total, hidden_units), jnp.float32),
        kept((row_total, hidden_units), jnp.float32),
        kept((row_total, hidden_units), jnp.bfloat16),
        kept((row_total, 8), jnp.float32),
        kept((8, model_width if stage == 3 else hidden_units), jnp.float32),
    ]
    scratch = [pltpu.VMEM((row_total, model_width), jnp.bfloat16)]
    weights, far = [gate_matrix, up_matrix], ()
    if stage == 0:
        far = (2, 3)
        outs += [kept(gate_matrix.shape, jnp.bfloat16), kept(up_matrix.shape, jnp.bfloat16)]
        scratch.append(pltpu.SemaphoreType.DMA((2, hidden_units // 256)))
    else:
        weights = [pinned(matrix) for matrix in weights]
    if stage == 1:
        far = (4 + len(pieces),)
        outs.append(kept(more[0].shape, jnp.bfloat16))
        scratch.append(pltpu.SemaphoreType.DMA)
    if stage == 3:
        more = [pinned(array) for array in more]
    slope, silu, act, gates, part, *held = kernel_call(
        functools.partial(front_kernel, stage, owners),
        "front",
        outs,
        [expert, pinned(router_rows), *weights, *pieces, *more],
        1,
        far,
        scratch,
        4 * row_total * hidden_units * model_width,
    )
    return (slope, silu, act, gates), part, held


def core_sum_kernel(own_ref, other_ref, out_ref):
    out_ref[...] = own_ref[...] + other_order(other_ref[...], CORE)


def near_kernel(
    own_ref, x_ref, y_ref, far_ref, head_ref, down_ref,
    near_ref, unit_ref, score_ref, own_score_ref, *, token_count,
):
    pooled = (
        (own_ref[...] + other_order(x_ref[...], ACROSS_X))
        + (other_order(y_ref[...], ACROSS_Y) + other_order(far_ref[...], ACROSS_X | ACROSS_Y))
    ) / token_count
    head = head_ref[...]
    scale = rms_scale(pooled)
    along = jnp.sum(pooled * head, axis=1, keepdims=True)
    own_score = (scale * along)[:1]
    own_score_ref[...] = own_score
    score_ref[...] = jnp.broadcast_to(own_score, score_ref.shape)
    unit = (
        scale * head - scale * scale * scale * (along / pooled.shape[1]) * pooled
    ) / token_count
    unit_ref[...] = unit[:1]
    near_ref[...] = exact_dot(unit, down_ref[...], across)


def back_kernel(places, expert_ref, near_ref, gate_ref, up_ref, *refs):
    *saved, own_ref, other_ref, d_gate_ref, d_up_ref = refs
    rows_out, wide = own_ref.shape
    size = rows_out // 2
    model_width = wide - 128
    for index, (owner, number, first) in enumerate(places):
        slope_ref, silu_ref, act_ref, gates_ref = saved[4 * number : 4 * number + 4]
        rows = slice(index * size, (index + 1) * size)
        held = slice(first, first + size)
        near = near_ref[owner : owner + 1, :]
        gates = gates_ref[held, :]
        lane = lax.broadcasted_iota(jnp.int32, gates.shape, 1)
        own = jnp.sum(jnp.where(lane == expert_ref[0, 0], gates, 0.0), axis=1, keepdims=True)
        d_act = own.astype(jnp.bfloat16).astype(jnp.float32) * near
        d_gate_ref[rows, :] = (d_act * slope_ref[held, :]).astype(jnp.bfloat16)
        d_up_ref[rows, :] = (d_act * silu_ref[held, :]).astype(jnp.bfloat16)
        gate_grad = jnp.sum(act_ref[held, :].astype(jnp.float32) * near, axis=1, keepdims=True)
        lane = lax.broadcasted_iota(jnp.int32, (size, 128), 1)
        out_ref = own_ref if index < 2 else other_ref
        out_rows = slice((index % 2) * size, (index % 2 + 1) * size)
        out_ref[out_rows, model_width:] = jnp.where(
            lane == expert_ref[0, 0], gate_grad, 0.0
        ).astype(jnp.bfloat16)

    for first in range(0, model_width, 256):
        columns = slice(first, first + 256)
        pick_grad = lax.dot_general(
            d_gate_ref[...], gate_ref[columns, :], across, preferred_element_type=jnp.float32
        ) + lax.dot_general(
            d_up_ref[...], up_ref[columns, :], across, preferred_element_type=jnp.float32
        )
        pick_grad = pick_grad.astype(jnp.bfloat16)
        own_ref[:, columns] = pick_grad[:rows_out]
        other_ref[:, columns] = pick_grad[rows_out:]


def back(places, saved, expert, near, gate_matrix, up_matrix):
    hidden_units = gate_matrix.shape[1]
    model_width = gate_matrix.shape[0]
    rows_out = saved[0][0].shape[0] // 2
    arrays = [near, gate_matrix, up_matrix] + [array for group in saved for array in group]
    return kernel_call(
        functools.partial(back_kernel, places),
        "back",
        [kept((rows_out, model_width + 128), jnp.bfloat16)] * 2,
        [expert] + [pinned(array) for array in arrays],
        1,
        (),
        [pltpu.VMEM((2 * rows_out, hidden_units), jnp.bfloat16)] * 2,
        8 * rows_out * hidden_units * model_width,
    )


def add_kernel(own_ref, other_ref, *refs):
    *more, first_ref, second_ref = refs
    half = first_ref.shape[0]
    for index, out_ref in enumerate((first_ref, second_ref)):
        rows = slice(index * half, (index + 1) * half)
        total = own_ref[rows, :].astype(jnp.float32) + other_ref[rows, :].astype(jnp.float32)
        if more:
            total = total + more[index][...].astype(jnp.float32)
        out_ref[...] = total.astype(jnp.bfloat16)


def add_pieces(own, other, *more):
    rows, wide = own.shape
    return kernel_call(
        add_kernel,
        "add",
        [kept((rows // 2, wide), jnp.bfloat16)] * 2,
        [pinned(own), other, *more],
    )


def rank_kernel(place_ref, grades_ref, ranks_ref, *refs):
    *score_refs, loss_ref, factor_ref = refs
    passages = len(score_refs)
    place = place_ref[0, 0]
    row = lax.broadcasted_iota(jnp.int32, (8, 128), 0)
    lane = lax.broadcasted_iota(jnp.int32, (8, 128), 1)

    def spread(index, values):
        total = jnp.zeros((8, 128), jnp.float32)
        for number, value in values:
            total = jnp.where(index == number, value, total)
        return total

    grade_list = [(number, grades_ref[0, number].astype(jnp.float32)) for number in range(passages)]
    rank_list = [(number, ranks_ref[0, number].astype(jnp.float32)) for number in range(passages)]
    score_list = [
        ((place - hop + passages) % passages, jnp.broadcast_to(ref[...], (8, 128)))
        for hop, ref in enumerate(score_refs)
    ]
    grade_row, grade_lane = spread(row, grade_list), spread(lane, grade_list)
    worth_row, worth_lane = jnp.exp2(grade_row), jnp.exp2(grade_lane)
    discount_row = 1.0 / jnp.log2(2.0 + spread(row, rank_list))
    discount_lane = 1.0 / jnp.log2(2.0 + spread(lane, rank_list))
    score_row, score_lane = spread(row, score_list), spread(lane, score_list)
    pair = jnp.logical_and(row < passages, lane < passages)
    ahead = jnp.logical_or(
        grade_lane > grade_row, jnp.logical_and(grade_lane == grade_row, lane < row)
    )
    ideal_rank = jnp.sum(
        jnp.where(jnp.logical_and(pair, ahead), 1.0, 0.0), axis=1, keepdims=True
    )
    ideal_terms = (worth_row - 1.0) / jnp.log2(2.0 + ideal_rank)
    one_lane = jnp.logical_and(pair, lane == 0)

    def whole_sum(values):
        return jnp.sum(jnp.sum(values, axis=1, keepdims=True), axis=0, keepdims=True)

    ideal_gain = whole_sum(jnp.where(one_lane, ideal_terms, 0.0))
    swap_gain = (
        jnp.abs((worth_row - worth_lane) * (discount_row - discount_lane)) / ideal_gain
    )
    swap_gain = jnp.where(jnp.logical_and(pair, grade_row > grade_lane), swap_gain, 0.0)
    margin = score_row - score_lane
    softplus = jnp.maximum(-margin, 0.0) + jnp.log1p(jnp.exp(-jnp.abs(margin)))
    loss_ref[...] = whole_sum(swap_gain * softplus)
    pull = swap_gain * jax.nn.sigmoid(-margin)
    gradient = whole_sum(jnp.where(lane == place, pull, 0.0) - jnp.where(row == place, pull, 0.0))
    factor_ref[...] = jnp.broadcast_to(gradient * loss_scale, factor_ref.shape)


def end_kernel(
    factor_ref, own_ref, core_ref, x_low_ref, x_high_ref, y_low_ref, y_high_ref,
    hidden_ref, gain_ref, gates_ref, router_ref, unit_ref, grad_ref,
):
    half = x_low_ref.shape[0]
    model_width = hidden_ref.shape[1]
    router_rows = router_ref[...]
    for part, x_ref, y_ref in ((0, x_low_ref, y_low_ref), (1, x_high_ref, y_high_ref)):
        rows = slice(part * half, (part + 1) * half)
        total = (own_ref[rows, :].astype(jnp.float32) + core_ref[rows, :].astype(jnp.float32)) + (
            x_ref[...].astype(jnp.float32) + y_ref[...].astype(jnp.float32)
        )
        gates = gates_ref[rows, :]
        slot_grad = total[:, model_width : model_width + 8]
        d_logit = gates * (slot_grad - jnp.sum(gates * slot_grad, axis=1, keepdims=True))
        d_normed = total[:, :model_width]
        for share in split_low(d_logit):
            d_normed = d_normed + jnp.dot(
                share, router_rows, preferred_element_type=jnp.float32
            )
        flat_rows = hidden_ref[rows, :].astype(jnp.float32)
        grad = norm_back(flat_rows, rms_scale(flat_rows), gain_ref[...], d_normed) + unit_ref[...]
        grad_ref[rows, :] = (grad * factor_ref[:, :1]).astype(jnp.bfloat16)


def every_expert(
    hidden,
    norm_gain,
    router,
    gate_proj,
    up_proj,
    down_proj,
    final_gain,
    score_vector,
    expert_ids,
    grades,
    passage_ranks,
):
    unused_query, unused_passage, token_count, model_width = hidden.shape
    half = token_count // 2
    flat = hidden.reshape(token_count, model_width)
    gate_matrix, up_matrix, down_matrix = gate_proj[0], up_proj[0], down_proj[0]
    expert = lax.axis_index("exp").astype(jnp.int32).reshape(1, 1)

    piece = kept((half, model_width), jnp.bfloat16)
    flat, gain, router_rows, low, high, token_sums = kernel_call(
        norm_kernel,
        "norm",
        [
            kept(flat.shape, jnp.bfloat16),
            kept((1, model_width), jnp.float32),
            kept((8, model_width), jnp.bfloat16),
            piece,
            piece,
            kept((1, model_width), jnp.float32),
        ],
        [flat, norm_gain.reshape(1, model_width), router.T],
        0,
        (0, 1, 2),
        [pltpu.SemaphoreType.DMA((3,))],
    )
    x_low = swap(low, ACROSS_X)
    y_high = swap(high, ACROSS_Y)
    core_low, core_high = swap(low, CORE), swap(high, CORE)
    x_high = swap(high, ACROSS_X)
    y_low = swap(low, ACROSS_Y)
    pieces = (low, high, core_low, core_high)
    owners = (0, 0, 1, 1)
    saved, parts = [None] * 4, [None] * 4
    saved[0], parts[0], (gate_matrix, up_matrix) = front(
        0, owners, pieces, expert, router_rows, gate_matrix, up_matrix
    )
    head = final_gain * score_vector.astype(jnp.float32)
    x_low, y_high = after(x_low, parts[0]), after(y_high, parts[0])
    far_low = swap(x_low, ACROSS_Y)
    far_high = swap(y_high, ACROSS_X)
    pieces = (x_low, x_high, y_low, y_high)
    saved[1], parts[1], (down_matrix,) = front(
        1, (2, 2, 4, 4), pieces, expert, router_rows, gate_matrix, up_matrix, (down_matrix,)
    )
    pieces = tuple(swap(piece, CORE) for piece in pieces)
    far_low, far_high, head, *pieces = lax.optimization_barrier((far_low, far_high, head, *pieces))
    saved[2], parts[2], unused = front(
        2, (3, 3, 5, 5), pieces, expert, router_rows, gate_matrix, up_matrix
    )
    pieces = (far_low, far_high, swap(far_low, CORE), swap(far_high, CORE))
    saved[3], terms, unused = front(
        3, (6, 6, 7, 7), pieces, expert, router_rows, gate_matrix, up_matrix,
        (token_sums, down_matrix, *parts[:3]),
    )

    (chip_terms,) = kernel_call(
        core_sum_kernel, "core_sum", [kept(terms.shape, jnp.float32)], [pinned(terms), swap(terms, CORE)]
    )
    near, unit_vector, travelling, own_score = kernel_call(
        functools.partial(near_kernel, token_count=token_count),
        "near",
        [
            kept((8, down_matrix.shape[0]), jnp.float32),
            kept((1, model_width), jnp.float32),
            kept((1, 128), jnp.float32),
            shape_of((1, 1), jnp.float32),
        ],
        [
            pinned(chip_terms),
            swap(chip_terms, ACROSS_X),
            swap(chip_terms, ACROSS_Y),
            swap(chip_terms, ACROSS_X | ACROSS_Y),
            head.reshape(1, model_width),
            pinned(down_matrix),
        ],
    )

    def go_back(places, numbers, *earlier):
        groups = [saved[number] for number in numbers]
        return back(places, groups, expert, after(near, *earlier), gate_matrix, up_matrix)

    far, other_far = go_back(
        ((6, 0, 0), (6, 0, half), (7, 0, 2 * half), (7, 0, 3 * half)), (3,)
    )
    first, other_first = go_back(
        ((2, 0, 0), (4, 0, 3 * half), (3, 1, 0), (5, 1, 3 * half)), (1, 2), far
    )
    far_low, far_high = add_pieces(far, swap(other_far, CORE))
    second, other_second = go_back(
        ((2, 0, half), (4, 0, 2 * half), (3, 1, half), (5, 1, 2 * half)), (1, 2), far_low
    )
    far_low = swap(far_low, ACROSS_X)
    far_high = swap(far_high, ACROSS_Y)
    x_low, y_high = add_pieces(first, swap(other_first, CORE))
    x_low = swap(x_low, ACROSS_X)
    y_high = swap(y_high, ACROSS_Y)
    x_high, y_low = add_pieces(second, swap(other_second, CORE), far_high, far_low)
    own, other = go_back(
        ((0, 0, 0), (0, 0, half), (1, 0, 2 * half), (1, 0, 3 * half)), (0,), x_low, y_high, x_high
    )
    travelling = after(travelling, x_high, y_low)
    x_high = swap(x_high, ACROSS_X)
    y_low = swap(y_low, ACROSS_Y)
    core = swap(other, CORE)

    passages = grades.shape[1]
    every_score = [travelling]
    for hop in range(1, passages):
        every_score.append(
            lax.ppermute(
                travelling, "psg", [(index, (index + hop) % passages) for index in range(passages)]
            )
        )
    loss, factor = kernel_call(
        rank_kernel,
        "rank",
        [shape_of((1, 1), jnp.float32), kept((1, 128), jnp.float32)],
        [
            lax.axis_index("psg").astype(jnp.int32).reshape(1, 1),
            grades,
            passage_ranks,
            *every_score,
        ],
        3,
    )
    (grad,) = kernel_call(
        end_kernel,
        "end",
        [shape_of((token_count, model_width), jnp.bfloat16)],
        [
            pinned(factor), pinned(own), core, x_low, x_high, y_low, y_high,
            pinned(flat), pinned(gain), pinned(saved[0][3]), pinned(router_rows), pinned(unit_vector),
        ],
    )
    return (loss.reshape(1), own_score, grad.reshape(hidden.shape))


def block(*arrays):
    hidden, router, expert_ids = arrays[0], arrays[2], arrays[8]
    if hidden.shape[1] == 1 and router.shape[1] == expert_ids.shape[3] == 8:
        return every_expert(*arrays)
    return local(*arrays)


def solution(mesh):
    placed = (
        P("exp", "psg", None, None),
        P(),
        P(),
        P("exp", None, None),
        P("exp", None, None),
        P("exp", None, None),
        P(),
        P(),
        P("exp", "psg", None, None),
        P("exp", None),
        P("exp", None),
    )
    return jax.shard_map(
        block,
        mesh=mesh,
        in_specs=placed,
        out_specs=(P("exp"), P("exp", "psg"), P("exp", "psg", None, None)),
        check_vma=False,
    )
```

```python
import functools
import math

import jax
import jax.numpy as jnp
from jax import lax
from jax.experimental import pallas as pl
from jax.experimental.pallas import tpu as pltpu
from jax.sharding import PartitionSpec as P

epsilon = 1e-06
loss_scale = 256.0
highest = lax.Precision.HIGHEST


def rms_scale(values):
    return lax.rsqrt(jnp.mean(values * values, axis=-1, keepdims=True) + epsilon)


def head_score(pooled, final_gain, score_vector):
    scaled = pooled * rms_scale(pooled) * final_gain
    return jnp.dot(scaled, score_vector.astype(jnp.float32), precision=highest)


def rank_loss(scores, grades, passage_ranks):
    grade_value = grades.astype(jnp.float32)
    worth_gain = jnp.exp2(grade_value)
    discount = 1.0 / jnp.log2(2.0 + passage_ranks.astype(jnp.float32))
    better_than = grades[None, :] > grades[:, None]
    equal_grade = grades[None, :] == grades[:, None]
    position = jnp.arange(grades.shape[0], dtype=jnp.int32)
    earlier = position[None, :] < position[:, None]
    ideal_rank = jnp.sum(
        jnp.logical_or(better_than, jnp.logical_and(equal_grade, earlier)).astype(jnp.float32),
        axis=1,
    )
    ideal_gain = jnp.sum((worth_gain - 1.0) / jnp.log2(2.0 + ideal_rank))
    ordered = (grades[:, None] > grades[None, :]).astype(jnp.float32)
    swap_gain = (
        jnp.abs(
            (worth_gain[:, None] - worth_gain[None, :]) * (discount[:, None] - discount[None, :])
        )
        / ideal_gain
    )
    margin = scores[:, None] - scores[None, :]
    return jnp.sum(ordered * swap_gain * jax.nn.softplus(-margin))


def pick_gates(normed, router, picked_ids):
    expert_total = router.shape[1]
    logits = jnp.dot(normed, router, preferred_element_type=jnp.float32)
    onehot = (
        picked_ids[:, :, None] == jnp.arange(expert_total, dtype=jnp.int32)[None, None, :]
    ).astype(jnp.float32)
    chosen = jnp.einsum("nke,ne->nk", onehot, logits, precision=highest)
    weights = jnp.exp(chosen)
    return (weights / jnp.sum(weights, axis=1, keepdims=True), onehot)


def gate_parts(pre_gate):
    sigmoid_gate = jax.nn.sigmoid(pre_gate)
    return (pre_gate * sigmoid_gate, sigmoid_gate * (1.0 + pre_gate * (1.0 - sigmoid_gate)))


def norm_back(flat_rows, inverse, norm_gain, d_normed):
    scaled = d_normed * norm_gain
    return inverse * scaled - flat_rows * inverse * inverse * inverse * jnp.mean(
        flat_rows * scaled, axis=-1, keepdims=True
    )


def unpack_front(front_out, buffer_rows):
    pre_gate, pre_up, received = front_out
    hidden_units = pre_gate.shape[2]
    pre_gate = pre_gate.reshape(buffer_rows, hidden_units)
    pre_up = pre_up.reshape(buffer_rows, hidden_units)
    silu_gate, slope = gate_parts(pre_gate)
    activation = (silu_gate * pre_up).astype(jnp.bfloat16)
    return (pre_up, received, silu_gate, slope, activation)


def local(
    hidden,
    norm_gain,
    router,
    gate_proj,
    up_proj,
    down_proj,
    final_gain,
    score_vector,
    expert_ids,
    grades,
    passage_ranks,
):
    unused_query, local_passages, local_positions, model_width = hidden.shape
    top_count = expert_ids.shape[3]
    expert_count = lax.axis_size("exp")
    token_count = local_passages * local_positions
    slot_count = token_count * top_count
    capacity = min(token_count, 9 * token_count * top_count // (8 * expert_count))
    buffer_rows = expert_count * capacity
    flat_rows = hidden.reshape(token_count, model_width).astype(jnp.float32)
    inverse = rms_scale(flat_rows)
    normed = (flat_rows * inverse * norm_gain).astype(jnp.bfloat16)
    picked_ids = expert_ids.reshape(token_count, top_count)
    gate_values, onehot = pick_gates(normed, router, picked_ids)
    slot_hits = onehot.reshape(slot_count, expert_count).astype(jnp.int32)
    slot_rank = jnp.sum((jnp.cumsum(slot_hits, axis=0) - slot_hits) * slot_hits, axis=1)
    target = picked_ids.reshape(slot_count) * capacity + slot_rank
    source_token = jnp.arange(slot_count, dtype=jnp.int32) // top_count
    passage_onehot = (
        source_token[:, None] // local_positions
        == jnp.arange(local_passages, dtype=jnp.int32)[None, :]
    ).astype(jnp.float32)
    weighted = (passage_onehot * gate_values.reshape(slot_count, 1)).astype(jnp.bfloat16)
    send_rows = (
        jnp.zeros((buffer_rows, model_width), jnp.bfloat16).at[target].set(normed[source_token])
    )
    send_weights = jnp.zeros((buffer_rows, local_passages), jnp.bfloat16).at[target].set(weighted)
    outgoing = (
        send_rows.reshape(expert_count, capacity, model_width),
        send_weights.reshape(expert_count, capacity, local_passages),
    )
    gate_matrix = gate_proj[0]
    up_matrix = up_proj[0]
    down_matrix = down_proj[0]
    rows_in = lax.all_to_all(outgoing[0], "exp", split_axis=0, concat_axis=0, tiled=True)
    weights_in = lax.all_to_all(outgoing[1], "exp", split_axis=0, concat_axis=0, tiled=True)
    pre_gate = jnp.einsum("end,df->enf", rows_in, gate_matrix, preferred_element_type=jnp.float32)
    pre_up = jnp.einsum("end,df->enf", rows_in, up_matrix, preferred_element_type=jnp.float32)
    front_out = (pre_gate, pre_up, weights_in)
    pre_up, received, silu_gate, slope, activation = unpack_front(front_out, buffer_rows)
    hidden_units = activation.shape[1]
    passage_part = jnp.einsum(
        "scp,scf->spf",
        received,
        activation.reshape(expert_count, capacity, hidden_units),
        preferred_element_type=jnp.float32,
    )
    down_wide = down_matrix.astype(jnp.float32)
    expert_terms = jnp.einsum("spf,fd->spd", passage_part, down_wide, precision=highest)
    came_back = lax.all_to_all(expert_terms, "exp", split_axis=0, concat_axis=0, tiled=True)
    token_sums = jnp.sum(flat_rows.reshape(local_passages, local_positions, model_width), axis=1)
    pooled = (token_sums + jnp.sum(came_back, axis=0)) / local_positions
    first_row = lax.axis_index("psg") * local_passages
    own_score = head_score(pooled, final_gain, score_vector)
    every_score = lax.all_gather(own_score, "psg", axis=0, tiled=True)
    loss_value, loss_grad = jax.value_and_grad(rank_loss)(every_score, grades[0], passage_ranks[0])
    d_own = lax.dynamic_slice_in_dim(loss_grad, first_row, local_passages, 0) * loss_scale
    unused_score, head_back = jax.vjp(
        lambda values: head_score(values, final_gain, score_vector), pooled
    )
    d_vector = head_back(d_own)[0] / local_positions
    every_vector = lax.all_gather(d_vector[None], "exp", axis=0, tiled=True)
    near_table = jnp.einsum("spd,fd->spf", every_vector, down_wide, precision=highest)
    present = (received != 0).astype(jnp.float32)
    near_rows = jnp.einsum("scp,spf->scf", present, near_table, precision=highest).reshape(
        buffer_rows, hidden_units
    )
    gate_weight = jnp.sum(received.astype(jnp.float32), axis=2).reshape(buffer_rows, 1)
    d_act = gate_weight * near_rows
    d_gate = (d_act * pre_up * slope).astype(jnp.bfloat16)
    d_up = (d_act * silu_gate).astype(jnp.bfloat16)
    contract = (((1,), (1,)), ((), ()))
    pick_grad = lax.dot_general(d_gate, gate_matrix, contract, preferred_element_type=jnp.float32)
    pick_grad = (
        pick_grad + lax.dot_general(d_up, up_matrix, contract, preferred_element_type=jnp.float32)
    ).astype(jnp.bfloat16)
    gate_grad = jnp.sum(activation.astype(jnp.float32) * near_rows, axis=1).astype(jnp.bfloat16)
    back_rows, back_gate = (
        lax.all_to_all(
            pick_grad.reshape(expert_count, capacity, model_width),
            "exp",
            split_axis=0,
            concat_axis=0,
            tiled=True,
        ),
        lax.all_to_all(
            gate_grad.reshape(expert_count, capacity),
            "exp",
            split_axis=0,
            concat_axis=0,
            tiled=True,
        ),
    )
    picked_rows = back_rows.reshape(buffer_rows, model_width)[target]
    d_normed = jnp.sum(
        picked_rows.reshape(token_count, top_count, model_width).astype(jnp.float32), axis=1
    )
    picked_gate = (
        back_gate.reshape(buffer_rows)[target].astype(jnp.float32).reshape(token_count, top_count)
    )
    d_logit = gate_values * (
        picked_gate - jnp.sum(gate_values * picked_gate, axis=1, keepdims=True)
    )
    dense_logit = jnp.einsum("nk,nke->ne", d_logit, onehot, precision=highest)
    d_normed = d_normed + jnp.einsum(
        "ne,de->nd", dense_logit, router.astype(jnp.float32), precision=highest
    )
    grad_flat = norm_back(flat_rows, inverse, norm_gain, d_normed)
    grad_hidden = (
        grad_flat.reshape(1, local_passages, local_positions, model_width)
        + d_vector[None, :, None, :]
    )
    return (
        loss_value.reshape(1),
        own_score.reshape(1, local_passages),
        grad_hidden.astype(jnp.bfloat16),
    )


CORE, ACROSS_X, ACROSS_Y = 1, 2, 4
forward = (((1,), (0,)), ((), ()))
across = (((1,), (1,)), ((), ()))
MIB = 1 << 20


def swap(value, bit, size=8):
    return lax.ppermute(value, "exp", [(index, index ^ bit) for index in range(size)])


def shape_of(shape, dtype):
    return jax.ShapeDtypeStruct(shape, dtype)


def after(value, *others):
    return lax.optimization_barrier((value, *others))[0]


def kept(shape, dtype):
    return pltpu.VMEM(shape, dtype)


def pinned(array):
    return pltpu.with_memory_space_constraint(array, pltpu.VMEM)


def kernel_call(body, name, outs, ins, scalars=0, far=(), scratch=()):
    spaces = [pltpu.SMEM] * scalars + [pltpu.VMEM] * (len(ins) - scalars)
    ins = list(ins)
    for index in far:
        spaces[index] = pl.ANY
        ins[index] = pltpu.with_memory_space_constraint(ins[index], pltpu.HBM)
    return pl.pallas_call(
        body,
        name=name,
        out_shape=outs,
        in_specs=[pl.BlockSpec(memory_space=space) for space in spaces],
        out_specs=[pl.BlockSpec(memory_space=pltpu.VMEM)] * len(outs),
        scratch_shapes=scratch,
        compiler_params=pltpu.CompilerParams(vmem_limit_bytes=12 * MIB),
        cost_estimate=pl.CostEstimate(flops=1, bytes_accessed=1, transcendentals=0),
    )(*ins)


def split_low(values):
    high = values.astype(jnp.bfloat16)
    rest = values - high.astype(jnp.float32)
    middle = rest.astype(jnp.bfloat16)
    low = (rest - middle.astype(jnp.float32)).astype(jnp.bfloat16)
    return high, middle, low


def exact_dot(values, low_matrix, contract):
    parts = lax.dot_general(
        jnp.concatenate(split_low(values), axis=0),
        low_matrix,
        contract,
        preferred_element_type=jnp.float32,
    )
    return parts[0:8] + parts[8:16] + parts[16:24]


def other_order(values, bits):
    row = lax.broadcasted_iota(jnp.int32, values.shape, 0)
    for bit in (1, 2, 4):
        if bits & bit:
            values = jnp.where(
                (row & bit) == 0, pltpu.roll(values, 8 - bit, 0), pltpu.roll(values, bit, 0)
            )
    return values


def norm_kernel(
    hidden_far, gain_far, router_far,
    hidden_ref, gain_ref, router_ref, normed_ref, sums_ref, copy_sems,
):
    pairs = ((hidden_far, hidden_ref), (gain_far, gain_ref), (router_far, router_ref))
    copies = [
        pltpu.make_async_copy(source, target, copy_sems.at[index])
        for index, (source, target) in enumerate(pairs)
    ]
    for copy in copies:
        copy.start()
    for copy in copies:
        copy.wait()
    rows = hidden_ref[...].astype(jnp.float32)
    normed_ref[...] = (rows * rms_scale(rows) * gain_ref[...]).astype(jnp.bfloat16)
    sums_ref[...] = jnp.sum(rows, axis=0, keepdims=True)


def front_kernel(stage, owners, count, expert_ref, router_ref, gate_ref, up_ref, *refs):
    pieces, refs = refs[:count], refs[count:]
    hidden_units = gate_ref.shape[1]
    tile = 256
    firsts = range(0, hidden_units, tile)
    if stage == 0:
        gate_far, up_far = gate_ref, up_ref
        *refs, gate_ref, up_ref, rows_ref, copy_sems = refs
        copies = [
            pltpu.make_async_copy(
                source.at[:, first : first + tile],
                target.at[:, first : first + tile],
                copy_sems.at[which, number],
            )
            for number, first in enumerate(firsts)
            for which, (source, target) in enumerate(((gate_far, gate_ref), (up_far, up_ref)))
        ]
        for copy in copies:
            copy.start()
    elif stage == 1:
        down_far, *refs, down_ref, rows_ref, copy_sem = refs
        down_copy = pltpu.make_async_copy(down_far, down_ref, copy_sem)
        down_copy.start()
    elif stage == 3:
        sums_ref, down_ref, *earlier = refs[:5]
        *refs, rows_ref = refs[5:]
    else:
        *refs, rows_ref = refs
    slope_ref, silu_ref, act_ref, gates_ref, part_ref = refs
    first = 0
    for piece in pieces:
        rows_ref[first : first + piece.shape[0], :] = piece[...]
        first += piece.shape[0]
    size = first // len(owners)
    logits = lax.dot_general(
        rows_ref[...], router_ref[...], across, preferred_element_type=jnp.float32
    )
    weights = jnp.exp(logits)
    gates = weights / jnp.sum(weights, axis=1, keepdims=True)
    gates_ref[...] = gates
    lane = lax.broadcasted_iota(jnp.int32, gates.shape, 1)
    own = jnp.sum(jnp.where(lane == expert_ref[0, 0], gates, 0.0), axis=1, keepdims=True)
    low = own.astype(jnp.bfloat16).astype(jnp.float32)

    parts = []
    for number, first in enumerate(firsts):
        columns = slice(first, first + tile)
        if stage == 0:
            copies[2 * number].wait()
            copies[2 * number + 1].wait()
        pre_gate = jnp.dot(rows_ref[...], gate_ref[:, columns], preferred_element_type=jnp.float32)
        pre_up = jnp.dot(rows_ref[...], up_ref[:, columns], preferred_element_type=jnp.float32)
        silu_gate, slope = gate_parts(pre_gate)
        activation = (silu_gate * pre_up).astype(jnp.bfloat16)
        slope_ref[:, columns] = slope * pre_up
        silu_ref[:, columns] = silu_gate
        act_ref[:, columns] = activation
        weighted = activation.astype(jnp.float32) * low
        found = {}
        for index, owner in enumerate(owners):
            piece = jnp.sum(weighted[index * size : (index + 1) * size], axis=0, keepdims=True)
            found[owner] = found[owner] + piece if owner in found else piece
        nothing = jnp.zeros_like(weighted[:1])
        parts.append(jnp.concatenate([found.get(owner, nothing) for owner in range(8)], axis=0))
    part = jnp.concatenate(parts, axis=1)
    if stage == 1:
        down_copy.wait()
    if stage < 3:
        part_ref[...] = part
        return
    for ref in earlier:
        part = part + ref[...]
    terms = exact_dot(part, down_ref[...], forward)
    row = lax.broadcasted_iota(jnp.int32, terms.shape, 0)
    part_ref[...] = terms + jnp.where(row == 0, sums_ref[...], 0.0)


def front(stage, owners, pieces, expert, router_rows, gate_matrix, up_matrix, more=()):
    model_width, hidden_units = gate_matrix.shape
    row_total = sum(piece.shape[0] for piece in pieces)
    outs = [
        kept((row_total, hidden_units), jnp.float32),
        kept((row_total, hidden_units), jnp.float32),
        kept((row_total, hidden_units), jnp.bfloat16),
        kept((row_total, 8), jnp.float32),
        kept((8, model_width if stage == 3 else hidden_units), jnp.float32),
    ]
    scratch = [pltpu.VMEM((row_total, model_width), jnp.bfloat16)]
    weights, far = [gate_matrix, up_matrix], ()
    if stage == 0:
        far = (2, 3)
        outs += [kept(gate_matrix.shape, jnp.bfloat16), kept(up_matrix.shape, jnp.bfloat16)]
        scratch.append(pltpu.SemaphoreType.DMA((2, hidden_units // 256)))
    else:
        weights = [pinned(matrix) for matrix in weights]
    if stage == 1:
        far = (4 + len(pieces),)
        outs.append(kept(more[0].shape, jnp.bfloat16))
        scratch.append(pltpu.SemaphoreType.DMA)
    if stage == 3:
        more = [pinned(array) for array in more]
    slope, silu, act, gates, part, *held = kernel_call(
        functools.partial(front_kernel, stage, owners, len(pieces)),
        "front",
        outs,
        [expert, pinned(router_rows), *weights, *pieces, *more],
        1,
        far,
        scratch,
    )
    return (slope, silu, act, gates), part, held


def core_sum_kernel(own_ref, other_ref, out_ref):
    out_ref[...] = own_ref[...] + other_order(other_ref[...], CORE)


def near_kernel(
    own_ref, x_ref, y_ref, far_ref, head_ref, down_ref,
    near_ref, unit_ref, score_ref, own_score_ref, *, token_count,
):
    pooled = (
        (own_ref[...] + other_order(x_ref[...], ACROSS_X))
        + (other_order(y_ref[...], ACROSS_Y) + other_order(far_ref[...], ACROSS_X | ACROSS_Y))
    ) / token_count
    head = head_ref[...]
    scale = rms_scale(pooled)
    along = jnp.sum(pooled * head, axis=1, keepdims=True)
    own_score = (scale * along)[:1]
    own_score_ref[...] = own_score
    score_ref[...] = jnp.broadcast_to(own_score, score_ref.shape)
    unit = (
        scale * head - scale * scale * scale * (along / pooled.shape[1]) * pooled
    ) / token_count
    unit_ref[...] = unit[:1]
    near_ref[...] = exact_dot(unit, down_ref[...], across)


def back_kernel(owners, start, expert_ref, near_ref, gate_ref, up_ref, *refs):
    slope_ref, silu_ref, act_ref, gates_ref, *out_refs, d_gate_ref, d_up_ref = refs
    size = d_gate_ref.shape[0] // len(owners)
    rows_out, wide = out_refs[0].shape
    model_width = wide - 128
    for index, owner in enumerate(owners):
        rows = slice(index * size, (index + 1) * size)
        held = slice(start + index * size, start + (index + 1) * size)
        near = near_ref[owner : owner + 1, :]
        gates = gates_ref[held, :]
        lane = lax.broadcasted_iota(jnp.int32, gates.shape, 1)
        own = jnp.sum(jnp.where(lane == expert_ref[0, 0], gates, 0.0), axis=1, keepdims=True)
        d_act = own.astype(jnp.bfloat16).astype(jnp.float32) * near
        d_gate_ref[rows, :] = (d_act * slope_ref[held, :]).astype(jnp.bfloat16)
        d_up_ref[rows, :] = (d_act * silu_ref[held, :]).astype(jnp.bfloat16)
        gate_grad = jnp.sum(act_ref[held, :].astype(jnp.float32) * near, axis=1, keepdims=True)
        lane = lax.broadcasted_iota(jnp.int32, (size, 128), 1)
        out_ref, first = out_refs[index * size // rows_out], index * size % rows_out
        out_ref[first : first + size, model_width:] = jnp.where(
            lane == expert_ref[0, 0], gate_grad, 0.0
        ).astype(jnp.bfloat16)

    for first in range(0, model_width, 256):
        columns = slice(first, first + 256)
        pick_grad = lax.dot_general(
            d_gate_ref[...], gate_ref[columns, :], across, preferred_element_type=jnp.float32
        ) + lax.dot_general(
            d_up_ref[...], up_ref[columns, :], across, preferred_element_type=jnp.float32
        )
        pick_grad = pick_grad.astype(jnp.bfloat16)
        for index, out_ref in enumerate(out_refs):
            out_ref[:, columns] = pick_grad[index * rows_out : (index + 1) * rows_out]


def back(owners, saved, expert, near, gate_matrix, up_matrix, parts, start):
    model_width, hidden_units = gate_matrix.shape
    row_total = len(owners) * (saved[0].shape[0] // 4)
    return kernel_call(
        functools.partial(back_kernel, owners, start),
        "back",
        [kept((row_total // parts, model_width + 128), jnp.bfloat16)] * parts,
        [expert] + [pinned(array) for array in (near, gate_matrix, up_matrix, *saved)],
        1,
        (),
        [pltpu.VMEM((row_total, hidden_units), jnp.bfloat16)] * 2,
    )


def add_kernel(own_ref, other_ref, *refs):
    *more, first_ref, second_ref = refs
    size = first_ref.shape[0]
    half = size // 2
    for index, out_ref in enumerate((first_ref, second_ref)):
        for part in range(2):
            rows = slice(part * half, (part + 1) * half)
            held = slice(index * size + part * half, index * size + (part + 1) * half)
            total = own_ref[held, :].astype(jnp.float32) + other_ref[held, :].astype(jnp.float32)
            if more and index + part == 1:
                total = total + more[index][...].astype(jnp.float32)
            out_ref[rows, :] = total.astype(jnp.bfloat16)


def add_pieces(own, other, *more):
    rows, wide = own.shape
    return kernel_call(
        add_kernel,
        "add",
        [kept((rows // 2, wide), jnp.bfloat16)] * 2,
        [pinned(own), other, *more],
    )


def split_kernel(x_ref, y_ref, low_ref, high_ref):
    half = low_ref.shape[0]
    low_ref[...] = x_ref[:half, :]
    high_ref[...] = y_ref[half:, :]


def pack_kernel(first_ref, second_ref, out_ref):
    rows = first_ref.shape[0]
    out_ref[:rows, :] = first_ref[...]
    out_ref[rows:, :] = second_ref[...]


def pack(first, second):
    rows, wide = first.shape
    return kernel_call(
        pack_kernel, "pack", [kept((2 * rows, wide), first.dtype)], [first, second]
    )[0]


def rank_kernel(place_ref, grades_far, ranks_far, *refs):
    near_scores_ref, far_scores_ref, loss_ref, factor_ref, grades_ref, ranks_ref, copy_sems = refs
    copies = [
        pltpu.make_async_copy(grades_far, grades_ref, copy_sems.at[0]),
        pltpu.make_async_copy(ranks_far, ranks_ref, copy_sems.at[1]),
    ]
    for copy in copies:
        copy.start()
    for copy in copies:
        copy.wait()
    passages = grades_ref.shape[1]
    place = place_ref[0, 0]
    row = lax.broadcasted_iota(jnp.int32, (8, 128), 0)
    lane = lax.broadcasted_iota(jnp.int32, (8, 128), 1)

    def spread(index, values):
        total = jnp.zeros((8, 128), jnp.float32)
        for number, value in values:
            total = jnp.where(index == number, value, total)
        return total

    grade_list = [(number, grades_ref[0, number].astype(jnp.float32)) for number in range(passages)]
    rank_list = [(number, ranks_ref[0, number].astype(jnp.float32)) for number in range(passages)]
    score_list = [
        (place ^ (base + number), jnp.broadcast_to(ref[number : number + 1, :], (8, 128)))
        for base, ref in ((0, near_scores_ref), (passages // 2, far_scores_ref))
        for number in range(passages // 2)
    ]
    grade_row, grade_lane = spread(row, grade_list), spread(lane, grade_list)
    worth_row, worth_lane = jnp.exp2(grade_row), jnp.exp2(grade_lane)
    discount_row = 1.0 / jnp.log2(2.0 + spread(row, rank_list))
    discount_lane = 1.0 / jnp.log2(2.0 + spread(lane, rank_list))
    score_row, score_lane = spread(row, score_list), spread(lane, score_list)
    pair = jnp.logical_and(row < passages, lane < passages)
    ahead = jnp.logical_or(
        grade_lane > grade_row, jnp.logical_and(grade_lane == grade_row, lane < row)
    )
    ideal_rank = jnp.sum(
        jnp.where(jnp.logical_and(pair, ahead), 1.0, 0.0), axis=1, keepdims=True
    )
    ideal_terms = (worth_row - 1.0) / jnp.log2(2.0 + ideal_rank)
    one_lane = jnp.logical_and(pair, lane == 0)

    def whole_sum(values):
        return jnp.sum(jnp.sum(values, axis=1, keepdims=True), axis=0, keepdims=True)

    ideal_gain = whole_sum(jnp.where(one_lane, ideal_terms, 0.0))
    swap_gain = (
        jnp.abs((worth_row - worth_lane) * (discount_row - discount_lane)) / ideal_gain
    )
    swap_gain = jnp.where(jnp.logical_and(pair, grade_row > grade_lane), swap_gain, 0.0)
    margin = score_row - score_lane
    softplus = jnp.maximum(-margin, 0.0) + jnp.log1p(jnp.exp(-jnp.abs(margin)))
    loss_ref[...] = whole_sum(swap_gain * softplus)
    pull = swap_gain * jax.nn.sigmoid(-margin)
    gradient = whole_sum(jnp.where(lane == place, pull, 0.0) - jnp.where(row == place, pull, 0.0))
    factor_ref[...] = jnp.broadcast_to(gradient * loss_scale, factor_ref.shape)


def end_kernel(
    factor_ref, own_ref, core_ref, x_ref, y_ref,
    hidden_ref, gain_ref, gates_ref, router_ref, unit_ref, grad_ref,
):
    half = hidden_ref.shape[0] // 2
    model_width = hidden_ref.shape[1]
    router_rows = jnp.concatenate([router_ref[...]] * 3, axis=0)
    for part in range(2):
        rows = slice(part * half, (part + 1) * half)
        total = (own_ref[rows, :].astype(jnp.float32) + core_ref[rows, :].astype(jnp.float32)) + (
            x_ref[rows, :].astype(jnp.float32) + y_ref[rows, :].astype(jnp.float32)
        )
        gates = gates_ref[rows, :]
        slot_grad = total[:, model_width : model_width + 8]
        d_logit = gates * (slot_grad - jnp.sum(gates * slot_grad, axis=1, keepdims=True))
        d_normed = total[:, :model_width]
        d_normed = d_normed + jnp.dot(
            jnp.concatenate(split_low(d_logit), axis=1),
            router_rows,
            preferred_element_type=jnp.float32,
        )
        flat_rows = hidden_ref[rows, :].astype(jnp.float32)
        grad = norm_back(flat_rows, rms_scale(flat_rows), gain_ref[...], d_normed) + unit_ref[...]
        grad_ref[rows, :] = (grad * factor_ref[:, :1]).astype(jnp.bfloat16)


def every_expert(
    hidden,
    norm_gain,
    router,
    gate_proj,
    up_proj,
    down_proj,
    final_gain,
    score_vector,
    expert_ids,
    grades,
    passage_ranks,
):
    unused_query, unused_passage, token_count, model_width = hidden.shape
    half = token_count // 2
    passages = grades.shape[1]
    flat = hidden.reshape(token_count, model_width)
    gate_matrix, up_matrix, down_matrix = gate_proj[0], up_proj[0], down_proj[0]
    expert = lax.axis_index("exp").astype(jnp.int32).reshape(1, 1)
    own_owners, side_owners, other_side_owners, far_owners = (
        (0, 0, 1, 1), (2, 2, 4, 4), (3, 3, 5, 5), (6, 6, 7, 7)
    )

    flat, gain, router_rows, normed, token_sums = kernel_call(
        norm_kernel,
        "norm",
        [
            kept(flat.shape, jnp.bfloat16),
            kept((1, model_width), jnp.float32),
            kept((8, model_width), jnp.bfloat16),
            kept(flat.shape, jnp.bfloat16),
            kept((1, model_width), jnp.float32),
        ],
        [flat, norm_gain.reshape(1, model_width), router.T],
        0,
        (0, 1, 2),
        [pltpu.SemaphoreType.DMA((3,))],
    )
    x_rows, y_rows, core_rows = (swap(normed, bit) for bit in (ACROSS_X, ACROSS_Y, CORE))
    saved, parts = [None] * 4, [None] * 4
    saved[0], parts[0], (gate_matrix, up_matrix) = front(
        0, own_owners, (normed, core_rows), expert, router_rows, gate_matrix, up_matrix
    )
    head = final_gain * score_vector.astype(jnp.float32)
    x_rows, y_rows, (head, unused) = lax.optimization_barrier((x_rows, y_rows, (head, parts[0])))
    piece = kept((half, model_width), jnp.bfloat16)
    x_low, y_high = kernel_call(split_kernel, "split", [piece] * 2, [x_rows, y_rows])
    far_low = swap(x_low, ACROSS_Y)
    far_high = swap(y_high, ACROSS_X)
    saved[1], parts[1], (down_matrix,) = front(
        1, side_owners, (x_rows, y_rows), expert, router_rows, gate_matrix, up_matrix,
        (down_matrix,),
    )
    pieces = (after(swap(x_rows, CORE), parts[1]), swap(y_rows, CORE))
    saved[2], parts[2], unused = front(
        2, other_side_owners, pieces, expert, router_rows, gate_matrix, up_matrix
    )
    far_low, far_high = after(far_low, parts[2]), after(far_high, parts[2])
    pieces = (far_low, far_high, swap(pack(far_low, far_high), CORE))
    saved[3], terms, unused = front(
        3, far_owners, pieces, expert, router_rows, gate_matrix, up_matrix,
        (token_sums, down_matrix, *parts[:3]),
    )

    (chip_terms,) = kernel_call(
        core_sum_kernel, "core_sum", [kept(terms.shape, jnp.float32)], [pinned(terms), swap(terms, CORE)]
    )
    near, unit_vector, travelling, own_score = kernel_call(
        functools.partial(near_kernel, token_count=token_count),
        "near",
        [
            kept((8, down_matrix.shape[0]), jnp.float32),
            kept((1, model_width), jnp.float32),
            kept((1, 128), jnp.float32),
            shape_of((1, 1), jnp.float32),
        ],
        [
            pinned(chip_terms),
            swap(chip_terms, ACROSS_X),
            swap(chip_terms, ACROSS_Y),
            swap(chip_terms, ACROSS_X | ACROSS_Y),
            head.reshape(1, model_width),
            pinned(down_matrix),
        ],
    )

    def go_back(owners, group, parts, *earlier, start=0):
        return back(
            owners, saved[group], expert, after(near, *earlier), gate_matrix, up_matrix, parts,
            start,
        )

    (other_far,) = go_back(far_owners[2:], 3, 1, start=token_count)
    (far,) = go_back(far_owners[:2], 3, 1)
    far_sums = add_pieces(far, swap(other_far, CORE))
    far_low = swap(far_sums[0], ACROSS_X)
    far_high = swap(far_sums[1], ACROSS_Y)
    (other_sides,) = go_back(other_side_owners, 2, 1, far_sums[0])
    (sides,) = go_back(side_owners, 1, 1, other_sides)
    other_sides = swap(other_sides, CORE)
    own, other = go_back(own_owners, 0, 2, sides)
    travelling = after(travelling, far_sums[0])
    met = lax.ppermute(travelling, "psg", [(index, index ^ 1) for index in range(passages)])
    near_scores = pack(travelling, met)
    far_scores = lax.ppermute(near_scores, "psg", [(index, index ^ 2) for index in range(passages)])
    loss, factor = kernel_call(
        rank_kernel,
        "rank",
        [shape_of((1, 1), jnp.float32), kept((1, 128), jnp.float32)],
        [
            lax.axis_index("psg").astype(jnp.int32).reshape(1, 1),
            grades,
            passage_ranks,
            pinned(near_scores),
            far_scores,
        ],
        1,
        (1, 2),
        [
            pltpu.SMEM(grades.shape, jnp.int32),
            pltpu.SMEM(grades.shape, jnp.int32),
            pltpu.SemaphoreType.DMA((2,)),
        ],
    )
    sides, unused = lax.optimization_barrier((sides, (own, factor)))
    x_sums, y_sums = add_pieces(sides, other_sides, far_high, far_low)
    x_sums, y_sums = swap(x_sums, ACROSS_X), swap(y_sums, ACROSS_Y)
    core_sums = swap(other, CORE)
    (grad,) = kernel_call(
        end_kernel,
        "end",
        [shape_of((token_count, model_width), jnp.bfloat16)],
        [
            pinned(factor), pinned(own), core_sums, x_sums, y_sums,
            pinned(flat), pinned(gain), pinned(saved[0][3]), pinned(router_rows), pinned(unit_vector),
        ],
    )
    return (loss.reshape(1), own_score, grad.reshape(hidden.shape))


def block(*arrays):
    hidden, router, expert_ids, grades = arrays[0], arrays[2], arrays[8], arrays[9]
    each_expert = router.shape[1] == expert_ids.shape[3] == 8
    if hidden.shape[1] == 1 and each_expert and grades.shape[1] == 4:
        return every_expert(*arrays)
    return local(*arrays)


def solution(mesh):
    placed = (
        P("exp", "psg", None, None),
        P(),
        P(),
        P("exp", None, None),
        P("exp", None, None),
        P("exp", None, None),
        P(),
        P(),
        P("exp", "psg", None, None),
        P("exp", None),
        P("exp", None),
    )
    return jax.shard_map(
        block,
        mesh=mesh,
        in_specs=placed,
        out_specs=(P("exp"), P("exp", "psg"), P("exp", "psg", None, None)),
        check_vma=False,
    )
```

```python
import functools
import math

import jax
import jax.numpy as jnp
from jax import lax
from jax.experimental import pallas as pl
from jax.experimental.pallas import tpu as pltpu
from jax.sharding import PartitionSpec as P

epsilon = 1e-06
loss_scale = 256.0
highest = lax.Precision.HIGHEST


def rms_scale(values):
    return lax.rsqrt(jnp.mean(values * values, axis=-1, keepdims=True) + epsilon)


def head_score(pooled, final_gain, score_vector):
    scaled = pooled * rms_scale(pooled) * final_gain
    return jnp.dot(scaled, score_vector.astype(jnp.float32), precision=highest)


def rank_loss(scores, grades, passage_ranks):
    grade_value = grades.astype(jnp.float32)
    worth_gain = jnp.exp2(grade_value)
    discount = 1.0 / jnp.log2(2.0 + passage_ranks.astype(jnp.float32))
    better_than = grades[None, :] > grades[:, None]
    equal_grade = grades[None, :] == grades[:, None]
    position = jnp.arange(grades.shape[0], dtype=jnp.int32)
    earlier = position[None, :] < position[:, None]
    ideal_rank = jnp.sum(
        jnp.logical_or(better_than, jnp.logical_and(equal_grade, earlier)).astype(jnp.float32),
        axis=1,
    )
    ideal_gain = jnp.sum((worth_gain - 1.0) / jnp.log2(2.0 + ideal_rank))
    ordered = (grades[:, None] > grades[None, :]).astype(jnp.float32)
    swap_gain = (
        jnp.abs(
            (worth_gain[:, None] - worth_gain[None, :]) * (discount[:, None] - discount[None, :])
        )
        / ideal_gain
    )
    margin = scores[:, None] - scores[None, :]
    return jnp.sum(ordered * swap_gain * jax.nn.softplus(-margin))


def pick_gates(normed, router, picked_ids):
    expert_total = router.shape[1]
    logits = jnp.dot(normed, router, preferred_element_type=jnp.float32)
    onehot = (
        picked_ids[:, :, None] == jnp.arange(expert_total, dtype=jnp.int32)[None, None, :]
    ).astype(jnp.float32)
    chosen = jnp.einsum("nke,ne->nk", onehot, logits, precision=highest)
    weights = jnp.exp(chosen)
    return (weights / jnp.sum(weights, axis=1, keepdims=True), onehot)


def gate_parts(pre_gate):
    sigmoid_gate = jax.nn.sigmoid(pre_gate)
    return (pre_gate * sigmoid_gate, sigmoid_gate * (1.0 + pre_gate * (1.0 - sigmoid_gate)))


def norm_back(flat_rows, inverse, norm_gain, d_normed):
    scaled = d_normed * norm_gain
    return inverse * scaled - flat_rows * inverse * inverse * inverse * jnp.mean(
        flat_rows * scaled, axis=-1, keepdims=True
    )


def unpack_front(front_out, buffer_rows):
    pre_gate, pre_up, received = front_out
    hidden_units = pre_gate.shape[2]
    pre_gate = pre_gate.reshape(buffer_rows, hidden_units)
    pre_up = pre_up.reshape(buffer_rows, hidden_units)
    silu_gate, slope = gate_parts(pre_gate)
    activation = (silu_gate * pre_up).astype(jnp.bfloat16)
    return (pre_up, received, silu_gate, slope, activation)


def local(
    hidden,
    norm_gain,
    router,
    gate_proj,
    up_proj,
    down_proj,
    final_gain,
    score_vector,
    expert_ids,
    grades,
    passage_ranks,
):
    unused_query, local_passages, local_positions, model_width = hidden.shape
    top_count = expert_ids.shape[3]
    expert_count = lax.axis_size("exp")
    token_count = local_passages * local_positions
    slot_count = token_count * top_count
    capacity = min(token_count, 9 * token_count * top_count // (8 * expert_count))
    buffer_rows = expert_count * capacity
    flat_rows = hidden.reshape(token_count, model_width).astype(jnp.float32)
    inverse = rms_scale(flat_rows)
    normed = (flat_rows * inverse * norm_gain).astype(jnp.bfloat16)
    picked_ids = expert_ids.reshape(token_count, top_count)
    gate_values, onehot = pick_gates(normed, router, picked_ids)
    slot_hits = onehot.reshape(slot_count, expert_count).astype(jnp.int32)
    slot_rank = jnp.sum((jnp.cumsum(slot_hits, axis=0) - slot_hits) * slot_hits, axis=1)
    target = picked_ids.reshape(slot_count) * capacity + slot_rank
    source_token = jnp.arange(slot_count, dtype=jnp.int32) // top_count
    passage_onehot = (
        source_token[:, None] // local_positions
        == jnp.arange(local_passages, dtype=jnp.int32)[None, :]
    ).astype(jnp.float32)
    weighted = (passage_onehot * gate_values.reshape(slot_count, 1)).astype(jnp.bfloat16)
    send_rows = (
        jnp.zeros((buffer_rows, model_width), jnp.bfloat16).at[target].set(normed[source_token])
    )
    send_weights = jnp.zeros((buffer_rows, local_passages), jnp.bfloat16).at[target].set(weighted)
    outgoing = (
        send_rows.reshape(expert_count, capacity, model_width),
        send_weights.reshape(expert_count, capacity, local_passages),
    )
    gate_matrix = gate_proj[0]
    up_matrix = up_proj[0]
    down_matrix = down_proj[0]
    rows_in = lax.all_to_all(outgoing[0], "exp", split_axis=0, concat_axis=0, tiled=True)
    weights_in = lax.all_to_all(outgoing[1], "exp", split_axis=0, concat_axis=0, tiled=True)
    pre_gate = jnp.einsum("end,df->enf", rows_in, gate_matrix, preferred_element_type=jnp.float32)
    pre_up = jnp.einsum("end,df->enf", rows_in, up_matrix, preferred_element_type=jnp.float32)
    front_out = (pre_gate, pre_up, weights_in)
    pre_up, received, silu_gate, slope, activation = unpack_front(front_out, buffer_rows)
    hidden_units = activation.shape[1]
    passage_part = jnp.einsum(
        "scp,scf->spf",
        received,
        activation.reshape(expert_count, capacity, hidden_units),
        preferred_element_type=jnp.float32,
    )
    down_wide = down_matrix.astype(jnp.float32)
    expert_terms = jnp.einsum("spf,fd->spd", passage_part, down_wide, precision=highest)
    came_back = lax.all_to_all(expert_terms, "exp", split_axis=0, concat_axis=0, tiled=True)
    token_sums = jnp.sum(flat_rows.reshape(local_passages, local_positions, model_width), axis=1)
    pooled = (token_sums + jnp.sum(came_back, axis=0)) / local_positions
    first_row = lax.axis_index("psg") * local_passages
    own_score = head_score(pooled, final_gain, score_vector)
    every_score = lax.all_gather(own_score, "psg", axis=0, tiled=True)
    loss_value, loss_grad = jax.value_and_grad(rank_loss)(every_score, grades[0], passage_ranks[0])
    d_own = lax.dynamic_slice_in_dim(loss_grad, first_row, local_passages, 0) * loss_scale
    unused_score, head_back = jax.vjp(
        lambda values: head_score(values, final_gain, score_vector), pooled
    )
    d_vector = head_back(d_own)[0] / local_positions
    every_vector = lax.all_gather(d_vector[None], "exp", axis=0, tiled=True)
    near_table = jnp.einsum("spd,fd->spf", every_vector, down_wide, precision=highest)
    present = (received != 0).astype(jnp.float32)
    near_rows = jnp.einsum("scp,spf->scf", present, near_table, precision=highest).reshape(
        buffer_rows, hidden_units
    )
    gate_weight = jnp.sum(received.astype(jnp.float32), axis=2).reshape(buffer_rows, 1)
    d_act = gate_weight * near_rows
    d_gate = (d_act * pre_up * slope).astype(jnp.bfloat16)
    d_up = (d_act * silu_gate).astype(jnp.bfloat16)
    contract = (((1,), (1,)), ((), ()))
    pick_grad = lax.dot_general(d_gate, gate_matrix, contract, preferred_element_type=jnp.float32)
    pick_grad = (
        pick_grad + lax.dot_general(d_up, up_matrix, contract, preferred_element_type=jnp.float32)
    ).astype(jnp.bfloat16)
    gate_grad = jnp.sum(activation.astype(jnp.float32) * near_rows, axis=1).astype(jnp.bfloat16)
    back_rows, back_gate = (
        lax.all_to_all(
            pick_grad.reshape(expert_count, capacity, model_width),
            "exp",
            split_axis=0,
            concat_axis=0,
            tiled=True,
        ),
        lax.all_to_all(
            gate_grad.reshape(expert_count, capacity),
            "exp",
            split_axis=0,
            concat_axis=0,
            tiled=True,
        ),
    )
    picked_rows = back_rows.reshape(buffer_rows, model_width)[target]
    d_normed = jnp.sum(
        picked_rows.reshape(token_count, top_count, model_width).astype(jnp.float32), axis=1
    )
    picked_gate = (
        back_gate.reshape(buffer_rows)[target].astype(jnp.float32).reshape(token_count, top_count)
    )
    d_logit = gate_values * (
        picked_gate - jnp.sum(gate_values * picked_gate, axis=1, keepdims=True)
    )
    dense_logit = jnp.einsum("nk,nke->ne", d_logit, onehot, precision=highest)
    d_normed = d_normed + jnp.einsum(
        "ne,de->nd", dense_logit, router.astype(jnp.float32), precision=highest
    )
    grad_flat = norm_back(flat_rows, inverse, norm_gain, d_normed)
    grad_hidden = (
        grad_flat.reshape(1, local_passages, local_positions, model_width)
        + d_vector[None, :, None, :]
    )
    return (
        loss_value.reshape(1),
        own_score.reshape(1, local_passages),
        grad_hidden.astype(jnp.bfloat16),
    )


CORE, ACROSS_X, ACROSS_Y = 1, 2, 4
forward = (((1,), (0,)), ((), ()))
across = (((1,), (1,)), ((), ()))
MIB = 1 << 20


def swap(value, bit, size=8):
    return lax.ppermute(value, "exp", [(index, index ^ bit) for index in range(size)])


def shape_of(shape, dtype):
    return jax.ShapeDtypeStruct(shape, dtype)


def after(value, *others):
    return lax.optimization_barrier((value, *others))[0]


def kept(shape, dtype):
    return pltpu.VMEM(shape, dtype)


def pinned(array):
    return pltpu.with_memory_space_constraint(array, pltpu.VMEM)


def kernel_call(body, name, outs, ins, far=(), scratch=(), work=1):
    spaces = [pltpu.VMEM] * len(ins)
    ins = list(ins)
    for index in far:
        spaces[index] = pl.ANY
        ins[index] = pltpu.with_memory_space_constraint(ins[index], pltpu.HBM)
    return pl.pallas_call(
        body,
        name=name,
        out_shape=outs,
        in_specs=[pl.BlockSpec(memory_space=space) for space in spaces],
        out_specs=[pl.BlockSpec(memory_space=pltpu.VMEM)] * len(outs),
        scratch_shapes=scratch,
        compiler_params=pltpu.CompilerParams(vmem_limit_bytes=8 * MIB),
        cost_estimate=pl.CostEstimate(flops=work, bytes_accessed=1, transcendentals=0),
    )(*ins)


def split_low(values):
    high = values.astype(jnp.bfloat16)
    rest = values - high.astype(jnp.float32)
    middle = rest.astype(jnp.bfloat16)
    low = (rest - middle.astype(jnp.float32)).astype(jnp.bfloat16)
    return high, middle, low


def exact_dot(values, low_matrix, contract):
    parts = lax.dot_general(
        jnp.concatenate(split_low(values), axis=0),
        low_matrix,
        contract,
        preferred_element_type=jnp.float32,
    )
    return parts[0:8] + parts[8:16] + parts[16:24]


def other_order(values, bits):
    row = lax.broadcasted_iota(jnp.int32, values.shape, 0)
    for bit in (1, 2, 4):
        if bits & bit:
            values = jnp.where(
                (row & bit) == 0, pltpu.roll(values, 8 - bit, 0), pltpu.roll(values, bit, 0)
            )
    return values


def norm_kernel(
    hidden_far, gain_far, router_far, final_far, vector_far,
    hidden_ref, gain_ref, router_ref, normed_ref, sums_ref, head_ref,
    final_ref, vector_ref, copy_sems,
):
    pairs = (
        (hidden_far, hidden_ref), (gain_far, gain_ref), (router_far, router_ref),
        (final_far, final_ref), (vector_far, vector_ref),
    )
    copies = [
        pltpu.make_async_copy(source, target, copy_sems.at[index])
        for index, (source, target) in enumerate(pairs)
    ]
    for copy in copies:
        copy.start()
    for copy in copies:
        copy.wait()
    vector = vector_ref[...].astype(jnp.float32)
    vector = jnp.concatenate([vector[row : row + 1] for row in range(vector.shape[0])], axis=1)
    head_ref[...] = final_ref[...] * vector
    rows = hidden_ref[...].astype(jnp.float32)
    normed_ref[...] = (rows * rms_scale(rows) * gain_ref[...]).astype(jnp.bfloat16)
    sums_ref[...] = jnp.sum(rows, axis=0, keepdims=True)


def front_kernel(stage, owners, count, router_ref, gate_ref, up_ref, *refs):
    pieces, refs = refs[:count], refs[count:]
    expert = lax.axis_index("exp")
    hidden_units = gate_ref.shape[1]
    tile = 256
    firsts = range(0, hidden_units, tile)
    if stage == 0:
        gate_far, up_far = gate_ref, up_ref
        *refs, gate_ref, up_ref, rows_ref, copy_sems = refs
        copies = [
            pltpu.make_async_copy(
                source.at[:, first : first + tile],
                target.at[:, first : first + tile],
                copy_sems.at[which, number],
            )
            for number, first in enumerate(firsts)
            for which, (source, target) in enumerate(((gate_far, gate_ref), (up_far, up_ref)))
        ]
        for copy in copies:
            copy.start()
    elif stage == 1:
        down_far, *refs, down_ref, rows_ref, copy_sem = refs
        down_copy = pltpu.make_async_copy(down_far, down_ref, copy_sem)
        down_copy.start()
    elif stage == 3:
        sums_ref, down_ref, *earlier = refs[:5]
        *refs, rows_ref = refs[5:]
    else:
        *refs, rows_ref = refs
    slope_ref, silu_ref, act_ref, gates_ref, part_ref = refs
    first = 0
    for piece in pieces:
        rows_ref[first : first + piece.shape[0], :] = piece[...]
        first += piece.shape[0]
    size = first // len(owners)
    logits = lax.dot_general(
        rows_ref[...], router_ref[...], across, preferred_element_type=jnp.float32
    )
    weights = jnp.exp(logits)
    gates = weights / jnp.sum(weights, axis=1, keepdims=True)
    gates_ref[...] = gates
    lane = lax.broadcasted_iota(jnp.int32, gates.shape, 1)
    own = jnp.sum(jnp.where(lane == expert, gates, 0.0), axis=1, keepdims=True)
    low = own.astype(jnp.bfloat16).astype(jnp.float32)

    parts = []
    for number, first in enumerate(firsts):
        columns = slice(first, first + tile)
        if stage == 0:
            copies[2 * number].wait()
            copies[2 * number + 1].wait()
        pre_gate = jnp.dot(rows_ref[...], gate_ref[:, columns], preferred_element_type=jnp.float32)
        pre_up = jnp.dot(rows_ref[...], up_ref[:, columns], preferred_element_type=jnp.float32)
        silu_gate, slope = gate_parts(pre_gate)
        activation = (silu_gate * pre_up).astype(jnp.bfloat16)
        slope_ref[:, columns] = slope * pre_up
        silu_ref[:, columns] = silu_gate
        act_ref[:, columns] = activation
        weighted = activation.astype(jnp.float32) * low
        found = {}
        for index, owner in enumerate(owners):
            piece = jnp.sum(weighted[index * size : (index + 1) * size], axis=0, keepdims=True)
            found[owner] = found[owner] + piece if owner in found else piece
        nothing = jnp.zeros_like(weighted[:1])
        parts.append(jnp.concatenate([found.get(owner, nothing) for owner in range(8)], axis=0))
    part = jnp.concatenate(parts, axis=1)
    if stage == 1:
        down_copy.wait()
    if stage < 3:
        part_ref[...] = part
        return
    for ref in earlier:
        part = part + ref[...]
    terms = exact_dot(part, down_ref[...], forward)
    row = lax.broadcasted_iota(jnp.int32, terms.shape, 0)
    part_ref[...] = terms + jnp.where(row == 0, sums_ref[...], 0.0)


def front(stage, owners, pieces, router_rows, gate_matrix, up_matrix, more=()):
    model_width, hidden_units = gate_matrix.shape
    row_total = sum(piece.shape[0] for piece in pieces)
    outs = [
        kept((row_total, hidden_units), jnp.float32),
        kept((row_total, hidden_units), jnp.float32),
        kept((row_total, hidden_units), jnp.bfloat16),
        kept((row_total, 8), jnp.float32),
        kept((8, model_width if stage == 3 else hidden_units), jnp.float32),
    ]
    scratch = [pltpu.VMEM((row_total, model_width), jnp.bfloat16)]
    weights, far = [gate_matrix, up_matrix], ()
    if stage == 0:
        far = (1, 2)
        outs += [kept(gate_matrix.shape, jnp.bfloat16), kept(up_matrix.shape, jnp.bfloat16)]
        scratch.append(pltpu.SemaphoreType.DMA((2, hidden_units // 256)))
    else:
        weights = [pinned(matrix) for matrix in weights]
    if stage == 1:
        far = (3 + len(pieces),)
        outs.append(kept(more[0].shape, jnp.bfloat16))
        scratch.append(pltpu.SemaphoreType.DMA)
    if stage == 3:
        more = [pinned(array) for array in more]
    slope, silu, act, gates, part, *held = kernel_call(
        functools.partial(front_kernel, stage, owners, len(pieces)),
        "front",
        outs,
        [pinned(router_rows), *weights, *pieces, *more],
        far,
        scratch,
    )
    return (slope, silu, act, gates), part, held


def core_sum_kernel(own_ref, other_ref, out_ref):
    out_ref[...] = own_ref[...] + other_order(other_ref[...], CORE)


def near_kernel(
    own_ref, x_ref, y_ref, far_ref, head_ref, down_ref,
    near_ref, unit_ref, score_ref, own_score_ref, *, token_count,
):
    pooled = (
        (own_ref[...] + other_order(x_ref[...], ACROSS_X))
        + (other_order(y_ref[...], ACROSS_Y) + other_order(far_ref[...], ACROSS_X | ACROSS_Y))
    ) / token_count
    head = head_ref[...]
    scale = rms_scale(pooled)
    along = jnp.sum(pooled * head, axis=1, keepdims=True)
    own_score = (scale * along)[:1]
    own_score_ref[...] = own_score
    score_ref[...] = jnp.broadcast_to(own_score, score_ref.shape)
    unit = (
        scale * head - scale * scale * scale * (along / pooled.shape[1]) * pooled
    ) / token_count
    unit_ref[...] = unit[:1]
    near_ref[...] = exact_dot(unit, down_ref[...], across)


def back_kernel(owners, near_ref, gate_ref, up_ref, *refs):
    slope_ref, silu_ref, act_ref, gates_ref, *out_refs, d_gate_ref, d_up_ref = refs
    expert = lax.axis_index("exp")
    size = d_gate_ref.shape[0] // len(owners)
    rows_out, wide = out_refs[0].shape
    model_width = wide - 128
    for index, owner in enumerate(owners):
        rows = slice(index * size, (index + 1) * size)
        near = near_ref[owner : owner + 1, :]
        gates = gates_ref[rows, :]
        lane = lax.broadcasted_iota(jnp.int32, gates.shape, 1)
        own = jnp.sum(jnp.where(lane == expert, gates, 0.0), axis=1, keepdims=True)
        d_act = own.astype(jnp.bfloat16).astype(jnp.float32) * near
        d_gate_ref[rows, :] = (d_act * slope_ref[rows, :]).astype(jnp.bfloat16)
        d_up_ref[rows, :] = (d_act * silu_ref[rows, :]).astype(jnp.bfloat16)
        gate_grad = jnp.sum(act_ref[rows, :].astype(jnp.float32) * near, axis=1, keepdims=True)
        lane = lax.broadcasted_iota(jnp.int32, (size, 128), 1)
        out_ref, first = out_refs[index * size // rows_out], index * size % rows_out
        out_ref[first : first + size, model_width:] = jnp.where(
            lane == expert, gate_grad, 0.0
        ).astype(jnp.bfloat16)

    for first in range(0, model_width, 256):
        columns = slice(first, first + 256)
        pick_grad = lax.dot_general(
            d_gate_ref[...], gate_ref[columns, :], across, preferred_element_type=jnp.float32
        ) + lax.dot_general(
            d_up_ref[...], up_ref[columns, :], across, preferred_element_type=jnp.float32
        )
        pick_grad = pick_grad.astype(jnp.bfloat16)
        for index, out_ref in enumerate(out_refs):
            out_ref[:, columns] = pick_grad[index * rows_out : (index + 1) * rows_out]


def back(owners, saved, near, gate_matrix, up_matrix, parts):
    model_width, hidden_units = gate_matrix.shape
    row_total = saved[0].shape[0]
    return kernel_call(
        functools.partial(back_kernel, owners),
        "back",
        [kept((row_total // parts, model_width + 128), jnp.bfloat16)] * parts,
        [pinned(array) for array in (near, gate_matrix, up_matrix, *saved)],
        (),
        [pltpu.VMEM((row_total, hidden_units), jnp.bfloat16)] * 2,
    )


def add_kernel(own_ref, other_ref, *refs):
    *more, first_ref, second_ref = refs
    size = first_ref.shape[0]
    half = size // 2
    for index, out_ref in enumerate((first_ref, second_ref)):
        for part in range(2):
            rows = slice(part * half, (part + 1) * half)
            held = slice(index * size + part * half, index * size + (part + 1) * half)
            total = own_ref[held, :].astype(jnp.float32) + other_ref[held, :].astype(jnp.float32)
            if more and index + part == 1:
                extra = slice(index * half, (index + 1) * half)
                total = total + more[0][extra, :].astype(jnp.float32)
            out_ref[rows, :] = total.astype(jnp.bfloat16)


def add_pieces(own, other, *more):
    rows, wide = own.shape
    return kernel_call(
        add_kernel,
        "add",
        [kept((rows // 2, wide), jnp.bfloat16)] * 2,
        [pinned(own), other, *(pinned(array) for array in more)],
    )


def split_kernel(x_ref, y_ref, low_ref, high_ref):
    half = low_ref.shape[0]
    low_ref[...] = x_ref[:half, :]
    high_ref[...] = y_ref[half:, :]


def pack_kernel(first_ref, second_ref, out_ref):
    rows = first_ref.shape[0]
    out_ref[:rows, :] = first_ref[...]
    out_ref[rows:, :] = second_ref[...]


def pack(first, second, work=1):
    rows, wide = first.shape
    return kernel_call(
        pack_kernel, "pack", [kept((2 * rows, wide), first.dtype)], [first, second], work=work
    )[0]


def rank_kernel(grades_far, ranks_far, *refs):
    near_scores_ref, far_scores_ref, loss_ref, factor_ref, grades_ref, ranks_ref, copy_sems = refs
    copies = [
        pltpu.make_async_copy(grades_far, grades_ref, copy_sems.at[0]),
        pltpu.make_async_copy(ranks_far, ranks_ref, copy_sems.at[1]),
    ]
    for copy in copies:
        copy.start()
    for copy in copies:
        copy.wait()
    passages = grades_ref.shape[1]
    place = lax.axis_index("psg")
    row = lax.broadcasted_iota(jnp.int32, (8, 128), 0)
    lane = lax.broadcasted_iota(jnp.int32, (8, 128), 1)

    def spread(index, values):
        total = jnp.zeros((8, 128), jnp.float32)
        for number, value in values:
            total = jnp.where(index == number, value, total)
        return total

    grade_list = [(number, grades_ref[0, number].astype(jnp.float32)) for number in range(passages)]
    rank_list = [(number, ranks_ref[0, number].astype(jnp.float32)) for number in range(passages)]
    score_list = [
        (place ^ (base + number), jnp.broadcast_to(ref[number : number + 1, :], (8, 128)))
        for base, ref in ((0, near_scores_ref), (passages // 2, far_scores_ref))
        for number in range(passages // 2)
    ]
    grade_row, grade_lane = spread(row, grade_list), spread(lane, grade_list)
    worth_row, worth_lane = jnp.exp2(grade_row), jnp.exp2(grade_lane)
    discount_row = 1.0 / jnp.log2(2.0 + spread(row, rank_list))
    discount_lane = 1.0 / jnp.log2(2.0 + spread(lane, rank_list))
    score_row, score_lane = spread(row, score_list), spread(lane, score_list)
    pair = jnp.logical_and(row < passages, lane < passages)
    ahead = jnp.logical_or(
        grade_lane > grade_row, jnp.logical_and(grade_lane == grade_row, lane < row)
    )
    ideal_rank = jnp.sum(
        jnp.where(jnp.logical_and(pair, ahead), 1.0, 0.0), axis=1, keepdims=True
    )
    ideal_terms = (worth_row - 1.0) / jnp.log2(2.0 + ideal_rank)
    one_lane = jnp.logical_and(pair, lane == 0)

    def whole_sum(values):
        return jnp.sum(jnp.sum(values, axis=1, keepdims=True), axis=0, keepdims=True)

    ideal_gain = whole_sum(jnp.where(one_lane, ideal_terms, 0.0))
    swap_gain = (
        jnp.abs((worth_row - worth_lane) * (discount_row - discount_lane)) / ideal_gain
    )
    swap_gain = jnp.where(jnp.logical_and(pair, grade_row > grade_lane), swap_gain, 0.0)
    margin = score_row - score_lane
    softplus = jnp.maximum(-margin, 0.0) + jnp.log1p(jnp.exp(-jnp.abs(margin)))
    loss_ref[...] = whole_sum(swap_gain * softplus)
    pull = swap_gain * jax.nn.sigmoid(-margin)
    gradient = whole_sum(jnp.where(lane == place, pull, 0.0) - jnp.where(row == place, pull, 0.0))
    factor_ref[...] = jnp.broadcast_to(gradient * loss_scale, factor_ref.shape)


def end_kernel(
    factor_ref, own_low_ref, own_high_ref, core_low_ref, core_high_ref, x_ref, y_ref,
    hidden_ref, gain_ref, gates_ref, router_ref, unit_ref, grad_ref,
):
    half = hidden_ref.shape[0] // 2
    model_width = hidden_ref.shape[1]
    router_rows = jnp.concatenate([router_ref[...]] * 3, axis=0)
    sums = ((own_low_ref, core_low_ref), (own_high_ref, core_high_ref))
    for part, (own_ref, core_ref) in enumerate(sums):
        rows = slice(part * half, (part + 1) * half)
        total = (own_ref[...].astype(jnp.float32) + core_ref[...].astype(jnp.float32)) + (
            x_ref[rows, :].astype(jnp.float32) + y_ref[rows, :].astype(jnp.float32)
        )
        gates = gates_ref[rows, :]
        slot_grad = total[:, model_width : model_width + 8]
        d_logit = gates * (slot_grad - jnp.sum(gates * slot_grad, axis=1, keepdims=True))
        d_normed = total[:, :model_width]
        d_normed = d_normed + jnp.dot(
            jnp.concatenate(split_low(d_logit), axis=1),
            router_rows,
            preferred_element_type=jnp.float32,
        )
        flat_rows = hidden_ref[rows, :].astype(jnp.float32)
        grad = norm_back(flat_rows, rms_scale(flat_rows), gain_ref[...], d_normed) + unit_ref[...]
        grad_ref[rows, :] = (grad * factor_ref[:, :1]).astype(jnp.bfloat16)


def every_expert(
    hidden,
    norm_gain,
    router,
    gate_proj,
    up_proj,
    down_proj,
    final_gain,
    score_vector,
    expert_ids,
    grades,
    passage_ranks,
):
    unused_query, unused_passage, token_count, model_width = hidden.shape
    half = token_count // 2
    passages = grades.shape[1]
    flat = hidden.reshape(token_count, model_width)
    gate_matrix, up_matrix, down_matrix = gate_proj[0], up_proj[0], down_proj[0]
    own_owners, side_owners, other_side_owners, far_owners = (
        (0, 0, 1, 1), (2, 2, 4, 4), (3, 3, 5, 5), (6, 6, 7, 7)
    )

    flat, gain, router_rows, normed, token_sums, head = kernel_call(
        norm_kernel,
        "norm",
        [
            kept(flat.shape, jnp.bfloat16),
            kept((1, model_width), jnp.float32),
            kept((8, model_width), jnp.bfloat16),
            kept(flat.shape, jnp.bfloat16),
            kept((1, model_width), jnp.float32),
            kept((1, model_width), jnp.float32),
        ],
        [
            flat,
            norm_gain.reshape(1, model_width),
            router.T,
            final_gain.reshape(1, model_width),
            score_vector.reshape(model_width // 128, 128),
        ],
        range(5),
        [
            pltpu.VMEM((1, model_width), jnp.float32),
            pltpu.VMEM((model_width // 128, 128), jnp.bfloat16),
            pltpu.SemaphoreType.DMA((5,)),
        ],
    )
    x_rows, y_rows, core_rows = (swap(normed, bit) for bit in (ACROSS_X, ACROSS_Y, CORE))
    saved, parts = [None] * 4, [None] * 4
    saved[0], parts[0], (gate_matrix, up_matrix) = front(
        0, own_owners, (normed, core_rows), router_rows, gate_matrix, up_matrix
    )
    x_rows, y_rows = after(x_rows, parts[0]), after(y_rows, parts[0])
    piece = kept((half, model_width), jnp.bfloat16)
    x_low, y_high = kernel_call(split_kernel, "split", [piece] * 2, [x_rows, y_rows])
    far_low = swap(x_low, ACROSS_Y)
    far_high = swap(y_high, ACROSS_X)
    saved[1], parts[1], (down_matrix,) = front(
        1, side_owners, (x_rows, y_rows), router_rows, gate_matrix, up_matrix,
        (down_matrix,),
    )
    pieces = (after(swap(x_rows, CORE), parts[1]), swap(y_rows, CORE))
    saved[2], parts[2], unused = front(
        2, other_side_owners, pieces, router_rows, gate_matrix, up_matrix
    )
    far_low, far_high = after(far_low, parts[2]), after(far_high, parts[2])
    pieces = (far_low, far_high, swap(pack(far_low, far_high), CORE))
    saved[3], terms, unused = front(
        3, far_owners, pieces, router_rows, gate_matrix, up_matrix,
        (token_sums, down_matrix, *parts[:3]),
    )

    (chip_terms,) = kernel_call(
        core_sum_kernel, "core_sum", [kept(terms.shape, jnp.float32)], [pinned(terms), swap(terms, CORE)]
    )
    near, unit_vector, travelling, own_score = kernel_call(
        functools.partial(near_kernel, token_count=token_count),
        "near",
        [
            kept((8, down_matrix.shape[0]), jnp.float32),
            kept((1, model_width), jnp.float32),
            kept((1, 128), jnp.float32),
            shape_of((1, 1), jnp.float32),
        ],
        [
            pinned(chip_terms),
            swap(chip_terms, ACROSS_X),
            swap(chip_terms, ACROSS_Y),
            swap(chip_terms, ACROSS_X | ACROSS_Y),
            pinned(head),
            pinned(down_matrix),
        ],
    )

    def go_back(owners, group, parts, *earlier):
        return back(owners, saved[group], after(near, *earlier), gate_matrix, up_matrix, parts)

    far, other_far = go_back(far_owners, 3, 2)
    far_sums = add_pieces(far, swap(other_far, CORE))
    far_low = swap(far_sums[0], ACROSS_X)
    far_high = swap(far_sums[1], ACROSS_Y)
    (other_sides,) = go_back(other_side_owners, 2, 1, far_sums[0])
    (sides,) = go_back(side_owners, 1, 1, other_sides)
    far_pair = pack(after(far_high, sides), far_low, work=1 << 40)
    x_sums, y_sums = add_pieces(sides, swap(other_sides, CORE), far_pair)
    x_sums, y_sums, (travelling, near) = lax.optimization_barrier(
        (x_sums, y_sums, (travelling, near))
    )
    x_sums, y_sums = swap(x_sums, ACROSS_X), swap(y_sums, ACROSS_Y)
    own_low, own_high, core_low, core_high = go_back(own_owners, 0, 4)
    core_low, core_high = swap(core_low, CORE), swap(core_high, CORE)
    met = lax.ppermute(travelling, "psg", [(index, index ^ 1) for index in range(passages)])
    near_scores = pack(travelling, met)
    far_scores = lax.ppermute(near_scores, "psg", [(index, index ^ 2) for index in range(passages)])
    loss, factor = kernel_call(
        rank_kernel,
        "rank",
        [shape_of((1, 1), jnp.float32), kept((1, 128), jnp.float32)],
        [
            grades,
            passage_ranks,
            pinned(near_scores),
            far_scores,
        ],
        (0, 1),
        [
            pltpu.SMEM(grades.shape, jnp.int32),
            pltpu.SMEM(grades.shape, jnp.int32),
            pltpu.SemaphoreType.DMA((2,)),
        ],
    )
    (grad,) = kernel_call(
        end_kernel,
        "end",
        [shape_of((token_count, model_width), jnp.bfloat16)],
        [
            pinned(factor), pinned(own_low), pinned(own_high), core_low, core_high,
            x_sums, y_sums,
            pinned(flat), pinned(gain), pinned(saved[0][3]), pinned(router_rows), pinned(unit_vector),
        ],
    )
    return (loss.reshape(1), own_score, grad.reshape(hidden.shape))


def block(*arrays):
    hidden, router, expert_ids, grades = arrays[0], arrays[2], arrays[8], arrays[9]
    each_expert = router.shape[1] == expert_ids.shape[3] == 8
    if hidden.shape[1] == 1 and each_expert and grades.shape[1] == 4:
        return every_expert(*arrays)
    return local(*arrays)


def solution(mesh):
    placed = (
        P("exp", "psg", None, None),
        P(),
        P(),
        P("exp", None, None),
        P("exp", None, None),
        P("exp", None, None),
        P(),
        P(),
        P("exp", "psg", None, None),
        P("exp", None),
        P("exp", None),
    )
    return jax.shard_map(
        block,
        mesh=mesh,
        in_specs=placed,
        out_specs=(P("exp"), P("exp", "psg"), P("exp", "psg", None, None)),
        check_vma=False,
    )
```

```python
import functools
import math

import jax
import jax.numpy as jnp
from jax import lax
from jax.experimental import pallas as pl
from jax.experimental.pallas import tpu as pltpu
from jax.sharding import PartitionSpec as P

epsilon = 1e-06
loss_scale = 256.0
highest = lax.Precision.HIGHEST


def rms_scale(values):
    return lax.rsqrt(jnp.mean(values * values, axis=-1, keepdims=True) + epsilon)


def head_score(pooled, final_gain, score_vector):
    scaled = pooled * rms_scale(pooled) * final_gain
    return jnp.dot(scaled, score_vector.astype(jnp.float32), precision=highest)


def rank_loss(scores, grades, passage_ranks):
    grade_value = grades.astype(jnp.float32)
    worth_gain = jnp.exp2(grade_value)
    discount = 1.0 / jnp.log2(2.0 + passage_ranks.astype(jnp.float32))
    better_than = grades[None, :] > grades[:, None]
    equal_grade = grades[None, :] == grades[:, None]
    position = jnp.arange(grades.shape[0], dtype=jnp.int32)
    earlier = position[None, :] < position[:, None]
    ideal_rank = jnp.sum(
        jnp.logical_or(better_than, jnp.logical_and(equal_grade, earlier)).astype(jnp.float32),
        axis=1,
    )
    ideal_gain = jnp.sum((worth_gain - 1.0) / jnp.log2(2.0 + ideal_rank))
    ordered = (grades[:, None] > grades[None, :]).astype(jnp.float32)
    swap_gain = (
        jnp.abs(
            (worth_gain[:, None] - worth_gain[None, :]) * (discount[:, None] - discount[None, :])
        )
        / ideal_gain
    )
    margin = scores[:, None] - scores[None, :]
    return jnp.sum(ordered * swap_gain * jax.nn.softplus(-margin))


def pick_gates(normed, router, picked_ids):
    expert_total = router.shape[1]
    logits = jnp.dot(normed, router, preferred_element_type=jnp.float32)
    onehot = (
        picked_ids[:, :, None] == jnp.arange(expert_total, dtype=jnp.int32)[None, None, :]
    ).astype(jnp.float32)
    chosen = jnp.einsum("nke,ne->nk", onehot, logits, precision=highest)
    weights = jnp.exp(chosen)
    return (weights / jnp.sum(weights, axis=1, keepdims=True), onehot)


def gate_parts(pre_gate):
    sigmoid_gate = jax.nn.sigmoid(pre_gate)
    return (pre_gate * sigmoid_gate, sigmoid_gate * (1.0 + pre_gate * (1.0 - sigmoid_gate)))


def norm_back(flat_rows, inverse, norm_gain, d_normed):
    scaled = d_normed * norm_gain
    return inverse * scaled - flat_rows * inverse * inverse * inverse * jnp.mean(
        flat_rows * scaled, axis=-1, keepdims=True
    )


def unpack_front(front_out, buffer_rows):
    pre_gate, pre_up, received = front_out
    hidden_units = pre_gate.shape[2]
    pre_gate = pre_gate.reshape(buffer_rows, hidden_units)
    pre_up = pre_up.reshape(buffer_rows, hidden_units)
    silu_gate, slope = gate_parts(pre_gate)
    activation = (silu_gate * pre_up).astype(jnp.bfloat16)
    return (pre_up, received, silu_gate, slope, activation)


def local(
    hidden,
    norm_gain,
    router,
    gate_proj,
    up_proj,
    down_proj,
    final_gain,
    score_vector,
    expert_ids,
    grades,
    passage_ranks,
):
    unused_query, local_passages, local_positions, model_width = hidden.shape
    top_count = expert_ids.shape[3]
    expert_count = lax.axis_size("exp")
    token_count = local_passages * local_positions
    slot_count = token_count * top_count
    capacity = min(token_count, 9 * token_count * top_count // (8 * expert_count))
    buffer_rows = expert_count * capacity
    flat_rows = hidden.reshape(token_count, model_width).astype(jnp.float32)
    inverse = rms_scale(flat_rows)
    normed = (flat_rows * inverse * norm_gain).astype(jnp.bfloat16)
    picked_ids = expert_ids.reshape(token_count, top_count)
    gate_values, onehot = pick_gates(normed, router, picked_ids)
    slot_hits = onehot.reshape(slot_count, expert_count).astype(jnp.int32)
    slot_rank = jnp.sum((jnp.cumsum(slot_hits, axis=0) - slot_hits) * slot_hits, axis=1)
    target = picked_ids.reshape(slot_count) * capacity + slot_rank
    source_token = jnp.arange(slot_count, dtype=jnp.int32) // top_count
    passage_onehot = (
        source_token[:, None] // local_positions
        == jnp.arange(local_passages, dtype=jnp.int32)[None, :]
    ).astype(jnp.float32)
    weighted = (passage_onehot * gate_values.reshape(slot_count, 1)).astype(jnp.bfloat16)
    send_rows = (
        jnp.zeros((buffer_rows, model_width), jnp.bfloat16).at[target].set(normed[source_token])
    )
    send_weights = jnp.zeros((buffer_rows, local_passages), jnp.bfloat16).at[target].set(weighted)
    outgoing = (
        send_rows.reshape(expert_count, capacity, model_width),
        send_weights.reshape(expert_count, capacity, local_passages),
    )
    gate_matrix = gate_proj[0]
    up_matrix = up_proj[0]
    down_matrix = down_proj[0]
    rows_in = lax.all_to_all(outgoing[0], "exp", split_axis=0, concat_axis=0, tiled=True)
    weights_in = lax.all_to_all(outgoing[1], "exp", split_axis=0, concat_axis=0, tiled=True)
    pre_gate = jnp.einsum("end,df->enf", rows_in, gate_matrix, preferred_element_type=jnp.float32)
    pre_up = jnp.einsum("end,df->enf", rows_in, up_matrix, preferred_element_type=jnp.float32)
    front_out = (pre_gate, pre_up, weights_in)
    pre_up, received, silu_gate, slope, activation = unpack_front(front_out, buffer_rows)
    hidden_units = activation.shape[1]
    passage_part = jnp.einsum(
        "scp,scf->spf",
        received,
        activation.reshape(expert_count, capacity, hidden_units),
        preferred_element_type=jnp.float32,
    )
    down_wide = down_matrix.astype(jnp.float32)
    expert_terms = jnp.einsum("spf,fd->spd", passage_part, down_wide, precision=highest)
    came_back = lax.all_to_all(expert_terms, "exp", split_axis=0, concat_axis=0, tiled=True)
    token_sums = jnp.sum(flat_rows.reshape(local_passages, local_positions, model_width), axis=1)
    pooled = (token_sums + jnp.sum(came_back, axis=0)) / local_positions
    first_row = lax.axis_index("psg") * local_passages
    own_score = head_score(pooled, final_gain, score_vector)
    every_score = lax.all_gather(own_score, "psg", axis=0, tiled=True)
    loss_value, loss_grad = jax.value_and_grad(rank_loss)(every_score, grades[0], passage_ranks[0])
    d_own = lax.dynamic_slice_in_dim(loss_grad, first_row, local_passages, 0) * loss_scale
    unused_score, head_back = jax.vjp(
        lambda values: head_score(values, final_gain, score_vector), pooled
    )
    d_vector = head_back(d_own)[0] / local_positions
    every_vector = lax.all_gather(d_vector[None], "exp", axis=0, tiled=True)
    near_table = jnp.einsum("spd,fd->spf", every_vector, down_wide, precision=highest)
    present = (received != 0).astype(jnp.float32)
    near_rows = jnp.einsum("scp,spf->scf", present, near_table, precision=highest).reshape(
        buffer_rows, hidden_units
    )
    gate_weight = jnp.sum(received.astype(jnp.float32), axis=2).reshape(buffer_rows, 1)
    d_act = gate_weight * near_rows
    d_gate = (d_act * pre_up * slope).astype(jnp.bfloat16)
    d_up = (d_act * silu_gate).astype(jnp.bfloat16)
    contract = (((1,), (1,)), ((), ()))
    pick_grad = lax.dot_general(d_gate, gate_matrix, contract, preferred_element_type=jnp.float32)
    pick_grad = (
        pick_grad + lax.dot_general(d_up, up_matrix, contract, preferred_element_type=jnp.float32)
    ).astype(jnp.bfloat16)
    gate_grad = jnp.sum(activation.astype(jnp.float32) * near_rows, axis=1).astype(jnp.bfloat16)
    back_rows, back_gate = (
        lax.all_to_all(
            pick_grad.reshape(expert_count, capacity, model_width),
            "exp",
            split_axis=0,
            concat_axis=0,
            tiled=True,
        ),
        lax.all_to_all(
            gate_grad.reshape(expert_count, capacity),
            "exp",
            split_axis=0,
            concat_axis=0,
            tiled=True,
        ),
    )
    picked_rows = back_rows.reshape(buffer_rows, model_width)[target]
    d_normed = jnp.sum(
        picked_rows.reshape(token_count, top_count, model_width).astype(jnp.float32), axis=1
    )
    picked_gate = (
        back_gate.reshape(buffer_rows)[target].astype(jnp.float32).reshape(token_count, top_count)
    )
    d_logit = gate_values * (
        picked_gate - jnp.sum(gate_values * picked_gate, axis=1, keepdims=True)
    )
    dense_logit = jnp.einsum("nk,nke->ne", d_logit, onehot, precision=highest)
    d_normed = d_normed + jnp.einsum(
        "ne,de->nd", dense_logit, router.astype(jnp.float32), precision=highest
    )
    grad_flat = norm_back(flat_rows, inverse, norm_gain, d_normed)
    grad_hidden = (
        grad_flat.reshape(1, local_passages, local_positions, model_width)
        + d_vector[None, :, None, :]
    )
    return (
        loss_value.reshape(1),
        own_score.reshape(1, local_passages),
        grad_hidden.astype(jnp.bfloat16),
    )


CORE, ACROSS_X, ACROSS_Y = 1, 2, 4
forward = (((1,), (0,)), ((), ()))
across = (((1,), (1,)), ((), ()))
MIB = 1 << 20


def swap(value, bit, size=8):
    return lax.ppermute(value, "exp", [(index, index ^ bit) for index in range(size)])


def shape_of(shape, dtype):
    return jax.ShapeDtypeStruct(shape, dtype)


def after(value, *others):
    return lax.optimization_barrier((value, *others))[0]


def kept(shape, dtype):
    return pltpu.VMEM(shape, dtype)


def pinned(array):
    return pltpu.with_memory_space_constraint(array, pltpu.VMEM)


def kernel_call(body, name, outs, ins, far=(), scratch=(), work=1):
    spaces = [pltpu.VMEM] * len(ins)
    ins = list(ins)
    for index in far:
        spaces[index] = pl.ANY
        ins[index] = pltpu.with_memory_space_constraint(ins[index], pltpu.HBM)
    return pl.pallas_call(
        body,
        name=name,
        out_shape=outs,
        in_specs=[pl.BlockSpec(memory_space=space) for space in spaces],
        out_specs=[pl.BlockSpec(memory_space=pltpu.VMEM)] * len(outs),
        scratch_shapes=scratch,
        compiler_params=pltpu.CompilerParams(vmem_limit_bytes=8 * MIB),
        cost_estimate=pl.CostEstimate(flops=work, bytes_accessed=1, transcendentals=0),
    )(*ins)


def split_low(values):
    high = values.astype(jnp.bfloat16)
    rest = values - high.astype(jnp.float32)
    middle = rest.astype(jnp.bfloat16)
    low = (rest - middle.astype(jnp.float32)).astype(jnp.bfloat16)
    return high, middle, low


def exact_dot(values, low_matrix, contract):
    parts = lax.dot_general(
        jnp.concatenate(split_low(values), axis=0),
        low_matrix,
        contract,
        preferred_element_type=jnp.float32,
    )
    return parts[0:8] + parts[8:16] + parts[16:24]


def other_order(values, bits):
    return jnp.concatenate([values[row ^ bits : (row ^ bits) + 1] for row in range(4)], axis=0)


def norm_kernel(
    hidden_far, gain_far, router_far, final_far, vector_far,
    hidden_ref, gain_ref, router_ref, normed_ref, sums_ref, head_ref,
    final_ref, vector_ref, copy_sems,
):
    pairs = (
        (hidden_far, hidden_ref), (gain_far, gain_ref), (router_far, router_ref),
        (final_far, final_ref), (vector_far, vector_ref),
    )
    copies = [
        pltpu.make_async_copy(source, target, copy_sems.at[index])
        for index, (source, target) in enumerate(pairs)
    ]
    for copy in copies:
        copy.start()
    for copy in copies:
        copy.wait()
    vector = vector_ref[...].astype(jnp.float32)
    vector = jnp.concatenate([vector[row : row + 1] for row in range(vector.shape[0])], axis=1)
    head_ref[...] = final_ref[...] * vector
    rows = hidden_ref[...].astype(jnp.float32)
    normed_ref[...] = (rows * rms_scale(rows) * gain_ref[...]).astype(jnp.bfloat16)
    sums_ref[...] = jnp.sum(rows, axis=0, keepdims=True)


def front_kernel(stage, owners, sets, count, router_ref, *refs):
    matrices, refs = refs[: 2 * len(sets)], refs[2 * len(sets) :]
    pieces, refs = refs[:count], refs[count:]
    matrices = list(matrices)
    hidden_units = matrices[0].shape[1]
    tile = 256
    firsts = range(0, hidden_units, tile)
    if stage == 0:
        far_matrices = matrices
        *refs, gate_held, up_held, rows_ref, copy_sems = refs
        matrices = [gate_held, up_held]
        copies = [
            pltpu.make_async_copy(
                source.at[:, first : first + tile],
                target.at[:, first : first + tile],
                copy_sems.at[which, number],
            )
            for number, first in enumerate(firsts)
            for which, (source, target) in enumerate(zip(far_matrices, matrices))
        ]
        for copy in copies:
            copy.start()
    elif stage == 1:
        down_far, *refs, down_ref, rows_ref, copy_sem = refs
        down_copy = pltpu.make_async_copy(down_far, down_ref, copy_sem)
        down_copy.start()
    elif stage == 3:
        sums_ref, *downs = refs[:3]
        earlier, refs = refs[3:6], refs[6:]
        *refs, terms_ref, rows_ref = refs
    else:
        *refs, rows_ref = refs
    gates_ref, *outs = refs
    expert = lax.axis_index("exp")
    first = 0
    for piece in pieces:
        rows_ref[first : first + piece.shape[0], :] = piece[...]
        first += piece.shape[0]
    size = first // len(owners)
    logits = lax.dot_general(
        rows_ref[...], router_ref[...], across, preferred_element_type=jnp.float32
    )
    weights = jnp.exp(logits)
    gates = weights / jnp.sum(weights, axis=1, keepdims=True)
    gates_ref[...] = gates
    lane = lax.broadcasted_iota(jnp.int32, gates.shape, 1)

    totals = []
    for place, which in enumerate(sets):
        gate_ref, up_ref = matrices[2 * place : 2 * place + 2]
        if stage == 3:
            slope_ref, silu_ref, act_ref = outs[3 * place : 3 * place + 3]
        else:
            slope_ref, silu_ref, act_ref, part_ref = outs
        own = jnp.sum(jnp.where(lane == expert ^ which, gates, 0.0), axis=1, keepdims=True)
        low = own.astype(jnp.bfloat16).astype(jnp.float32)
        parts = []
        for number, first in enumerate(firsts):
            columns = slice(first, first + tile)
            if stage == 0:
                copies[2 * number].wait()
                copies[2 * number + 1].wait()
            rows = rows_ref[...]
            pre_gate = jnp.dot(rows, gate_ref[:, columns], preferred_element_type=jnp.float32)
            pre_up = jnp.dot(rows, up_ref[:, columns], preferred_element_type=jnp.float32)
            silu_gate, slope = gate_parts(pre_gate)
            activation = (silu_gate * pre_up).astype(jnp.bfloat16)
            slope_ref[:, columns] = slope * pre_up
            silu_ref[:, columns] = silu_gate
            act_ref[:, columns] = activation
            weighted = activation.astype(jnp.float32) * low
            found = {
                owner: jnp.sum(weighted[index * size : (index + 1) * size], axis=0, keepdims=True)
                for index, owner in enumerate(owners)
            }
            nothing = jnp.zeros_like(weighted[:1])
            parts.append(
                jnp.concatenate([found.get(owner, nothing) for owner in range(8)], axis=0)
            )
        totals.append(jnp.concatenate(parts, axis=1))
    if stage == 1:
        down_copy.wait()
    if stage < 3:
        part_ref[...] = totals[0]
        return
    own_first, own_second, other_first = earlier
    totals[0] = totals[0] + (own_first[...] + own_second[...])
    totals[1] = totals[1] + other_first[...]
    terms = exact_dot(totals[0], downs[0][...], forward) + exact_dot(
        totals[1], downs[1][...], forward
    )
    row = lax.broadcasted_iota(jnp.int32, terms.shape, 0)
    terms_ref[...] = (terms + jnp.where(row == 0, sums_ref[...], 0.0))[:4]


def front(stage, owners, sets, pieces, router_rows, matrices, more=()):
    model_width, hidden_units = matrices[0].shape
    row_total = sum(piece.shape[0] for piece in pieces)
    outs = [kept((row_total, 8), jnp.float32)]
    for which in sets:
        outs += [
            kept((row_total, hidden_units), jnp.float32),
            kept((row_total, hidden_units), jnp.float32),
            kept((row_total, hidden_units), jnp.bfloat16),
        ]
    outs.append(
        kept((4, model_width), jnp.float32) if stage == 3 else kept((8, hidden_units), jnp.float32)
    )
    scratch = [pltpu.VMEM((row_total, model_width), jnp.bfloat16)]
    far = ()
    if stage == 0:
        far = (1, 2)
        outs += [kept(matrix.shape, jnp.bfloat16) for matrix in matrices]
        scratch.append(pltpu.SemaphoreType.DMA((2, hidden_units // 256)))
    else:
        matrices = [pinned(matrix) for matrix in matrices]
    if stage == 1:
        far = (3 + len(pieces),)
        outs.append(kept(more[0].shape, jnp.bfloat16))
        scratch.append(pltpu.SemaphoreType.DMA)
    if stage == 3:
        more = [pinned(array) for array in more]
    return kernel_call(
        functools.partial(front_kernel, stage, owners, sets, len(pieces)),
        "front",
        outs,
        [pinned(router_rows), *matrices, *(pinned(piece) for piece in pieces), *more],
        far,
        scratch,
    )


def near_kernel(
    own_ref, x_ref, y_ref, far_ref, head_ref, down_ref, other_down_ref,
    near_ref, other_near_ref, unit_ref, score_ref, own_score_ref, *, token_count,
):
    pooled = (
        (own_ref[...] + other_order(x_ref[...], 1))
        + (other_order(y_ref[...], 2) + other_order(far_ref[...], 3))
    ) / token_count
    pooled = jnp.concatenate([pooled, jnp.zeros_like(pooled)], axis=0)
    head = head_ref[...]
    scale = rms_scale(pooled)
    along = jnp.sum(pooled * head, axis=1, keepdims=True)
    own_score = (scale * along)[:1]
    own_score_ref[...] = own_score
    score_ref[...] = jnp.broadcast_to(own_score, score_ref.shape)
    unit = (
        scale * head - scale * scale * scale * (along / pooled.shape[1]) * pooled
    ) / token_count
    unit_ref[...] = unit[:1]
    near_ref[...] = exact_dot(unit, down_ref[...], across)
    other_near_ref[...] = exact_dot(unit, other_down_ref[...], across)


def back_kernel(owners, starts, near_ref, other_near_ref, gates_ref, *refs):
    saved, matrices, refs = refs[:6], refs[6:10], refs[10:]
    *out_refs, d_gate_ref, d_up_ref, other_d_gate_ref, other_d_up_ref = refs
    expert = lax.axis_index("exp")
    size, wide = out_refs[0].shape
    model_width = wide - 128
    lane = lax.broadcasted_iota(jnp.int32, (size, 8), 1)
    wide_lane = lax.broadcasted_iota(jnp.int32, (size, 128), 1)
    experts = (
        (near_ref, saved[:3], d_gate_ref, d_up_ref),
        (other_near_ref, saved[3:], other_d_gate_ref, other_d_up_ref),
    )
    for index, owner in enumerate(owners):
        rows = slice(index * size, (index + 1) * size)
        columns = jnp.zeros((size, 128), jnp.float32)
        for which, (table_ref, arrays, d_gate_out, d_up_out) in enumerate(experts):
            slope_ref, silu_ref, act_ref = arrays
            held = slice(starts[which] + index * size, starts[which] + (index + 1) * size)
            near = table_ref[owner : owner + 1, :]
            own = jnp.sum(
                jnp.where(lane == expert ^ which, gates_ref[rows, :], 0.0), axis=1, keepdims=True
            )
            d_act = own.astype(jnp.bfloat16).astype(jnp.float32) * near
            d_gate_out[rows, :] = (d_act * slope_ref[held, :]).astype(jnp.bfloat16)
            d_up_out[rows, :] = (d_act * silu_ref[held, :]).astype(jnp.bfloat16)
            gate_grad = jnp.sum(act_ref[held, :].astype(jnp.float32) * near, axis=1, keepdims=True)
            columns = jnp.where(wide_lane == expert ^ which, gate_grad, columns)
        out_refs[index][:, model_width:] = columns.astype(jnp.bfloat16)

    sides = (d_gate_ref, d_up_ref, other_d_gate_ref, other_d_up_ref)
    for first in range(0, model_width, 256):
        columns = slice(first, first + 256)
        pick_grad = None
        for side_ref, matrix in zip(sides, matrices):
            term = lax.dot_general(
                side_ref[...], matrix[columns, :], across, preferred_element_type=jnp.float32
            )
            pick_grad = term if pick_grad is None else pick_grad + term
        pick_grad = pick_grad.astype(jnp.bfloat16)
        for index, out_ref in enumerate(out_refs):
            out_ref[:, columns] = pick_grad[index * size : (index + 1) * size]


def back(owners, starts, near, other_near, gates, saved, matrices):
    model_width, hidden_units = matrices[0].shape
    size = gates.shape[0] // len(owners)
    return kernel_call(
        functools.partial(back_kernel, owners, starts),
        "back",
        [kept((size, model_width + 128), jnp.bfloat16)] * len(owners),
        [pinned(array) for array in (near, other_near, gates, *saved, *matrices)],
        (),
        [pltpu.VMEM((len(owners) * size, hidden_units), jnp.bfloat16)] * 4,
    )


def add_kernel(x_ref, y_ref, high_ref, low_ref, x_out, y_out):
    half = high_ref.shape[0]
    x_out[:half, :] = x_ref[:half, :]
    y_out[half:, :] = y_ref[half:, :]
    x_out[half:, :] = (
        x_ref[half:, :].astype(jnp.float32) + high_ref[...].astype(jnp.float32)
    ).astype(jnp.bfloat16)
    y_out[:half, :] = (
        y_ref[:half, :].astype(jnp.float32) + low_ref[...].astype(jnp.float32)
    ).astype(jnp.bfloat16)


def half_kernel(part, rows_ref, out_ref):
    half = out_ref.shape[0]
    out_ref[...] = rows_ref[part * half : (part + 1) * half, :]


def half_of(rows, part):
    total, wide = rows.shape
    (out,) = kernel_call(
        functools.partial(half_kernel, part), "half", [kept((total // 2, wide), rows.dtype)], [rows]
    )
    return out


def pack_kernel(first_ref, second_ref, out_ref):
    rows = first_ref.shape[0]
    out_ref[:rows, :] = first_ref[...]
    out_ref[rows:, :] = second_ref[...]


def pack(first, second, work=1):
    rows, wide = first.shape
    return kernel_call(
        pack_kernel, "pack", [kept((2 * rows, wide), first.dtype)], [first, second], work=work
    )[0]


def rank_kernel(grades_far, ranks_far, *refs):
    near_scores_ref, far_scores_ref, loss_ref, factor_ref, grades_ref, ranks_ref, copy_sems = refs
    copies = [
        pltpu.make_async_copy(grades_far, grades_ref, copy_sems.at[0]),
        pltpu.make_async_copy(ranks_far, ranks_ref, copy_sems.at[1]),
    ]
    for copy in copies:
        copy.start()
    for copy in copies:
        copy.wait()
    passages = grades_ref.shape[1]
    place = lax.axis_index("psg")
    row = lax.broadcasted_iota(jnp.int32, (8, 128), 0)
    lane = lax.broadcasted_iota(jnp.int32, (8, 128), 1)

    def spread(index, values):
        total = jnp.zeros((8, 128), jnp.float32)
        for number, value in values:
            total = jnp.where(index == number, value, total)
        return total

    grade_list = [(number, grades_ref[0, number].astype(jnp.float32)) for number in range(passages)]
    rank_list = [(number, ranks_ref[0, number].astype(jnp.float32)) for number in range(passages)]
    score_list = [
        (place ^ (base + number), jnp.broadcast_to(ref[number : number + 1, :], (8, 128)))
        for base, ref in ((0, near_scores_ref), (passages // 2, far_scores_ref))
        for number in range(passages // 2)
    ]
    grade_row, grade_lane = spread(row, grade_list), spread(lane, grade_list)
    worth_row, worth_lane = jnp.exp2(grade_row), jnp.exp2(grade_lane)
    discount_row = 1.0 / jnp.log2(2.0 + spread(row, rank_list))
    discount_lane = 1.0 / jnp.log2(2.0 + spread(lane, rank_list))
    score_row, score_lane = spread(row, score_list), spread(lane, score_list)
    pair = jnp.logical_and(row < passages, lane < passages)
    ahead = jnp.logical_or(
        grade_lane > grade_row, jnp.logical_and(grade_lane == grade_row, lane < row)
    )
    ideal_rank = jnp.sum(
        jnp.where(jnp.logical_and(pair, ahead), 1.0, 0.0), axis=1, keepdims=True
    )
    ideal_terms = (worth_row - 1.0) / jnp.log2(2.0 + ideal_rank)
    one_lane = jnp.logical_and(pair, lane == 0)

    def whole_sum(values):
        return jnp.sum(jnp.sum(values, axis=1, keepdims=True), axis=0, keepdims=True)

    ideal_gain = whole_sum(jnp.where(one_lane, ideal_terms, 0.0))
    swap_gain = (
        jnp.abs((worth_row - worth_lane) * (discount_row - discount_lane)) / ideal_gain
    )
    swap_gain = jnp.where(jnp.logical_and(pair, grade_row > grade_lane), swap_gain, 0.0)
    margin = score_row - score_lane
    softplus = jnp.maximum(-margin, 0.0) + jnp.log1p(jnp.exp(-jnp.abs(margin)))
    loss_ref[...] = whole_sum(swap_gain * softplus)
    pull = swap_gain * jax.nn.sigmoid(-margin)
    gradient = whole_sum(jnp.where(lane == place, pull, 0.0) - jnp.where(row == place, pull, 0.0))
    factor_ref[...] = jnp.broadcast_to(gradient * loss_scale, factor_ref.shape)


def end_kernel(
    factor_ref, own_ref, x_ref, y_ref,
    hidden_ref, gain_ref, gates_ref, router_ref, unit_ref, grad_ref,
):
    model_width = hidden_ref.shape[1]
    size = 32
    router_rows = jnp.concatenate([router_ref[...]] * 3, axis=0)
    gain = gain_ref[...]
    factor = factor_ref[:, :1]
    for first in range(0, hidden_ref.shape[0], size):
        rows = slice(first, first + size)
        total = own_ref[rows, :].astype(jnp.float32) + (
            x_ref[rows, :].astype(jnp.float32) + y_ref[rows, :].astype(jnp.float32)
        )
        gates = gates_ref[rows, :]
        slot_grad = total[:, model_width : model_width + 8]
        d_logit = gates * (slot_grad - jnp.sum(gates * slot_grad, axis=1, keepdims=True))
        d_normed = total[:, :model_width] + jnp.dot(
            jnp.concatenate(split_low(d_logit), axis=1),
            router_rows,
            preferred_element_type=jnp.float32,
        )
        flat_rows = hidden_ref[rows, :].astype(jnp.float32)
        grad = norm_back(flat_rows, rms_scale(flat_rows), gain, d_normed) + unit_ref[...]
        grad_ref[rows, :] = (grad * factor).astype(jnp.bfloat16)


def every_expert(
    hidden,
    norm_gain,
    router,
    gate_proj,
    up_proj,
    down_proj,
    final_gain,
    score_vector,
    expert_ids,
    grades,
    passage_ranks,
):
    unused_query, unused_passage, token_count, model_width = hidden.shape
    passages = grades.shape[1]
    flat = hidden.reshape(token_count, model_width)
    gate_matrix, up_matrix, down_matrix = gate_proj[0], up_proj[0], down_proj[0]
    mine = [gate_matrix, up_matrix, down_matrix]
    others = [swap(matrix, CORE) for matrix in mine]

    flat, gain, router_rows, normed, token_sums, head = kernel_call(
        norm_kernel,
        "norm",
        [
            kept(flat.shape, jnp.bfloat16),
            kept((1, model_width), jnp.float32),
            kept((8, model_width), jnp.bfloat16),
            kept(flat.shape, jnp.bfloat16),
            kept((1, model_width), jnp.float32),
            kept((1, model_width), jnp.float32),
        ],
        [
            flat,
            norm_gain.reshape(1, model_width),
            router.T,
            final_gain.reshape(1, model_width),
            score_vector.reshape(model_width // 128, 128),
        ],
        range(5),
        [
            pltpu.VMEM((1, model_width), jnp.float32),
            pltpu.VMEM((model_width // 128, 128), jnp.bfloat16),
            pltpu.SemaphoreType.DMA((5,)),
        ],
    )
    x_rows, y_rows = swap(normed, ACROSS_X), swap(normed, ACROSS_Y)
    own_gates, *own_saved, own_part, mine[0], mine[1] = front(
        0, (0,), (0,), [normed], router_rows, mine[:2]
    )
    x_rows, y_rows = after(x_rows, own_part), after(y_rows, own_part)
    far_low = swap(half_of(x_rows, 0), ACROSS_Y)
    far_high = swap(half_of(y_rows, 1), ACROSS_X)
    side_gates, *side_saved, side_part, mine[2] = front(
        1, (1, 2), (0,), [x_rows, y_rows], router_rows, mine[:2], mine[2:]
    )
    others[0] = after(others[0], side_part)
    unused, *other_saved, other_part = front(
        2, (0, 1, 2), (1,), [normed, x_rows, y_rows], router_rows, others[:2]
    )
    far_low, far_high = after(far_low, other_part), after(far_high, other_part)
    far_gates, *far_saved, terms = front(
        3, (3,), (0, 1), [far_low, far_high], router_rows, mine[:2] + others[:2],
        (token_sums, mine[2], others[2], own_part, side_part, other_part),
    )

    near, other_near, unit_vector, travelling, own_score = kernel_call(
        functools.partial(near_kernel, token_count=token_count),
        "near",
        [
            kept((8, down_matrix.shape[0]), jnp.float32),
            kept((8, down_matrix.shape[0]), jnp.float32),
            kept((1, model_width), jnp.float32),
            kept((1, 128), jnp.float32),
            shape_of((1, 1), jnp.float32),
        ],
        [
            pinned(terms),
            swap(terms, ACROSS_X),
            swap(terms, ACROSS_Y),
            swap(terms, ACROSS_X | ACROSS_Y),
            pinned(head),
            pinned(mine[2]),
            pinned(others[2]),
        ],
    )
    matrices = mine[:2] + others[:2]
    (far,) = back((3,), (0, 0), near, other_near, far_gates, far_saved, matrices)
    far_low = swap(half_of(far, 0), ACROSS_X)
    far_high = swap(half_of(far, 1), ACROSS_Y)
    x_sums, y_sums = back(
        (1, 2), (0, token_count), after(near, far), other_near, side_gates,
        side_saved + other_saved, matrices,
    )
    (own_sums,) = back(
        (0,), (0, 0), after(near, x_sums), other_near, own_gates, own_saved + other_saved, matrices
    )
    far_high = after(far_high, own_sums)
    x_sums, y_sums = kernel_call(
        add_kernel,
        "add",
        [kept(x_sums.shape, jnp.bfloat16)] * 2,
        [pinned(x_sums), pinned(y_sums), far_high, far_low],
    )
    x_sums, y_sums, travelling = lax.optimization_barrier((x_sums, y_sums, travelling))
    x_sums, y_sums = swap(x_sums, ACROSS_X), swap(y_sums, ACROSS_Y)
    met = lax.ppermute(travelling, "psg", [(index, index ^ 1) for index in range(passages)])
    near_scores = pack(travelling, met)
    far_scores = lax.ppermute(near_scores, "psg", [(index, index ^ 2) for index in range(passages)])
    loss, factor = kernel_call(
        rank_kernel,
        "rank",
        [shape_of((1, 1), jnp.float32), kept((1, 128), jnp.float32)],
        [
            grades,
            passage_ranks,
            pinned(near_scores),
            far_scores,
        ],
        (0, 1),
        [
            pltpu.SMEM(grades.shape, jnp.int32),
            pltpu.SMEM(grades.shape, jnp.int32),
            pltpu.SemaphoreType.DMA((2,)),
        ],
    )
    (grad,) = kernel_call(
        end_kernel,
        "end",
        [shape_of((token_count, model_width), jnp.bfloat16)],
        [
            pinned(factor), pinned(own_sums), x_sums, y_sums, pinned(flat), pinned(gain),
            pinned(own_gates), pinned(router_rows), pinned(unit_vector),
        ],
    )
    return (loss.reshape(1), own_score, grad.reshape(hidden.shape))


def block(*arrays):
    hidden, router, expert_ids, grades = arrays[0], arrays[2], arrays[8], arrays[9]
    each_expert = router.shape[1] == expert_ids.shape[3] == 8
    if hidden.shape[1] == 1 and each_expert and grades.shape[1] == 4:
        return every_expert(*arrays)
    return local(*arrays)


def solution(mesh):
    placed = (
        P("exp", "psg", None, None),
        P(),
        P(),
        P("exp", None, None),
        P("exp", None, None),
        P("exp", None, None),
        P(),
        P(),
        P("exp", "psg", None, None),
        P("exp", None),
        P("exp", None),
    )
    return jax.shard_map(
        block,
        mesh=mesh,
        in_specs=placed,
        out_specs=(P("exp"), P("exp", "psg"), P("exp", "psg", None, None)),
        check_vma=False,
    )
```

```python
import functools
import math

import jax
import jax.numpy as jnp
from jax import lax
from jax.experimental import pallas as pl
from jax.experimental.pallas import tpu as pltpu
from jax.sharding import PartitionSpec as P

epsilon = 1e-06
loss_scale = 256.0
highest = lax.Precision.HIGHEST


def rms_scale(values):
    return lax.rsqrt(jnp.mean(values * values, axis=-1, keepdims=True) + epsilon)


def head_score(pooled, final_gain, score_vector):
    scaled = pooled * rms_scale(pooled) * final_gain
    return jnp.dot(scaled, score_vector.astype(jnp.float32), precision=highest)


def rank_loss(scores, grades, passage_ranks):
    grade_value = grades.astype(jnp.float32)
    worth_gain = jnp.exp2(grade_value)
    discount = 1.0 / jnp.log2(2.0 + passage_ranks.astype(jnp.float32))
    better_than = grades[None, :] > grades[:, None]
    equal_grade = grades[None, :] == grades[:, None]
    position = jnp.arange(grades.shape[0], dtype=jnp.int32)
    earlier = position[None, :] < position[:, None]
    ideal_rank = jnp.sum(
        jnp.logical_or(better_than, jnp.logical_and(equal_grade, earlier)).astype(jnp.float32),
        axis=1,
    )
    ideal_gain = jnp.sum((worth_gain - 1.0) / jnp.log2(2.0 + ideal_rank))
    ordered = (grades[:, None] > grades[None, :]).astype(jnp.float32)
    swap_gain = (
        jnp.abs(
            (worth_gain[:, None] - worth_gain[None, :]) * (discount[:, None] - discount[None, :])
        )
        / ideal_gain
    )
    margin = scores[:, None] - scores[None, :]
    return jnp.sum(ordered * swap_gain * jax.nn.softplus(-margin))


def pick_gates(normed, router, picked_ids):
    expert_total = router.shape[1]
    logits = jnp.dot(normed, router, preferred_element_type=jnp.float32)
    onehot = (
        picked_ids[:, :, None] == jnp.arange(expert_total, dtype=jnp.int32)[None, None, :]
    ).astype(jnp.float32)
    chosen = jnp.einsum("nke,ne->nk", onehot, logits, precision=highest)
    weights = jnp.exp(chosen)
    return (weights / jnp.sum(weights, axis=1, keepdims=True), onehot)


def gate_parts(pre_gate):
    sigmoid_gate = jax.nn.sigmoid(pre_gate)
    return (pre_gate * sigmoid_gate, sigmoid_gate * (1.0 + pre_gate * (1.0 - sigmoid_gate)))


def norm_back(flat_rows, inverse, norm_gain, d_normed):
    scaled = d_normed * norm_gain
    return inverse * scaled - flat_rows * inverse * inverse * inverse * jnp.mean(
        flat_rows * scaled, axis=-1, keepdims=True
    )


def unpack_front(front_out, buffer_rows):
    pre_gate, pre_up, received = front_out
    hidden_units = pre_gate.shape[2]
    pre_gate = pre_gate.reshape(buffer_rows, hidden_units)
    pre_up = pre_up.reshape(buffer_rows, hidden_units)
    silu_gate, slope = gate_parts(pre_gate)
    activation = (silu_gate * pre_up).astype(jnp.bfloat16)
    return (pre_up, received, silu_gate, slope, activation)


def local(
    hidden,
    norm_gain,
    router,
    gate_proj,
    up_proj,
    down_proj,
    final_gain,
    score_vector,
    expert_ids,
    grades,
    passage_ranks,
):
    unused_query, local_passages, local_positions, model_width = hidden.shape
    top_count = expert_ids.shape[3]
    expert_count = lax.axis_size("exp")
    token_count = local_passages * local_positions
    slot_count = token_count * top_count
    capacity = min(token_count, 9 * token_count * top_count // (8 * expert_count))
    buffer_rows = expert_count * capacity
    flat_rows = hidden.reshape(token_count, model_width).astype(jnp.float32)
    inverse = rms_scale(flat_rows)
    normed = (flat_rows * inverse * norm_gain).astype(jnp.bfloat16)
    picked_ids = expert_ids.reshape(token_count, top_count)
    gate_values, onehot = pick_gates(normed, router, picked_ids)
    slot_hits = onehot.reshape(slot_count, expert_count).astype(jnp.int32)
    slot_rank = jnp.sum((jnp.cumsum(slot_hits, axis=0) - slot_hits) * slot_hits, axis=1)
    target = picked_ids.reshape(slot_count) * capacity + slot_rank
    source_token = jnp.arange(slot_count, dtype=jnp.int32) // top_count
    passage_onehot = (
        source_token[:, None] // local_positions
        == jnp.arange(local_passages, dtype=jnp.int32)[None, :]
    ).astype(jnp.float32)
    weighted = (passage_onehot * gate_values.reshape(slot_count, 1)).astype(jnp.bfloat16)
    send_rows = (
        jnp.zeros((buffer_rows, model_width), jnp.bfloat16).at[target].set(normed[source_token])
    )
    send_weights = jnp.zeros((buffer_rows, local_passages), jnp.bfloat16).at[target].set(weighted)
    outgoing = (
        send_rows.reshape(expert_count, capacity, model_width),
        send_weights.reshape(expert_count, capacity, local_passages),
    )
    gate_matrix = gate_proj[0]
    up_matrix = up_proj[0]
    down_matrix = down_proj[0]
    rows_in = lax.all_to_all(outgoing[0], "exp", split_axis=0, concat_axis=0, tiled=True)
    weights_in = lax.all_to_all(outgoing[1], "exp", split_axis=0, concat_axis=0, tiled=True)
    pre_gate = jnp.einsum("end,df->enf", rows_in, gate_matrix, preferred_element_type=jnp.float32)
    pre_up = jnp.einsum("end,df->enf", rows_in, up_matrix, preferred_element_type=jnp.float32)
    front_out = (pre_gate, pre_up, weights_in)
    pre_up, received, silu_gate, slope, activation = unpack_front(front_out, buffer_rows)
    hidden_units = activation.shape[1]
    passage_part = jnp.einsum(
        "scp,scf->spf",
        received,
        activation.reshape(expert_count, capacity, hidden_units),
        preferred_element_type=jnp.float32,
    )
    down_wide = down_matrix.astype(jnp.float32)
    expert_terms = jnp.einsum("spf,fd->spd", passage_part, down_wide, precision=highest)
    came_back = lax.all_to_all(expert_terms, "exp", split_axis=0, concat_axis=0, tiled=True)
    token_sums = jnp.sum(flat_rows.reshape(local_passages, local_positions, model_width), axis=1)
    pooled = (token_sums + jnp.sum(came_back, axis=0)) / local_positions
    first_row = lax.axis_index("psg") * local_passages
    own_score = head_score(pooled, final_gain, score_vector)
    every_score = lax.all_gather(own_score, "psg", axis=0, tiled=True)
    loss_value, loss_grad = jax.value_and_grad(rank_loss)(every_score, grades[0], passage_ranks[0])
    d_own = lax.dynamic_slice_in_dim(loss_grad, first_row, local_passages, 0) * loss_scale
    unused_score, head_back = jax.vjp(
        lambda values: head_score(values, final_gain, score_vector), pooled
    )
    d_vector = head_back(d_own)[0] / local_positions
    every_vector = lax.all_gather(d_vector[None], "exp", axis=0, tiled=True)
    near_table = jnp.einsum("spd,fd->spf", every_vector, down_wide, precision=highest)
    present = (received != 0).astype(jnp.float32)
    near_rows = jnp.einsum("scp,spf->scf", present, near_table, precision=highest).reshape(
        buffer_rows, hidden_units
    )
    gate_weight = jnp.sum(received.astype(jnp.float32), axis=2).reshape(buffer_rows, 1)
    d_act = gate_weight * near_rows
    d_gate = (d_act * pre_up * slope).astype(jnp.bfloat16)
    d_up = (d_act * silu_gate).astype(jnp.bfloat16)
    contract = (((1,), (1,)), ((), ()))
    pick_grad = lax.dot_general(d_gate, gate_matrix, contract, preferred_element_type=jnp.float32)
    pick_grad = (
        pick_grad + lax.dot_general(d_up, up_matrix, contract, preferred_element_type=jnp.float32)
    ).astype(jnp.bfloat16)
    gate_grad = jnp.sum(activation.astype(jnp.float32) * near_rows, axis=1).astype(jnp.bfloat16)
    back_rows, back_gate = (
        lax.all_to_all(
            pick_grad.reshape(expert_count, capacity, model_width),
            "exp",
            split_axis=0,
            concat_axis=0,
            tiled=True,
        ),
        lax.all_to_all(
            gate_grad.reshape(expert_count, capacity),
            "exp",
            split_axis=0,
            concat_axis=0,
            tiled=True,
        ),
    )
    picked_rows = back_rows.reshape(buffer_rows, model_width)[target]
    d_normed = jnp.sum(
        picked_rows.reshape(token_count, top_count, model_width).astype(jnp.float32), axis=1
    )
    picked_gate = (
        back_gate.reshape(buffer_rows)[target].astype(jnp.float32).reshape(token_count, top_count)
    )
    d_logit = gate_values * (
        picked_gate - jnp.sum(gate_values * picked_gate, axis=1, keepdims=True)
    )
    dense_logit = jnp.einsum("nk,nke->ne", d_logit, onehot, precision=highest)
    d_normed = d_normed + jnp.einsum(
        "ne,de->nd", dense_logit, router.astype(jnp.float32), precision=highest
    )
    grad_flat = norm_back(flat_rows, inverse, norm_gain, d_normed)
    grad_hidden = (
        grad_flat.reshape(1, local_passages, local_positions, model_width)
        + d_vector[None, :, None, :]
    )
    return (
        loss_value.reshape(1),
        own_score.reshape(1, local_passages),
        grad_hidden.astype(jnp.bfloat16),
    )


CORE, ACROSS_X, ACROSS_Y = 1, 2, 4
forward = (((1,), (0,)), ((), ()))
across = (((1,), (1,)), ((), ()))
MIB = 1 << 20


def swap(value, bit, size=8):
    return lax.ppermute(value, "exp", [(index, index ^ bit) for index in range(size)])


def shape_of(shape, dtype):
    return jax.ShapeDtypeStruct(shape, dtype)


def after(value, *others):
    return lax.optimization_barrier((value, *others))[0]


def kept(shape, dtype):
    return pltpu.VMEM(shape, dtype)


def pinned(array):
    return pltpu.with_memory_space_constraint(array, pltpu.VMEM)


def kernel_call(body, name, outs, ins, far=(), scratch=(), work=1, result=pltpu.VMEM):
    spaces = [pltpu.VMEM] * len(ins)
    ins = list(ins)
    for index in far:
        spaces[index] = pl.ANY
        ins[index] = pltpu.with_memory_space_constraint(ins[index], pltpu.HBM)
    return pl.pallas_call(
        body,
        name=name,
        out_shape=outs,
        in_specs=[pl.BlockSpec(memory_space=space) for space in spaces],
        out_specs=[pl.BlockSpec(memory_space=result)] * len(outs),
        scratch_shapes=scratch,
        compiler_params=pltpu.CompilerParams(vmem_limit_bytes=8 * MIB),
        cost_estimate=pl.CostEstimate(flops=work, bytes_accessed=1, transcendentals=0),
    )(*ins)


def split_low(values):
    high = values.astype(jnp.bfloat16)
    rest = values - high.astype(jnp.float32)
    middle = rest.astype(jnp.bfloat16)
    low = (rest - middle.astype(jnp.float32)).astype(jnp.bfloat16)
    return high, middle, low


def exact_dot(values, low_matrix, contract):
    parts = lax.dot_general(
        jnp.concatenate(split_low(values), axis=0),
        low_matrix,
        contract,
        preferred_element_type=jnp.float32,
    )
    return parts[0:8] + parts[8:16] + parts[16:24]


def other_order(values, bits):
    return jnp.concatenate([values[row ^ bits : (row ^ bits) + 1] for row in range(4)], axis=0)


def norm_kernel(
    hidden_far, gain_far, router_far, final_far, vector_far,
    hidden_ref, gain_ref, router_ref, normed_ref, sums_ref, head_ref,
    final_ref, vector_ref, copy_sems,
):
    pairs = (
        (hidden_far, hidden_ref), (gain_far, gain_ref), (router_far, router_ref),
        (final_far, final_ref), (vector_far, vector_ref),
    )
    copies = [
        pltpu.make_async_copy(source, target, copy_sems.at[index])
        for index, (source, target) in enumerate(pairs)
    ]
    for copy in copies:
        copy.start()
    for copy in copies:
        copy.wait()
    vector = vector_ref[...].astype(jnp.float32)
    vector = jnp.concatenate([vector[row : row + 1] for row in range(vector.shape[0])], axis=1)
    head_ref[...] = final_ref[...] * vector
    rows = hidden_ref[...].astype(jnp.float32)
    normed_ref[...] = (rows * rms_scale(rows) * gain_ref[...]).astype(jnp.bfloat16)
    sums_ref[...] = jnp.sum(rows, axis=0, keepdims=True)


def front_kernel(stage, owners, sets, count, router_ref, *refs):
    matrices, refs = refs[: 2 * len(sets)], refs[2 * len(sets) :]
    pieces, refs = refs[:count], refs[count:]
    matrices = list(matrices)
    hidden_units = matrices[0].shape[1]
    tile = 256
    firsts = range(0, hidden_units, tile)
    if stage == 0:
        far_matrices = matrices
        *refs, gate_held, up_held, rows_ref, copy_sems = refs
        matrices = [gate_held, up_held]
        copies = [
            pltpu.make_async_copy(
                source.at[:, first : first + tile],
                target.at[:, first : first + tile],
                copy_sems.at[which, number],
            )
            for number, first in enumerate(firsts)
            for which, (source, target) in enumerate(zip(far_matrices, matrices))
        ]
        for copy in copies:
            copy.start()
        turned_ref, *refs = refs
    elif stage == 1:
        down_far, *refs, down_ref, rows_ref, copy_sem = refs
        down_copy = pltpu.make_async_copy(down_far, down_ref, copy_sem)
        down_copy.start()
    elif stage == 3:
        sums_ref, *downs = refs[:3]
        earlier, refs = refs[3:6], refs[6:]
        *refs, terms_ref, rows_ref = refs
    else:
        *refs, rows_ref = refs
    gates_ref, *outs = refs
    expert = lax.axis_index("exp")
    first = 0
    for piece in pieces:
        rows_ref[first : first + piece.shape[0], :] = piece[...]
        first += piece.shape[0]
    size = first // len(owners)
    logits = lax.dot_general(
        rows_ref[...], router_ref[...], across, preferred_element_type=jnp.float32
    )
    weights = jnp.exp(logits)
    gates = weights / jnp.sum(weights, axis=1, keepdims=True)
    gates_ref[...] = gates
    lane = lax.broadcasted_iota(jnp.int32, gates.shape, 1)
    if stage == 0:
        weights = jnp.exp(
            lax.dot_general(
                router_ref[...], rows_ref[...], across, preferred_element_type=jnp.float32
            )
        )
        turned_ref[...] = weights / jnp.sum(weights, axis=0, keepdims=True)

    totals = []
    for place, which in enumerate(sets):
        gate_ref, up_ref = matrices[2 * place : 2 * place + 2]
        if stage == 3:
            slope_ref, silu_ref, act_ref = outs[3 * place : 3 * place + 3]
        else:
            slope_ref, silu_ref, act_ref, part_ref = outs
        own = jnp.sum(jnp.where(lane == expert ^ which, gates, 0.0), axis=1, keepdims=True)
        low = own.astype(jnp.bfloat16).astype(jnp.float32)
        parts = []
        for number, first in enumerate(firsts):
            columns = slice(first, first + tile)
            if stage == 0:
                copies[2 * number].wait()
                copies[2 * number + 1].wait()
            rows = rows_ref[...]
            pre_gate = jnp.dot(rows, gate_ref[:, columns], preferred_element_type=jnp.float32)
            pre_up = jnp.dot(rows, up_ref[:, columns], preferred_element_type=jnp.float32)
            silu_gate, slope = gate_parts(pre_gate)
            activation = (silu_gate * pre_up).astype(jnp.bfloat16)
            slope_ref[:, columns] = slope * pre_up
            silu_ref[:, columns] = silu_gate
            act_ref[:, columns] = activation
            weighted = activation.astype(jnp.float32) * low
            found = {
                owner: jnp.sum(weighted[index * size : (index + 1) * size], axis=0, keepdims=True)
                for index, owner in enumerate(owners)
            }
            nothing = jnp.zeros_like(weighted[:1])
            parts.append(
                jnp.concatenate([found.get(owner, nothing) for owner in range(8)], axis=0)
            )
        totals.append(jnp.concatenate(parts, axis=1))
    if stage == 1:
        down_copy.wait()
    if stage < 3:
        part_ref[...] = totals[0]
        return
    own_first, own_second, other_first = earlier
    totals[0] = totals[0] + (own_first[...] + own_second[...])
    totals[1] = totals[1] + other_first[...]
    terms = exact_dot(totals[0], downs[0][...], forward) + exact_dot(
        totals[1], downs[1][...], forward
    )
    row = lax.broadcasted_iota(jnp.int32, terms.shape, 0)
    terms_ref[...] = (terms + jnp.where(row == 0, sums_ref[...], 0.0))[:4]


def front(stage, owners, sets, pieces, router_rows, matrices, more=()):
    model_width, hidden_units = matrices[0].shape
    row_total = sum(piece.shape[0] for piece in pieces)
    outs = [kept((row_total, 8), jnp.float32)]
    if stage == 0:
        outs.insert(0, kept((8, row_total), jnp.float32))
    for which in sets:
        outs += [
            kept((row_total, hidden_units), jnp.float32),
            kept((row_total, hidden_units), jnp.float32),
            kept((row_total, hidden_units), jnp.bfloat16),
        ]
    outs.append(
        kept((4, model_width), jnp.float32) if stage == 3 else kept((8, hidden_units), jnp.float32)
    )
    scratch = [pltpu.VMEM((row_total, model_width), jnp.bfloat16)]
    far = ()
    if stage == 0:
        far = (1, 2)
        outs += [kept(matrix.shape, jnp.bfloat16) for matrix in matrices]
        scratch.append(pltpu.SemaphoreType.DMA((2, hidden_units // 256)))
    else:
        matrices = [pinned(matrix) for matrix in matrices]
    if stage == 1:
        far = (3 + len(pieces),)
        outs.append(kept(more[0].shape, jnp.bfloat16))
        scratch.append(pltpu.SemaphoreType.DMA)
    if stage == 3:
        more = [pinned(array) for array in more]
    return kernel_call(
        functools.partial(front_kernel, stage, owners, sets, len(pieces)),
        "front",
        outs,
        [pinned(router_rows), *matrices, *(pinned(piece) for piece in pieces), *more],
        far,
        scratch,
    )


def near_kernel(
    own_ref, x_ref, y_ref, far_ref, head_ref, down_ref, other_down_ref,
    near_ref, other_near_ref, unit_ref, score_ref, own_score_ref, *, token_count,
):
    pooled = (
        (own_ref[...] + other_order(x_ref[...], 1))
        + (other_order(y_ref[...], 2) + other_order(far_ref[...], 3))
    ) / token_count
    pooled = jnp.concatenate([pooled, jnp.zeros_like(pooled)], axis=0)
    head = head_ref[...]
    scale = rms_scale(pooled)
    along = jnp.sum(pooled * head, axis=1, keepdims=True)
    own_score = (scale * along)[:1]
    own_score_ref[...] = own_score
    score_ref[...] = jnp.broadcast_to(own_score, score_ref.shape)
    unit = (
        scale * head - scale * scale * scale * (along / pooled.shape[1]) * pooled
    ) / token_count
    unit_ref[...] = unit[:1]
    parts = jnp.concatenate(split_low(unit), axis=0)
    parts = jnp.concatenate([parts, jnp.zeros((104, parts.shape[1]), jnp.bfloat16)], axis=0)
    for table_ref, matrix_ref in ((near_ref, down_ref), (other_near_ref, other_down_ref)):
        turned = lax.dot_general(
            matrix_ref[...], parts, across, preferred_element_type=jnp.float32
        ).T
        table_ref[...] = turned[0:8] + turned[8:16] + turned[16:24]


def back_kernel(owners, starts, cuts, near_ref, other_near_ref, gates_ref, *refs):
    saved, matrices, refs = refs[:6], refs[6:10], refs[10:]
    *out_refs, d_gate_ref, d_up_ref, other_d_gate_ref, other_d_up_ref = refs
    expert = lax.axis_index("exp")
    size = out_refs[0].shape[1]
    model_width = matrices[0].shape[0]
    lane = lax.broadcasted_iota(jnp.int32, (size, 8), 1)
    line = lax.broadcasted_iota(jnp.int32, (16, size), 0)
    experts = (
        (near_ref, saved[:3], d_gate_ref, d_up_ref),
        (other_near_ref, saved[3:], other_d_gate_ref, other_d_up_ref),
    )
    for index, owner in enumerate(owners):
        rows = slice(index * size, (index + 1) * size)
        lines = jnp.zeros((16, size), jnp.float32)
        for which, (table_ref, arrays, d_gate_out, d_up_out) in enumerate(experts):
            slope_ref, silu_ref, act_ref = arrays
            held = slice(starts[which] + index * size, starts[which] + (index + 1) * size)
            near = table_ref[owner : owner + 1, :]
            own = jnp.sum(
                jnp.where(lane == expert ^ which, gates_ref[rows, :], 0.0), axis=1, keepdims=True
            )
            d_act = own.astype(jnp.bfloat16).astype(jnp.float32) * near
            d_gate_out[rows, :] = (d_act * slope_ref[held, :]).astype(jnp.bfloat16)
            d_up_out[rows, :] = (d_act * silu_ref[held, :]).astype(jnp.bfloat16)
            gate_grad = exact_dot(table_ref[...], act_ref[held, :], across)[owner : owner + 1]
            lines = jnp.where(line == expert ^ which, gate_grad, lines)
        last = out_refs[(index + 1) * len(cuts) - 1]
        last[model_width - cuts[-1] :, :] = lines.astype(jnp.bfloat16)

    sides = (d_gate_ref, d_up_ref, other_d_gate_ref, other_d_up_ref)
    for first in range(0, model_width, 256):
        pick_grad = None
        for side_ref, matrix in zip(sides, matrices):
            term = lax.dot_general(
                matrix[first : first + 256, :],
                side_ref[...],
                across,
                preferred_element_type=jnp.float32,
            )
            pick_grad = term if pick_grad is None else pick_grad + term
        pick_grad = pick_grad.astype(jnp.bfloat16)
        place = max(number for number, cut in enumerate(cuts) if cut <= first)
        rows = slice(first - cuts[place], first - cuts[place] + 256)
        for index in range(len(owners)):
            out_ref = out_refs[index * len(cuts) + place]
            out_ref[rows, :] = pick_grad[:, index * size : (index + 1) * size]


def back(owners, starts, cuts, near, other_near, gates, saved, matrices):
    model_width, hidden_units = matrices[0].shape
    size = gates.shape[0] // len(owners)
    ends = cuts[1:] + (model_width + 16,)
    heights = [end - cut for cut, end in zip(cuts, ends)] * len(owners)
    return kernel_call(
        functools.partial(back_kernel, owners, starts, cuts),
        "back",
        [kept((height, size), jnp.bfloat16) for height in heights],
        [pinned(array) for array in (near, other_near, gates, *saved, *matrices)],
        (),
        [pltpu.VMEM((len(owners) * size, hidden_units), jnp.bfloat16)] * 4,
    )


def add_kernel(x_ref, y_ref, high_ref, low_ref, x_out, y_out):
    cut = low_ref.shape[0]
    x_out[:cut, :] = x_ref[:cut, :]
    y_out[cut:, :] = y_ref[cut:, :]
    x_out[cut:, :] = (
        x_ref[cut:, :].astype(jnp.float32) + high_ref[...].astype(jnp.float32)
    ).astype(jnp.bfloat16)
    y_out[:cut, :] = (
        y_ref[:cut, :].astype(jnp.float32) + low_ref[...].astype(jnp.float32)
    ).astype(jnp.bfloat16)


def half_kernel(part, rows_ref, out_ref):
    half = out_ref.shape[0]
    out_ref[...] = rows_ref[part * half : (part + 1) * half, :]


def half_of(rows, part):
    total, wide = rows.shape
    (out,) = kernel_call(
        functools.partial(half_kernel, part), "half", [kept((total // 2, wide), rows.dtype)], [rows]
    )
    return out


def pack_kernel(first_ref, second_ref, out_ref):
    rows = first_ref.shape[0]
    out_ref[:rows, :] = first_ref[...]
    out_ref[rows:, :] = second_ref[...]


def pack(first, second, work=1):
    rows, wide = first.shape
    return kernel_call(
        pack_kernel, "pack", [kept((2 * rows, wide), first.dtype)], [first, second], work=work
    )[0]


def rank_kernel(grades_far, ranks_far, *refs):
    near_scores_ref, far_scores_ref, loss_ref, factor_ref, grades_ref, ranks_ref, copy_sems = refs
    copies = [
        pltpu.make_async_copy(grades_far, grades_ref, copy_sems.at[0]),
        pltpu.make_async_copy(ranks_far, ranks_ref, copy_sems.at[1]),
    ]
    for copy in copies:
        copy.start()
    for copy in copies:
        copy.wait()
    passages = grades_ref.shape[1]
    place = lax.axis_index("psg")
    row = lax.broadcasted_iota(jnp.int32, (8, 128), 0)
    lane = lax.broadcasted_iota(jnp.int32, (8, 128), 1)

    def spread(index, values):
        total = jnp.zeros((8, 128), jnp.float32)
        for number, value in values:
            total = jnp.where(index == number, value, total)
        return total

    grade_list = [(number, grades_ref[0, number].astype(jnp.float32)) for number in range(passages)]
    rank_list = [(number, ranks_ref[0, number].astype(jnp.float32)) for number in range(passages)]
    score_list = [
        (place ^ (base + number), jnp.broadcast_to(ref[number : number + 1, :], (8, 128)))
        for base, ref in ((0, near_scores_ref), (passages // 2, far_scores_ref))
        for number in range(passages // 2)
    ]
    grade_row, grade_lane = spread(row, grade_list), spread(lane, grade_list)
    worth_row, worth_lane = jnp.exp2(grade_row), jnp.exp2(grade_lane)
    discount_row = 1.0 / jnp.log2(2.0 + spread(row, rank_list))
    discount_lane = 1.0 / jnp.log2(2.0 + spread(lane, rank_list))
    score_row, score_lane = spread(row, score_list), spread(lane, score_list)
    pair = jnp.logical_and(row < passages, lane < passages)
    ahead = jnp.logical_or(
        grade_lane > grade_row, jnp.logical_and(grade_lane == grade_row, lane < row)
    )
    ideal_rank = jnp.sum(
        jnp.where(jnp.logical_and(pair, ahead), 1.0, 0.0), axis=1, keepdims=True
    )
    ideal_terms = (worth_row - 1.0) / jnp.log2(2.0 + ideal_rank)
    one_lane = jnp.logical_and(pair, lane == 0)

    def whole_sum(values):
        return jnp.sum(jnp.sum(values, axis=1, keepdims=True), axis=0, keepdims=True)

    ideal_gain = whole_sum(jnp.where(one_lane, ideal_terms, 0.0))
    swap_gain = (
        jnp.abs((worth_row - worth_lane) * (discount_row - discount_lane)) / ideal_gain
    )
    swap_gain = jnp.where(jnp.logical_and(pair, grade_row > grade_lane), swap_gain, 0.0)
    margin = score_row - score_lane
    softplus = jnp.maximum(-margin, 0.0) + jnp.log1p(jnp.exp(-jnp.abs(margin)))
    loss_ref[...] = whole_sum(swap_gain * softplus)
    pull = swap_gain * jax.nn.sigmoid(-margin)
    gradient = whole_sum(jnp.where(lane == place, pull, 0.0) - jnp.where(row == place, pull, 0.0))
    factor_ref[...] = jnp.broadcast_to(gradient * loss_scale, factor_ref.shape)


def end_kernel(
    factor_ref, own_ref, x_ref, y_ref, hidden_ref, gain_ref, gates_ref, router_ref, unit_ref,
    grad_far, turned_ref, grad_ref, copy_sems,
):
    token_count, model_width = hidden_ref.shape
    slot_grad = sum(
        ref[model_width : model_width + 8, :].astype(jnp.float32)
        for ref in (own_ref, x_ref, y_ref)
    )
    gates = gates_ref[...]
    d_logit = gates * (slot_grad - jnp.sum(gates * slot_grad, axis=0, keepdims=True))
    d_logit = jnp.concatenate([d_logit, jnp.zeros((120, token_count), jnp.float32)], axis=0).T
    d_logit = jnp.concatenate(split_low(d_logit[:, :8]), axis=1)
    router_rows = jnp.concatenate([router_ref[...]] * 3, axis=0)
    for first in range(0, model_width, 256):
        columns = slice(first, first + 256)
        total = own_ref[columns, :].astype(jnp.float32) + (
            x_ref[columns, :].astype(jnp.float32) + y_ref[columns, :].astype(jnp.float32)
        )
        turned_ref[:, columns] = total.T + jnp.dot(
            d_logit, router_rows[:, columns], preferred_element_type=jnp.float32
        )
    gain = gain_ref[...]
    factor = factor_ref[:, :1]
    size = 32
    copies = []
    for first in range(0, token_count, size):
        rows = slice(first, first + size)
        flat_rows = hidden_ref[rows, :].astype(jnp.float32)
        grad = norm_back(flat_rows, rms_scale(flat_rows), gain, turned_ref[rows, :])
        grad_ref[rows, :] = ((grad + unit_ref[...]) * factor).astype(jnp.bfloat16)
        copies.append(
            pltpu.make_async_copy(
                grad_ref.at[rows, :], grad_far.at[rows, :], copy_sems.at[first // size]
            )
        )
        copies[-1].start()
    for copy in copies:
        copy.wait()


def every_expert(
    hidden,
    norm_gain,
    router,
    gate_proj,
    up_proj,
    down_proj,
    final_gain,
    score_vector,
    expert_ids,
    grades,
    passage_ranks,
):
    unused_query, unused_passage, token_count, model_width = hidden.shape
    passages = grades.shape[1]
    flat = hidden.reshape(token_count, model_width)
    gate_matrix, up_matrix, down_matrix = gate_proj[0], up_proj[0], down_proj[0]
    mine = [gate_matrix, up_matrix, down_matrix]
    others = [swap(matrix, CORE) for matrix in mine]

    flat, gain, router_rows, normed, token_sums, head = kernel_call(
        norm_kernel,
        "norm",
        [
            kept(flat.shape, jnp.bfloat16),
            kept((1, model_width), jnp.float32),
            kept((8, model_width), jnp.bfloat16),
            kept(flat.shape, jnp.bfloat16),
            kept((1, model_width), jnp.float32),
            kept((1, model_width), jnp.float32),
        ],
        [
            flat,
            norm_gain.reshape(1, model_width),
            router.T,
            final_gain.reshape(1, model_width),
            score_vector.reshape(model_width // 128, 128),
        ],
        range(5),
        [
            pltpu.VMEM((1, model_width), jnp.float32),
            pltpu.VMEM((model_width // 128, 128), jnp.bfloat16),
            pltpu.SemaphoreType.DMA((5,)),
        ],
    )
    x_rows, y_rows = swap(normed, ACROSS_X), swap(normed, ACROSS_Y)
    turned_gates, own_gates, *own_saved, own_part, mine[0], mine[1] = front(
        0, (0,), (0,), [normed], router_rows, mine[:2]
    )
    x_rows, y_rows = after(x_rows, own_part), after(y_rows, own_part)
    far_low = swap(half_of(x_rows, 0), ACROSS_Y)
    far_high = swap(half_of(y_rows, 1), ACROSS_X)
    side_gates, *side_saved, side_part, mine[2] = front(
        1, (1, 2), (0,), [x_rows, y_rows], router_rows, mine[:2], mine[2:]
    )
    others[0] = after(others[0], side_part)
    unused, *other_saved, other_part = front(
        2, (0, 1, 2), (1,), [normed, x_rows, y_rows], router_rows, others[:2]
    )
    far_low, far_high = after(far_low, other_part), after(far_high, other_part)
    far_gates, *far_saved, terms = front(
        3, (3,), (0, 1), [far_low, far_high], router_rows, mine[:2] + others[:2],
        (token_sums, mine[2], others[2], own_part, side_part, other_part),
    )

    near, other_near, unit_vector, travelling, own_score = kernel_call(
        functools.partial(near_kernel, token_count=token_count),
        "near",
        [
            kept((8, down_matrix.shape[0]), jnp.float32),
            kept((8, down_matrix.shape[0]), jnp.float32),
            kept((1, model_width), jnp.float32),
            kept((1, 128), jnp.float32),
            shape_of((1, 1), jnp.float32),
        ],
        [
            pinned(terms),
            swap(terms, ACROSS_X),
            swap(terms, ACROSS_Y),
            swap(terms, ACROSS_X | ACROSS_Y),
            pinned(head),
            pinned(mine[2]),
            pinned(others[2]),
        ],
    )
    matrices = mine[:2] + others[:2]
    far_low, far_high = back(
        (3,), (0, 0), (0, model_width // 2), near, other_near, far_gates, far_saved, matrices
    )
    far_sent = far_high
    far_low, far_high = swap(far_low, ACROSS_X), swap(far_high, ACROSS_Y)
    x_sums, y_sums = back(
        (1, 2), (0, token_count), (0,), after(near, far_sent), other_near, side_gates,
        side_saved + other_saved, matrices,
    )
    (own_sums,) = back(
        (0,), (0, 0), (0,), after(near, x_sums), other_near, own_gates, own_saved + other_saved,
        matrices,
    )
    travelling = after(travelling, x_sums)
    met = lax.ppermute(travelling, "psg", [(index, index ^ 1) for index in range(passages)])
    near_scores = pack(travelling, met)
    far_high = after(far_high, own_sums, near_scores)
    x_sums, y_sums = kernel_call(
        add_kernel,
        "add",
        [kept(x_sums.shape, jnp.bfloat16)] * 2,
        [pinned(x_sums), pinned(y_sums), far_high, far_low],
    )
    x_sums, y_sums, near_scores = lax.optimization_barrier((x_sums, y_sums, near_scores))
    x_sums, y_sums = swap(x_sums, ACROSS_X), swap(y_sums, ACROSS_Y)
    far_scores = lax.ppermute(near_scores, "psg", [(index, index ^ 2) for index in range(passages)])
    loss, factor = kernel_call(
        rank_kernel,
        "rank",
        [shape_of((1, 1), jnp.float32), kept((1, 128), jnp.float32)],
        [
            grades,
            passage_ranks,
            pinned(near_scores),
            far_scores,
        ],
        (0, 1),
        [
            pltpu.SMEM(grades.shape, jnp.int32),
            pltpu.SMEM(grades.shape, jnp.int32),
            pltpu.SemaphoreType.DMA((2,)),
        ],
    )
    (grad,) = kernel_call(
        end_kernel,
        "end",
        [shape_of((token_count, model_width), jnp.bfloat16)],
        [
            pinned(factor), pinned(own_sums), x_sums, y_sums, pinned(flat), pinned(gain),
            pinned(turned_gates), pinned(router_rows), pinned(unit_vector),
        ],
        scratch=[
            pltpu.VMEM((token_count, model_width), jnp.float32),
            pltpu.VMEM((token_count, model_width), jnp.bfloat16),
            pltpu.SemaphoreType.DMA((token_count // 32,)),
        ],
        result=pl.ANY,
    )
    return (loss.reshape(1), own_score, grad.reshape(hidden.shape))


def block(*arrays):
    hidden, router, expert_ids, grades = arrays[0], arrays[2], arrays[8], arrays[9]
    each_expert = router.shape[1] == expert_ids.shape[3] == 8
    if hidden.shape[1] == 1 and each_expert and grades.shape[1] == 4:
        return every_expert(*arrays)
    return local(*arrays)


def solution(mesh):
    placed = (
        P("exp", "psg", None, None),
        P(),
        P(),
        P("exp", None, None),
        P("exp", None, None),
        P("exp", None, None),
        P(),
        P(),
        P("exp", "psg", None, None),
        P("exp", None),
        P("exp", None),
    )
    return jax.shard_map(
        block,
        mesh=mesh,
        in_specs=placed,
        out_specs=(P("exp"), P("exp", "psg"), P("exp", "psg", None, None)),
        check_vma=False,
    )
```

```python
import functools
import math

import jax
import jax.numpy as jnp
from jax import lax
from jax.experimental import pallas as pl
from jax.experimental.pallas import tpu as pltpu
from jax.sharding import PartitionSpec as P

epsilon = 1e-06
loss_scale = 256.0
highest = lax.Precision.HIGHEST


def rms_scale(values):
    return lax.rsqrt(jnp.mean(values * values, axis=-1, keepdims=True) + epsilon)


def head_score(pooled, final_gain, score_vector):
    scaled = pooled * rms_scale(pooled) * final_gain
    return jnp.dot(scaled, score_vector.astype(jnp.float32), precision=highest)


def rank_loss(scores, grades, passage_ranks):
    grade_value = grades.astype(jnp.float32)
    worth_gain = jnp.exp2(grade_value)
    discount = 1.0 / jnp.log2(2.0 + passage_ranks.astype(jnp.float32))
    better_than = grades[None, :] > grades[:, None]
    equal_grade = grades[None, :] == grades[:, None]
    position = jnp.arange(grades.shape[0], dtype=jnp.int32)
    earlier = position[None, :] < position[:, None]
    ideal_rank = jnp.sum(
        jnp.logical_or(better_than, jnp.logical_and(equal_grade, earlier)).astype(jnp.float32),
        axis=1,
    )
    ideal_gain = jnp.sum((worth_gain - 1.0) / jnp.log2(2.0 + ideal_rank))
    ordered = (grades[:, None] > grades[None, :]).astype(jnp.float32)
    swap_gain = (
        jnp.abs(
            (worth_gain[:, None] - worth_gain[None, :]) * (discount[:, None] - discount[None, :])
        )
        / ideal_gain
    )
    margin = scores[:, None] - scores[None, :]
    return jnp.sum(ordered * swap_gain * jax.nn.softplus(-margin))


def pick_gates(normed, router, picked_ids):
    expert_total = router.shape[1]
    logits = jnp.dot(normed, router, preferred_element_type=jnp.float32)
    onehot = (
        picked_ids[:, :, None] == jnp.arange(expert_total, dtype=jnp.int32)[None, None, :]
    ).astype(jnp.float32)
    chosen = jnp.einsum("nke,ne->nk", onehot, logits, precision=highest)
    weights = jnp.exp(chosen)
    return (weights / jnp.sum(weights, axis=1, keepdims=True), onehot)


def gate_parts(pre_gate):
    sigmoid_gate = jax.nn.sigmoid(pre_gate)
    return (pre_gate * sigmoid_gate, sigmoid_gate * (1.0 + pre_gate * (1.0 - sigmoid_gate)))


def norm_back(flat_rows, inverse, norm_gain, d_normed):
    scaled = d_normed * norm_gain
    return inverse * scaled - flat_rows * inverse * inverse * inverse * jnp.mean(
        flat_rows * scaled, axis=-1, keepdims=True
    )


def unpack_front(front_out, buffer_rows):
    pre_gate, pre_up, received = front_out
    hidden_units = pre_gate.shape[2]
    pre_gate = pre_gate.reshape(buffer_rows, hidden_units)
    pre_up = pre_up.reshape(buffer_rows, hidden_units)
    silu_gate, slope = gate_parts(pre_gate)
    activation = (silu_gate * pre_up).astype(jnp.bfloat16)
    return (pre_up, received, silu_gate, slope, activation)


def local(
    hidden,
    norm_gain,
    router,
    gate_proj,
    up_proj,
    down_proj,
    final_gain,
    score_vector,
    expert_ids,
    grades,
    passage_ranks,
):
    unused_query, local_passages, local_positions, model_width = hidden.shape
    top_count = expert_ids.shape[3]
    expert_count = lax.axis_size("exp")
    token_count = local_passages * local_positions
    slot_count = token_count * top_count
    capacity = min(token_count, 9 * token_count * top_count // (8 * expert_count))
    buffer_rows = expert_count * capacity
    flat_rows = hidden.reshape(token_count, model_width).astype(jnp.float32)
    inverse = rms_scale(flat_rows)
    normed = (flat_rows * inverse * norm_gain).astype(jnp.bfloat16)
    picked_ids = expert_ids.reshape(token_count, top_count)
    gate_values, onehot = pick_gates(normed, router, picked_ids)
    slot_hits = onehot.reshape(slot_count, expert_count).astype(jnp.int32)
    slot_rank = jnp.sum((jnp.cumsum(slot_hits, axis=0) - slot_hits) * slot_hits, axis=1)
    target = picked_ids.reshape(slot_count) * capacity + slot_rank
    source_token = jnp.arange(slot_count, dtype=jnp.int32) // top_count
    passage_onehot = (
        source_token[:, None] // local_positions
        == jnp.arange(local_passages, dtype=jnp.int32)[None, :]
    ).astype(jnp.float32)
    weighted = (passage_onehot * gate_values.reshape(slot_count, 1)).astype(jnp.bfloat16)
    send_rows = (
        jnp.zeros((buffer_rows, model_width), jnp.bfloat16).at[target].set(normed[source_token])
    )
    send_weights = jnp.zeros((buffer_rows, local_passages), jnp.bfloat16).at[target].set(weighted)
    outgoing = (
        send_rows.reshape(expert_count, capacity, model_width),
        send_weights.reshape(expert_count, capacity, local_passages),
    )
    gate_matrix = gate_proj[0]
    up_matrix = up_proj[0]
    down_matrix = down_proj[0]
    rows_in = lax.all_to_all(outgoing[0], "exp", split_axis=0, concat_axis=0, tiled=True)
    weights_in = lax.all_to_all(outgoing[1], "exp", split_axis=0, concat_axis=0, tiled=True)
    pre_gate = jnp.einsum("end,df->enf", rows_in, gate_matrix, preferred_element_type=jnp.float32)
    pre_up = jnp.einsum("end,df->enf", rows_in, up_matrix, preferred_element_type=jnp.float32)
    front_out = (pre_gate, pre_up, weights_in)
    pre_up, received, silu_gate, slope, activation = unpack_front(front_out, buffer_rows)
    hidden_units = activation.shape[1]
    passage_part = jnp.einsum(
        "scp,scf->spf",
        received,
        activation.reshape(expert_count, capacity, hidden_units),
        preferred_element_type=jnp.float32,
    )
    down_wide = down_matrix.astype(jnp.float32)
    expert_terms = jnp.einsum("spf,fd->spd", passage_part, down_wide, precision=highest)
    came_back = lax.all_to_all(expert_terms, "exp", split_axis=0, concat_axis=0, tiled=True)
    token_sums = jnp.sum(flat_rows.reshape(local_passages, local_positions, model_width), axis=1)
    pooled = (token_sums + jnp.sum(came_back, axis=0)) / local_positions
    first_row = lax.axis_index("psg") * local_passages
    own_score = head_score(pooled, final_gain, score_vector)
    every_score = lax.all_gather(own_score, "psg", axis=0, tiled=True)
    loss_value, loss_grad = jax.value_and_grad(rank_loss)(every_score, grades[0], passage_ranks[0])
    d_own = lax.dynamic_slice_in_dim(loss_grad, first_row, local_passages, 0) * loss_scale
    unused_score, head_back = jax.vjp(
        lambda values: head_score(values, final_gain, score_vector), pooled
    )
    d_vector = head_back(d_own)[0] / local_positions
    every_vector = lax.all_gather(d_vector[None], "exp", axis=0, tiled=True)
    near_table = jnp.einsum("spd,fd->spf", every_vector, down_wide, precision=highest)
    present = (received != 0).astype(jnp.float32)
    near_rows = jnp.einsum("scp,spf->scf", present, near_table, precision=highest).reshape(
        buffer_rows, hidden_units
    )
    gate_weight = jnp.sum(received.astype(jnp.float32), axis=2).reshape(buffer_rows, 1)
    d_act = gate_weight * near_rows
    d_gate = (d_act * pre_up * slope).astype(jnp.bfloat16)
    d_up = (d_act * silu_gate).astype(jnp.bfloat16)
    contract = (((1,), (1,)), ((), ()))
    pick_grad = lax.dot_general(d_gate, gate_matrix, contract, preferred_element_type=jnp.float32)
    pick_grad = (
        pick_grad + lax.dot_general(d_up, up_matrix, contract, preferred_element_type=jnp.float32)
    ).astype(jnp.bfloat16)
    gate_grad = jnp.sum(activation.astype(jnp.float32) * near_rows, axis=1).astype(jnp.bfloat16)
    back_rows, back_gate = (
        lax.all_to_all(
            pick_grad.reshape(expert_count, capacity, model_width),
            "exp",
            split_axis=0,
            concat_axis=0,
            tiled=True,
        ),
        lax.all_to_all(
            gate_grad.reshape(expert_count, capacity),
            "exp",
            split_axis=0,
            concat_axis=0,
            tiled=True,
        ),
    )
    picked_rows = back_rows.reshape(buffer_rows, model_width)[target]
    d_normed = jnp.sum(
        picked_rows.reshape(token_count, top_count, model_width).astype(jnp.float32), axis=1
    )
    picked_gate = (
        back_gate.reshape(buffer_rows)[target].astype(jnp.float32).reshape(token_count, top_count)
    )
    d_logit = gate_values * (
        picked_gate - jnp.sum(gate_values * picked_gate, axis=1, keepdims=True)
    )
    dense_logit = jnp.einsum("nk,nke->ne", d_logit, onehot, precision=highest)
    d_normed = d_normed + jnp.einsum(
        "ne,de->nd", dense_logit, router.astype(jnp.float32), precision=highest
    )
    grad_flat = norm_back(flat_rows, inverse, norm_gain, d_normed)
    grad_hidden = (
        grad_flat.reshape(1, local_passages, local_positions, model_width)
        + d_vector[None, :, None, :]
    )
    return (
        loss_value.reshape(1),
        own_score.reshape(1, local_passages),
        grad_hidden.astype(jnp.bfloat16),
    )


CORE, ACROSS_X, ACROSS_Y = 1, 2, 4
forward = (((1,), (0,)), ((), ()))
across = (((1,), (1,)), ((), ()))
MIB = 1 << 20


def swap(value, bit, size=8):
    return lax.ppermute(value, "exp", [(index, index ^ bit) for index in range(size)])


def shape_of(shape, dtype):
    return jax.ShapeDtypeStruct(shape, dtype)


def after(value, *others):
    return lax.optimization_barrier((value, *others))[0]


def kept(shape, dtype):
    return pltpu.VMEM(shape, dtype)


def pinned(array):
    return pltpu.with_memory_space_constraint(array, pltpu.VMEM)


def kernel_call(body, name, outs, ins, far=(), scratch=(), work=1, result=pltpu.VMEM):
    spaces = [pltpu.VMEM] * len(ins)
    ins = list(ins)
    for index in far:
        spaces[index] = pl.ANY
        ins[index] = pltpu.with_memory_space_constraint(ins[index], pltpu.HBM)
    return pl.pallas_call(
        body,
        name=name,
        out_shape=outs,
        in_specs=[pl.BlockSpec(memory_space=space) for space in spaces],
        out_specs=[pl.BlockSpec(memory_space=result)] * len(outs),
        scratch_shapes=scratch,
        compiler_params=pltpu.CompilerParams(vmem_limit_bytes=8 * MIB),
        cost_estimate=pl.CostEstimate(flops=work, bytes_accessed=1, transcendentals=0),
    )(*ins)


def split_low(values):
    high = values.astype(jnp.bfloat16)
    rest = values - high.astype(jnp.float32)
    middle = rest.astype(jnp.bfloat16)
    low = (rest - middle.astype(jnp.float32)).astype(jnp.bfloat16)
    return high, middle, low


def exact_dot(values, low_matrix, contract):
    parts = lax.dot_general(
        jnp.concatenate(split_low(values), axis=0),
        low_matrix,
        contract,
        preferred_element_type=jnp.float32,
    )
    return parts[0:8] + parts[8:16] + parts[16:24]


def other_order(values, bits):
    return jnp.concatenate([values[row ^ bits : (row ^ bits) + 1] for row in range(4)], axis=0)


def norm_kernel(
    hidden_far, gain_far, router_far, final_far, vector_far,
    hidden_ref, gain_ref, router_ref, normed_ref, sums_ref, head_ref,
    final_ref, vector_ref, copy_sems,
):
    pairs = (
        (hidden_far, hidden_ref), (gain_far, gain_ref), (router_far, router_ref),
        (final_far, final_ref), (vector_far, vector_ref),
    )
    copies = [
        pltpu.make_async_copy(source, target, copy_sems.at[index])
        for index, (source, target) in enumerate(pairs)
    ]
    for copy in copies:
        copy.start()
    for copy in copies:
        copy.wait()
    vector = vector_ref[...].astype(jnp.float32)
    vector = jnp.concatenate([vector[row : row + 1] for row in range(vector.shape[0])], axis=1)
    head_ref[...] = final_ref[...] * vector
    rows = hidden_ref[...].astype(jnp.float32)
    normed_ref[...] = (rows * rms_scale(rows) * gain_ref[...]).astype(jnp.bfloat16)
    sums_ref[...] = jnp.sum(rows, axis=0, keepdims=True)


def front_kernel(stage, owners, sets, count, router_ref, *refs):
    matrices, refs = refs[: 2 * len(sets)], refs[2 * len(sets) :]
    pieces, refs = refs[:count], refs[count:]
    matrices = list(matrices)
    hidden_units = matrices[0].shape[1]
    tile = 256
    firsts = range(0, hidden_units, tile)
    if stage == 0:
        far_matrices = matrices
        *refs, gate_held, up_held, rows_ref, copy_sems = refs
        matrices = [gate_held, up_held]
        copies = [
            pltpu.make_async_copy(
                source.at[:, first : first + tile],
                target.at[:, first : first + tile],
                copy_sems.at[which, number],
            )
            for number, first in enumerate(firsts)
            for which, (source, target) in enumerate(zip(far_matrices, matrices))
        ]
        for copy in copies:
            copy.start()
        turned_ref, *refs = refs
    elif stage == 1:
        down_far, *refs, down_ref, rows_ref, copy_sem = refs
        down_copy = pltpu.make_async_copy(down_far, down_ref, copy_sem)
        down_copy.start()
    elif stage == 3:
        sums_ref, *downs = refs[:3]
        earlier, refs = refs[3:6], refs[6:]
        *refs, terms_ref, rows_ref = refs
    else:
        *refs, rows_ref = refs
    gates_ref, *outs = refs
    expert = lax.axis_index("exp")
    first = 0
    for piece in pieces:
        rows_ref[first : first + piece.shape[0], :] = piece[...]
        first += piece.shape[0]
    size = first // len(owners)
    logits = lax.dot_general(
        rows_ref[...], router_ref[...], across, preferred_element_type=jnp.float32
    )
    weights = jnp.exp(logits)
    gates = weights / jnp.sum(weights, axis=1, keepdims=True)
    gates_ref[...] = gates
    lane = lax.broadcasted_iota(jnp.int32, gates.shape, 1)
    if stage == 0:
        weights = jnp.exp(
            lax.dot_general(
                router_ref[...], rows_ref[...], across, preferred_element_type=jnp.float32
            )
        )
        turned_ref[...] = weights / jnp.sum(weights, axis=0, keepdims=True)

    totals = []
    for place, which in enumerate(sets):
        gate_ref, up_ref = matrices[2 * place : 2 * place + 2]
        if stage == 3:
            slope_ref, silu_ref, act_ref = outs[3 * place : 3 * place + 3]
        else:
            slope_ref, silu_ref, act_ref, part_ref = outs
        own = jnp.sum(jnp.where(lane == expert ^ which, gates, 0.0), axis=1, keepdims=True)
        low = own.astype(jnp.bfloat16).astype(jnp.float32)
        parts = []
        for number, first in enumerate(firsts):
            columns = slice(first, first + tile)
            if stage == 0:
                copies[2 * number].wait()
                copies[2 * number + 1].wait()
            rows = rows_ref[...]
            pre_gate = jnp.dot(rows, gate_ref[:, columns], preferred_element_type=jnp.float32)
            pre_up = jnp.dot(rows, up_ref[:, columns], preferred_element_type=jnp.float32)
            silu_gate, slope = gate_parts(pre_gate)
            activation = (silu_gate * pre_up).astype(jnp.bfloat16)
            slope_ref[:, columns] = slope * pre_up
            silu_ref[:, columns] = silu_gate
            act_ref[:, columns] = activation
            weighted = activation.astype(jnp.float32) * low
            found = {
                owner: jnp.sum(weighted[index * size : (index + 1) * size], axis=0, keepdims=True)
                for index, owner in enumerate(owners)
            }
            nothing = jnp.zeros_like(weighted[:1])
            parts.append(
                jnp.concatenate([found.get(owner, nothing) for owner in range(8)], axis=0)
            )
        totals.append(jnp.concatenate(parts, axis=1))
    if stage == 1:
        down_copy.wait()
    if stage < 3:
        part_ref[...] = totals[0]
        return
    own_first, own_second, other_first = earlier
    totals[0] = totals[0] + (own_first[...] + own_second[...])
    totals[1] = totals[1] + other_first[...]
    terms = exact_dot(totals[0], downs[0][...], forward) + exact_dot(
        totals[1], downs[1][...], forward
    )
    row = lax.broadcasted_iota(jnp.int32, terms.shape, 0)
    terms_ref[...] = (terms + jnp.where(row == 0, sums_ref[...], 0.0))[:4]


def front(stage, owners, sets, pieces, router_rows, matrices, more=()):
    model_width, hidden_units = matrices[0].shape
    row_total = sum(piece.shape[0] for piece in pieces)
    outs = [kept((row_total, 8), jnp.float32)]
    if stage == 0:
        outs.insert(0, kept((8, row_total), jnp.float32))
    for which in sets:
        outs += [
            kept((row_total, hidden_units), jnp.float32),
            kept((row_total, hidden_units), jnp.float32),
            kept((row_total, hidden_units), jnp.bfloat16),
        ]
    outs.append(
        kept((4, model_width), jnp.float32) if stage == 3 else kept((8, hidden_units), jnp.float32)
    )
    scratch = [pltpu.VMEM((row_total, model_width), jnp.bfloat16)]
    far = ()
    if stage == 0:
        far = (1, 2)
        outs += [kept(matrix.shape, jnp.bfloat16) for matrix in matrices]
        scratch.append(pltpu.SemaphoreType.DMA((2, hidden_units // 256)))
    else:
        matrices = [pinned(matrix) for matrix in matrices]
    if stage == 1:
        far = (3 + len(pieces),)
        outs.append(kept(more[0].shape, jnp.bfloat16))
        scratch.append(pltpu.SemaphoreType.DMA)
    if stage == 3:
        more = [pinned(array) for array in more]
    return kernel_call(
        functools.partial(front_kernel, stage, owners, sets, len(pieces)),
        "front",
        outs,
        [pinned(router_rows), *matrices, *(pinned(piece) for piece in pieces), *more],
        far,
        scratch,
    )


def near_kernel(
    own_ref, x_ref, y_ref, far_ref, head_ref, down_ref, other_down_ref,
    near_ref, other_near_ref, unit_ref, score_ref, own_score_ref, *, token_count,
):
    pooled = (
        (own_ref[...] + other_order(x_ref[...], 1))
        + (other_order(y_ref[...], 2) + other_order(far_ref[...], 3))
    ) / token_count
    pooled = jnp.concatenate([pooled, jnp.zeros_like(pooled)], axis=0)
    head = head_ref[...]
    scale = rms_scale(pooled)
    along = jnp.sum(pooled * head, axis=1, keepdims=True)
    own_score = (scale * along)[:1]
    own_score_ref[...] = own_score
    score_ref[...] = jnp.broadcast_to(own_score, score_ref.shape)
    unit = (
        scale * head - scale * scale * scale * (along / pooled.shape[1]) * pooled
    ) / token_count
    unit_ref[...] = unit[:1]
    parts = jnp.concatenate(split_low(unit), axis=0)
    parts = jnp.concatenate([parts, jnp.zeros((104, parts.shape[1]), jnp.bfloat16)], axis=0)
    for table_ref, matrix_ref in ((near_ref, down_ref), (other_near_ref, other_down_ref)):
        turned = lax.dot_general(
            matrix_ref[...], parts, across, preferred_element_type=jnp.float32
        ).T
        table_ref[...] = turned[0:8] + turned[8:16] + turned[16:24]


def back_kernel(passages, gate_count, saved_count, near_ref, other_near_ref, *refs):
    gates_refs, refs = refs[:gate_count], refs[gate_count:]
    saved, refs = refs[: 3 * saved_count], refs[3 * saved_count :]
    matrices, refs = refs[:4], refs[4:]
    *out_refs, d_gate_ref, d_up_ref, other_d_gate_ref, other_d_up_ref = refs
    expert = lax.axis_index("exp")
    size = out_refs[0].shape[1]
    model_width = matrices[0].shape[0]
    lane = lax.broadcasted_iota(jnp.int32, (size, 8), 1)
    line = lax.broadcasted_iota(jnp.int32, (16, size), 0)
    experts = (
        (near_ref, d_gate_ref, d_up_ref), (other_near_ref, other_d_gate_ref, other_d_up_ref)
    )
    outs = []
    for index, (owner, gates_place, saved_places, cuts, unused) in enumerate(passages):
        outs.append(out_refs[: len(cuts)])
        out_refs = out_refs[len(cuts) :]
        rows = slice(index * size, (index + 1) * size)
        lines = jnp.zeros((16, size), jnp.float32)
        gates = gates_refs[gates_place[0]][gates_place[1] : gates_place[1] + size, :]
        for which, (table_ref, d_gate_out, d_up_out) in enumerate(experts):
            number, first = saved_places[which]
            slope_ref, silu_ref, act_ref = saved[3 * number : 3 * number + 3]
            held = slice(first, first + size)
            near = table_ref[owner : owner + 1, :]
            own = jnp.sum(
                jnp.where(lane == expert ^ which, gates, 0.0), axis=1, keepdims=True
            )
            d_act = own.astype(jnp.bfloat16).astype(jnp.float32) * near
            d_gate_out[rows, :] = (d_act * slope_ref[held, :]).astype(jnp.bfloat16)
            d_up_out[rows, :] = (d_act * silu_ref[held, :]).astype(jnp.bfloat16)
            gate_grad = exact_dot(table_ref[...], act_ref[held, :], across)[owner : owner + 1]
            lines = jnp.where(line == expert ^ which, gate_grad, lines)
        bounds = cuts + (model_width + 16,)
        for out_ref, cut, end in zip(outs[-1], bounds, bounds[1:]):
            if out_ref.shape[0] > end - cut:
                rest = out_ref.shape[0] - (end - cut)
                out_ref[end - cut :, :] = jnp.zeros((rest, size), jnp.bfloat16)
        outs[-1][-1][model_width - cuts[-1] : model_width + 16 - cuts[-1], :] = lines.astype(
            jnp.bfloat16
        )

    sides = (d_gate_ref, d_up_ref, other_d_gate_ref, other_d_up_ref)
    for first in range(0, model_width, 256):
        pick_grad = None
        for side_ref, matrix in zip(sides, matrices):
            term = lax.dot_general(
                matrix[first : first + 256, :],
                side_ref[...],
                across,
                preferred_element_type=jnp.float32,
            )
            pick_grad = term if pick_grad is None else pick_grad + term
        pick_grad = pick_grad.astype(jnp.bfloat16)
        for index, passage in enumerate(passages):
            cuts = passage[3]
            place = max(number for number, cut in enumerate(cuts) if cut <= first)
            rows = slice(first - cuts[place], first - cuts[place] + 256)
            outs[index][place][rows, :] = pick_grad[:, index * size : (index + 1) * size]


def back(passages, near, other_near, gates, saved, matrices, size):
    model_width, hidden_units = matrices[0].shape
    heights = []
    for passage in passages:
        cuts, least = passage[3:]
        ends = cuts[1:] + (model_width + 16,)
        heights += [max(low, end - cut) for low, cut, end in zip(least, cuts, ends)]
    arrays = [array for group in saved for array in group]
    return kernel_call(
        functools.partial(back_kernel, passages, len(gates), len(saved)),
        "back",
        [kept((height, size), jnp.bfloat16) for height in heights],
        [pinned(array) for array in (near, other_near, *gates, *arrays, *matrices)],
        (),
        [pltpu.VMEM((len(passages) * size, hidden_units), jnp.bfloat16)] * 4,
    )


def add_kernel(x_ref, y_ref, high_ref, low_ref, x_out, y_out):
    for own_ref, other_ref, out_ref in ((x_ref, high_ref, x_out), (y_ref, low_ref, y_out)):
        out_ref[...] = (
            own_ref[...].astype(jnp.float32)
            + other_ref[: own_ref.shape[0], :].astype(jnp.float32)
        ).astype(jnp.bfloat16)


def half_kernel(part, rows_ref, out_ref):
    half = out_ref.shape[0]
    out_ref[...] = rows_ref[part * half : (part + 1) * half, :]


def half_of(rows, part):
    total, wide = rows.shape
    (out,) = kernel_call(
        functools.partial(half_kernel, part), "half", [kept((total // 2, wide), rows.dtype)], [rows]
    )
    return out


def pack_kernel(first_ref, second_ref, out_ref):
    rows = first_ref.shape[0]
    out_ref[:rows, :] = first_ref[...]
    out_ref[rows:, :] = second_ref[...]


def pack(first, second, work=1):
    rows, wide = first.shape
    return kernel_call(
        pack_kernel, "pack", [kept((2 * rows, wide), first.dtype)], [first, second], work=work
    )[0]


def rank_kernel(grades_far, ranks_far, *refs):
    near_scores_ref, far_scores_ref, loss_ref, factor_ref, grades_ref, ranks_ref, copy_sems = refs
    copies = [
        pltpu.make_async_copy(grades_far, grades_ref, copy_sems.at[0]),
        pltpu.make_async_copy(ranks_far, ranks_ref, copy_sems.at[1]),
    ]
    for copy in copies:
        copy.start()
    for copy in copies:
        copy.wait()
    passages = grades_ref.shape[1]
    place = lax.axis_index("psg")
    row = lax.broadcasted_iota(jnp.int32, (8, 128), 0)
    lane = lax.broadcasted_iota(jnp.int32, (8, 128), 1)

    def spread(index, values):
        total = jnp.zeros((8, 128), jnp.float32)
        for number, value in values:
            total = jnp.where(index == number, value, total)
        return total

    grade_list = [(number, grades_ref[0, number].astype(jnp.float32)) for number in range(passages)]
    rank_list = [(number, ranks_ref[0, number].astype(jnp.float32)) for number in range(passages)]
    score_list = [
        (place ^ (base + number), jnp.broadcast_to(ref[number : number + 1, :], (8, 128)))
        for base, ref in ((0, near_scores_ref), (passages // 2, far_scores_ref))
        for number in range(passages // 2)
    ]
    grade_row, grade_lane = spread(row, grade_list), spread(lane, grade_list)
    worth_row, worth_lane = jnp.exp2(grade_row), jnp.exp2(grade_lane)
    discount_row = 1.0 / jnp.log2(2.0 + spread(row, rank_list))
    discount_lane = 1.0 / jnp.log2(2.0 + spread(lane, rank_list))
    score_row, score_lane = spread(row, score_list), spread(lane, score_list)
    pair = jnp.logical_and(row < passages, lane < passages)
    ahead = jnp.logical_or(
        grade_lane > grade_row, jnp.logical_and(grade_lane == grade_row, lane < row)
    )
    ideal_rank = jnp.sum(
        jnp.where(jnp.logical_and(pair, ahead), 1.0, 0.0), axis=1, keepdims=True
    )
    ideal_terms = (worth_row - 1.0) / jnp.log2(2.0 + ideal_rank)
    one_lane = jnp.logical_and(pair, lane == 0)

    def whole_sum(values):
        return jnp.sum(jnp.sum(values, axis=1, keepdims=True), axis=0, keepdims=True)

    ideal_gain = whole_sum(jnp.where(one_lane, ideal_terms, 0.0))
    swap_gain = (
        jnp.abs((worth_row - worth_lane) * (discount_row - discount_lane)) / ideal_gain
    )
    swap_gain = jnp.where(jnp.logical_and(pair, grade_row > grade_lane), swap_gain, 0.0)
    margin = score_row - score_lane
    softplus = jnp.maximum(-margin, 0.0) + jnp.log1p(jnp.exp(-jnp.abs(margin)))
    loss_ref[...] = whole_sum(swap_gain * softplus)
    pull = swap_gain * jax.nn.sigmoid(-margin)
    gradient = whole_sum(jnp.where(lane == place, pull, 0.0) - jnp.where(row == place, pull, 0.0))
    factor_ref[...] = jnp.broadcast_to(gradient * loss_scale, factor_ref.shape)


def first_end_kernel(own_ref, x_low_ref, y_high_ref, total_ref, lines_ref):
    model_width = total_ref.shape[1]
    cut = model_width // 2
    for first in range(0, model_width, 256):
        rows = slice(first, first + 256)
        if first < cut:
            term = x_low_ref[rows, :]
        else:
            term = y_high_ref[first - cut : first - cut + 256, :]
        total = own_ref[rows, :].astype(jnp.float32) + term.astype(jnp.float32)
        total_ref[:, rows] = total.T
    end = slice(model_width, model_width + 8)
    end_high = slice(model_width - cut, model_width - cut + 8)
    lines_ref[...] = own_ref[end, :].astype(jnp.float32) + y_high_ref[end_high, :].astype(
        jnp.float32
    )


def end_kernel(
    factor_ref, total_ref, lines_ref, x_high_ref, y_low_ref,
    hidden_ref, gain_ref, gates_ref, router_ref, unit_ref,
    grad_far, turned_ref, grad_ref, copy_sems,
):
    token_count, model_width = hidden_ref.shape
    cut = y_low_ref.shape[0]
    end_high = slice(model_width - cut, model_width - cut + 8)
    slot_grad = lines_ref[...] + x_high_ref[end_high, :].astype(jnp.float32)
    gates = gates_ref[...]
    d_logit = gates * (slot_grad - jnp.sum(gates * slot_grad, axis=0, keepdims=True))
    d_logit = jnp.concatenate([d_logit, jnp.zeros((120, token_count), jnp.float32)], axis=0).T
    d_logit = jnp.concatenate(split_low(d_logit[:, :8]), axis=1)
    router_rows = jnp.concatenate([router_ref[...]] * 3, axis=0)
    for first in range(0, model_width, 256):
        columns = slice(first, first + 256)
        if first < cut:
            term = y_low_ref[columns, :]
        else:
            term = x_high_ref[first - cut : first - cut + 256, :]
        turned_ref[:, columns] = (
            total_ref[:, columns]
            + term.astype(jnp.float32).T
            + jnp.dot(d_logit, router_rows[:, columns], preferred_element_type=jnp.float32)
        )
    gain = gain_ref[...]
    factor = factor_ref[:, :1]
    size = 32
    copies = []
    for first in range(0, token_count, size):
        rows = slice(first, first + size)
        flat_rows = hidden_ref[rows, :].astype(jnp.float32)
        grad = norm_back(flat_rows, rms_scale(flat_rows), gain, turned_ref[rows, :])
        grad_ref[rows, :] = ((grad + unit_ref[...]) * factor).astype(jnp.bfloat16)
        copies.append(
            pltpu.make_async_copy(
                grad_ref.at[rows, :], grad_far.at[rows, :], copy_sems.at[first // size]
            )
        )
        copies[-1].start()
    for copy in copies:
        copy.wait()


def every_expert(
    hidden,
    norm_gain,
    router,
    gate_proj,
    up_proj,
    down_proj,
    final_gain,
    score_vector,
    expert_ids,
    grades,
    passage_ranks,
):
    unused_query, unused_passage, token_count, model_width = hidden.shape
    passages = grades.shape[1]
    flat = hidden.reshape(token_count, model_width)
    gate_matrix, up_matrix, down_matrix = gate_proj[0], up_proj[0], down_proj[0]
    mine = [gate_matrix, up_matrix, down_matrix]
    others = [swap(matrix, CORE) for matrix in mine]

    flat, gain, router_rows, normed, token_sums, head = kernel_call(
        norm_kernel,
        "norm",
        [
            kept(flat.shape, jnp.bfloat16),
            kept((1, model_width), jnp.float32),
            kept((8, model_width), jnp.bfloat16),
            kept(flat.shape, jnp.bfloat16),
            kept((1, model_width), jnp.float32),
            kept((1, model_width), jnp.float32),
        ],
        [
            flat,
            norm_gain.reshape(1, model_width),
            router.T,
            final_gain.reshape(1, model_width),
            score_vector.reshape(model_width // 128, 128),
        ],
        range(5),
        [
            pltpu.VMEM((1, model_width), jnp.float32),
            pltpu.VMEM((model_width // 128, 128), jnp.bfloat16),
            pltpu.SemaphoreType.DMA((5,)),
        ],
    )
    x_rows, y_rows = swap(normed, ACROSS_X), swap(normed, ACROSS_Y)
    turned_gates, own_gates, *own_saved, own_part, mine[0], mine[1] = front(
        0, (0,), (0,), [normed], router_rows, mine[:2]
    )
    x_rows, y_rows = after(x_rows, own_part), after(y_rows, own_part)
    far_low = swap(half_of(x_rows, 0), ACROSS_Y)
    far_high = swap(half_of(y_rows, 1), ACROSS_X)
    side_gates, *side_saved, side_part, mine[2] = front(
        1, (1, 2), (0,), [x_rows, y_rows], router_rows, mine[:2], mine[2:]
    )
    others[0] = after(others[0], side_part)
    unused, *other_saved, other_part = front(
        2, (0, 1, 2), (1,), [normed, x_rows, y_rows], router_rows, others[:2]
    )
    far_low, far_high = after(far_low, other_part), after(far_high, other_part)
    far_gates, *far_saved, terms = front(
        3, (3,), (0, 1), [far_low, far_high], router_rows, mine[:2] + others[:2],
        (token_sums, mine[2], others[2], own_part, side_part, other_part),
    )

    near, other_near, unit_vector, travelling, own_score = kernel_call(
        functools.partial(near_kernel, token_count=token_count),
        "near",
        [
            kept((8, down_matrix.shape[0]), jnp.float32),
            kept((8, down_matrix.shape[0]), jnp.float32),
            kept((1, model_width), jnp.float32),
            kept((1, 128), jnp.float32),
            shape_of((1, 1), jnp.float32),
        ],
        [
            pinned(terms),
            swap(terms, ACROSS_X),
            swap(terms, ACROSS_Y),
            swap(terms, ACROSS_X | ACROSS_Y),
            pinned(head),
            pinned(mine[2]),
            pinned(others[2]),
        ],
    )
    matrices = mine[:2] + others[:2]
    cuts, early, earlier = (0, model_width // 2), model_width // 2 + 32, model_width // 2 + 64
    far_low, far_high, own_sums = back(
        (
            (3, (0, 0), ((0, 0), (1, 0)), cuts, (earlier, earlier)),
            (0, (1, 0), ((2, 0), (3, 0)), (0,), (0,)),
        ),
        near, other_near, [far_gates, own_gates],
        [far_saved[:3], far_saved[3:], own_saved, other_saved], matrices, token_count,
    )
    far_low, far_high = swap(far_low, ACROSS_X), swap(far_high, ACROSS_Y)
    x_low, x_high, y_low, y_high = back(
        (
            (1, (0, 0), ((0, 0), (1, token_count)), cuts, (early, 0)),
            (2, (0, token_count), ((0, token_count), (1, 2 * token_count)), cuts, (0, early)),
        ),
        after(near, own_sums), other_near, [side_gates], [side_saved, other_saved], matrices,
        token_count,
    )
    travelling = after(travelling, x_low)
    x_low, y_high = swap(x_low, ACROSS_X), swap(y_high, ACROSS_Y)
    met = lax.ppermute(travelling, "psg", [(index, index ^ 1) for index in range(passages)])
    near_scores = pack(travelling, met)
    far_high = after(far_high, near_scores)
    x_high, y_low = kernel_call(
        add_kernel,
        "add",
        [kept(x_high.shape, jnp.bfloat16), kept(y_low.shape, jnp.bfloat16)],
        [pinned(x_high), pinned(y_low), far_high, far_low],
    )
    x_high, y_low, near_scores = lax.optimization_barrier((x_high, y_low, near_scores))
    x_high, y_low = swap(x_high, ACROSS_X), swap(y_low, ACROSS_Y)
    far_scores = lax.ppermute(near_scores, "psg", [(index, index ^ 2) for index in range(passages)])
    loss, factor = kernel_call(
        rank_kernel,
        "rank",
        [shape_of((1, 1), jnp.float32), kept((1, 128), jnp.float32)],
        [
            grades,
            passage_ranks,
            pinned(near_scores),
            far_scores,
        ],
        (0, 1),
        [
            pltpu.SMEM(grades.shape, jnp.int32),
            pltpu.SMEM(grades.shape, jnp.int32),
            pltpu.SemaphoreType.DMA((2,)),
        ],
    )
    total, lines = kernel_call(
        first_end_kernel,
        "first_end",
        [
            kept((token_count, model_width), jnp.float32),
            kept((8, token_count), jnp.float32),
        ],
        [pinned(own_sums), after(x_low, factor), y_high],
    )
    (grad,) = kernel_call(
        end_kernel,
        "end",
        [shape_of((token_count, model_width), jnp.bfloat16)],
        [
            pinned(factor), pinned(total), pinned(lines), x_high, y_low, pinned(flat), pinned(gain),
            pinned(turned_gates), pinned(router_rows), pinned(unit_vector),
        ],
        scratch=[
            pltpu.VMEM((token_count, model_width), jnp.float32),
            pltpu.VMEM((token_count, model_width), jnp.bfloat16),
            pltpu.SemaphoreType.DMA((token_count // 32,)),
        ],
        result=pl.ANY,
    )
    return (loss.reshape(1), own_score, grad.reshape(hidden.shape))


def block(*arrays):
    hidden, router, expert_ids, grades = arrays[0], arrays[2], arrays[8], arrays[9]
    each_expert = router.shape[1] == expert_ids.shape[3] == 8
    if hidden.shape[1] == 1 and each_expert and grades.shape[1] == 4:
        return every_expert(*arrays)
    return local(*arrays)


def solution(mesh):
    placed = (
        P("exp", "psg", None, None),
        P(),
        P(),
        P("exp", None, None),
        P("exp", None, None),
        P("exp", None, None),
        P(),
        P(),
        P("exp", "psg", None, None),
        P("exp", None),
        P("exp", None),
    )
    return jax.shard_map(
        block,
        mesh=mesh,
        in_specs=placed,
        out_specs=(P("exp"), P("exp", "psg"), P("exp", "psg", None, None)),
        check_vma=False,
    )
```

```python
import functools
import math

import jax
import jax.numpy as jnp
from jax import lax
from jax.experimental import pallas as pl
from jax.experimental.pallas import tpu as pltpu
from jax.sharding import PartitionSpec as P

epsilon = 1e-06
loss_scale = 256.0
highest = lax.Precision.HIGHEST


def rms_scale(values):
    return lax.rsqrt(jnp.mean(values * values, axis=-1, keepdims=True) + epsilon)


def head_score(pooled, final_gain, score_vector):
    scaled = pooled * rms_scale(pooled) * final_gain
    return jnp.dot(scaled, score_vector.astype(jnp.float32), precision=highest)


def rank_loss(scores, grades, passage_ranks):
    grade_value = grades.astype(jnp.float32)
    worth_gain = jnp.exp2(grade_value)
    discount = 1.0 / jnp.log2(2.0 + passage_ranks.astype(jnp.float32))
    better_than = grades[None, :] > grades[:, None]
    equal_grade = grades[None, :] == grades[:, None]
    position = jnp.arange(grades.shape[0], dtype=jnp.int32)
    earlier = position[None, :] < position[:, None]
    ideal_rank = jnp.sum(
        jnp.logical_or(better_than, jnp.logical_and(equal_grade, earlier)).astype(jnp.float32),
        axis=1,
    )
    ideal_gain = jnp.sum((worth_gain - 1.0) / jnp.log2(2.0 + ideal_rank))
    ordered = (grades[:, None] > grades[None, :]).astype(jnp.float32)
    swap_gain = (
        jnp.abs(
            (worth_gain[:, None] - worth_gain[None, :]) * (discount[:, None] - discount[None, :])
        )
        / ideal_gain
    )
    margin = scores[:, None] - scores[None, :]
    return jnp.sum(ordered * swap_gain * jax.nn.softplus(-margin))


def pick_gates(normed, router, picked_ids):
    expert_total = router.shape[1]
    logits = jnp.dot(normed, router, preferred_element_type=jnp.float32)
    onehot = (
        picked_ids[:, :, None] == jnp.arange(expert_total, dtype=jnp.int32)[None, None, :]
    ).astype(jnp.float32)
    chosen = jnp.einsum("nke,ne->nk", onehot, logits, precision=highest)
    weights = jnp.exp(chosen)
    return (weights / jnp.sum(weights, axis=1, keepdims=True), onehot)


def gate_parts(pre_gate):
    sigmoid_gate = jax.nn.sigmoid(pre_gate)
    return (pre_gate * sigmoid_gate, sigmoid_gate * (1.0 + pre_gate * (1.0 - sigmoid_gate)))


def norm_back(flat_rows, inverse, norm_gain, d_normed):
    scaled = d_normed * norm_gain
    return inverse * scaled - flat_rows * inverse * inverse * inverse * jnp.mean(
        flat_rows * scaled, axis=-1, keepdims=True
    )


def unpack_front(front_out, buffer_rows):
    pre_gate, pre_up, received = front_out
    hidden_units = pre_gate.shape[2]
    pre_gate = pre_gate.reshape(buffer_rows, hidden_units)
    pre_up = pre_up.reshape(buffer_rows, hidden_units)
    silu_gate, slope = gate_parts(pre_gate)
    activation = (silu_gate * pre_up).astype(jnp.bfloat16)
    return (pre_up, received, silu_gate, slope, activation)


def local(
    hidden,
    norm_gain,
    router,
    gate_proj,
    up_proj,
    down_proj,
    final_gain,
    score_vector,
    expert_ids,
    grades,
    passage_ranks,
):
    unused_query, local_passages, local_positions, model_width = hidden.shape
    top_count = expert_ids.shape[3]
    expert_count = lax.axis_size("exp")
    token_count = local_passages * local_positions
    slot_count = token_count * top_count
    capacity = min(token_count, 9 * token_count * top_count // (8 * expert_count))
    buffer_rows = expert_count * capacity
    flat_rows = hidden.reshape(token_count, model_width).astype(jnp.float32)
    inverse = rms_scale(flat_rows)
    normed = (flat_rows * inverse * norm_gain).astype(jnp.bfloat16)
    picked_ids = expert_ids.reshape(token_count, top_count)
    gate_values, onehot = pick_gates(normed, router, picked_ids)
    slot_hits = onehot.reshape(slot_count, expert_count).astype(jnp.int32)
    slot_rank = jnp.sum((jnp.cumsum(slot_hits, axis=0) - slot_hits) * slot_hits, axis=1)
    target = picked_ids.reshape(slot_count) * capacity + slot_rank
    source_token = jnp.arange(slot_count, dtype=jnp.int32) // top_count
    passage_onehot = (
        source_token[:, None] // local_positions
        == jnp.arange(local_passages, dtype=jnp.int32)[None, :]
    ).astype(jnp.float32)
    weighted = (passage_onehot * gate_values.reshape(slot_count, 1)).astype(jnp.bfloat16)
    send_rows = (
        jnp.zeros((buffer_rows, model_width), jnp.bfloat16).at[target].set(normed[source_token])
    )
    send_weights = jnp.zeros((buffer_rows, local_passages), jnp.bfloat16).at[target].set(weighted)
    outgoing = (
        send_rows.reshape(expert_count, capacity, model_width),
        send_weights.reshape(expert_count, capacity, local_passages),
    )
    gate_matrix = gate_proj[0]
    up_matrix = up_proj[0]
    down_matrix = down_proj[0]
    rows_in = lax.all_to_all(outgoing[0], "exp", split_axis=0, concat_axis=0, tiled=True)
    weights_in = lax.all_to_all(outgoing[1], "exp", split_axis=0, concat_axis=0, tiled=True)
    pre_gate = jnp.einsum("end,df->enf", rows_in, gate_matrix, preferred_element_type=jnp.float32)
    pre_up = jnp.einsum("end,df->enf", rows_in, up_matrix, preferred_element_type=jnp.float32)
    front_out = (pre_gate, pre_up, weights_in)
    pre_up, received, silu_gate, slope, activation = unpack_front(front_out, buffer_rows)
    hidden_units = activation.shape[1]
    passage_part = jnp.einsum(
        "scp,scf->spf",
        received,
        activation.reshape(expert_count, capacity, hidden_units),
        preferred_element_type=jnp.float32,
    )
    down_wide = down_matrix.astype(jnp.float32)
    expert_terms = jnp.einsum("spf,fd->spd", passage_part, down_wide, precision=highest)
    came_back = lax.all_to_all(expert_terms, "exp", split_axis=0, concat_axis=0, tiled=True)
    token_sums = jnp.sum(flat_rows.reshape(local_passages, local_positions, model_width), axis=1)
    pooled = (token_sums + jnp.sum(came_back, axis=0)) / local_positions
    first_row = lax.axis_index("psg") * local_passages
    own_score = head_score(pooled, final_gain, score_vector)
    every_score = lax.all_gather(own_score, "psg", axis=0, tiled=True)
    loss_value, loss_grad = jax.value_and_grad(rank_loss)(every_score, grades[0], passage_ranks[0])
    d_own = lax.dynamic_slice_in_dim(loss_grad, first_row, local_passages, 0) * loss_scale
    unused_score, head_back = jax.vjp(
        lambda values: head_score(values, final_gain, score_vector), pooled
    )
    d_vector = head_back(d_own)[0] / local_positions
    every_vector = lax.all_gather(d_vector[None], "exp", axis=0, tiled=True)
    near_table = jnp.einsum("spd,fd->spf", every_vector, down_wide, precision=highest)
    present = (received != 0).astype(jnp.float32)
    near_rows = jnp.einsum("scp,spf->scf", present, near_table, precision=highest).reshape(
        buffer_rows, hidden_units
    )
    gate_weight = jnp.sum(received.astype(jnp.float32), axis=2).reshape(buffer_rows, 1)
    d_act = gate_weight * near_rows
    d_gate = (d_act * pre_up * slope).astype(jnp.bfloat16)
    d_up = (d_act * silu_gate).astype(jnp.bfloat16)
    contract = (((1,), (1,)), ((), ()))
    pick_grad = lax.dot_general(d_gate, gate_matrix, contract, preferred_element_type=jnp.float32)
    pick_grad = (
        pick_grad + lax.dot_general(d_up, up_matrix, contract, preferred_element_type=jnp.float32)
    ).astype(jnp.bfloat16)
    gate_grad = jnp.sum(activation.astype(jnp.float32) * near_rows, axis=1).astype(jnp.bfloat16)
    back_rows, back_gate = (
        lax.all_to_all(
            pick_grad.reshape(expert_count, capacity, model_width),
            "exp",
            split_axis=0,
            concat_axis=0,
            tiled=True,
        ),
        lax.all_to_all(
            gate_grad.reshape(expert_count, capacity),
            "exp",
            split_axis=0,
            concat_axis=0,
            tiled=True,
        ),
    )
    picked_rows = back_rows.reshape(buffer_rows, model_width)[target]
    d_normed = jnp.sum(
        picked_rows.reshape(token_count, top_count, model_width).astype(jnp.float32), axis=1
    )
    picked_gate = (
        back_gate.reshape(buffer_rows)[target].astype(jnp.float32).reshape(token_count, top_count)
    )
    d_logit = gate_values * (
        picked_gate - jnp.sum(gate_values * picked_gate, axis=1, keepdims=True)
    )
    dense_logit = jnp.einsum("nk,nke->ne", d_logit, onehot, precision=highest)
    d_normed = d_normed + jnp.einsum(
        "ne,de->nd", dense_logit, router.astype(jnp.float32), precision=highest
    )
    grad_flat = norm_back(flat_rows, inverse, norm_gain, d_normed)
    grad_hidden = (
        grad_flat.reshape(1, local_passages, local_positions, model_width)
        + d_vector[None, :, None, :]
    )
    return (
        loss_value.reshape(1),
        own_score.reshape(1, local_passages),
        grad_hidden.astype(jnp.bfloat16),
    )


CORE, ACROSS_X, ACROSS_Y = 1, 2, 4
forward = (((1,), (0,)), ((), ()))
across = (((1,), (1,)), ((), ()))
MIB = 1 << 20


def swap(value, bit, size=8):
    return lax.ppermute(value, "exp", [(index, index ^ bit) for index in range(size)])


def shape_of(shape, dtype):
    return jax.ShapeDtypeStruct(shape, dtype)


def after(value, *others):
    return lax.optimization_barrier((value, *others))[0]


def kept(shape, dtype):
    return pltpu.VMEM(shape, dtype)


def pinned(array):
    return pltpu.with_memory_space_constraint(array, pltpu.VMEM)


def kernel_call(body, name, outs, ins, far=(), scratch=(), work=1, result=pltpu.VMEM):
    spaces = [pltpu.VMEM] * len(ins)
    ins = list(ins)
    for index in far:
        spaces[index] = pl.ANY
        ins[index] = pltpu.with_memory_space_constraint(ins[index], pltpu.HBM)
    return pl.pallas_call(
        body,
        name=name,
        out_shape=outs,
        in_specs=[pl.BlockSpec(memory_space=space) for space in spaces],
        out_specs=[pl.BlockSpec(memory_space=result)] * len(outs),
        scratch_shapes=scratch,
        compiler_params=pltpu.CompilerParams(vmem_limit_bytes=8 * MIB),
        cost_estimate=pl.CostEstimate(flops=work, bytes_accessed=1, transcendentals=0),
    )(*ins)


def split_low(values):
    high = values.astype(jnp.bfloat16)
    rest = values - high.astype(jnp.float32)
    middle = rest.astype(jnp.bfloat16)
    low = (rest - middle.astype(jnp.float32)).astype(jnp.bfloat16)
    return high, middle, low


def exact_dot(values, low_matrix, contract):
    parts = lax.dot_general(
        jnp.concatenate(split_low(values), axis=0),
        low_matrix,
        contract,
        preferred_element_type=jnp.float32,
    )
    return parts[0:8] + parts[8:16] + parts[16:24]


def other_order(values, bits):
    return jnp.concatenate([values[row ^ bits : (row ^ bits) + 1] for row in range(4)], axis=0)


def norm_kernel(
    hidden_far, gain_far, router_far, final_far, vector_far,
    hidden_ref, gain_ref, router_ref, normed_ref, sums_ref, head_ref,
    final_ref, vector_ref, copy_sems,
):
    pairs = (
        (hidden_far, hidden_ref), (gain_far, gain_ref), (router_far, router_ref),
        (final_far, final_ref), (vector_far, vector_ref),
    )
    copies = [
        pltpu.make_async_copy(source, target, copy_sems.at[index])
        for index, (source, target) in enumerate(pairs)
    ]
    for copy in copies:
        copy.start()
    for copy in copies:
        copy.wait()
    vector = vector_ref[...].astype(jnp.float32)
    vector = jnp.concatenate([vector[row : row + 1] for row in range(vector.shape[0])], axis=1)
    head_ref[...] = final_ref[...] * vector
    rows = hidden_ref[...].astype(jnp.float32)
    normed_ref[...] = (rows * rms_scale(rows) * gain_ref[...]).astype(jnp.bfloat16)
    sums_ref[...] = jnp.sum(rows, axis=0, keepdims=True)


def front_kernel(stage, owners, sets, count, router_ref, *refs):
    matrices, refs = refs[: 2 * len(sets)], refs[2 * len(sets) :]
    pieces, refs = refs[:count], refs[count:]
    matrices = list(matrices)
    hidden_units = matrices[0].shape[1]
    tile = 256
    firsts = range(0, hidden_units, tile)
    if stage == 0:
        far_matrices = matrices
        *refs, gate_held, up_held, rows_ref, copy_sems = refs
        matrices = [gate_held, up_held]
        copies = [
            pltpu.make_async_copy(
                source.at[:, first : first + tile],
                target.at[:, first : first + tile],
                copy_sems.at[which, number],
            )
            for number, first in enumerate(firsts)
            for which, (source, target) in enumerate(zip(far_matrices, matrices))
        ]
        for copy in copies:
            copy.start()
        turned_ref, *refs = refs
    elif stage == 1:
        down_far, *refs, down_ref, rows_ref, copy_sem = refs
        down_copy = pltpu.make_async_copy(down_far, down_ref, copy_sem)
        down_copy.start()
    elif stage == 3:
        sums_ref, *downs = refs[:3]
        earlier, refs = refs[3:6], refs[6:]
        *refs, terms_ref, rows_ref = refs
    else:
        *refs, rows_ref = refs
    gates_ref, *outs = refs
    expert = lax.axis_index("exp")
    first = 0
    for piece in pieces:
        rows_ref[first : first + piece.shape[0], :] = piece[...]
        first += piece.shape[0]
    size = first // len(owners)
    logits = lax.dot_general(
        rows_ref[...], router_ref[...], across, preferred_element_type=jnp.float32
    )
    weights = jnp.exp(logits)
    gates = weights / jnp.sum(weights, axis=1, keepdims=True)
    gates_ref[...] = gates
    lane = lax.broadcasted_iota(jnp.int32, gates.shape, 1)
    if stage == 0:
        weights = jnp.exp(
            lax.dot_general(
                router_ref[...], rows_ref[...], across, preferred_element_type=jnp.float32
            )
        )
        turned_ref[...] = weights / jnp.sum(weights, axis=0, keepdims=True)

    totals = []
    for place, which in enumerate(sets):
        gate_ref, up_ref = matrices[2 * place : 2 * place + 2]
        if stage == 3:
            slope_ref, silu_ref, act_ref = outs[3 * place : 3 * place + 3]
        else:
            slope_ref, silu_ref, act_ref, part_ref = outs
        own = jnp.sum(jnp.where(lane == expert ^ which, gates, 0.0), axis=1, keepdims=True)
        low = own.astype(jnp.bfloat16).astype(jnp.float32)
        parts = []
        for number, first in enumerate(firsts):
            columns = slice(first, first + tile)
            if stage == 0:
                copies[2 * number].wait()
                copies[2 * number + 1].wait()
            rows = rows_ref[...]
            pre_gate = jnp.dot(rows, gate_ref[:, columns], preferred_element_type=jnp.float32)
            pre_up = jnp.dot(rows, up_ref[:, columns], preferred_element_type=jnp.float32)
            silu_gate, slope = gate_parts(pre_gate)
            activation = (silu_gate * pre_up).astype(jnp.bfloat16)
            slope_ref[:, columns] = slope * pre_up
            silu_ref[:, columns] = silu_gate
            act_ref[:, columns] = activation
            weighted = activation.astype(jnp.float32) * low
            found = {
                owner: jnp.sum(weighted[index * size : (index + 1) * size], axis=0, keepdims=True)
                for index, owner in enumerate(owners)
            }
            nothing = jnp.zeros_like(weighted[:1])
            parts.append(
                jnp.concatenate([found.get(owner, nothing) for owner in range(8)], axis=0)
            )
        totals.append(jnp.concatenate(parts, axis=1))
    if stage == 1:
        down_copy.wait()
    if stage < 3:
        part_ref[...] = totals[0]
        return
    own_first, own_second, other_first = earlier
    totals[0] = totals[0] + (own_first[...] + own_second[...])
    totals[1] = totals[1] + other_first[...]
    terms = exact_dot(totals[0], downs[0][...], forward) + exact_dot(
        totals[1], downs[1][...], forward
    )
    row = lax.broadcasted_iota(jnp.int32, terms.shape, 0)
    terms_ref[...] = (terms + jnp.where(row == 0, sums_ref[...], 0.0))[:4]


def front(stage, owners, sets, pieces, router_rows, matrices, more=()):
    model_width, hidden_units = matrices[0].shape
    row_total = sum(piece.shape[0] for piece in pieces)
    outs = [kept((row_total, 8), jnp.float32)]
    if stage == 0:
        outs.insert(0, kept((8, row_total), jnp.float32))
    for which in sets:
        outs += [
            kept((row_total, hidden_units), jnp.float32),
            kept((row_total, hidden_units), jnp.float32),
            kept((row_total, hidden_units), jnp.bfloat16),
        ]
    outs.append(
        kept((4, model_width), jnp.float32) if stage == 3 else kept((8, hidden_units), jnp.float32)
    )
    scratch = [pltpu.VMEM((row_total, model_width), jnp.bfloat16)]
    far = ()
    if stage == 0:
        far = (1, 2)
        outs += [kept(matrix.shape, jnp.bfloat16) for matrix in matrices]
        scratch.append(pltpu.SemaphoreType.DMA((2, hidden_units // 256)))
    else:
        matrices = [pinned(matrix) for matrix in matrices]
    if stage == 1:
        far = (3 + len(pieces),)
        outs.append(kept(more[0].shape, jnp.bfloat16))
        scratch.append(pltpu.SemaphoreType.DMA)
    if stage == 3:
        more = [pinned(array) for array in more]
    return kernel_call(
        functools.partial(front_kernel, stage, owners, sets, len(pieces)),
        "front",
        outs,
        [pinned(router_rows), *matrices, *(pinned(piece) for piece in pieces), *more],
        far,
        scratch,
    )


def near_kernel(
    own_ref, x_ref, y_ref, far_ref, head_ref, down_ref, other_down_ref,
    near_ref, other_near_ref, unit_ref, score_ref, own_score_ref, *, token_count,
):
    pooled = (
        (own_ref[...] + other_order(x_ref[...], 1))
        + (other_order(y_ref[...], 2) + other_order(far_ref[...], 3))
    ) / token_count
    pooled = jnp.concatenate([pooled, jnp.zeros_like(pooled)], axis=0)
    head = head_ref[...]
    scale = rms_scale(pooled)
    along = jnp.sum(pooled * head, axis=1, keepdims=True)
    own_score = (scale * along)[:1]
    own_score_ref[...] = own_score
    score_ref[...] = jnp.broadcast_to(own_score, score_ref.shape)
    unit = (
        scale * head - scale * scale * scale * (along / pooled.shape[1]) * pooled
    ) / token_count
    unit_ref[...] = unit[:1]
    parts = jnp.concatenate(split_low(unit), axis=0)
    parts = jnp.concatenate([parts, jnp.zeros((104, parts.shape[1]), jnp.bfloat16)], axis=0)
    for table_ref, matrix_ref in ((near_ref, down_ref), (other_near_ref, other_down_ref)):
        turned = lax.dot_general(
            matrix_ref[...], parts, across, preferred_element_type=jnp.float32
        ).T
        table_ref[...] = turned[0:8] + turned[8:16] + turned[16:24]


def back_kernel(passages, gate_count, saved_count, near_ref, other_near_ref, *refs):
    gates_refs, refs = refs[:gate_count], refs[gate_count:]
    saved, refs = refs[: 3 * saved_count], refs[3 * saved_count :]
    matrices, refs = refs[:4], refs[4:]
    *out_refs, d_gate_ref, d_up_ref, other_d_gate_ref, other_d_up_ref = refs
    expert = lax.axis_index("exp")
    size = out_refs[0].shape[1]
    model_width = matrices[0].shape[0]
    lane = lax.broadcasted_iota(jnp.int32, (size, 8), 1)
    line = lax.broadcasted_iota(jnp.int32, (16, size), 0)
    experts = (
        (near_ref, d_gate_ref, d_up_ref), (other_near_ref, other_d_gate_ref, other_d_up_ref)
    )
    outs = []
    for index, (owner, gates_place, saved_places, cuts, unused) in enumerate(passages):
        outs.append(out_refs[: len(cuts)])
        out_refs = out_refs[len(cuts) :]
        rows = slice(index * size, (index + 1) * size)
        lines = jnp.zeros((16, size), jnp.float32)
        gates = gates_refs[gates_place[0]][gates_place[1] : gates_place[1] + size, :]
        for which, (table_ref, d_gate_out, d_up_out) in enumerate(experts):
            number, first = saved_places[which]
            slope_ref, silu_ref, act_ref = saved[3 * number : 3 * number + 3]
            held = slice(first, first + size)
            near = table_ref[owner : owner + 1, :]
            own = jnp.sum(
                jnp.where(lane == expert ^ which, gates, 0.0), axis=1, keepdims=True
            )
            d_act = own.astype(jnp.bfloat16).astype(jnp.float32) * near
            d_gate_out[rows, :] = (d_act * slope_ref[held, :]).astype(jnp.bfloat16)
            d_up_out[rows, :] = (d_act * silu_ref[held, :]).astype(jnp.bfloat16)
            gate_grad = exact_dot(table_ref[...], act_ref[held, :], across)[owner : owner + 1]
            lines = jnp.where(line == expert ^ which, gate_grad, lines)
        bounds = cuts + (model_width + 16,)
        for out_ref, cut, end in zip(outs[-1], bounds, bounds[1:]):
            if out_ref.shape[0] > end - cut:
                rest = out_ref.shape[0] - (end - cut)
                out_ref[end - cut :, :] = jnp.zeros((rest, size), jnp.bfloat16)
        outs[-1][-1][model_width - cuts[-1] : model_width + 16 - cuts[-1], :] = lines.astype(
            jnp.bfloat16
        )

    sides = (d_gate_ref, d_up_ref, other_d_gate_ref, other_d_up_ref)
    for first in range(0, model_width, 256):
        pick_grad = None
        for side_ref, matrix in zip(sides, matrices):
            term = lax.dot_general(
                matrix[first : first + 256, :],
                side_ref[...],
                across,
                preferred_element_type=jnp.float32,
            )
            pick_grad = term if pick_grad is None else pick_grad + term
        pick_grad = pick_grad.astype(jnp.bfloat16)
        for index, passage in enumerate(passages):
            cuts = passage[3]
            place = max(number for number, cut in enumerate(cuts) if cut <= first)
            rows = slice(first - cuts[place], first - cuts[place] + 256)
            outs[index][place][rows, :] = pick_grad[:, index * size : (index + 1) * size]


def back(passages, near, other_near, gates, saved, matrices, size):
    model_width, hidden_units = matrices[0].shape
    heights = []
    for passage in passages:
        cuts, least = passage[3:]
        ends = cuts[1:] + (model_width + 16,)
        heights += [max(low, end - cut) for low, cut, end in zip(least, cuts, ends)]
    arrays = [array for group in saved for array in group]
    return kernel_call(
        functools.partial(back_kernel, passages, len(gates), len(saved)),
        "back",
        [kept((height, size), jnp.bfloat16) for height in heights],
        [pinned(array) for array in (near, other_near, *gates, *arrays, *matrices)],
        (),
        [pltpu.VMEM((len(passages) * size, hidden_units), jnp.bfloat16)] * 4,
    )


def add_kernel(x_ref, y_ref, high_ref, low_ref, x_out, y_out):
    for own_ref, other_ref, out_ref in ((x_ref, high_ref, x_out), (y_ref, low_ref, y_out)):
        out_ref[...] = (
            own_ref[...].astype(jnp.float32)
            + other_ref[: own_ref.shape[0], :].astype(jnp.float32)
        ).astype(jnp.bfloat16)


def half_kernel(part, rows_ref, out_ref):
    half = out_ref.shape[0]
    out_ref[...] = rows_ref[part * half : (part + 1) * half, :]


def half_of(rows, part):
    total, wide = rows.shape
    (out,) = kernel_call(
        functools.partial(half_kernel, part), "half", [kept((total // 2, wide), rows.dtype)], [rows]
    )
    return out


def pack_kernel(first_ref, second_ref, out_ref):
    rows = first_ref.shape[0]
    out_ref[:rows, :] = first_ref[...]
    out_ref[rows:, :] = second_ref[...]


def pack(first, second, work=1):
    rows, wide = first.shape
    return kernel_call(
        pack_kernel, "pack", [kept((2 * rows, wide), first.dtype)], [first, second], work=work
    )[0]


def pairs_of(passages):
    row = lax.broadcasted_iota(jnp.int32, (8, 128), 0)
    lane = lax.broadcasted_iota(jnp.int32, (8, 128), 1)
    return row, lane, jnp.logical_and(row < passages, lane < passages)


def spread(index, values):
    total = jnp.zeros((8, 128), jnp.float32)
    for number, value in values:
        total = jnp.where(index == number, value, total)
    return total


def whole_sum(values):
    return jnp.sum(jnp.sum(values, axis=1, keepdims=True), axis=0, keepdims=True)


def pair_kernel(grades_far, ranks_far, swap_gain_ref, grades_ref, ranks_ref, copy_sems):
    copies = [
        pltpu.make_async_copy(grades_far, grades_ref, copy_sems.at[0]),
        pltpu.make_async_copy(ranks_far, ranks_ref, copy_sems.at[1]),
    ]
    for copy in copies:
        copy.start()
    for copy in copies:
        copy.wait()
    passages = grades_ref.shape[1]
    row, lane, pair = pairs_of(passages)
    grade_list = [(number, grades_ref[0, number].astype(jnp.float32)) for number in range(passages)]
    rank_list = [(number, ranks_ref[0, number].astype(jnp.float32)) for number in range(passages)]
    grade_row, grade_lane = spread(row, grade_list), spread(lane, grade_list)
    worth_row, worth_lane = jnp.exp2(grade_row), jnp.exp2(grade_lane)
    discount_row = 1.0 / jnp.log2(2.0 + spread(row, rank_list))
    discount_lane = 1.0 / jnp.log2(2.0 + spread(lane, rank_list))
    ahead = jnp.logical_or(
        grade_lane > grade_row, jnp.logical_and(grade_lane == grade_row, lane < row)
    )
    ideal_rank = jnp.sum(
        jnp.where(jnp.logical_and(pair, ahead), 1.0, 0.0), axis=1, keepdims=True
    )
    ideal_terms = (worth_row - 1.0) / jnp.log2(2.0 + ideal_rank)
    one_lane = jnp.logical_and(pair, lane == 0)
    ideal_gain = whole_sum(jnp.where(one_lane, ideal_terms, 0.0))
    swap_gain = (
        jnp.abs((worth_row - worth_lane) * (discount_row - discount_lane)) / ideal_gain
    )
    swap_gain_ref[...] = jnp.where(
        jnp.logical_and(pair, grade_row > grade_lane), swap_gain, 0.0
    )


def rank_kernel(swap_gain_ref, near_scores_ref, far_scores_ref, loss_ref, factor_ref):
    passages = 2 * near_scores_ref.shape[0]
    place = lax.axis_index("psg")
    row, lane, unused = pairs_of(passages)
    score_list = [
        (place ^ (base + number), jnp.broadcast_to(ref[number : number + 1, :], (8, 128)))
        for base, ref in ((0, near_scores_ref), (passages // 2, far_scores_ref))
        for number in range(passages // 2)
    ]
    swap_gain = swap_gain_ref[...]
    margin = spread(row, score_list) - spread(lane, score_list)
    softplus = jnp.maximum(-margin, 0.0) + jnp.log1p(jnp.exp(-jnp.abs(margin)))
    loss_ref[...] = whole_sum(swap_gain * softplus)
    pull = swap_gain * jax.nn.sigmoid(-margin)
    gradient = whole_sum(jnp.where(lane == place, pull, 0.0) - jnp.where(row == place, pull, 0.0))
    factor_ref[...] = jnp.broadcast_to(gradient * loss_scale, factor_ref.shape)


def first_end_kernel(own_ref, x_low_ref, y_high_ref, total_ref, lines_ref):
    model_width = total_ref.shape[1]
    cut = model_width // 2
    for first in range(0, model_width, 256):
        rows = slice(first, first + 256)
        if first < cut:
            term = x_low_ref[rows, :]
        else:
            term = y_high_ref[first - cut : first - cut + 256, :]
        total = own_ref[rows, :].astype(jnp.float32) + term.astype(jnp.float32)
        total_ref[:, rows] = total.T
    end = slice(model_width, model_width + 8)
    end_high = slice(model_width - cut, model_width - cut + 8)
    lines_ref[...] = own_ref[end, :].astype(jnp.float32) + y_high_ref[end_high, :].astype(
        jnp.float32
    )


def end_kernel(
    factor_ref, total_ref, lines_ref, x_high_ref, y_low_ref,
    hidden_ref, gain_ref, gates_ref, router_ref, unit_ref,
    grad_far, turned_ref, grad_ref, copy_sems,
):
    token_count, model_width = hidden_ref.shape
    cut = y_low_ref.shape[0]
    end_high = slice(model_width - cut, model_width - cut + 8)
    slot_grad = lines_ref[...] + x_high_ref[end_high, :].astype(jnp.float32)
    gates = gates_ref[...]
    d_logit = gates * (slot_grad - jnp.sum(gates * slot_grad, axis=0, keepdims=True))
    d_logit = jnp.concatenate([d_logit, jnp.zeros((120, token_count), jnp.float32)], axis=0).T
    d_logit = jnp.concatenate(split_low(d_logit[:, :8]), axis=1)
    router_rows = jnp.concatenate([router_ref[...]] * 3, axis=0)
    for first in range(0, model_width, 256):
        columns = slice(first, first + 256)
        if first < cut:
            term = y_low_ref[columns, :]
        else:
            term = x_high_ref[first - cut : first - cut + 256, :]
        turned_ref[:, columns] = (
            total_ref[:, columns]
            + term.astype(jnp.float32).T
            + jnp.dot(d_logit, router_rows[:, columns], preferred_element_type=jnp.float32)
        )
    gain = gain_ref[...]
    factor = factor_ref[:, :1]
    size = 32
    copies = []
    for first in range(0, token_count, size):
        rows = slice(first, first + size)
        flat_rows = hidden_ref[rows, :].astype(jnp.float32)
        grad = norm_back(flat_rows, rms_scale(flat_rows), gain, turned_ref[rows, :])
        grad_ref[rows, :] = ((grad + unit_ref[...]) * factor).astype(jnp.bfloat16)
        copies.append(
            pltpu.make_async_copy(
                grad_ref.at[rows, :], grad_far.at[rows, :], copy_sems.at[first // size]
            )
        )
        copies[-1].start()
    for copy in copies:
        copy.wait()


def every_expert(
    hidden,
    norm_gain,
    router,
    gate_proj,
    up_proj,
    down_proj,
    final_gain,
    score_vector,
    expert_ids,
    grades,
    passage_ranks,
):
    unused_query, unused_passage, token_count, model_width = hidden.shape
    passages = grades.shape[1]
    flat = hidden.reshape(token_count, model_width)
    gate_matrix, up_matrix, down_matrix = gate_proj[0], up_proj[0], down_proj[0]
    mine = [gate_matrix, up_matrix, down_matrix]
    flat, gain, router_rows, normed, token_sums, head = kernel_call(
        norm_kernel,
        "norm",
        [
            kept(flat.shape, jnp.bfloat16),
            kept((1, model_width), jnp.float32),
            kept((8, model_width), jnp.bfloat16),
            kept(flat.shape, jnp.bfloat16),
            kept((1, model_width), jnp.float32),
            kept((1, model_width), jnp.float32),
        ],
        [
            flat,
            norm_gain.reshape(1, model_width),
            router.T,
            final_gain.reshape(1, model_width),
            score_vector.reshape(model_width // 128, 128),
        ],
        range(5),
        [
            pltpu.VMEM((1, model_width), jnp.float32),
            pltpu.VMEM((model_width // 128, 128), jnp.bfloat16),
            pltpu.SemaphoreType.DMA((5,)),
        ],
    )
    others = [swap(matrix, CORE) for matrix in mine]
    x_rows, y_rows = swap(normed, ACROSS_X), swap(normed, ACROSS_Y)
    turned_gates, own_gates, *own_saved, own_part, mine[0], mine[1] = front(
        0, (0,), (0,), [normed], router_rows, mine[:2]
    )
    (swap_gain,) = kernel_call(
        pair_kernel,
        "pairs",
        [kept((8, 128), jnp.float32)],
        [grades, after(passage_ranks, own_part)],
        (0, 1),
        [
            pltpu.SMEM(grades.shape, jnp.int32),
            pltpu.SMEM(grades.shape, jnp.int32),
            pltpu.SemaphoreType.DMA((2,)),
        ],
    )
    x_rows, y_rows = after(x_rows, swap_gain), after(y_rows, swap_gain)
    far_low = swap(half_of(x_rows, 0), ACROSS_Y)
    far_high = swap(half_of(y_rows, 1), ACROSS_X)
    side_gates, *side_saved, side_part, mine[2] = front(
        1, (1, 2), (0,), [x_rows, y_rows], router_rows, mine[:2], mine[2:]
    )
    others[0] = after(others[0], side_part)
    unused, *other_saved, other_part = front(
        2, (0, 1, 2), (1,), [normed, x_rows, y_rows], router_rows, others[:2]
    )
    far_low, far_high = after(far_low, other_part), after(far_high, other_part)
    far_gates, *far_saved, terms = front(
        3, (3,), (0, 1), [far_low, far_high], router_rows, mine[:2] + others[:2],
        (token_sums, mine[2], others[2], own_part, side_part, other_part),
    )

    near, other_near, unit_vector, travelling, own_score = kernel_call(
        functools.partial(near_kernel, token_count=token_count),
        "near",
        [
            kept((8, down_matrix.shape[0]), jnp.float32),
            kept((8, down_matrix.shape[0]), jnp.float32),
            kept((1, model_width), jnp.float32),
            kept((1, 128), jnp.float32),
            shape_of((1, 1), jnp.float32),
        ],
        [
            pinned(terms),
            swap(terms, ACROSS_X),
            swap(terms, ACROSS_Y),
            swap(terms, ACROSS_X | ACROSS_Y),
            pinned(head),
            pinned(mine[2]),
            pinned(others[2]),
        ],
    )
    matrices = mine[:2] + others[:2]
    cuts, early, earlier = (0, model_width // 2), model_width // 2 + 32, model_width // 2 + 64
    far_low, far_high, own_sums = back(
        (
            (3, (0, 0), ((0, 0), (1, 0)), cuts, (earlier, earlier)),
            (0, (1, 0), ((2, 0), (3, 0)), (0,), (0,)),
        ),
        near, other_near, [far_gates, own_gates],
        [far_saved[:3], far_saved[3:], own_saved, other_saved], matrices, token_count,
    )
    far_low, far_high = swap(far_low, ACROSS_X), swap(far_high, ACROSS_Y)
    x_low, x_high, y_low, y_high = back(
        (
            (1, (0, 0), ((0, 0), (1, token_count)), cuts, (early, 0)),
            (2, (0, token_count), ((0, token_count), (1, 2 * token_count)), cuts, (0, early)),
        ),
        after(near, own_sums), other_near, [side_gates], [side_saved, other_saved], matrices,
        token_count,
    )
    travelling = after(travelling, own_sums)
    met = lax.ppermute(travelling, "psg", [(index, index ^ 1) for index in range(passages)])
    near_scores = pack(travelling, met)
    x_low, y_high, near_scores = lax.optimization_barrier((x_low, y_high, near_scores))
    x_low, y_high = swap(x_low, ACROSS_X), swap(y_high, ACROSS_Y)
    x_high, y_low = kernel_call(
        add_kernel,
        "add",
        [kept(x_high.shape, jnp.bfloat16), kept(y_low.shape, jnp.bfloat16)],
        [pinned(x_high), pinned(y_low), far_high, far_low],
    )
    x_high, y_low, near_scores = lax.optimization_barrier((x_high, y_low, near_scores))
    x_high, y_low = swap(x_high, ACROSS_X), swap(y_low, ACROSS_Y)
    far_scores = lax.ppermute(near_scores, "psg", [(index, index ^ 2) for index in range(passages)])
    loss, factor = kernel_call(
        rank_kernel,
        "rank",
        [shape_of((1, 1), jnp.float32), kept((1, 128), jnp.float32)],
        [pinned(swap_gain), pinned(near_scores), far_scores],
    )
    total, lines = kernel_call(
        first_end_kernel,
        "first_end",
        [
            kept((token_count, model_width), jnp.float32),
            kept((8, token_count), jnp.float32),
        ],
        [pinned(own_sums), after(x_low, factor), y_high],
    )
    (grad,) = kernel_call(
        end_kernel,
        "end",
        [shape_of((token_count, model_width), jnp.bfloat16)],
        [
            pinned(factor), pinned(total), pinned(lines), x_high, y_low, pinned(flat), pinned(gain),
            pinned(turned_gates), pinned(router_rows), pinned(unit_vector),
        ],
        scratch=[
            pltpu.VMEM((token_count, model_width), jnp.float32),
            pltpu.VMEM((token_count, model_width), jnp.bfloat16),
            pltpu.SemaphoreType.DMA((token_count // 32,)),
        ],
        result=pl.ANY,
    )
    return (loss.reshape(1), own_score, grad.reshape(hidden.shape))


def block(*arrays):
    hidden, router, expert_ids, grades = arrays[0], arrays[2], arrays[8], arrays[9]
    each_expert = router.shape[1] == expert_ids.shape[3] == 8
    if hidden.shape[1] == 1 and each_expert and grades.shape[1] == 4:
        return every_expert(*arrays)
    return local(*arrays)


def solution(mesh):
    placed = (
        P("exp", "psg", None, None),
        P(),
        P(),
        P("exp", None, None),
        P("exp", None, None),
        P("exp", None, None),
        P(),
        P(),
        P("exp", "psg", None, None),
        P("exp", None),
        P("exp", None),
    )
    return jax.shard_map(
        block,
        mesh=mesh,
        in_specs=placed,
        out_specs=(P("exp"), P("exp", "psg"), P("exp", "psg", None, None)),
        check_vma=False,
    )
```

```python
import functools
import math

import jax
import jax.numpy as jnp
from jax import lax
from jax.experimental import pallas as pl
from jax.experimental.pallas import tpu as pltpu
from jax.sharding import PartitionSpec as P

epsilon = 1e-06
loss_scale = 256.0
highest = lax.Precision.HIGHEST


def rms_scale(values):
    return lax.rsqrt(jnp.mean(values * values, axis=-1, keepdims=True) + epsilon)


def head_score(pooled, final_gain, score_vector):
    scaled = pooled * rms_scale(pooled) * final_gain
    return jnp.dot(scaled, score_vector.astype(jnp.float32), precision=highest)


def rank_loss(scores, grades, passage_ranks):
    grade_value = grades.astype(jnp.float32)
    worth_gain = jnp.exp2(grade_value)
    discount = 1.0 / jnp.log2(2.0 + passage_ranks.astype(jnp.float32))
    better_than = grades[None, :] > grades[:, None]
    equal_grade = grades[None, :] == grades[:, None]
    position = jnp.arange(grades.shape[0], dtype=jnp.int32)
    earlier = position[None, :] < position[:, None]
    ideal_rank = jnp.sum(
        jnp.logical_or(better_than, jnp.logical_and(equal_grade, earlier)).astype(jnp.float32),
        axis=1,
    )
    ideal_gain = jnp.sum((worth_gain - 1.0) / jnp.log2(2.0 + ideal_rank))
    ordered = (grades[:, None] > grades[None, :]).astype(jnp.float32)
    swap_gain = (
        jnp.abs(
            (worth_gain[:, None] - worth_gain[None, :]) * (discount[:, None] - discount[None, :])
        )
        / ideal_gain
    )
    margin = scores[:, None] - scores[None, :]
    return jnp.sum(ordered * swap_gain * jax.nn.softplus(-margin))


def pick_gates(normed, router, picked_ids):
    expert_total = router.shape[1]
    logits = jnp.dot(normed, router, preferred_element_type=jnp.float32)
    onehot = (
        picked_ids[:, :, None] == jnp.arange(expert_total, dtype=jnp.int32)[None, None, :]
    ).astype(jnp.float32)
    chosen = jnp.einsum("nke,ne->nk", onehot, logits, precision=highest)
    weights = jnp.exp(chosen)
    return (weights / jnp.sum(weights, axis=1, keepdims=True), onehot)


def gate_parts(pre_gate):
    sigmoid_gate = jax.nn.sigmoid(pre_gate)
    return (pre_gate * sigmoid_gate, sigmoid_gate * (1.0 + pre_gate * (1.0 - sigmoid_gate)))


def norm_back(flat_rows, inverse, norm_gain, d_normed):
    scaled = d_normed * norm_gain
    return inverse * scaled - flat_rows * inverse * inverse * inverse * jnp.mean(
        flat_rows * scaled, axis=-1, keepdims=True
    )


def unpack_front(front_out, buffer_rows):
    pre_gate, pre_up, received = front_out
    hidden_units = pre_gate.shape[2]
    pre_gate = pre_gate.reshape(buffer_rows, hidden_units)
    pre_up = pre_up.reshape(buffer_rows, hidden_units)
    silu_gate, slope = gate_parts(pre_gate)
    activation = (silu_gate * pre_up).astype(jnp.bfloat16)
    return (pre_up, received, silu_gate, slope, activation)


def local(
    hidden,
    norm_gain,
    router,
    gate_proj,
    up_proj,
    down_proj,
    final_gain,
    score_vector,
    expert_ids,
    grades,
    passage_ranks,
):
    unused_query, local_passages, local_positions, model_width = hidden.shape
    top_count = expert_ids.shape[3]
    expert_count = lax.axis_size("exp")
    token_count = local_passages * local_positions
    slot_count = token_count * top_count
    capacity = min(token_count, 9 * token_count * top_count // (8 * expert_count))
    buffer_rows = expert_count * capacity
    flat_rows = hidden.reshape(token_count, model_width).astype(jnp.float32)
    inverse = rms_scale(flat_rows)
    normed = (flat_rows * inverse * norm_gain).astype(jnp.bfloat16)
    picked_ids = expert_ids.reshape(token_count, top_count)
    gate_values, onehot = pick_gates(normed, router, picked_ids)
    slot_hits = onehot.reshape(slot_count, expert_count).astype(jnp.int32)
    slot_rank = jnp.sum((jnp.cumsum(slot_hits, axis=0) - slot_hits) * slot_hits, axis=1)
    target = picked_ids.reshape(slot_count) * capacity + slot_rank
    source_token = jnp.arange(slot_count, dtype=jnp.int32) // top_count
    passage_onehot = (
        source_token[:, None] // local_positions
        == jnp.arange(local_passages, dtype=jnp.int32)[None, :]
    ).astype(jnp.float32)
    weighted = (passage_onehot * gate_values.reshape(slot_count, 1)).astype(jnp.bfloat16)
    send_rows = (
        jnp.zeros((buffer_rows, model_width), jnp.bfloat16).at[target].set(normed[source_token])
    )
    send_weights = jnp.zeros((buffer_rows, local_passages), jnp.bfloat16).at[target].set(weighted)
    outgoing = (
        send_rows.reshape(expert_count, capacity, model_width),
        send_weights.reshape(expert_count, capacity, local_passages),
    )
    gate_matrix = gate_proj[0]
    up_matrix = up_proj[0]
    down_matrix = down_proj[0]
    rows_in = lax.all_to_all(outgoing[0], "exp", split_axis=0, concat_axis=0, tiled=True)
    weights_in = lax.all_to_all(outgoing[1], "exp", split_axis=0, concat_axis=0, tiled=True)
    pre_gate = jnp.einsum("end,df->enf", rows_in, gate_matrix, preferred_element_type=jnp.float32)
    pre_up = jnp.einsum("end,df->enf", rows_in, up_matrix, preferred_element_type=jnp.float32)
    front_out = (pre_gate, pre_up, weights_in)
    pre_up, received, silu_gate, slope, activation = unpack_front(front_out, buffer_rows)
    hidden_units = activation.shape[1]
    passage_part = jnp.einsum(
        "scp,scf->spf",
        received,
        activation.reshape(expert_count, capacity, hidden_units),
        preferred_element_type=jnp.float32,
    )
    down_wide = down_matrix.astype(jnp.float32)
    expert_terms = jnp.einsum("spf,fd->spd", passage_part, down_wide, precision=highest)
    came_back = lax.all_to_all(expert_terms, "exp", split_axis=0, concat_axis=0, tiled=True)
    token_sums = jnp.sum(flat_rows.reshape(local_passages, local_positions, model_width), axis=1)
    pooled = (token_sums + jnp.sum(came_back, axis=0)) / local_positions
    first_row = lax.axis_index("psg") * local_passages
    own_score = head_score(pooled, final_gain, score_vector)
    every_score = lax.all_gather(own_score, "psg", axis=0, tiled=True)
    loss_value, loss_grad = jax.value_and_grad(rank_loss)(every_score, grades[0], passage_ranks[0])
    d_own = lax.dynamic_slice_in_dim(loss_grad, first_row, local_passages, 0) * loss_scale
    unused_score, head_back = jax.vjp(
        lambda values: head_score(values, final_gain, score_vector), pooled
    )
    d_vector = head_back(d_own)[0] / local_positions
    every_vector = lax.all_gather(d_vector[None], "exp", axis=0, tiled=True)
    near_table = jnp.einsum("spd,fd->spf", every_vector, down_wide, precision=highest)
    present = (received != 0).astype(jnp.float32)
    near_rows = jnp.einsum("scp,spf->scf", present, near_table, precision=highest).reshape(
        buffer_rows, hidden_units
    )
    gate_weight = jnp.sum(received.astype(jnp.float32), axis=2).reshape(buffer_rows, 1)
    d_act = gate_weight * near_rows
    d_gate = (d_act * pre_up * slope).astype(jnp.bfloat16)
    d_up = (d_act * silu_gate).astype(jnp.bfloat16)
    contract = (((1,), (1,)), ((), ()))
    pick_grad = lax.dot_general(d_gate, gate_matrix, contract, preferred_element_type=jnp.float32)
    pick_grad = (
        pick_grad + lax.dot_general(d_up, up_matrix, contract, preferred_element_type=jnp.float32)
    ).astype(jnp.bfloat16)
    gate_grad = jnp.sum(activation.astype(jnp.float32) * near_rows, axis=1).astype(jnp.bfloat16)
    back_rows, back_gate = (
        lax.all_to_all(
            pick_grad.reshape(expert_count, capacity, model_width),
            "exp",
            split_axis=0,
            concat_axis=0,
            tiled=True,
        ),
        lax.all_to_all(
            gate_grad.reshape(expert_count, capacity),
            "exp",
            split_axis=0,
            concat_axis=0,
            tiled=True,
        ),
    )
    picked_rows = back_rows.reshape(buffer_rows, model_width)[target]
    d_normed = jnp.sum(
        picked_rows.reshape(token_count, top_count, model_width).astype(jnp.float32), axis=1
    )
    picked_gate = (
        back_gate.reshape(buffer_rows)[target].astype(jnp.float32).reshape(token_count, top_count)
    )
    d_logit = gate_values * (
        picked_gate - jnp.sum(gate_values * picked_gate, axis=1, keepdims=True)
    )
    dense_logit = jnp.einsum("nk,nke->ne", d_logit, onehot, precision=highest)
    d_normed = d_normed + jnp.einsum(
        "ne,de->nd", dense_logit, router.astype(jnp.float32), precision=highest
    )
    grad_flat = norm_back(flat_rows, inverse, norm_gain, d_normed)
    grad_hidden = (
        grad_flat.reshape(1, local_passages, local_positions, model_width)
        + d_vector[None, :, None, :]
    )
    return (
        loss_value.reshape(1),
        own_score.reshape(1, local_passages),
        grad_hidden.astype(jnp.bfloat16),
    )


CORE, ACROSS_X, ACROSS_Y = 1, 2, 4
forward = (((1,), (0,)), ((), ()))
across = (((1,), (1,)), ((), ()))
MIB = 1 << 20


def swap(value, bit, size=8):
    return lax.ppermute(value, "exp", [(index, index ^ bit) for index in range(size)])


def shape_of(shape, dtype):
    return jax.ShapeDtypeStruct(shape, dtype)


def after(value, *others):
    return lax.optimization_barrier((value, *others))[0]


def kept(shape, dtype):
    return pltpu.VMEM(shape, dtype)


def pinned(array):
    return pltpu.with_memory_space_constraint(array, pltpu.VMEM)


def kernel_call(body, name, outs, ins, far=(), scratch=(), work=1, result=pltpu.VMEM):
    spaces = [pltpu.VMEM] * len(ins)
    ins = list(ins)
    for index in far:
        spaces[index] = pl.ANY
        ins[index] = pltpu.with_memory_space_constraint(ins[index], pltpu.HBM)
    return pl.pallas_call(
        body,
        name=name,
        out_shape=outs,
        in_specs=[pl.BlockSpec(memory_space=space) for space in spaces],
        out_specs=[pl.BlockSpec(memory_space=result)] * len(outs),
        scratch_shapes=scratch,
        compiler_params=pltpu.CompilerParams(vmem_limit_bytes=8 * MIB),
        cost_estimate=pl.CostEstimate(flops=work, bytes_accessed=1, transcendentals=0),
    )(*ins)


def split_low(values):
    high = values.astype(jnp.bfloat16)
    rest = values - high.astype(jnp.float32)
    middle = rest.astype(jnp.bfloat16)
    low = (rest - middle.astype(jnp.float32)).astype(jnp.bfloat16)
    return high, middle, low


def exact_dot(values, low_matrix, contract):
    parts = lax.dot_general(
        jnp.concatenate(split_low(values), axis=0),
        low_matrix,
        contract,
        preferred_element_type=jnp.float32,
    )
    return parts[0:8] + parts[8:16] + parts[16:24]


def other_order(values, bits):
    return jnp.concatenate([values[row ^ bits : (row ^ bits) + 1] for row in range(4)], axis=0)


def norm_kernel(
    hidden_far, gain_far, router_far, final_far, vector_far,
    hidden_ref, gain_ref, router_ref, low_ref, high_ref, sums_ref, head_ref,
    final_ref, vector_ref, copy_sems,
):
    pairs = (
        (hidden_far, hidden_ref), (gain_far, gain_ref), (router_far, router_ref),
        (final_far, final_ref), (vector_far, vector_ref),
    )
    copies = [
        pltpu.make_async_copy(source, target, copy_sems.at[index])
        for index, (source, target) in enumerate(pairs)
    ]
    for copy in copies:
        copy.start()
    for copy in copies:
        copy.wait()
    vector = vector_ref[...].astype(jnp.float32)
    vector = jnp.concatenate([vector[row : row + 1] for row in range(vector.shape[0])], axis=1)
    head_ref[...] = final_ref[...] * vector
    rows = hidden_ref[...].astype(jnp.float32)
    normed = (rows * rms_scale(rows) * gain_ref[...]).astype(jnp.bfloat16)
    half = low_ref.shape[0]
    low_ref[...] = normed[:half]
    high_ref[...] = normed[half:]
    sums_ref[...] = jnp.sum(rows, axis=0, keepdims=True)


def front_kernel(stage, owners, sets, count, router_ref, *refs):
    matrices, refs = refs[: 2 * len(sets)], refs[2 * len(sets) :]
    pieces, refs = refs[:count], refs[count:]
    matrices = list(matrices)
    hidden_units = matrices[0].shape[1]
    tile = 256
    firsts = range(0, hidden_units, tile)
    if stage == 0:
        far_matrices = matrices
        *refs, gate_held, up_held, rows_ref, copy_sems = refs
        matrices = [gate_held, up_held]
        copies = [
            pltpu.make_async_copy(
                source.at[:, first : first + tile],
                target.at[:, first : first + tile],
                copy_sems.at[which, number],
            )
            for number, first in enumerate(firsts)
            for which, (source, target) in enumerate(zip(far_matrices, matrices))
        ]
        for copy in copies:
            copy.start()
        turned_ref, *refs = refs
    elif stage == 3:
        sums_ref, *downs = refs[:3]
        earlier, refs = (refs[3:6], refs[6:9]), refs[9:]
        *refs, terms_ref, rows_ref = refs
    else:
        *refs, rows_ref = refs
    gates_ref, *outs = refs
    expert = lax.axis_index("exp")
    first = 0
    for piece in pieces:
        rows_ref[first : first + piece.shape[0], :] = piece[...]
        first += piece.shape[0]
    size = first // len(owners)
    logits = lax.dot_general(
        rows_ref[...], router_ref[...], across, preferred_element_type=jnp.float32
    )
    weights = jnp.exp(logits)
    gates = weights / jnp.sum(weights, axis=1, keepdims=True)
    gates_ref[...] = gates
    lane = lax.broadcasted_iota(jnp.int32, gates.shape, 1)
    if stage == 0:
        weights = jnp.exp(
            lax.dot_general(
                router_ref[...], rows_ref[...], across, preferred_element_type=jnp.float32
            )
        )
        turned_ref[...] = weights / jnp.sum(weights, axis=0, keepdims=True)

    totals = []
    for place, which in enumerate(sets):
        gate_ref, up_ref = matrices[2 * place : 2 * place + 2]
        slope_ref, silu_ref, act_ref = outs[3 * place : 3 * place + 3]
        own = jnp.sum(jnp.where(lane == expert ^ which, gates, 0.0), axis=1, keepdims=True)
        low = own.astype(jnp.bfloat16).astype(jnp.float32)
        parts = []
        for number, first in enumerate(firsts):
            columns = slice(first, first + tile)
            if stage == 0:
                copies[2 * number].wait()
                copies[2 * number + 1].wait()
            rows = rows_ref[...]
            pre_gate = jnp.dot(rows, gate_ref[:, columns], preferred_element_type=jnp.float32)
            pre_up = jnp.dot(rows, up_ref[:, columns], preferred_element_type=jnp.float32)
            silu_gate, slope = gate_parts(pre_gate)
            activation = (silu_gate * pre_up).astype(jnp.bfloat16)
            slope_ref[:, columns] = slope * pre_up
            silu_ref[:, columns] = silu_gate
            act_ref[:, columns] = activation
            weighted = activation.astype(jnp.float32) * low
            found = {}
            for index, owner in enumerate(owners):
                piece = jnp.sum(weighted[index * size : (index + 1) * size], axis=0, keepdims=True)
                found[owner] = found[owner] + piece if owner in found else piece
            nothing = jnp.zeros_like(weighted[:1])
            parts.append(
                jnp.concatenate([found.get(owner, nothing) for owner in range(8)], axis=0)
            )
        totals.append(jnp.concatenate(parts, axis=1))
    if stage < 3:
        for part_ref, total in zip(outs[3 * len(sets) :], totals):
            part_ref[...] = total
        return
    totals = [
        total + (first_ref[...] + (second_ref[...] + third_ref[...]))
        for total, (first_ref, second_ref, third_ref) in zip(totals, earlier)
    ]
    terms = exact_dot(totals[0], downs[0][...], forward) + exact_dot(
        totals[1], downs[1][...], forward
    )
    row = lax.broadcasted_iota(jnp.int32, terms.shape, 0)
    terms_ref[...] = (terms + jnp.where(row == 0, sums_ref[...], 0.0))[:4]


def front(stage, owners, sets, pieces, router_rows, matrices, more=()):
    model_width, hidden_units = matrices[0].shape
    row_total = sum(piece.shape[0] for piece in pieces)
    outs = [kept((row_total, 8), jnp.float32)]
    if stage == 0:
        outs.insert(0, kept((8, row_total), jnp.float32))
    for which in sets:
        outs += [
            kept((row_total, hidden_units), jnp.float32),
            kept((row_total, hidden_units), jnp.float32),
            kept((row_total, hidden_units), jnp.bfloat16),
        ]
    if stage == 3:
        outs.append(kept((4, model_width), jnp.float32))
    else:
        outs += [kept((8, hidden_units), jnp.float32)] * len(sets)
    scratch = [pltpu.VMEM((row_total, model_width), jnp.bfloat16)]
    far = ()
    if stage == 0:
        far = (1, 2)
        outs += [kept(matrix.shape, jnp.bfloat16) for matrix in matrices]
        scratch.append(pltpu.SemaphoreType.DMA((2, hidden_units // 256)))
    else:
        matrices = [pinned(matrix) for matrix in matrices]
    if stage == 3:
        more = [pinned(array) for array in more]
    return kernel_call(
        functools.partial(front_kernel, stage, owners, sets, len(pieces)),
        "front",
        outs,
        [pinned(router_rows), *matrices, *(pinned(piece) for piece in pieces), *more],
        far,
        scratch,
    )


def near_kernel(
    own_ref, x_ref, y_ref, far_ref, head_ref, down_ref, other_down_ref,
    near_ref, other_near_ref, unit_ref, score_ref, own_score_ref, *, token_count,
):
    pooled = (
        (own_ref[...] + other_order(x_ref[...], 1))
        + (other_order(y_ref[...], 2) + other_order(far_ref[...], 3))
    ) / token_count
    pooled = jnp.concatenate([pooled, jnp.zeros_like(pooled)], axis=0)
    head = head_ref[...]
    scale = rms_scale(pooled)
    along = jnp.sum(pooled * head, axis=1, keepdims=True)
    own_score = (scale * along)[:1]
    own_score_ref[...] = own_score
    score_ref[...] = jnp.broadcast_to(own_score, score_ref.shape)
    unit = (
        scale * head - scale * scale * scale * (along / pooled.shape[1]) * pooled
    ) / token_count
    unit_ref[...] = unit[:1]
    parts = jnp.concatenate(split_low(unit), axis=0)
    parts = jnp.concatenate([parts, jnp.zeros((104, parts.shape[1]), jnp.bfloat16)], axis=0)
    for table_ref, matrix_ref in ((near_ref, down_ref), (other_near_ref, other_down_ref)):
        turned = lax.dot_general(
            matrix_ref[...], parts, across, preferred_element_type=jnp.float32
        ).T
        table_ref[...] = turned[0:8] + turned[8:16] + turned[16:24]


def back_kernel(passages, gate_count, saved_count, near_ref, other_near_ref, *refs):
    gates_refs, refs = refs[:gate_count], refs[gate_count:]
    saved, refs = refs[: 3 * saved_count], refs[3 * saved_count :]
    matrices, refs = refs[:4], refs[4:]
    *out_refs, d_gate_ref, d_up_ref, other_d_gate_ref, other_d_up_ref = refs
    expert = lax.axis_index("exp")
    size = out_refs[0].shape[1]
    model_width = matrices[0].shape[0]
    line = lax.broadcasted_iota(jnp.int32, (16, size), 0)
    experts = (
        (near_ref, d_gate_ref, d_up_ref), (other_near_ref, other_d_gate_ref, other_d_up_ref)
    )
    outs = []
    for index, (owner, segments, cuts, unused) in enumerate(passages):
        outs.append(out_refs[: len(cuts)])
        out_refs = out_refs[len(cuts) :]
        lines = jnp.zeros((16, size), jnp.float32)
        length = size // len(segments)
        for which, (table_ref, d_gate_out, d_up_out) in enumerate(experts):
            near = table_ref[owner : owner + 1, :]
            acts = []
            for number, (gates_place, saved_places, first) in enumerate(segments):
                slope_ref, silu_ref, act_ref = saved[3 * saved_places[which] :][:3]
                held = slice(first, first + length)
                lane = lax.broadcasted_iota(jnp.int32, (length, 8), 1)
                rows = slice(index * size + number * length, index * size + (number + 1) * length)
                own = jnp.sum(
                    jnp.where(lane == expert ^ which, gates_refs[gates_place][held, :], 0.0),
                    axis=1,
                    keepdims=True,
                )
                d_act = own.astype(jnp.bfloat16).astype(jnp.float32) * near
                d_gate_out[rows, :] = (d_act * slope_ref[held, :]).astype(jnp.bfloat16)
                d_up_out[rows, :] = (d_act * silu_ref[held, :]).astype(jnp.bfloat16)
                acts.append(act_ref[held, :])
            gate_grad = exact_dot(table_ref[...], jnp.concatenate(acts, axis=0), across)
            lines = jnp.where(line == expert ^ which, gate_grad[owner : owner + 1], lines)
        bounds = cuts + (model_width + 16,)
        for out_ref, cut, end in zip(outs[-1], bounds, bounds[1:]):
            if out_ref.shape[0] > end - cut:
                rest = out_ref.shape[0] - (end - cut)
                out_ref[end - cut :, :] = jnp.zeros((rest, size), jnp.bfloat16)
        outs[-1][-1][model_width - cuts[-1] : model_width + 16 - cuts[-1], :] = lines.astype(
            jnp.bfloat16
        )

    sides = (d_gate_ref, d_up_ref, other_d_gate_ref, other_d_up_ref)
    for first in range(0, model_width, 256):
        pick_grad = None
        for side_ref, matrix in zip(sides, matrices):
            term = lax.dot_general(
                matrix[first : first + 256, :],
                side_ref[...],
                across,
                preferred_element_type=jnp.float32,
            )
            pick_grad = term if pick_grad is None else pick_grad + term
        pick_grad = pick_grad.astype(jnp.bfloat16)
        for index, passage in enumerate(passages):
            cuts = passage[2]
            place = max(number for number, cut in enumerate(cuts) if cut <= first)
            rows = slice(first - cuts[place], first - cuts[place] + 256)
            outs[index][place][rows, :] = pick_grad[:, index * size : (index + 1) * size]


def back(passages, near, other_near, gates, saved, matrices, size):
    model_width, hidden_units = matrices[0].shape
    heights = []
    for passage in passages:
        cuts, least = passage[2:]
        ends = cuts[1:] + (model_width + 16,)
        heights += [max(low, end - cut) for low, cut, end in zip(least, cuts, ends)]
    arrays = [array for group in saved for array in group]
    return kernel_call(
        functools.partial(back_kernel, passages, len(gates), len(saved)),
        "back",
        [kept((height, size), jnp.bfloat16) for height in heights],
        [pinned(array) for array in (near, other_near, *gates, *arrays, *matrices)],
        (),
        [pltpu.VMEM((len(passages) * size, hidden_units), jnp.bfloat16)] * 4,
    )


def add_kernel(x_ref, y_ref, high_ref, low_ref, x_out, y_out):
    for own_ref, other_ref, out_ref in ((x_ref, high_ref, x_out), (y_ref, low_ref, y_out)):
        out_ref[...] = (
            own_ref[...].astype(jnp.float32)
            + other_ref[: own_ref.shape[0], :].astype(jnp.float32)
        ).astype(jnp.bfloat16)


def pack_kernel(first_ref, second_ref, out_ref):
    rows = first_ref.shape[0]
    out_ref[:rows, :] = first_ref[...]
    out_ref[rows:, :] = second_ref[...]


def pack(first, second, work=1):
    rows, wide = first.shape
    return kernel_call(
        pack_kernel, "pack", [kept((2 * rows, wide), first.dtype)], [first, second], work=work
    )[0]


def pairs_of(passages):
    row = lax.broadcasted_iota(jnp.int32, (8, 128), 0)
    lane = lax.broadcasted_iota(jnp.int32, (8, 128), 1)
    return row, lane, jnp.logical_and(row < passages, lane < passages)


def spread(index, values):
    total = jnp.zeros((8, 128), jnp.float32)
    for number, value in values:
        total = jnp.where(index == number, value, total)
    return total


def whole_sum(values):
    return jnp.sum(jnp.sum(values, axis=1, keepdims=True), axis=0, keepdims=True)


def pair_kernel(
    grades_far, ranks_far, down_far, swap_gain_ref, down_ref, grades_ref, ranks_ref, copy_sems
):
    down_copy = pltpu.make_async_copy(down_far, down_ref, copy_sems.at[2])
    down_copy.start()
    copies = [
        pltpu.make_async_copy(grades_far, grades_ref, copy_sems.at[0]),
        pltpu.make_async_copy(ranks_far, ranks_ref, copy_sems.at[1]),
    ]
    for copy in copies:
        copy.start()
    for copy in copies:
        copy.wait()
    passages = grades_ref.shape[1]
    row, lane, pair = pairs_of(passages)
    grade_list = [(number, grades_ref[0, number].astype(jnp.float32)) for number in range(passages)]
    rank_list = [(number, ranks_ref[0, number].astype(jnp.float32)) for number in range(passages)]
    grade_row, grade_lane = spread(row, grade_list), spread(lane, grade_list)
    worth_row, worth_lane = jnp.exp2(grade_row), jnp.exp2(grade_lane)
    discount_row = 1.0 / jnp.log2(2.0 + spread(row, rank_list))
    discount_lane = 1.0 / jnp.log2(2.0 + spread(lane, rank_list))
    ahead = jnp.logical_or(
        grade_lane > grade_row, jnp.logical_and(grade_lane == grade_row, lane < row)
    )
    ideal_rank = jnp.sum(
        jnp.where(jnp.logical_and(pair, ahead), 1.0, 0.0), axis=1, keepdims=True
    )
    ideal_terms = (worth_row - 1.0) / jnp.log2(2.0 + ideal_rank)
    one_lane = jnp.logical_and(pair, lane == 0)
    ideal_gain = whole_sum(jnp.where(one_lane, ideal_terms, 0.0))
    swap_gain = (
        jnp.abs((worth_row - worth_lane) * (discount_row - discount_lane)) / ideal_gain
    )
    swap_gain_ref[...] = jnp.where(
        jnp.logical_and(pair, grade_row > grade_lane), swap_gain, 0.0
    )
    down_copy.wait()


def rank_kernel(swap_gain_ref, near_scores_ref, far_scores_ref, loss_ref, factor_ref):
    passages = 2 * near_scores_ref.shape[0]
    place = lax.axis_index("psg")
    row, lane, unused = pairs_of(passages)
    score_list = [
        (place ^ (base + number), jnp.broadcast_to(ref[number : number + 1, :], (8, 128)))
        for base, ref in ((0, near_scores_ref), (passages // 2, far_scores_ref))
        for number in range(passages // 2)
    ]
    swap_gain = swap_gain_ref[...]
    margin = spread(row, score_list) - spread(lane, score_list)
    softplus = jnp.maximum(-margin, 0.0) + jnp.log1p(jnp.exp(-jnp.abs(margin)))
    loss_ref[...] = whole_sum(swap_gain * softplus)
    pull = swap_gain * jax.nn.sigmoid(-margin)
    gradient = whole_sum(jnp.where(lane == place, pull, 0.0) - jnp.where(row == place, pull, 0.0))
    factor_ref[...] = jnp.broadcast_to(gradient * loss_scale, factor_ref.shape)


def first_end_kernel(own_ref, x_low_ref, y_high_ref, total_ref, lines_ref):
    model_width = total_ref.shape[1]
    cut = model_width // 2
    for first in range(0, model_width, 256):
        rows = slice(first, first + 256)
        if first < cut:
            term = x_low_ref[rows, :]
        else:
            term = y_high_ref[first - cut : first - cut + 256, :]
        total = own_ref[rows, :].astype(jnp.float32) + term.astype(jnp.float32)
        total_ref[:, rows] = total.T
    end = slice(model_width, model_width + 8)
    end_high = slice(model_width - cut, model_width - cut + 8)
    lines_ref[...] = own_ref[end, :].astype(jnp.float32) + y_high_ref[end_high, :].astype(
        jnp.float32
    )


def end_kernel(
    factor_ref, total_ref, lines_ref, x_high_ref, y_low_ref,
    hidden_ref, gain_ref, gates_ref, router_ref, unit_ref,
    grad_far, turned_ref, grad_ref, copy_sems,
):
    token_count, model_width = hidden_ref.shape
    cut = y_low_ref.shape[0]
    end_high = slice(model_width - cut, model_width - cut + 8)
    slot_grad = lines_ref[...] + x_high_ref[end_high, :].astype(jnp.float32)
    gates = gates_ref[...]
    d_logit = gates * (slot_grad - jnp.sum(gates * slot_grad, axis=0, keepdims=True))
    d_logit = jnp.concatenate([d_logit, jnp.zeros((120, token_count), jnp.float32)], axis=0).T
    d_logit = jnp.concatenate(split_low(d_logit[:, :8]), axis=1)
    router_rows = jnp.concatenate([router_ref[...]] * 3, axis=0)
    for first in range(0, model_width, 256):
        columns = slice(first, first + 256)
        if first < cut:
            term = y_low_ref[columns, :]
        else:
            term = x_high_ref[first - cut : first - cut + 256, :]
        turned_ref[:, columns] = (
            total_ref[:, columns]
            + term.astype(jnp.float32).T
            + jnp.dot(d_logit, router_rows[:, columns], preferred_element_type=jnp.float32)
        )
    gain = gain_ref[...]
    factor = factor_ref[:, :1]
    size = 32
    copies = []
    for first in range(0, token_count, size):
        rows = slice(first, first + size)
        flat_rows = hidden_ref[rows, :].astype(jnp.float32)
        grad = norm_back(flat_rows, rms_scale(flat_rows), gain, turned_ref[rows, :])
        grad_ref[rows, :] = ((grad + unit_ref[...]) * factor).astype(jnp.bfloat16)
        copies.append(
            pltpu.make_async_copy(
                grad_ref.at[rows, :], grad_far.at[rows, :], copy_sems.at[first // size]
            )
        )
        copies[-1].start()
    for copy in copies:
        copy.wait()


def every_expert(
    hidden,
    norm_gain,
    router,
    gate_proj,
    up_proj,
    down_proj,
    final_gain,
    score_vector,
    expert_ids,
    grades,
    passage_ranks,
):
    unused_query, unused_passage, token_count, model_width = hidden.shape
    half = token_count // 2
    passages = grades.shape[1]
    flat = hidden.reshape(token_count, model_width)
    gate_matrix, up_matrix, down_matrix = gate_proj[0], up_proj[0], down_proj[0]
    mine = [gate_matrix, up_matrix, down_matrix]
    flat, gain, router_rows, low, high, token_sums, head = kernel_call(
        norm_kernel,
        "norm",
        [
            kept(flat.shape, jnp.bfloat16),
            kept((1, model_width), jnp.float32),
            kept((8, model_width), jnp.bfloat16),
            kept((half, model_width), jnp.bfloat16),
            kept((half, model_width), jnp.bfloat16),
            kept((1, model_width), jnp.float32),
            kept((1, model_width), jnp.float32),
        ],
        [
            flat,
            norm_gain.reshape(1, model_width),
            router.T,
            final_gain.reshape(1, model_width),
            score_vector.reshape(model_width // 128, 128),
        ],
        range(5),
        [
            pltpu.VMEM((1, model_width), jnp.float32),
            pltpu.VMEM((model_width // 128, 128), jnp.bfloat16),
            pltpu.SemaphoreType.DMA((5,)),
        ],
    )
    others = [swap(matrix, CORE) for matrix in mine[:2]]
    x_low, y_high = swap(low, ACROSS_X), swap(high, ACROSS_Y)
    turned_gates, own_gates, *own_saved, own_part, mine[0], mine[1] = front(
        0, (0, 0), (0,), [low, high], router_rows, mine[:2]
    )
    swap_gain, mine[2] = kernel_call(
        pair_kernel,
        "pairs",
        [kept((8, 128), jnp.float32), kept(down_matrix.shape, jnp.bfloat16)],
        [grades, after(passage_ranks, own_part), down_matrix],
        (0, 1, 2),
        [
            pltpu.SMEM(grades.shape, jnp.int32),
            pltpu.SMEM(grades.shape, jnp.int32),
            pltpu.SemaphoreType.DMA((3,)),
        ],
    )
    x_low, y_high, second_low, second_high, mine[2], unused = lax.optimization_barrier(
        (x_low, y_high, low, high, mine[2], swap_gain)
    )
    others.append(swap(mine[2], CORE))
    x_high, y_low = swap(second_high, ACROSS_X), swap(second_low, ACROSS_Y)
    far_low, far_high = swap(x_low, ACROSS_Y), swap(y_high, ACROSS_X)
    unused, *other_saved, other_part = front(
        2, (0, 0), (1,), [second_low, second_high], router_rows, others[:2]
    )
    first_gates, *first_saved, first_part, first_other_part = front(
        2, (1, 2), (0, 1), [after(x_low, other_part), y_high], router_rows, mine[:2] + others[:2]
    )
    x_high, y_low = after(x_high, first_part), after(y_low, first_part)
    second_gates, *second_saved, second_part, second_other_part = front(
        2, (1, 2), (0, 1), [x_high, y_low], router_rows, mine[:2] + others[:2]
    )
    far_low, far_high = after(far_low, second_part), after(far_high, second_part)
    far_gates, *far_saved, terms = front(
        3, (3, 3), (0, 1), [far_low, far_high], router_rows, mine[:2] + others[:2],
        (
            token_sums, mine[2], others[2], own_part, first_part, second_part,
            other_part, first_other_part, second_other_part,
        ),
    )

    near, other_near, unit_vector, travelling, own_score = kernel_call(
        functools.partial(near_kernel, token_count=token_count),
        "near",
        [
            kept((8, down_matrix.shape[0]), jnp.float32),
            kept((8, down_matrix.shape[0]), jnp.float32),
            kept((1, model_width), jnp.float32),
            kept((1, 128), jnp.float32),
            shape_of((1, 1), jnp.float32),
        ],
        [
            pinned(terms),
            swap(terms, ACROSS_X),
            swap(terms, ACROSS_Y),
            swap(terms, ACROSS_X | ACROSS_Y),
            pinned(head),
            pinned(mine[2]),
            pinned(others[2]),
        ],
    )
    matrices = mine[:2] + others[:2]
    cuts, early, earlier = (0, model_width // 2), model_width // 2 + 32, model_width // 2 + 64
    far_low, far_high, own_sums = back(
        (
            (3, ((0, (0, 1), 0),), cuts, (earlier, earlier)),
            (0, ((1, (2, 3), 0),), (0,), (0,)),
        ),
        near, other_near, [far_gates, own_gates],
        [far_saved[:3], far_saved[3:], own_saved, other_saved], matrices, token_count,
    )
    far_low, far_high = swap(far_low, ACROSS_X), swap(far_high, ACROSS_Y)
    x_low, x_high, y_low, y_high = back(
        (
            (1, ((0, (0, 1), 0), (1, (2, 3), 0)), cuts, (early, 0)),
            (2, ((1, (2, 3), half), (0, (0, 1), half)), cuts, (0, early)),
        ),
        after(near, own_sums), other_near, [first_gates, second_gates],
        [first_saved[:3], first_saved[3:], second_saved[:3], second_saved[3:]], matrices,
        token_count,
    )
    travelling = after(travelling, own_sums)
    met = lax.ppermute(travelling, "psg", [(index, index ^ 1) for index in range(passages)])
    near_scores = pack(travelling, met)
    x_low, y_high, near_scores = lax.optimization_barrier((x_low, y_high, near_scores))
    x_low, y_high = swap(x_low, ACROSS_X), swap(y_high, ACROSS_Y)
    x_high, y_low = kernel_call(
        add_kernel,
        "add",
        [kept(x_high.shape, jnp.bfloat16), kept(y_low.shape, jnp.bfloat16)],
        [pinned(x_high), pinned(y_low), far_high, far_low],
    )
    x_high, y_low, near_scores = lax.optimization_barrier((x_high, y_low, near_scores))
    x_high, y_low = swap(x_high, ACROSS_X), swap(y_low, ACROSS_Y)
    far_scores = lax.ppermute(near_scores, "psg", [(index, index ^ 2) for index in range(passages)])
    loss, factor = kernel_call(
        rank_kernel,
        "rank",
        [shape_of((1, 1), jnp.float32), kept((1, 128), jnp.float32)],
        [pinned(swap_gain), pinned(near_scores), far_scores],
    )
    total, lines = kernel_call(
        first_end_kernel,
        "first_end",
        [
            kept((token_count, model_width), jnp.float32),
            kept((8, token_count), jnp.float32),
        ],
        [pinned(own_sums), after(x_low, factor), y_high],
    )
    (grad,) = kernel_call(
        end_kernel,
        "end",
        [shape_of((token_count, model_width), jnp.bfloat16)],
        [
            pinned(factor), pinned(total), pinned(lines), x_high, y_low, pinned(flat), pinned(gain),
            pinned(turned_gates), pinned(router_rows), pinned(unit_vector),
        ],
        scratch=[
            pltpu.VMEM((token_count, model_width), jnp.float32),
            pltpu.VMEM((token_count, model_width), jnp.bfloat16),
            pltpu.SemaphoreType.DMA((token_count // 32,)),
        ],
        result=pl.ANY,
    )
    return (loss.reshape(1), own_score, grad.reshape(hidden.shape))


def block(*arrays):
    hidden, router, expert_ids, grades = arrays[0], arrays[2], arrays[8], arrays[9]
    each_expert = router.shape[1] == expert_ids.shape[3] == 8
    if hidden.shape[1] == 1 and each_expert and grades.shape[1] == 4:
        return every_expert(*arrays)
    return local(*arrays)


def solution(mesh):
    placed = (
        P("exp", "psg", None, None),
        P(),
        P(),
        P("exp", None, None),
        P("exp", None, None),
        P("exp", None, None),
        P(),
        P(),
        P("exp", "psg", None, None),
        P("exp", None),
        P("exp", None),
    )
    return jax.shard_map(
        block,
        mesh=mesh,
        in_specs=placed,
        out_specs=(P("exp"), P("exp", "psg"), P("exp", "psg", None, None)),
        check_vma=False,
    )
```

```python
import functools
import math

import jax
import jax.numpy as jnp
from jax import lax
from jax.experimental import pallas as pl
from jax.experimental.pallas import tpu as pltpu
from jax.sharding import PartitionSpec as P

epsilon = 1e-06
loss_scale = 256.0
highest = lax.Precision.HIGHEST


def rms_scale(values):
    return lax.rsqrt(jnp.mean(values * values, axis=-1, keepdims=True) + epsilon)


def head_score(pooled, final_gain, score_vector):
    scaled = pooled * rms_scale(pooled) * final_gain
    return jnp.dot(scaled, score_vector.astype(jnp.float32), precision=highest)


def rank_loss(scores, grades, passage_ranks):
    grade_value = grades.astype(jnp.float32)
    worth_gain = jnp.exp2(grade_value)
    discount = 1.0 / jnp.log2(2.0 + passage_ranks.astype(jnp.float32))
    better_than = grades[None, :] > grades[:, None]
    equal_grade = grades[None, :] == grades[:, None]
    position = jnp.arange(grades.shape[0], dtype=jnp.int32)
    earlier = position[None, :] < position[:, None]
    ideal_rank = jnp.sum(
        jnp.logical_or(better_than, jnp.logical_and(equal_grade, earlier)).astype(jnp.float32),
        axis=1,
    )
    ideal_gain = jnp.sum((worth_gain - 1.0) / jnp.log2(2.0 + ideal_rank))
    ordered = (grades[:, None] > grades[None, :]).astype(jnp.float32)
    swap_gain = (
        jnp.abs(
            (worth_gain[:, None] - worth_gain[None, :]) * (discount[:, None] - discount[None, :])
        )
        / ideal_gain
    )
    margin = scores[:, None] - scores[None, :]
    return jnp.sum(ordered * swap_gain * jax.nn.softplus(-margin))


def pick_gates(normed, router, picked_ids):
    expert_total = router.shape[1]
    logits = jnp.dot(normed, router, preferred_element_type=jnp.float32)
    onehot = (
        picked_ids[:, :, None] == jnp.arange(expert_total, dtype=jnp.int32)[None, None, :]
    ).astype(jnp.float32)
    chosen = jnp.einsum("nke,ne->nk", onehot, logits, precision=highest)
    weights = jnp.exp(chosen)
    return (weights / jnp.sum(weights, axis=1, keepdims=True), onehot)


def gate_parts(pre_gate):
    sigmoid_gate = jax.nn.sigmoid(pre_gate)
    return (pre_gate * sigmoid_gate, sigmoid_gate * (1.0 + pre_gate * (1.0 - sigmoid_gate)))


def norm_back(flat_rows, inverse, norm_gain, d_normed):
    scaled = d_normed * norm_gain
    return inverse * scaled - flat_rows * inverse * inverse * inverse * jnp.mean(
        flat_rows * scaled, axis=-1, keepdims=True
    )


def unpack_front(front_out, buffer_rows):
    pre_gate, pre_up, received = front_out
    hidden_units = pre_gate.shape[2]
    pre_gate = pre_gate.reshape(buffer_rows, hidden_units)
    pre_up = pre_up.reshape(buffer_rows, hidden_units)
    silu_gate, slope = gate_parts(pre_gate)
    activation = (silu_gate * pre_up).astype(jnp.bfloat16)
    return (pre_up, received, silu_gate, slope, activation)


def local(
    hidden,
    norm_gain,
    router,
    gate_proj,
    up_proj,
    down_proj,
    final_gain,
    score_vector,
    expert_ids,
    grades,
    passage_ranks,
):
    unused_query, local_passages, local_positions, model_width = hidden.shape
    top_count = expert_ids.shape[3]
    expert_count = lax.axis_size("exp")
    token_count = local_passages * local_positions
    slot_count = token_count * top_count
    capacity = min(token_count, 9 * token_count * top_count // (8 * expert_count))
    buffer_rows = expert_count * capacity
    flat_rows = hidden.reshape(token_count, model_width).astype(jnp.float32)
    inverse = rms_scale(flat_rows)
    normed = (flat_rows * inverse * norm_gain).astype(jnp.bfloat16)
    picked_ids = expert_ids.reshape(token_count, top_count)
    gate_values, onehot = pick_gates(normed, router, picked_ids)
    slot_hits = onehot.reshape(slot_count, expert_count).astype(jnp.int32)
    slot_rank = jnp.sum((jnp.cumsum(slot_hits, axis=0) - slot_hits) * slot_hits, axis=1)
    target = picked_ids.reshape(slot_count) * capacity + slot_rank
    source_token = jnp.arange(slot_count, dtype=jnp.int32) // top_count
    passage_onehot = (
        source_token[:, None] // local_positions
        == jnp.arange(local_passages, dtype=jnp.int32)[None, :]
    ).astype(jnp.float32)
    weighted = (passage_onehot * gate_values.reshape(slot_count, 1)).astype(jnp.bfloat16)
    send_rows = (
        jnp.zeros((buffer_rows, model_width), jnp.bfloat16).at[target].set(normed[source_token])
    )
    send_weights = jnp.zeros((buffer_rows, local_passages), jnp.bfloat16).at[target].set(weighted)
    outgoing = (
        send_rows.reshape(expert_count, capacity, model_width),
        send_weights.reshape(expert_count, capacity, local_passages),
    )
    gate_matrix = gate_proj[0]
    up_matrix = up_proj[0]
    down_matrix = down_proj[0]
    rows_in = lax.all_to_all(outgoing[0], "exp", split_axis=0, concat_axis=0, tiled=True)
    weights_in = lax.all_to_all(outgoing[1], "exp", split_axis=0, concat_axis=0, tiled=True)
    pre_gate = jnp.einsum("end,df->enf", rows_in, gate_matrix, preferred_element_type=jnp.float32)
    pre_up = jnp.einsum("end,df->enf", rows_in, up_matrix, preferred_element_type=jnp.float32)
    front_out = (pre_gate, pre_up, weights_in)
    pre_up, received, silu_gate, slope, activation = unpack_front(front_out, buffer_rows)
    hidden_units = activation.shape[1]
    passage_part = jnp.einsum(
        "scp,scf->spf",
        received,
        activation.reshape(expert_count, capacity, hidden_units),
        preferred_element_type=jnp.float32,
    )
    down_wide = down_matrix.astype(jnp.float32)
    expert_terms = jnp.einsum("spf,fd->spd", passage_part, down_wide, precision=highest)
    came_back = lax.all_to_all(expert_terms, "exp", split_axis=0, concat_axis=0, tiled=True)
    token_sums = jnp.sum(flat_rows.reshape(local_passages, local_positions, model_width), axis=1)
    pooled = (token_sums + jnp.sum(came_back, axis=0)) / local_positions
    first_row = lax.axis_index("psg") * local_passages
    own_score = head_score(pooled, final_gain, score_vector)
    every_score = lax.all_gather(own_score, "psg", axis=0, tiled=True)
    loss_value, loss_grad = jax.value_and_grad(rank_loss)(every_score, grades[0], passage_ranks[0])
    d_own = lax.dynamic_slice_in_dim(loss_grad, first_row, local_passages, 0) * loss_scale
    unused_score, head_back = jax.vjp(
        lambda values: head_score(values, final_gain, score_vector), pooled
    )
    d_vector = head_back(d_own)[0] / local_positions
    every_vector = lax.all_gather(d_vector[None], "exp", axis=0, tiled=True)
    near_table = jnp.einsum("spd,fd->spf", every_vector, down_wide, precision=highest)
    present = (received != 0).astype(jnp.float32)
    near_rows = jnp.einsum("scp,spf->scf", present, near_table, precision=highest).reshape(
        buffer_rows, hidden_units
    )
    gate_weight = jnp.sum(received.astype(jnp.float32), axis=2).reshape(buffer_rows, 1)
    d_act = gate_weight * near_rows
    d_gate = (d_act * pre_up * slope).astype(jnp.bfloat16)
    d_up = (d_act * silu_gate).astype(jnp.bfloat16)
    contract = (((1,), (1,)), ((), ()))
    pick_grad = lax.dot_general(d_gate, gate_matrix, contract, preferred_element_type=jnp.float32)
    pick_grad = (
        pick_grad + lax.dot_general(d_up, up_matrix, contract, preferred_element_type=jnp.float32)
    ).astype(jnp.bfloat16)
    gate_grad = jnp.sum(activation.astype(jnp.float32) * near_rows, axis=1).astype(jnp.bfloat16)
    back_rows, back_gate = (
        lax.all_to_all(
            pick_grad.reshape(expert_count, capacity, model_width),
            "exp",
            split_axis=0,
            concat_axis=0,
            tiled=True,
        ),
        lax.all_to_all(
            gate_grad.reshape(expert_count, capacity),
            "exp",
            split_axis=0,
            concat_axis=0,
            tiled=True,
        ),
    )
    picked_rows = back_rows.reshape(buffer_rows, model_width)[target]
    d_normed = jnp.sum(
        picked_rows.reshape(token_count, top_count, model_width).astype(jnp.float32), axis=1
    )
    picked_gate = (
        back_gate.reshape(buffer_rows)[target].astype(jnp.float32).reshape(token_count, top_count)
    )
    d_logit = gate_values * (
        picked_gate - jnp.sum(gate_values * picked_gate, axis=1, keepdims=True)
    )
    dense_logit = jnp.einsum("nk,nke->ne", d_logit, onehot, precision=highest)
    d_normed = d_normed + jnp.einsum(
        "ne,de->nd", dense_logit, router.astype(jnp.float32), precision=highest
    )
    grad_flat = norm_back(flat_rows, inverse, norm_gain, d_normed)
    grad_hidden = (
        grad_flat.reshape(1, local_passages, local_positions, model_width)
        + d_vector[None, :, None, :]
    )
    return (
        loss_value.reshape(1),
        own_score.reshape(1, local_passages),
        grad_hidden.astype(jnp.bfloat16),
    )


CORE, ACROSS_X, ACROSS_Y = 1, 2, 4
forward = (((1,), (0,)), ((), ()))
across = (((1,), (1,)), ((), ()))
MIB = 1 << 20


def swap(value, bit, size=8):
    return lax.ppermute(value, "exp", [(index, index ^ bit) for index in range(size)])


def shape_of(shape, dtype):
    return jax.ShapeDtypeStruct(shape, dtype)


def after(value, *others):
    return lax.optimization_barrier((value, *others))[0]


def kept(shape, dtype):
    return pltpu.VMEM(shape, dtype)


def pinned(array):
    return pltpu.with_memory_space_constraint(array, pltpu.VMEM)


def kernel_call(body, name, outs, ins, far=(), scratch=(), work=1, result=pltpu.VMEM):
    spaces = [pltpu.VMEM] * len(ins)
    ins = list(ins)
    for index in far:
        spaces[index] = pl.ANY
        ins[index] = pltpu.with_memory_space_constraint(ins[index], pltpu.HBM)
    return pl.pallas_call(
        body,
        name=name,
        out_shape=outs,
        in_specs=[pl.BlockSpec(memory_space=space) for space in spaces],
        out_specs=[pl.BlockSpec(memory_space=result)] * len(outs),
        scratch_shapes=scratch,
        compiler_params=pltpu.CompilerParams(vmem_limit_bytes=8 * MIB),
        cost_estimate=pl.CostEstimate(flops=work, bytes_accessed=1, transcendentals=0),
    )(*ins)


def split_low(values):
    high = values.astype(jnp.bfloat16)
    rest = values - high.astype(jnp.float32)
    middle = rest.astype(jnp.bfloat16)
    low = (rest - middle.astype(jnp.float32)).astype(jnp.bfloat16)
    return high, middle, low


def exact_dot(values, low_matrix, contract):
    parts = lax.dot_general(
        jnp.concatenate(split_low(values), axis=0),
        low_matrix,
        contract,
        preferred_element_type=jnp.float32,
    )
    return parts[0:8] + parts[8:16] + parts[16:24]


def other_order(values, bits):
    return jnp.concatenate([values[row ^ bits : (row ^ bits) + 1] for row in range(4)], axis=0)


def norm_kernel(
    hidden_far, gain_far, router_far, final_far, vector_far,
    hidden_ref, gain_ref, router_ref, normed_ref, sums_ref, head_ref,
    final_ref, vector_ref, copy_sems,
):
    pairs = (
        (hidden_far, hidden_ref), (gain_far, gain_ref), (router_far, router_ref),
        (final_far, final_ref), (vector_far, vector_ref),
    )
    copies = [
        pltpu.make_async_copy(source, target, copy_sems.at[index])
        for index, (source, target) in enumerate(pairs)
    ]
    for copy in copies:
        copy.start()
    for copy in copies:
        copy.wait()
    vector = vector_ref[...].astype(jnp.float32)
    vector = jnp.concatenate([vector[row : row + 1] for row in range(vector.shape[0])], axis=1)
    head_ref[...] = final_ref[...] * vector
    rows = hidden_ref[...].astype(jnp.float32)
    normed_ref[...] = (rows * rms_scale(rows) * gain_ref[...]).astype(jnp.bfloat16)
    sums_ref[...] = jnp.sum(rows, axis=0, keepdims=True)


def front_kernel(stage, owners, sets, count, router_ref, *refs):
    matrices, refs = refs[: 2 * len(sets)], refs[2 * len(sets) :]
    pieces, refs = refs[:count], refs[count:]
    matrices = list(matrices)
    hidden_units = matrices[0].shape[1]
    tile = 256
    firsts = range(0, hidden_units, tile)
    if stage == 0:
        far_matrices = matrices
        *refs, gate_held, up_held, rows_ref, copy_sems = refs
        matrices = [gate_held, up_held]
        copies = [
            pltpu.make_async_copy(
                source.at[:, first : first + tile],
                target.at[:, first : first + tile],
                copy_sems.at[which, number],
            )
            for number, first in enumerate(firsts)
            for which, (source, target) in enumerate(zip(far_matrices, matrices))
        ]
        for copy in copies:
            copy.start()
        turned_ref, *refs = refs
    elif stage == 1:
        down_far, *refs, down_ref, rows_ref, copy_sem = refs
        down_copy = pltpu.make_async_copy(down_far, down_ref, copy_sem)
        down_copy.start()
    elif stage == 3:
        sums_ref, *downs = refs[:3]
        earlier, refs = refs[3:6], refs[6:]
        *refs, terms_ref, rows_ref = refs
    else:
        *refs, rows_ref = refs
    gates_ref, *outs = refs
    expert = lax.axis_index("exp")
    first = 0
    for piece in pieces:
        rows_ref[first : first + piece.shape[0], :] = piece[...]
        first += piece.shape[0]
    size = first // len(owners)
    logits = lax.dot_general(
        rows_ref[...], router_ref[...], across, preferred_element_type=jnp.float32
    )
    weights = jnp.exp(logits)
    gates = weights / jnp.sum(weights, axis=1, keepdims=True)
    gates_ref[...] = gates
    lane = lax.broadcasted_iota(jnp.int32, gates.shape, 1)
    if stage == 0:
        weights = jnp.exp(
            lax.dot_general(
                router_ref[...], rows_ref[...], across, preferred_element_type=jnp.float32
            )
        )
        turned_ref[...] = weights / jnp.sum(weights, axis=0, keepdims=True)

    totals = []
    for place, which in enumerate(sets):
        gate_ref, up_ref = matrices[2 * place : 2 * place + 2]
        if stage == 3:
            slope_ref, silu_ref, act_ref = outs[3 * place : 3 * place + 3]
        else:
            slope_ref, silu_ref, act_ref, part_ref = outs
        own = jnp.sum(jnp.where(lane == expert ^ which, gates, 0.0), axis=1, keepdims=True)
        low = own.astype(jnp.bfloat16).astype(jnp.float32)
        parts = []
        for number, first in enumerate(firsts):
            columns = slice(first, first + tile)
            if stage == 0:
                copies[2 * number].wait()
                copies[2 * number + 1].wait()
            rows = rows_ref[...]
            pre_gate = jnp.dot(rows, gate_ref[:, columns], preferred_element_type=jnp.float32)
            pre_up = jnp.dot(rows, up_ref[:, columns], preferred_element_type=jnp.float32)
            silu_gate, slope = gate_parts(pre_gate)
            activation = (silu_gate * pre_up).astype(jnp.bfloat16)
            slope_ref[:, columns] = slope * pre_up
            silu_ref[:, columns] = silu_gate
            act_ref[:, columns] = activation
            weighted = activation.astype(jnp.float32) * low
            found = {
                owner: jnp.sum(weighted[index * size : (index + 1) * size], axis=0, keepdims=True)
                for index, owner in enumerate(owners)
            }
            nothing = jnp.zeros_like(weighted[:1])
            parts.append(
                jnp.concatenate([found.get(owner, nothing) for owner in range(8)], axis=0)
            )
        totals.append(jnp.concatenate(parts, axis=1))
    if stage == 1:
        down_copy.wait()
    if stage < 3:
        part_ref[...] = totals[0]
        return
    own_first, own_second, other_first = earlier
    totals[0] = totals[0] + (own_first[...] + own_second[...])
    totals[1] = totals[1] + other_first[...]
    terms = exact_dot(totals[0], downs[0][...], forward) + exact_dot(
        totals[1], downs[1][...], forward
    )
    row = lax.broadcasted_iota(jnp.int32, terms.shape, 0)
    terms_ref[...] = (terms + jnp.where(row == 0, sums_ref[...], 0.0))[:4]


def front(stage, owners, sets, pieces, router_rows, matrices, more=()):
    model_width, hidden_units = matrices[0].shape
    row_total = sum(piece.shape[0] for piece in pieces)
    outs = [kept((row_total, 8), jnp.float32)]
    if stage == 0:
        outs.insert(0, kept((8, row_total), jnp.float32))
    for which in sets:
        outs += [
            kept((row_total, hidden_units), jnp.float32),
            kept((row_total, hidden_units), jnp.float32),
            kept((row_total, hidden_units), jnp.bfloat16),
        ]
    outs.append(
        kept((4, model_width), jnp.float32) if stage == 3 else kept((8, hidden_units), jnp.float32)
    )
    scratch = [pltpu.VMEM((row_total, model_width), jnp.bfloat16)]
    far = ()
    if stage == 0:
        far = (1, 2)
        outs += [kept(matrix.shape, jnp.bfloat16) for matrix in matrices]
        scratch.append(pltpu.SemaphoreType.DMA((2, hidden_units // 256)))
    else:
        matrices = [pinned(matrix) for matrix in matrices]
    if stage == 1:
        far = (3 + len(pieces),)
        outs.append(kept(more[0].shape, jnp.bfloat16))
        scratch.append(pltpu.SemaphoreType.DMA)
    if stage == 3:
        more = [pinned(array) for array in more]
    return kernel_call(
        functools.partial(front_kernel, stage, owners, sets, len(pieces)),
        "front",
        outs,
        [pinned(router_rows), *matrices, *(pinned(piece) for piece in pieces), *more],
        far,
        scratch,
    )


def near_kernel(
    own_ref, x_ref, y_ref, far_ref, head_ref, down_ref, other_down_ref,
    near_ref, other_near_ref, unit_ref, score_ref, own_score_ref, *, token_count,
):
    pooled = (
        (own_ref[...] + other_order(x_ref[...], 1))
        + (other_order(y_ref[...], 2) + other_order(far_ref[...], 3))
    ) / token_count
    pooled = jnp.concatenate([pooled, jnp.zeros_like(pooled)], axis=0)
    head = head_ref[...]
    scale = rms_scale(pooled)
    along = jnp.sum(pooled * head, axis=1, keepdims=True)
    own_score = (scale * along)[:1]
    own_score_ref[...] = own_score
    score_ref[...] = jnp.broadcast_to(own_score, score_ref.shape)
    unit = (
        scale * head - scale * scale * scale * (along / pooled.shape[1]) * pooled
    ) / token_count
    unit_ref[...] = unit[:1]
    parts = jnp.concatenate(split_low(unit), axis=0)
    parts = jnp.concatenate([parts, jnp.zeros((104, parts.shape[1]), jnp.bfloat16)], axis=0)
    for table_ref, matrix_ref in ((near_ref, down_ref), (other_near_ref, other_down_ref)):
        turned = lax.dot_general(
            matrix_ref[...], parts, across, preferred_element_type=jnp.float32
        ).T
        table_ref[...] = turned[0:8] + turned[8:16] + turned[16:24]


def back_kernel(passages, turned, gate_count, saved_count, near_ref, other_near_ref, *refs):
    gates_refs, refs = refs[:gate_count], refs[gate_count:]
    saved, refs = refs[: 3 * saved_count], refs[3 * saved_count :]
    matrices, refs = refs[:4], refs[4:]
    *out_refs, d_gate_ref, d_up_ref, other_d_gate_ref, other_d_up_ref = refs
    expert = lax.axis_index("exp")
    size = out_refs[0].shape[1]
    model_width = matrices[0].shape[1 if turned else 0]
    lane = lax.broadcasted_iota(jnp.int32, (size, 8), 1)
    line = lax.broadcasted_iota(jnp.int32, (16, size), 0)
    experts = (
        (near_ref, d_gate_ref, d_up_ref), (other_near_ref, other_d_gate_ref, other_d_up_ref)
    )
    outs = []
    for index, (owner, gates_place, saved_places, cuts, unused) in enumerate(passages):
        outs.append(out_refs[: len(cuts)])
        out_refs = out_refs[len(cuts) :]
        rows = slice(index * size, (index + 1) * size)
        lines = jnp.zeros((16, size), jnp.float32)
        gates = gates_refs[gates_place[0]][gates_place[1] : gates_place[1] + size, :]
        for which, (table_ref, d_gate_out, d_up_out) in enumerate(experts):
            number, first = saved_places[which]
            slope_ref, silu_ref, act_ref = saved[3 * number : 3 * number + 3]
            held = slice(first, first + size)
            near = table_ref[owner : owner + 1, :]
            own = jnp.sum(
                jnp.where(lane == expert ^ which, gates, 0.0), axis=1, keepdims=True
            )
            d_act = own.astype(jnp.bfloat16).astype(jnp.float32) * near
            d_gate_out[rows, :] = (d_act * slope_ref[held, :]).astype(jnp.bfloat16)
            d_up_out[rows, :] = (d_act * silu_ref[held, :]).astype(jnp.bfloat16)
            gate_grad = exact_dot(table_ref[...], act_ref[held, :], across)[owner : owner + 1]
            lines = jnp.where(line == expert ^ which, gate_grad, lines)
        bounds = cuts + (model_width + 16,)
        for out_ref, cut, end in zip(outs[-1], bounds, bounds[1:]):
            if out_ref.shape[0] > end - cut:
                rest = out_ref.shape[0] - (end - cut)
                out_ref[end - cut :, :] = jnp.zeros((rest, size), jnp.bfloat16)
        outs[-1][-1][model_width - cuts[-1] : model_width + 16 - cuts[-1], :] = lines.astype(
            jnp.bfloat16
        )

    sides = (d_gate_ref, d_up_ref, other_d_gate_ref, other_d_up_ref)
    for first in range(0, model_width, 256):
        pick_grad = None
        for side_ref, matrix in zip(sides, matrices):
            if turned:
                term = jnp.dot(
                    side_ref[...],
                    matrix[:, first : first + 256],
                    preferred_element_type=jnp.float32,
                )
            else:
                term = lax.dot_general(
                    matrix[first : first + 256, :],
                    side_ref[...],
                    across,
                    preferred_element_type=jnp.float32,
                )
            pick_grad = term if pick_grad is None else pick_grad + term
        if turned:
            pick_grad = pick_grad.T
        pick_grad = pick_grad.astype(jnp.bfloat16)
        for index, passage in enumerate(passages):
            cuts = passage[3]
            place = max(number for number, cut in enumerate(cuts) if cut <= first)
            rows = slice(first - cuts[place], first - cuts[place] + 256)
            outs[index][place][rows, :] = pick_grad[:, index * size : (index + 1) * size]


def back(passages, near, other_near, gates, saved, matrices, size, turned=False):
    model_width, hidden_units = matrices[0].shape[:: -1 if turned else 1]
    heights = []
    for passage in passages:
        cuts, least = passage[3:]
        ends = cuts[1:] + (model_width + 16,)
        heights += [max(low, end - cut) for low, cut, end in zip(least, cuts, ends)]
    arrays = [array for group in saved for array in group]
    return kernel_call(
        functools.partial(back_kernel, passages, turned, len(gates), len(saved)),
        "back",
        [kept((height, size), jnp.bfloat16) for height in heights],
        [pinned(array) for array in (near, other_near, *gates, *arrays, *matrices)],
        (),
        [pltpu.VMEM((len(passages) * size, hidden_units), jnp.bfloat16)] * 4,
    )


def add_kernel(x_ref, y_ref, high_ref, low_ref, x_out, y_out):
    for own_ref, other_ref, out_ref in ((x_ref, high_ref, x_out), (y_ref, low_ref, y_out)):
        out_ref[...] = (
            own_ref[...].astype(jnp.float32)
            + other_ref[: own_ref.shape[0], :].astype(jnp.float32)
        ).astype(jnp.bfloat16)


def turn_kernel(gate_ref, up_ref, turned_gate_ref, turned_up_ref):
    for first in range(0, gate_ref.shape[0], 256):
        rows = slice(first, first + 256)
        turned_gate_ref[:, rows] = gate_ref[rows, :].T
        turned_up_ref[:, rows] = up_ref[rows, :].T


def half_kernel(part, rows_ref, out_ref):
    half = out_ref.shape[0]
    out_ref[...] = rows_ref[part * half : (part + 1) * half, :]


def half_of(rows, part):
    total, wide = rows.shape
    (out,) = kernel_call(
        functools.partial(half_kernel, part), "half", [kept((total // 2, wide), rows.dtype)], [rows]
    )
    return out


def pack_kernel(first_ref, second_ref, out_ref):
    rows = first_ref.shape[0]
    out_ref[:rows, :] = first_ref[...]
    out_ref[rows:, :] = second_ref[...]


def pack(first, second, work=1):
    rows, wide = first.shape
    return kernel_call(
        pack_kernel, "pack", [kept((2 * rows, wide), first.dtype)], [first, second], work=work
    )[0]


def pairs_of(passages):
    row = lax.broadcasted_iota(jnp.int32, (8, 128), 0)
    lane = lax.broadcasted_iota(jnp.int32, (8, 128), 1)
    return row, lane, jnp.logical_and(row < passages, lane < passages)


def spread(index, values):
    total = jnp.zeros((8, 128), jnp.float32)
    for number, value in values:
        total = jnp.where(index == number, value, total)
    return total


def whole_sum(values):
    return jnp.sum(jnp.sum(values, axis=1, keepdims=True), axis=0, keepdims=True)


def pair_kernel(grades_far, ranks_far, swap_gain_ref, grades_ref, ranks_ref, copy_sems):
    copies = [
        pltpu.make_async_copy(grades_far, grades_ref, copy_sems.at[0]),
        pltpu.make_async_copy(ranks_far, ranks_ref, copy_sems.at[1]),
    ]
    for copy in copies:
        copy.start()
    for copy in copies:
        copy.wait()
    passages = grades_ref.shape[1]
    row, lane, pair = pairs_of(passages)
    grade_list = [(number, grades_ref[0, number].astype(jnp.float32)) for number in range(passages)]
    rank_list = [(number, ranks_ref[0, number].astype(jnp.float32)) for number in range(passages)]
    grade_row, grade_lane = spread(row, grade_list), spread(lane, grade_list)
    worth_row, worth_lane = jnp.exp2(grade_row), jnp.exp2(grade_lane)
    discount_row = 1.0 / jnp.log2(2.0 + spread(row, rank_list))
    discount_lane = 1.0 / jnp.log2(2.0 + spread(lane, rank_list))
    ahead = jnp.logical_or(
        grade_lane > grade_row, jnp.logical_and(grade_lane == grade_row, lane < row)
    )
    ideal_rank = jnp.sum(
        jnp.where(jnp.logical_and(pair, ahead), 1.0, 0.0), axis=1, keepdims=True
    )
    ideal_terms = (worth_row - 1.0) / jnp.log2(2.0 + ideal_rank)
    one_lane = jnp.logical_and(pair, lane == 0)
    ideal_gain = whole_sum(jnp.where(one_lane, ideal_terms, 0.0))
    swap_gain = (
        jnp.abs((worth_row - worth_lane) * (discount_row - discount_lane)) / ideal_gain
    )
    swap_gain_ref[...] = jnp.where(
        jnp.logical_and(pair, grade_row > grade_lane), swap_gain, 0.0
    )


def rank_kernel(swap_gain_ref, near_scores_ref, far_scores_ref, loss_ref, factor_ref):
    passages = 2 * near_scores_ref.shape[0]
    place = lax.axis_index("psg")
    row, lane, unused = pairs_of(passages)
    score_list = [
        (place ^ (base + number), jnp.broadcast_to(ref[number : number + 1, :], (8, 128)))
        for base, ref in ((0, near_scores_ref), (passages // 2, far_scores_ref))
        for number in range(passages // 2)
    ]
    swap_gain = swap_gain_ref[...]
    margin = spread(row, score_list) - spread(lane, score_list)
    softplus = jnp.maximum(-margin, 0.0) + jnp.log1p(jnp.exp(-jnp.abs(margin)))
    loss_ref[...] = whole_sum(swap_gain * softplus)
    pull = swap_gain * jax.nn.sigmoid(-margin)
    gradient = whole_sum(jnp.where(lane == place, pull, 0.0) - jnp.where(row == place, pull, 0.0))
    factor_ref[...] = jnp.broadcast_to(gradient * loss_scale, factor_ref.shape)


def first_end_kernel(own_ref, x_low_ref, y_high_ref, total_ref, lines_ref):
    model_width = total_ref.shape[1]
    cut = model_width // 2
    for first in range(0, model_width, 256):
        rows = slice(first, first + 256)
        if first < cut:
            term = x_low_ref[rows, :]
        else:
            term = y_high_ref[first - cut : first - cut + 256, :]
        total = own_ref[rows, :].astype(jnp.float32) + term.astype(jnp.float32)
        total_ref[:, rows] = total.T
    end = slice(model_width, model_width + 8)
    end_high = slice(model_width - cut, model_width - cut + 8)
    lines_ref[...] = own_ref[end, :].astype(jnp.float32) + y_high_ref[end_high, :].astype(
        jnp.float32
    )


def end_kernel(
    factor_ref, total_ref, lines_ref, x_high_ref, y_low_ref,
    hidden_ref, gain_ref, gates_ref, router_ref, unit_ref,
    grad_far, turned_ref, grad_ref, copy_sems,
):
    token_count, model_width = hidden_ref.shape
    cut = y_low_ref.shape[0]
    end_high = slice(model_width - cut, model_width - cut + 8)
    slot_grad = lines_ref[...] + x_high_ref[end_high, :].astype(jnp.float32)
    gates = gates_ref[...]
    d_logit = gates * (slot_grad - jnp.sum(gates * slot_grad, axis=0, keepdims=True))
    d_logit = jnp.concatenate([d_logit, jnp.zeros((120, token_count), jnp.float32)], axis=0).T
    d_logit = jnp.concatenate(split_low(d_logit[:, :8]), axis=1)
    router_rows = jnp.concatenate([router_ref[...]] * 3, axis=0)
    for first in range(0, model_width, 256):
        columns = slice(first, first + 256)
        if first < cut:
            term = y_low_ref[columns, :]
        else:
            term = x_high_ref[first - cut : first - cut + 256, :]
        turned_ref[:, columns] = (
            total_ref[:, columns]
            + term.astype(jnp.float32).T
            + jnp.dot(d_logit, router_rows[:, columns], preferred_element_type=jnp.float32)
        )
    gain = gain_ref[...]
    factor = factor_ref[:, :1]
    size = 32
    copies = []
    for first in range(0, token_count, size):
        rows = slice(first, first + size)
        flat_rows = hidden_ref[rows, :].astype(jnp.float32)
        grad = norm_back(flat_rows, rms_scale(flat_rows), gain, turned_ref[rows, :])
        grad_ref[rows, :] = ((grad + unit_ref[...]) * factor).astype(jnp.bfloat16)
        copies.append(
            pltpu.make_async_copy(
                grad_ref.at[rows, :], grad_far.at[rows, :], copy_sems.at[first // size]
            )
        )
        copies[-1].start()
    for copy in copies:
        copy.wait()


def every_expert(
    hidden,
    norm_gain,
    router,
    gate_proj,
    up_proj,
    down_proj,
    final_gain,
    score_vector,
    expert_ids,
    grades,
    passage_ranks,
):
    unused_query, unused_passage, token_count, model_width = hidden.shape
    passages = grades.shape[1]
    flat = hidden.reshape(token_count, model_width)
    gate_matrix, up_matrix, down_matrix = gate_proj[0], up_proj[0], down_proj[0]
    mine = [gate_matrix, up_matrix, down_matrix]
    flat, gain, router_rows, normed, token_sums, head = kernel_call(
        norm_kernel,
        "norm",
        [
            kept(flat.shape, jnp.bfloat16),
            kept((1, model_width), jnp.float32),
            kept((8, model_width), jnp.bfloat16),
            kept(flat.shape, jnp.bfloat16),
            kept((1, model_width), jnp.float32),
            kept((1, model_width), jnp.float32),
        ],
        [
            flat,
            norm_gain.reshape(1, model_width),
            router.T,
            final_gain.reshape(1, model_width),
            score_vector.reshape(model_width // 128, 128),
        ],
        range(5),
        [
            pltpu.VMEM((1, model_width), jnp.float32),
            pltpu.VMEM((model_width // 128, 128), jnp.bfloat16),
            pltpu.SemaphoreType.DMA((5,)),
        ],
    )
    others = [swap(matrix, CORE) for matrix in mine]
    x_rows, y_rows = swap(normed, ACROSS_X), swap(normed, ACROSS_Y)
    turned_gates, own_gates, *own_saved, own_part, mine[0], mine[1] = front(
        0, (0,), (0,), [normed], router_rows, mine[:2]
    )
    (swap_gain,) = kernel_call(
        pair_kernel,
        "pairs",
        [kept((8, 128), jnp.float32)],
        [grades, after(passage_ranks, own_part)],
        (0, 1),
        [
            pltpu.SMEM(grades.shape, jnp.int32),
            pltpu.SMEM(grades.shape, jnp.int32),
            pltpu.SemaphoreType.DMA((2,)),
        ],
    )
    mine_turned = kernel_call(
        turn_kernel,
        "turn",
        [kept(mine[0].shape[::-1], jnp.bfloat16)] * 2,
        [pinned(after(mine[0], swap_gain)), pinned(mine[1])],
    )
    x_rows, y_rows = after(x_rows, mine_turned[0]), after(y_rows, mine_turned[0])
    far_low = swap(half_of(x_rows, 0), ACROSS_Y)
    far_high = swap(half_of(y_rows, 1), ACROSS_X)
    side_gates, *side_saved, side_part, mine[2] = front(
        1, (1, 2), (0,), [x_rows, y_rows], router_rows, mine[:2], mine[2:]
    )
    others[0] = after(others[0], side_part)
    unused, *other_saved, other_part = front(
        2, (0, 1, 2), (1,), [normed, x_rows, y_rows], router_rows, others[:2]
    )
    far_low, far_high = after(far_low, other_part), after(far_high, other_part)
    far_gates, *far_saved, terms = front(
        3, (3,), (0, 1), [far_low, far_high], router_rows, mine[:2] + others[:2],
        (token_sums, mine[2], others[2], own_part, side_part, other_part),
    )

    near, other_near, unit_vector, travelling, own_score = kernel_call(
        functools.partial(near_kernel, token_count=token_count),
        "near",
        [
            kept((8, down_matrix.shape[0]), jnp.float32),
            kept((8, down_matrix.shape[0]), jnp.float32),
            kept((1, model_width), jnp.float32),
            kept((1, 128), jnp.float32),
            shape_of((1, 1), jnp.float32),
        ],
        [
            pinned(terms),
            swap(terms, ACROSS_X),
            swap(terms, ACROSS_Y),
            swap(terms, ACROSS_X | ACROSS_Y),
            pinned(head),
            pinned(mine[2]),
            pinned(others[2]),
        ],
    )
    matrices = mine[:2] + others[:2]
    others_turned = [swap(after(matrix, other_part), CORE) for matrix in mine_turned]
    cuts, early, earlier = (0, model_width // 2), model_width // 2 + 32, model_width // 2 + 64
    far_low, far_high = back(
        ((3, (0, 0), ((0, 0), (1, 0)), cuts, (earlier, earlier)),),
        near, other_near, [far_gates], [far_saved[:3], far_saved[3:]],
        [*mine_turned, *others_turned], token_count, True,
    )
    far_sent = far_low
    far_low, far_high = swap(far_low, ACROSS_X), swap(far_high, ACROSS_Y)
    x_low, x_high, y_low, y_high = back(
        (
            (1, (0, 0), ((0, 0), (1, token_count)), cuts, (early, 0)),
            (2, (0, token_count), ((0, token_count), (1, 2 * token_count)), cuts, (0, early)),
        ),
        after(near, far_sent), other_near, [side_gates], [side_saved, other_saved], matrices,
        token_count,
    )
    travelling = after(travelling, far_sent)
    met = lax.ppermute(travelling, "psg", [(index, index ^ 1) for index in range(passages)])
    near_scores = pack(travelling, met)
    x_low, y_high, near_scores = lax.optimization_barrier((x_low, y_high, near_scores))
    x_low, y_high = swap(x_low, ACROSS_X), swap(y_high, ACROSS_Y)
    x_high, y_low = kernel_call(
        add_kernel,
        "add",
        [kept(x_high.shape, jnp.bfloat16), kept(y_low.shape, jnp.bfloat16)],
        [pinned(x_high), pinned(y_low), far_high, far_low],
    )
    x_high, y_low, near_scores, other_near = lax.optimization_barrier(
        (x_high, y_low, near_scores, other_near)
    )
    x_high, y_low = swap(x_high, ACROSS_X), swap(y_low, ACROSS_Y)
    (own_sums,) = back(
        ((0, (0, 0), ((0, 0), (1, 0)), (0,), (0,)),),
        near, other_near, [own_gates], [own_saved, other_saved],
        [*mine_turned, *others_turned], token_count, True,
    )
    far_scores = lax.ppermute(near_scores, "psg", [(index, index ^ 2) for index in range(passages)])
    loss, factor = kernel_call(
        rank_kernel,
        "rank",
        [shape_of((1, 1), jnp.float32), kept((1, 128), jnp.float32)],
        [pinned(swap_gain), pinned(near_scores), far_scores],
    )
    total, lines = kernel_call(
        first_end_kernel,
        "first_end",
        [
            kept((token_count, model_width), jnp.float32),
            kept((8, token_count), jnp.float32),
        ],
        [pinned(own_sums), after(x_low, factor), y_high],
    )
    (grad,) = kernel_call(
        end_kernel,
        "end",
        [shape_of((token_count, model_width), jnp.bfloat16)],
        [
            pinned(factor), pinned(total), pinned(lines), x_high, y_low, pinned(flat), pinned(gain),
            pinned(turned_gates), pinned(router_rows), pinned(unit_vector),
        ],
        scratch=[
            pltpu.VMEM((token_count, model_width), jnp.float32),
            pltpu.VMEM((token_count, model_width), jnp.bfloat16),
            pltpu.SemaphoreType.DMA((token_count // 32,)),
        ],
        result=pl.ANY,
    )
    return (loss.reshape(1), own_score, grad.reshape(hidden.shape))


def block(*arrays):
    hidden, router, expert_ids, grades = arrays[0], arrays[2], arrays[8], arrays[9]
    each_expert = router.shape[1] == expert_ids.shape[3] == 8
    if hidden.shape[1] == 1 and each_expert and grades.shape[1] == 4:
        return every_expert(*arrays)
    return local(*arrays)


def solution(mesh):
    placed = (
        P("exp", "psg", None, None),
        P(),
        P(),
        P("exp", None, None),
        P("exp", None, None),
        P("exp", None, None),
        P(),
        P(),
        P("exp", "psg", None, None),
        P("exp", None),
        P("exp", None),
    )
    return jax.shard_map(
        block,
        mesh=mesh,
        in_specs=placed,
        out_specs=(P("exp"), P("exp", "psg"), P("exp", "psg", None, None)),
        check_vma=False,
    )
```

```python
import functools
import math

import jax
import jax.numpy as jnp
from jax import lax
from jax.experimental import pallas as pl
from jax.experimental.pallas import tpu as pltpu
from jax.sharding import PartitionSpec as P

epsilon = 1e-06
loss_scale = 256.0
highest = lax.Precision.HIGHEST


def rms_scale(values):
    return lax.rsqrt(jnp.mean(values * values, axis=-1, keepdims=True) + epsilon)


def head_score(pooled, final_gain, score_vector):
    scaled = pooled * rms_scale(pooled) * final_gain
    return jnp.dot(scaled, score_vector.astype(jnp.float32), precision=highest)


def rank_loss(scores, grades, passage_ranks):
    grade_value = grades.astype(jnp.float32)
    worth_gain = jnp.exp2(grade_value)
    discount = 1.0 / jnp.log2(2.0 + passage_ranks.astype(jnp.float32))
    better_than = grades[None, :] > grades[:, None]
    equal_grade = grades[None, :] == grades[:, None]
    position = jnp.arange(grades.shape[0], dtype=jnp.int32)
    earlier = position[None, :] < position[:, None]
    ideal_rank = jnp.sum(
        jnp.logical_or(better_than, jnp.logical_and(equal_grade, earlier)).astype(jnp.float32),
        axis=1,
    )
    ideal_gain = jnp.sum((worth_gain - 1.0) / jnp.log2(2.0 + ideal_rank))
    ordered = (grades[:, None] > grades[None, :]).astype(jnp.float32)
    swap_gain = (
        jnp.abs(
            (worth_gain[:, None] - worth_gain[None, :]) * (discount[:, None] - discount[None, :])
        )
        / ideal_gain
    )
    margin = scores[:, None] - scores[None, :]
    return jnp.sum(ordered * swap_gain * jax.nn.softplus(-margin))


def pick_gates(normed, router, picked_ids):
    expert_total = router.shape[1]
    logits = jnp.dot(normed, router, preferred_element_type=jnp.float32)
    onehot = (
        picked_ids[:, :, None] == jnp.arange(expert_total, dtype=jnp.int32)[None, None, :]
    ).astype(jnp.float32)
    chosen = jnp.einsum("nke,ne->nk", onehot, logits, precision=highest)
    weights = jnp.exp(chosen)
    return (weights / jnp.sum(weights, axis=1, keepdims=True), onehot)


def gate_parts(pre_gate):
    sigmoid_gate = jax.nn.sigmoid(pre_gate)
    return (pre_gate * sigmoid_gate, sigmoid_gate * (1.0 + pre_gate * (1.0 - sigmoid_gate)))


def norm_back(flat_rows, inverse, norm_gain, d_normed):
    scaled = d_normed * norm_gain
    return inverse * scaled - flat_rows * inverse * inverse * inverse * jnp.mean(
        flat_rows * scaled, axis=-1, keepdims=True
    )


def unpack_front(front_out, buffer_rows):
    pre_gate, pre_up, received = front_out
    hidden_units = pre_gate.shape[2]
    pre_gate = pre_gate.reshape(buffer_rows, hidden_units)
    pre_up = pre_up.reshape(buffer_rows, hidden_units)
    silu_gate, slope = gate_parts(pre_gate)
    activation = (silu_gate * pre_up).astype(jnp.bfloat16)
    return (pre_up, received, silu_gate, slope, activation)


def local(
    hidden,
    norm_gain,
    router,
    gate_proj,
    up_proj,
    down_proj,
    final_gain,
    score_vector,
    expert_ids,
    grades,
    passage_ranks,
):
    unused_query, local_passages, local_positions, model_width = hidden.shape
    top_count = expert_ids.shape[3]
    expert_count = lax.axis_size("exp")
    token_count = local_passages * local_positions
    slot_count = token_count * top_count
    capacity = min(token_count, 9 * token_count * top_count // (8 * expert_count))
    buffer_rows = expert_count * capacity
    flat_rows = hidden.reshape(token_count, model_width).astype(jnp.float32)
    inverse = rms_scale(flat_rows)
    normed = (flat_rows * inverse * norm_gain).astype(jnp.bfloat16)
    picked_ids = expert_ids.reshape(token_count, top_count)
    gate_values, onehot = pick_gates(normed, router, picked_ids)
    slot_hits = onehot.reshape(slot_count, expert_count).astype(jnp.int32)
    slot_rank = jnp.sum((jnp.cumsum(slot_hits, axis=0) - slot_hits) * slot_hits, axis=1)
    target = picked_ids.reshape(slot_count) * capacity + slot_rank
    source_token = jnp.arange(slot_count, dtype=jnp.int32) // top_count
    passage_onehot = (
        source_token[:, None] // local_positions
        == jnp.arange(local_passages, dtype=jnp.int32)[None, :]
    ).astype(jnp.float32)
    weighted = (passage_onehot * gate_values.reshape(slot_count, 1)).astype(jnp.bfloat16)
    send_rows = (
        jnp.zeros((buffer_rows, model_width), jnp.bfloat16).at[target].set(normed[source_token])
    )
    send_weights = jnp.zeros((buffer_rows, local_passages), jnp.bfloat16).at[target].set(weighted)
    outgoing = (
        send_rows.reshape(expert_count, capacity, model_width),
        send_weights.reshape(expert_count, capacity, local_passages),
    )
    gate_matrix = gate_proj[0]
    up_matrix = up_proj[0]
    down_matrix = down_proj[0]
    rows_in = lax.all_to_all(outgoing[0], "exp", split_axis=0, concat_axis=0, tiled=True)
    weights_in = lax.all_to_all(outgoing[1], "exp", split_axis=0, concat_axis=0, tiled=True)
    pre_gate = jnp.einsum("end,df->enf", rows_in, gate_matrix, preferred_element_type=jnp.float32)
    pre_up = jnp.einsum("end,df->enf", rows_in, up_matrix, preferred_element_type=jnp.float32)
    front_out = (pre_gate, pre_up, weights_in)
    pre_up, received, silu_gate, slope, activation = unpack_front(front_out, buffer_rows)
    hidden_units = activation.shape[1]
    passage_part = jnp.einsum(
        "scp,scf->spf",
        received,
        activation.reshape(expert_count, capacity, hidden_units),
        preferred_element_type=jnp.float32,
    )
    down_wide = down_matrix.astype(jnp.float32)
    expert_terms = jnp.einsum("spf,fd->spd", passage_part, down_wide, precision=highest)
    came_back = lax.all_to_all(expert_terms, "exp", split_axis=0, concat_axis=0, tiled=True)
    token_sums = jnp.sum(flat_rows.reshape(local_passages, local_positions, model_width), axis=1)
    pooled = (token_sums + jnp.sum(came_back, axis=0)) / local_positions
    first_row = lax.axis_index("psg") * local_passages
    own_score = head_score(pooled, final_gain, score_vector)
    every_score = lax.all_gather(own_score, "psg", axis=0, tiled=True)
    loss_value, loss_grad = jax.value_and_grad(rank_loss)(every_score, grades[0], passage_ranks[0])
    d_own = lax.dynamic_slice_in_dim(loss_grad, first_row, local_passages, 0) * loss_scale
    unused_score, head_back = jax.vjp(
        lambda values: head_score(values, final_gain, score_vector), pooled
    )
    d_vector = head_back(d_own)[0] / local_positions
    every_vector = lax.all_gather(d_vector[None], "exp", axis=0, tiled=True)
    near_table = jnp.einsum("spd,fd->spf", every_vector, down_wide, precision=highest)
    present = (received != 0).astype(jnp.float32)
    near_rows = jnp.einsum("scp,spf->scf", present, near_table, precision=highest).reshape(
        buffer_rows, hidden_units
    )
    gate_weight = jnp.sum(received.astype(jnp.float32), axis=2).reshape(buffer_rows, 1)
    d_act = gate_weight * near_rows
    d_gate = (d_act * pre_up * slope).astype(jnp.bfloat16)
    d_up = (d_act * silu_gate).astype(jnp.bfloat16)
    contract = (((1,), (1,)), ((), ()))
    pick_grad = lax.dot_general(d_gate, gate_matrix, contract, preferred_element_type=jnp.float32)
    pick_grad = (
        pick_grad + lax.dot_general(d_up, up_matrix, contract, preferred_element_type=jnp.float32)
    ).astype(jnp.bfloat16)
    gate_grad = jnp.sum(activation.astype(jnp.float32) * near_rows, axis=1).astype(jnp.bfloat16)
    back_rows, back_gate = (
        lax.all_to_all(
            pick_grad.reshape(expert_count, capacity, model_width),
            "exp",
            split_axis=0,
            concat_axis=0,
            tiled=True,
        ),
        lax.all_to_all(
            gate_grad.reshape(expert_count, capacity),
            "exp",
            split_axis=0,
            concat_axis=0,
            tiled=True,
        ),
    )
    picked_rows = back_rows.reshape(buffer_rows, model_width)[target]
    d_normed = jnp.sum(
        picked_rows.reshape(token_count, top_count, model_width).astype(jnp.float32), axis=1
    )
    picked_gate = (
        back_gate.reshape(buffer_rows)[target].astype(jnp.float32).reshape(token_count, top_count)
    )
    d_logit = gate_values * (
        picked_gate - jnp.sum(gate_values * picked_gate, axis=1, keepdims=True)
    )
    dense_logit = jnp.einsum("nk,nke->ne", d_logit, onehot, precision=highest)
    d_normed = d_normed + jnp.einsum(
        "ne,de->nd", dense_logit, router.astype(jnp.float32), precision=highest
    )
    grad_flat = norm_back(flat_rows, inverse, norm_gain, d_normed)
    grad_hidden = (
        grad_flat.reshape(1, local_passages, local_positions, model_width)
        + d_vector[None, :, None, :]
    )
    return (
        loss_value.reshape(1),
        own_score.reshape(1, local_passages),
        grad_hidden.astype(jnp.bfloat16),
    )


CORE, ACROSS_X, ACROSS_Y = 1, 2, 4
forward = (((1,), (0,)), ((), ()))
across = (((1,), (1,)), ((), ()))
MIB = 1 << 20


def swap(value, bit, size=8):
    return lax.ppermute(value, "exp", [(index, index ^ bit) for index in range(size)])


def shape_of(shape, dtype):
    return jax.ShapeDtypeStruct(shape, dtype)


def after(value, *others):
    return lax.optimization_barrier((value, *others))[0]


def kept(shape, dtype):
    return pltpu.VMEM(shape, dtype)


def pinned(array):
    return pltpu.with_memory_space_constraint(array, pltpu.VMEM)


def kernel_call(body, name, outs, ins, far=(), scratch=(), work=1, result=pltpu.VMEM):
    spaces = [pltpu.VMEM] * len(ins)
    ins = list(ins)
    for index in far:
        spaces[index] = pl.ANY
        ins[index] = pltpu.with_memory_space_constraint(ins[index], pltpu.HBM)
    return pl.pallas_call(
        body,
        name=name,
        out_shape=outs,
        in_specs=[pl.BlockSpec(memory_space=space) for space in spaces],
        out_specs=[pl.BlockSpec(memory_space=result)] * len(outs),
        scratch_shapes=scratch,
        compiler_params=pltpu.CompilerParams(vmem_limit_bytes=8 * MIB),
        cost_estimate=pl.CostEstimate(flops=work, bytes_accessed=1, transcendentals=0),
    )(*ins)


def split_low(values):
    high = values.astype(jnp.bfloat16)
    rest = values - high.astype(jnp.float32)
    middle = rest.astype(jnp.bfloat16)
    low = (rest - middle.astype(jnp.float32)).astype(jnp.bfloat16)
    return high, middle, low


def exact_dot(values, low_matrix, contract):
    parts = lax.dot_general(
        jnp.concatenate(split_low(values), axis=0),
        low_matrix,
        contract,
        preferred_element_type=jnp.float32,
    )
    return parts[0:8] + parts[8:16] + parts[16:24]


def other_order(values, bits):
    return jnp.concatenate([values[row ^ bits : (row ^ bits) + 1] for row in range(4)], axis=0)


def norm_kernel(
    hidden_far, gain_far, router_far, final_far, vector_far,
    hidden_ref, gain_ref, router_ref, normed_ref, sums_ref, head_ref,
    final_ref, vector_ref, copy_sems,
):
    pairs = (
        (hidden_far, hidden_ref), (gain_far, gain_ref), (router_far, router_ref),
        (final_far, final_ref), (vector_far, vector_ref),
    )
    copies = [
        pltpu.make_async_copy(source, target, copy_sems.at[index])
        for index, (source, target) in enumerate(pairs)
    ]
    for copy in copies:
        copy.start()
    for copy in copies:
        copy.wait()
    vector = vector_ref[...].astype(jnp.float32)
    vector = jnp.concatenate([vector[row : row + 1] for row in range(vector.shape[0])], axis=1)
    head_ref[...] = final_ref[...] * vector
    rows = hidden_ref[...].astype(jnp.float32)
    normed_ref[...] = (rows * rms_scale(rows) * gain_ref[...]).astype(jnp.bfloat16)
    sums_ref[...] = jnp.sum(rows, axis=0, keepdims=True)


def front_kernel(stage, owners, sets, count, router_ref, *refs):
    matrices, refs = refs[: 2 * len(sets)], refs[2 * len(sets) :]
    pieces, refs = refs[:count], refs[count:]
    matrices = list(matrices)
    hidden_units = matrices[0].shape[1]
    tile = 256
    firsts = range(0, hidden_units, tile)
    if stage == 0:
        far_matrices = matrices
        *refs, gate_held, up_held, rows_ref, copy_sems = refs
        matrices = [gate_held, up_held]
        copies = [
            pltpu.make_async_copy(
                source.at[:, first : first + tile],
                target.at[:, first : first + tile],
                copy_sems.at[which, number],
            )
            for number, first in enumerate(firsts)
            for which, (source, target) in enumerate(zip(far_matrices, matrices))
        ]
        for copy in copies:
            copy.start()
        turned_ref, *refs = refs
    elif stage == 1:
        down_far, *refs, down_ref, rows_ref, copy_sem = refs
        down_copy = pltpu.make_async_copy(down_far, down_ref, copy_sem)
        down_copy.start()
    elif stage == 3:
        sums_ref, *downs = refs[:3]
        earlier, refs = refs[3:6], refs[6:]
        *refs, terms_ref, rows_ref = refs
    else:
        *refs, rows_ref = refs
    gates_ref, *outs = refs
    expert = lax.axis_index("exp")
    first = 0
    for piece in pieces:
        rows_ref[first : first + piece.shape[0], :] = piece[...]
        first += piece.shape[0]
    size = first // len(owners)
    logits = lax.dot_general(
        rows_ref[...], router_ref[...], across, preferred_element_type=jnp.float32
    )
    weights = jnp.exp(logits)
    gates = weights / jnp.sum(weights, axis=1, keepdims=True)
    gates_ref[...] = gates
    lane = lax.broadcasted_iota(jnp.int32, gates.shape, 1)
    if stage == 0:
        weights = jnp.exp(
            lax.dot_general(
                router_ref[...], rows_ref[...], across, preferred_element_type=jnp.float32
            )
        )
        turned_ref[...] = weights / jnp.sum(weights, axis=0, keepdims=True)

    totals = []
    for place, which in enumerate(sets):
        gate_ref, up_ref = matrices[2 * place : 2 * place + 2]
        if stage == 3:
            slope_ref, silu_ref, act_ref = outs[3 * place : 3 * place + 3]
        else:
            slope_ref, silu_ref, act_ref, part_ref = outs
        own = jnp.sum(jnp.where(lane == expert ^ which, gates, 0.0), axis=1, keepdims=True)
        low = own.astype(jnp.bfloat16).astype(jnp.float32)
        parts = []
        for number, first in enumerate(firsts):
            columns = slice(first, first + tile)
            if stage == 0:
                copies[2 * number].wait()
                copies[2 * number + 1].wait()
            rows = rows_ref[...]
            pre_gate = jnp.dot(rows, gate_ref[:, columns], preferred_element_type=jnp.float32)
            pre_up = jnp.dot(rows, up_ref[:, columns], preferred_element_type=jnp.float32)
            silu_gate, slope = gate_parts(pre_gate)
            activation = (silu_gate * pre_up).astype(jnp.bfloat16)
            slope_ref[:, columns] = slope * pre_up
            silu_ref[:, columns] = silu_gate
            act_ref[:, columns] = activation
            weighted = activation.astype(jnp.float32) * low
            found = {
                owner: jnp.sum(weighted[index * size : (index + 1) * size], axis=0, keepdims=True)
                for index, owner in enumerate(owners)
            }
            nothing = jnp.zeros_like(weighted[:1])
            parts.append(
                jnp.concatenate([found.get(owner, nothing) for owner in range(8)], axis=0)
            )
        totals.append(jnp.concatenate(parts, axis=1))
    if stage == 1:
        down_copy.wait()
    if stage < 3:
        part_ref[...] = totals[0]
        return
    own_first, own_second, other_first = earlier
    totals[0] = totals[0] + (own_first[...] + own_second[...])
    totals[1] = totals[1] + other_first[...]
    terms = exact_dot(totals[0], downs[0][...], forward) + exact_dot(
        totals[1], downs[1][...], forward
    )
    row = lax.broadcasted_iota(jnp.int32, terms.shape, 0)
    terms_ref[...] = (terms + jnp.where(row == 0, sums_ref[...], 0.0))[:4]


def front(stage, owners, sets, pieces, router_rows, matrices, more=()):
    model_width, hidden_units = matrices[0].shape
    row_total = sum(piece.shape[0] for piece in pieces)
    outs = [kept((row_total, 8), jnp.float32)]
    if stage == 0:
        outs.insert(0, kept((8, row_total), jnp.float32))
    for which in sets:
        outs += [
            kept((row_total, hidden_units), jnp.float32),
            kept((row_total, hidden_units), jnp.float32),
            kept((row_total, hidden_units), jnp.bfloat16),
        ]
    outs.append(
        kept((4, model_width), jnp.float32) if stage == 3 else kept((8, hidden_units), jnp.float32)
    )
    scratch = [pltpu.VMEM((row_total, model_width), jnp.bfloat16)]
    far = ()
    if stage == 0:
        far = (1, 2)
        outs += [kept(matrix.shape, jnp.bfloat16) for matrix in matrices]
        scratch.append(pltpu.SemaphoreType.DMA((2, hidden_units // 256)))
    else:
        matrices = [pinned(matrix) for matrix in matrices]
    if stage == 1:
        far = (3 + len(pieces),)
        outs.append(kept(more[0].shape, jnp.bfloat16))
        scratch.append(pltpu.SemaphoreType.DMA)
    if stage == 3:
        more = [pinned(array) for array in more]
    return kernel_call(
        functools.partial(front_kernel, stage, owners, sets, len(pieces)),
        "front",
        outs,
        [pinned(router_rows), *matrices, *(pinned(piece) for piece in pieces), *more],
        far,
        scratch,
    )


def near_kernel(
    own_ref, x_ref, y_ref, far_ref, head_ref, down_ref, other_down_ref,
    near_ref, other_near_ref, unit_ref, score_ref, own_score_ref, *, token_count,
):
    pooled = (
        (own_ref[...] + other_order(x_ref[...], 1))
        + (other_order(y_ref[...], 2) + other_order(far_ref[...], 3))
    ) / token_count
    pooled = jnp.concatenate([pooled, jnp.zeros_like(pooled)], axis=0)
    head = head_ref[...]
    scale = rms_scale(pooled)
    along = jnp.sum(pooled * head, axis=1, keepdims=True)
    own_score = (scale * along)[:1]
    own_score_ref[...] = own_score
    score_ref[...] = jnp.broadcast_to(own_score, score_ref.shape)
    unit = (
        scale * head - scale * scale * scale * (along / pooled.shape[1]) * pooled
    ) / token_count
    unit_ref[...] = unit[:1]
    parts = jnp.concatenate(split_low(unit), axis=0)
    parts = jnp.concatenate([parts, jnp.zeros((104, parts.shape[1]), jnp.bfloat16)], axis=0)
    for table_ref, matrix_ref in ((near_ref, down_ref), (other_near_ref, other_down_ref)):
        turned = lax.dot_general(
            matrix_ref[...], parts, across, preferred_element_type=jnp.float32
        ).T
        table_ref[...] = turned[0:8] + turned[8:16] + turned[16:24]


def back_kernel(passages, turned, gate_count, saved_count, near_ref, other_near_ref, *refs):
    gates_refs, refs = refs[:gate_count], refs[gate_count:]
    saved, refs = refs[: 3 * saved_count], refs[3 * saved_count :]
    matrices, refs = refs[:4], refs[4:]
    *out_refs, d_gate_ref, d_up_ref, other_d_gate_ref, other_d_up_ref = refs
    expert = lax.axis_index("exp")
    size = out_refs[0].shape[1]
    model_width = matrices[0].shape[1 if turned else 0]
    lane = lax.broadcasted_iota(jnp.int32, (size, 8), 1)
    line = lax.broadcasted_iota(jnp.int32, (16, size), 0)
    experts = (
        (near_ref, d_gate_ref, d_up_ref), (other_near_ref, other_d_gate_ref, other_d_up_ref)
    )
    outs = []
    for index, (owner, gates_place, saved_places, cuts, unused) in enumerate(passages):
        outs.append(out_refs[: len(cuts)])
        out_refs = out_refs[len(cuts) :]
        rows = slice(index * size, (index + 1) * size)
        lines = jnp.zeros((16, size), jnp.float32)
        gates = gates_refs[gates_place[0]][gates_place[1] : gates_place[1] + size, :]
        for which, (table_ref, d_gate_out, d_up_out) in enumerate(experts):
            number, first = saved_places[which]
            slope_ref, silu_ref, act_ref = saved[3 * number : 3 * number + 3]
            held = slice(first, first + size)
            near = table_ref[owner : owner + 1, :]
            own = jnp.sum(
                jnp.where(lane == expert ^ which, gates, 0.0), axis=1, keepdims=True
            )
            d_act = own.astype(jnp.bfloat16).astype(jnp.float32) * near
            d_gate_out[rows, :] = (d_act * slope_ref[held, :]).astype(jnp.bfloat16)
            d_up_out[rows, :] = (d_act * silu_ref[held, :]).astype(jnp.bfloat16)
            gate_grad = exact_dot(table_ref[...], act_ref[held, :], across)[owner : owner + 1]
            lines = jnp.where(line == expert ^ which, gate_grad, lines)
        bounds = cuts + (model_width + 16,)
        for out_ref, cut, end in zip(outs[-1], bounds, bounds[1:]):
            if out_ref.shape[0] > end - cut:
                rest = out_ref.shape[0] - (end - cut)
                out_ref[end - cut :, :] = jnp.zeros((rest, size), jnp.bfloat16)
        outs[-1][-1][model_width - cuts[-1] : model_width + 16 - cuts[-1], :] = lines.astype(
            jnp.bfloat16
        )

    sides = (d_gate_ref, d_up_ref, other_d_gate_ref, other_d_up_ref)
    for first in range(0, model_width, 256):
        pick_grad = None
        for side_ref, matrix in zip(sides, matrices):
            if turned:
                term = jnp.dot(
                    side_ref[...],
                    matrix[:, first : first + 256],
                    preferred_element_type=jnp.float32,
                )
            else:
                term = lax.dot_general(
                    matrix[first : first + 256, :],
                    side_ref[...],
                    across,
                    preferred_element_type=jnp.float32,
                )
            pick_grad = term if pick_grad is None else pick_grad + term
        if turned:
            pick_grad = pick_grad.T
        pick_grad = pick_grad.astype(jnp.bfloat16)
        for index, passage in enumerate(passages):
            cuts = passage[3]
            place = max(number for number, cut in enumerate(cuts) if cut <= first)
            rows = slice(first - cuts[place], first - cuts[place] + 256)
            outs[index][place][rows, :] = pick_grad[:, index * size : (index + 1) * size]


def back(passages, near, other_near, gates, saved, matrices, size, turned=False):
    model_width, hidden_units = matrices[0].shape[:: -1 if turned else 1]
    heights = []
    for passage in passages:
        cuts, least = passage[3:]
        ends = cuts[1:] + (model_width + 16,)
        heights += [max(low, end - cut) for low, cut, end in zip(least, cuts, ends)]
    arrays = [array for group in saved for array in group]
    return kernel_call(
        functools.partial(back_kernel, passages, turned, len(gates), len(saved)),
        "back",
        [kept((height, size), jnp.bfloat16) for height in heights],
        [pinned(array) for array in (near, other_near, *gates, *arrays, *matrices)],
        (),
        [pltpu.VMEM((len(passages) * size, hidden_units), jnp.bfloat16)] * 4,
    )


def add_kernel(x_ref, y_ref, high_ref, low_ref, x_out, y_out):
    for own_ref, other_ref, out_ref in ((x_ref, high_ref, x_out), (y_ref, low_ref, y_out)):
        out_ref[...] = (
            own_ref[...].astype(jnp.float32)
            + other_ref[: own_ref.shape[0], :].astype(jnp.float32)
        ).astype(jnp.bfloat16)


def turn_kernel(gate_ref, up_ref, turned_gate_ref, turned_up_ref):
    for first in range(0, gate_ref.shape[0], 256):
        rows = slice(first, first + 256)
        turned_gate_ref[:, rows] = gate_ref[rows, :].T
        turned_up_ref[:, rows] = up_ref[rows, :].T


def half_kernel(part, rows_ref, out_ref):
    half = out_ref.shape[0]
    out_ref[...] = rows_ref[part * half : (part + 1) * half, :]


def half_of(rows, part):
    total, wide = rows.shape
    (out,) = kernel_call(
        functools.partial(half_kernel, part), "half", [kept((total // 2, wide), rows.dtype)], [rows]
    )
    return out


def pack_kernel(first_ref, second_ref, out_ref):
    rows = first_ref.shape[0]
    out_ref[:rows, :] = first_ref[...]
    out_ref[rows:, :] = second_ref[...]


def pack(first, second, work=1):
    rows, wide = first.shape
    return kernel_call(
        pack_kernel, "pack", [kept((2 * rows, wide), first.dtype)], [first, second], work=work
    )[0]


def pairs_of(passages):
    row = lax.broadcasted_iota(jnp.int32, (8, 128), 0)
    lane = lax.broadcasted_iota(jnp.int32, (8, 128), 1)
    return row, lane, jnp.logical_and(row < passages, lane < passages)


def spread(index, values):
    total = jnp.zeros((8, 128), jnp.float32)
    for number, value in values:
        total = jnp.where(index == number, value, total)
    return total


def whole_sum(values):
    return jnp.sum(jnp.sum(values, axis=1, keepdims=True), axis=0, keepdims=True)


def pair_kernel(grades_far, ranks_far, swap_gain_ref, grades_ref, ranks_ref, copy_sems):
    copies = [
        pltpu.make_async_copy(grades_far, grades_ref, copy_sems.at[0]),
        pltpu.make_async_copy(ranks_far, ranks_ref, copy_sems.at[1]),
    ]
    for copy in copies:
        copy.start()
    for copy in copies:
        copy.wait()
    passages = grades_ref.shape[1]
    row, lane, pair = pairs_of(passages)
    grade_list = [(number, grades_ref[0, number].astype(jnp.float32)) for number in range(passages)]
    rank_list = [(number, ranks_ref[0, number].astype(jnp.float32)) for number in range(passages)]
    grade_row, grade_lane = spread(row, grade_list), spread(lane, grade_list)
    worth_row, worth_lane = jnp.exp2(grade_row), jnp.exp2(grade_lane)
    discount_row = 1.0 / jnp.log2(2.0 + spread(row, rank_list))
    discount_lane = 1.0 / jnp.log2(2.0 + spread(lane, rank_list))
    ahead = jnp.logical_or(
        grade_lane > grade_row, jnp.logical_and(grade_lane == grade_row, lane < row)
    )
    ideal_rank = jnp.sum(
        jnp.where(jnp.logical_and(pair, ahead), 1.0, 0.0), axis=1, keepdims=True
    )
    ideal_terms = (worth_row - 1.0) / jnp.log2(2.0 + ideal_rank)
    one_lane = jnp.logical_and(pair, lane == 0)
    ideal_gain = whole_sum(jnp.where(one_lane, ideal_terms, 0.0))
    swap_gain = (
        jnp.abs((worth_row - worth_lane) * (discount_row - discount_lane)) / ideal_gain
    )
    swap_gain_ref[...] = jnp.where(
        jnp.logical_and(pair, grade_row > grade_lane), swap_gain, 0.0
    )


def rank_kernel(swap_gain_ref, near_scores_ref, far_scores_ref, loss_ref, factor_ref):
    passages = 2 * near_scores_ref.shape[0]
    place = lax.axis_index("psg")
    row, lane, unused = pairs_of(passages)
    score_list = [
        (place ^ (base + number), jnp.broadcast_to(ref[number : number + 1, :], (8, 128)))
        for base, ref in ((0, near_scores_ref), (passages // 2, far_scores_ref))
        for number in range(passages // 2)
    ]
    swap_gain = swap_gain_ref[...]
    margin = spread(row, score_list) - spread(lane, score_list)
    softplus = jnp.maximum(-margin, 0.0) + jnp.log1p(jnp.exp(-jnp.abs(margin)))
    loss_ref[...] = whole_sum(swap_gain * softplus)
    pull = swap_gain * jax.nn.sigmoid(-margin)
    gradient = whole_sum(jnp.where(lane == place, pull, 0.0) - jnp.where(row == place, pull, 0.0))
    factor_ref[...] = jnp.broadcast_to(gradient * loss_scale, factor_ref.shape)


def first_end_kernel(own_ref, x_low_ref, y_high_ref, total_ref, lines_ref):
    model_width = total_ref.shape[1]
    cut = model_width // 2
    for first in range(0, model_width, 256):
        rows = slice(first, first + 256)
        if first < cut:
            term = x_low_ref[rows, :]
        else:
            term = y_high_ref[first - cut : first - cut + 256, :]
        total = own_ref[rows, :].astype(jnp.float32) + term.astype(jnp.float32)
        total_ref[:, rows] = total.T
    end = slice(model_width, model_width + 8)
    end_high = slice(model_width - cut, model_width - cut + 8)
    lines_ref[...] = own_ref[end, :].astype(jnp.float32) + y_high_ref[end_high, :].astype(
        jnp.float32
    )


def end_kernel(
    factor_ref, total_ref, lines_ref, x_high_ref, y_low_ref,
    hidden_ref, gain_ref, gates_ref, router_ref, unit_ref,
    grad_far, turned_ref, grad_ref, copy_sems,
):
    token_count, model_width = hidden_ref.shape
    cut = y_low_ref.shape[0]
    end_high = slice(model_width - cut, model_width - cut + 8)
    slot_grad = lines_ref[...] + x_high_ref[end_high, :].astype(jnp.float32)
    gates = gates_ref[...]
    d_logit = gates * (slot_grad - jnp.sum(gates * slot_grad, axis=0, keepdims=True))
    d_logit = jnp.concatenate([d_logit, jnp.zeros((120, token_count), jnp.float32)], axis=0).T
    d_logit = jnp.concatenate(split_low(d_logit[:, :8]), axis=1)
    router_rows = jnp.concatenate([router_ref[...]] * 3, axis=0)
    for first in range(0, model_width, 256):
        columns = slice(first, first + 256)
        if first < cut:
            term = y_low_ref[columns, :]
        else:
            term = x_high_ref[first - cut : first - cut + 256, :]
        turned_ref[:, columns] = (
            total_ref[:, columns]
            + term.astype(jnp.float32).T
            + jnp.dot(d_logit, router_rows[:, columns], preferred_element_type=jnp.float32)
        )
    gain = gain_ref[...]
    factor = factor_ref[:, :1]
    size = 32
    copies = []
    for first in range(0, token_count, size):
        rows = slice(first, first + size)
        flat_rows = hidden_ref[rows, :].astype(jnp.float32)
        grad = norm_back(flat_rows, rms_scale(flat_rows), gain, turned_ref[rows, :])
        grad_ref[rows, :] = ((grad + unit_ref[...]) * factor).astype(jnp.bfloat16)
        copies.append(
            pltpu.make_async_copy(
                grad_ref.at[rows, :], grad_far.at[rows, :], copy_sems.at[first // size]
            )
        )
        copies[-1].start()
    for copy in copies:
        copy.wait()


def every_expert(
    hidden,
    norm_gain,
    router,
    gate_proj,
    up_proj,
    down_proj,
    final_gain,
    score_vector,
    expert_ids,
    grades,
    passage_ranks,
):
    unused_query, unused_passage, token_count, model_width = hidden.shape
    passages = grades.shape[1]
    flat = hidden.reshape(token_count, model_width)
    gate_matrix, up_matrix, down_matrix = gate_proj[0], up_proj[0], down_proj[0]
    mine = [gate_matrix, up_matrix, down_matrix]
    flat, gain, router_rows, normed, token_sums, head = kernel_call(
        norm_kernel,
        "norm",
        [
            kept(flat.shape, jnp.bfloat16),
            kept((1, model_width), jnp.float32),
            kept((8, model_width), jnp.bfloat16),
            kept(flat.shape, jnp.bfloat16),
            kept((1, model_width), jnp.float32),
            kept((1, model_width), jnp.float32),
        ],
        [
            flat,
            norm_gain.reshape(1, model_width),
            router.T,
            final_gain.reshape(1, model_width),
            score_vector.reshape(model_width // 128, 128),
        ],
        range(5),
        [
            pltpu.VMEM((1, model_width), jnp.float32),
            pltpu.VMEM((model_width // 128, 128), jnp.bfloat16),
            pltpu.SemaphoreType.DMA((5,)),
        ],
    )
    others = [swap(matrix, CORE) for matrix in mine]
    x_rows, y_rows = swap(normed, ACROSS_X), swap(normed, ACROSS_Y)
    turned_gates, own_gates, *own_saved, own_part, mine[0], mine[1] = front(
        0, (0,), (0,), [normed], router_rows, mine[:2]
    )
    (swap_gain,) = kernel_call(
        pair_kernel,
        "pairs",
        [kept((8, 128), jnp.float32)],
        [grades, after(passage_ranks, own_part)],
        (0, 1),
        [
            pltpu.SMEM(grades.shape, jnp.int32),
            pltpu.SMEM(grades.shape, jnp.int32),
            pltpu.SemaphoreType.DMA((2,)),
        ],
    )
    mine_turned = kernel_call(
        turn_kernel,
        "turn",
        [kept(mine[0].shape[::-1], jnp.bfloat16)] * 2,
        [pinned(after(mine[0], swap_gain)), pinned(mine[1])],
    )
    x_rows, y_rows = after(x_rows, mine_turned[0]), after(y_rows, mine_turned[0])
    far_low = swap(half_of(x_rows, 0), ACROSS_Y)
    far_high = swap(half_of(y_rows, 1), ACROSS_X)
    side_gates, *side_saved, side_part, mine[2] = front(
        1, (1, 2), (0,), [x_rows, y_rows], router_rows, mine[:2], mine[2:]
    )
    others[0] = after(others[0], side_part)
    unused, *other_saved, other_part = front(
        2, (0, 1, 2), (1,), [normed, x_rows, y_rows], router_rows, others[:2]
    )
    far_low, far_high = after(far_low, other_part), after(far_high, other_part)
    far_gates, *far_saved, terms = front(
        3, (3,), (0, 1), [far_low, far_high], router_rows, mine[:2] + others[:2],
        (token_sums, mine[2], others[2], own_part, side_part, other_part),
    )

    others_turned = kernel_call(
        turn_kernel,
        "turn",
        [kept(others[0].shape[::-1], jnp.bfloat16)] * 2,
        [pinned(after(others[0], terms)), pinned(others[1])],
    )
    head = after(head, others_turned[0])
    near, other_near, unit_vector, travelling, own_score = kernel_call(
        functools.partial(near_kernel, token_count=token_count),
        "near",
        [
            kept((8, down_matrix.shape[0]), jnp.float32),
            kept((8, down_matrix.shape[0]), jnp.float32),
            kept((1, model_width), jnp.float32),
            kept((1, 128), jnp.float32),
            shape_of((1, 1), jnp.float32),
        ],
        [
            pinned(terms),
            swap(terms, ACROSS_X),
            swap(terms, ACROSS_Y),
            swap(terms, ACROSS_X | ACROSS_Y),
            pinned(head),
            pinned(mine[2]),
            pinned(others[2]),
        ],
    )
    matrices = mine[:2] + others[:2]
    cuts, early, earlier = (0, model_width // 2), model_width // 2 + 32, model_width // 2 + 64
    far_low, far_high = back(
        ((3, (0, 0), ((0, 0), (1, 0)), cuts, (earlier, earlier)),),
        near, other_near, [far_gates], [far_saved[:3], far_saved[3:]],
        [*mine_turned, *others_turned], token_count, True,
    )
    far_sent = far_low
    far_low, far_high = swap(far_low, ACROSS_X), swap(far_high, ACROSS_Y)
    x_low, x_high, y_low, y_high = back(
        (
            (1, (0, 0), ((0, 0), (1, token_count)), cuts, (early, 0)),
            (2, (0, token_count), ((0, token_count), (1, 2 * token_count)), cuts, (0, early)),
        ),
        after(near, far_sent), other_near, [side_gates], [side_saved, other_saved], matrices,
        token_count,
    )
    travelling = after(travelling, far_sent)
    met = lax.ppermute(travelling, "psg", [(index, index ^ 1) for index in range(passages)])
    near_scores = pack(travelling, met)
    x_low, y_high, near_scores = lax.optimization_barrier((x_low, y_high, near_scores))
    x_low, y_high = swap(x_low, ACROSS_X), swap(y_high, ACROSS_Y)
    x_high, y_low = kernel_call(
        add_kernel,
        "add",
        [kept(x_high.shape, jnp.bfloat16), kept(y_low.shape, jnp.bfloat16)],
        [pinned(x_high), pinned(y_low), far_high, far_low],
    )
    x_high, y_low, near_scores, other_near = lax.optimization_barrier(
        (x_high, y_low, near_scores, other_near)
    )
    x_high, y_low = swap(x_high, ACROSS_X), swap(y_low, ACROSS_Y)
    (own_sums,) = back(
        ((0, (0, 0), ((0, 0), (1, 0)), (0,), (0,)),),
        near, other_near, [own_gates], [own_saved, other_saved],
        [*mine_turned, *others_turned], token_count, True,
    )
    far_scores = lax.ppermute(near_scores, "psg", [(index, index ^ 2) for index in range(passages)])
    loss, factor = kernel_call(
        rank_kernel,
        "rank",
        [shape_of((1, 1), jnp.float32), kept((1, 128), jnp.float32)],
        [pinned(swap_gain), pinned(near_scores), far_scores],
    )
    total, lines = kernel_call(
        first_end_kernel,
        "first_end",
        [
            kept((token_count, model_width), jnp.float32),
            kept((8, token_count), jnp.float32),
        ],
        [pinned(own_sums), after(x_low, factor), y_high],
    )
    (grad,) = kernel_call(
        end_kernel,
        "end",
        [shape_of((token_count, model_width), jnp.bfloat16)],
        [
            pinned(factor), pinned(total), pinned(lines), x_high, y_low, pinned(flat), pinned(gain),
            pinned(turned_gates), pinned(router_rows), pinned(unit_vector),
        ],
        scratch=[
            pltpu.VMEM((token_count, model_width), jnp.float32),
            pltpu.VMEM((token_count, model_width), jnp.bfloat16),
            pltpu.SemaphoreType.DMA((token_count // 32,)),
        ],
        result=pl.ANY,
    )
    return (loss.reshape(1), own_score, grad.reshape(hidden.shape))


def block(*arrays):
    hidden, router, expert_ids, grades = arrays[0], arrays[2], arrays[8], arrays[9]
    each_expert = router.shape[1] == expert_ids.shape[3] == 8
    if hidden.shape[1] == 1 and each_expert and grades.shape[1] == 4:
        return every_expert(*arrays)
    return local(*arrays)


def solution(mesh):
    placed = (
        P("exp", "psg", None, None),
        P(),
        P(),
        P("exp", None, None),
        P("exp", None, None),
        P("exp", None, None),
        P(),
        P(),
        P("exp", "psg", None, None),
        P("exp", None),
        P("exp", None),
    )
    return jax.shard_map(
        block,
        mesh=mesh,
        in_specs=placed,
        out_specs=(P("exp"), P("exp", "psg"), P("exp", "psg", None, None)),
        check_vma=False,
    )
```

```python
import functools
import math

import jax
import jax.numpy as jnp
from jax import lax
from jax.experimental import pallas as pl
from jax.experimental.pallas import tpu as pltpu
from jax.sharding import PartitionSpec as P

epsilon = 1e-06
loss_scale = 256.0
highest = lax.Precision.HIGHEST


def rms_scale(values):
    return lax.rsqrt(jnp.mean(values * values, axis=-1, keepdims=True) + epsilon)


def head_score(pooled, final_gain, score_vector):
    scaled = pooled * rms_scale(pooled) * final_gain
    return jnp.dot(scaled, score_vector.astype(jnp.float32), precision=highest)


def rank_loss(scores, grades, passage_ranks):
    grade_value = grades.astype(jnp.float32)
    worth_gain = jnp.exp2(grade_value)
    discount = 1.0 / jnp.log2(2.0 + passage_ranks.astype(jnp.float32))
    better_than = grades[None, :] > grades[:, None]
    equal_grade = grades[None, :] == grades[:, None]
    position = jnp.arange(grades.shape[0], dtype=jnp.int32)
    earlier = position[None, :] < position[:, None]
    ideal_rank = jnp.sum(
        jnp.logical_or(better_than, jnp.logical_and(equal_grade, earlier)).astype(jnp.float32),
        axis=1,
    )
    ideal_gain = jnp.sum((worth_gain - 1.0) / jnp.log2(2.0 + ideal_rank))
    ordered = (grades[:, None] > grades[None, :]).astype(jnp.float32)
    swap_gain = (
        jnp.abs(
            (worth_gain[:, None] - worth_gain[None, :]) * (discount[:, None] - discount[None, :])
        )
        / ideal_gain
    )
    margin = scores[:, None] - scores[None, :]
    return jnp.sum(ordered * swap_gain * jax.nn.softplus(-margin))


def pick_gates(normed, router, picked_ids):
    expert_total = router.shape[1]
    logits = jnp.dot(normed, router, preferred_element_type=jnp.float32)
    onehot = (
        picked_ids[:, :, None] == jnp.arange(expert_total, dtype=jnp.int32)[None, None, :]
    ).astype(jnp.float32)
    chosen = jnp.einsum("nke,ne->nk", onehot, logits, precision=highest)
    weights = jnp.exp(chosen)
    return (weights / jnp.sum(weights, axis=1, keepdims=True), onehot)


def gate_parts(pre_gate):
    sigmoid_gate = jax.nn.sigmoid(pre_gate)
    return (pre_gate * sigmoid_gate, sigmoid_gate * (1.0 + pre_gate * (1.0 - sigmoid_gate)))


def norm_back(flat_rows, inverse, norm_gain, d_normed):
    scaled = d_normed * norm_gain
    return inverse * scaled - flat_rows * inverse * inverse * inverse * jnp.mean(
        flat_rows * scaled, axis=-1, keepdims=True
    )


def unpack_front(front_out, buffer_rows):
    pre_gate, pre_up, received = front_out
    hidden_units = pre_gate.shape[2]
    pre_gate = pre_gate.reshape(buffer_rows, hidden_units)
    pre_up = pre_up.reshape(buffer_rows, hidden_units)
    silu_gate, slope = gate_parts(pre_gate)
    activation = (silu_gate * pre_up).astype(jnp.bfloat16)
    return (pre_up, received, silu_gate, slope, activation)


def local(
    hidden,
    norm_gain,
    router,
    gate_proj,
    up_proj,
    down_proj,
    final_gain,
    score_vector,
    expert_ids,
    grades,
    passage_ranks,
):
    unused_query, local_passages, local_positions, model_width = hidden.shape
    top_count = expert_ids.shape[3]
    expert_count = lax.axis_size("exp")
    token_count = local_passages * local_positions
    slot_count = token_count * top_count
    capacity = min(token_count, 9 * token_count * top_count // (8 * expert_count))
    buffer_rows = expert_count * capacity
    flat_rows = hidden.reshape(token_count, model_width).astype(jnp.float32)
    inverse = rms_scale(flat_rows)
    normed = (flat_rows * inverse * norm_gain).astype(jnp.bfloat16)
    picked_ids = expert_ids.reshape(token_count, top_count)
    gate_values, onehot = pick_gates(normed, router, picked_ids)
    slot_hits = onehot.reshape(slot_count, expert_count).astype(jnp.int32)
    slot_rank = jnp.sum((jnp.cumsum(slot_hits, axis=0) - slot_hits) * slot_hits, axis=1)
    target = picked_ids.reshape(slot_count) * capacity + slot_rank
    source_token = jnp.arange(slot_count, dtype=jnp.int32) // top_count
    passage_onehot = (
        source_token[:, None] // local_positions
        == jnp.arange(local_passages, dtype=jnp.int32)[None, :]
    ).astype(jnp.float32)
    weighted = (passage_onehot * gate_values.reshape(slot_count, 1)).astype(jnp.bfloat16)
    send_rows = (
        jnp.zeros((buffer_rows, model_width), jnp.bfloat16).at[target].set(normed[source_token])
    )
    send_weights = jnp.zeros((buffer_rows, local_passages), jnp.bfloat16).at[target].set(weighted)
    outgoing = (
        send_rows.reshape(expert_count, capacity, model_width),
        send_weights.reshape(expert_count, capacity, local_passages),
    )
    gate_matrix = gate_proj[0]
    up_matrix = up_proj[0]
    down_matrix = down_proj[0]
    rows_in = lax.all_to_all(outgoing[0], "exp", split_axis=0, concat_axis=0, tiled=True)
    weights_in = lax.all_to_all(outgoing[1], "exp", split_axis=0, concat_axis=0, tiled=True)
    pre_gate = jnp.einsum("end,df->enf", rows_in, gate_matrix, preferred_element_type=jnp.float32)
    pre_up = jnp.einsum("end,df->enf", rows_in, up_matrix, preferred_element_type=jnp.float32)
    front_out = (pre_gate, pre_up, weights_in)
    pre_up, received, silu_gate, slope, activation = unpack_front(front_out, buffer_rows)
    hidden_units = activation.shape[1]
    passage_part = jnp.einsum(
        "scp,scf->spf",
        received,
        activation.reshape(expert_count, capacity, hidden_units),
        preferred_element_type=jnp.float32,
    )
    down_wide = down_matrix.astype(jnp.float32)
    expert_terms = jnp.einsum("spf,fd->spd", passage_part, down_wide, precision=highest)
    came_back = lax.all_to_all(expert_terms, "exp", split_axis=0, concat_axis=0, tiled=True)
    token_sums = jnp.sum(flat_rows.reshape(local_passages, local_positions, model_width), axis=1)
    pooled = (token_sums + jnp.sum(came_back, axis=0)) / local_positions
    first_row = lax.axis_index("psg") * local_passages
    own_score = head_score(pooled, final_gain, score_vector)
    every_score = lax.all_gather(own_score, "psg", axis=0, tiled=True)
    loss_value, loss_grad = jax.value_and_grad(rank_loss)(every_score, grades[0], passage_ranks[0])
    d_own = lax.dynamic_slice_in_dim(loss_grad, first_row, local_passages, 0) * loss_scale
    unused_score, head_back = jax.vjp(
        lambda values: head_score(values, final_gain, score_vector), pooled
    )
    d_vector = head_back(d_own)[0] / local_positions
    every_vector = lax.all_gather(d_vector[None], "exp", axis=0, tiled=True)
    near_table = jnp.einsum("spd,fd->spf", every_vector, down_wide, precision=highest)
    present = (received != 0).astype(jnp.float32)
    near_rows = jnp.einsum("scp,spf->scf", present, near_table, precision=highest).reshape(
        buffer_rows, hidden_units
    )
    gate_weight = jnp.sum(received.astype(jnp.float32), axis=2).reshape(buffer_rows, 1)
    d_act = gate_weight * near_rows
    d_gate = (d_act * pre_up * slope).astype(jnp.bfloat16)
    d_up = (d_act * silu_gate).astype(jnp.bfloat16)
    contract = (((1,), (1,)), ((), ()))
    pick_grad = lax.dot_general(d_gate, gate_matrix, contract, preferred_element_type=jnp.float32)
    pick_grad = (
        pick_grad + lax.dot_general(d_up, up_matrix, contract, preferred_element_type=jnp.float32)
    ).astype(jnp.bfloat16)
    gate_grad = jnp.sum(activation.astype(jnp.float32) * near_rows, axis=1).astype(jnp.bfloat16)
    back_rows, back_gate = (
        lax.all_to_all(
            pick_grad.reshape(expert_count, capacity, model_width),
            "exp",
            split_axis=0,
            concat_axis=0,
            tiled=True,
        ),
        lax.all_to_all(
            gate_grad.reshape(expert_count, capacity),
            "exp",
            split_axis=0,
            concat_axis=0,
            tiled=True,
        ),
    )
    picked_rows = back_rows.reshape(buffer_rows, model_width)[target]
    d_normed = jnp.sum(
        picked_rows.reshape(token_count, top_count, model_width).astype(jnp.float32), axis=1
    )
    picked_gate = (
        back_gate.reshape(buffer_rows)[target].astype(jnp.float32).reshape(token_count, top_count)
    )
    d_logit = gate_values * (
        picked_gate - jnp.sum(gate_values * picked_gate, axis=1, keepdims=True)
    )
    dense_logit = jnp.einsum("nk,nke->ne", d_logit, onehot, precision=highest)
    d_normed = d_normed + jnp.einsum(
        "ne,de->nd", dense_logit, router.astype(jnp.float32), precision=highest
    )
    grad_flat = norm_back(flat_rows, inverse, norm_gain, d_normed)
    grad_hidden = (
        grad_flat.reshape(1, local_passages, local_positions, model_width)
        + d_vector[None, :, None, :]
    )
    return (
        loss_value.reshape(1),
        own_score.reshape(1, local_passages),
        grad_hidden.astype(jnp.bfloat16),
    )


CORE, ACROSS_X, ACROSS_Y = 1, 2, 4
forward = (((1,), (0,)), ((), ()))
across = (((1,), (1,)), ((), ()))
MIB = 1 << 20


def swap(value, bit, size=8):
    return lax.ppermute(value, "exp", [(index, index ^ bit) for index in range(size)])


def shape_of(shape, dtype):
    return jax.ShapeDtypeStruct(shape, dtype)


def after(value, *others):
    return lax.optimization_barrier((value, *others))[0]


def kept(shape, dtype):
    return pltpu.VMEM(shape, dtype)


def pinned(array):
    return pltpu.with_memory_space_constraint(array, pltpu.VMEM)


def kernel_call(body, name, outs, ins, far=(), scratch=(), result=pltpu.VMEM):
    spaces = [pltpu.VMEM] * len(ins)
    ins = list(ins)
    for index in far:
        spaces[index] = pl.ANY
        ins[index] = pltpu.with_memory_space_constraint(ins[index], pltpu.HBM)
    return pl.pallas_call(
        body,
        name=name,
        out_shape=outs,
        in_specs=[pl.BlockSpec(memory_space=space) for space in spaces],
        out_specs=[pl.BlockSpec(memory_space=result)] * len(outs),
        scratch_shapes=scratch,
        compiler_params=pltpu.CompilerParams(vmem_limit_bytes=8 * MIB),
        cost_estimate=pl.CostEstimate(flops=1, bytes_accessed=1, transcendentals=0),
    )(*ins)


def split_low(values):
    high = values.astype(jnp.bfloat16)
    rest = values - high.astype(jnp.float32)
    middle = rest.astype(jnp.bfloat16)
    low = (rest - middle.astype(jnp.float32)).astype(jnp.bfloat16)
    return high, middle, low


def exact_dot(values, low_matrix, contract):
    parts = lax.dot_general(
        jnp.concatenate(split_low(values), axis=0),
        low_matrix,
        contract,
        preferred_element_type=jnp.float32,
    )
    return parts[0:8] + parts[8:16] + parts[16:24]


def other_order(values, bits):
    return jnp.concatenate([values[row ^ bits : (row ^ bits) + 1] for row in range(4)], axis=0)


def norm_kernel(
    hidden_far, gain_far, router_far, final_far, vector_far,
    hidden_ref, gain_ref, router_ref, normed_ref, sums_ref, head_ref,
    final_ref, vector_ref, copy_sems,
):
    pairs = (
        (hidden_far, hidden_ref), (gain_far, gain_ref), (router_far, router_ref),
        (final_far, final_ref), (vector_far, vector_ref),
    )
    copies = [
        pltpu.make_async_copy(source, target, copy_sems.at[index])
        for index, (source, target) in enumerate(pairs)
    ]
    for copy in copies:
        copy.start()
    for copy in copies:
        copy.wait()
    vector = vector_ref[...].astype(jnp.float32)
    vector = jnp.concatenate([vector[row : row + 1] for row in range(vector.shape[0])], axis=1)
    head_ref[...] = final_ref[...] * vector
    rows = hidden_ref[...].astype(jnp.float32)
    normed_ref[...] = (rows * rms_scale(rows) * gain_ref[...]).astype(jnp.bfloat16)
    sums_ref[...] = jnp.sum(rows, axis=0, keepdims=True)


def front_kernel(stage, owners, sets, count, router_ref, *refs):
    matrices, refs = refs[: 2 * len(sets)], refs[2 * len(sets) :]
    pieces, refs = refs[:count], refs[count:]
    matrices = list(matrices)
    hidden_units = matrices[0].shape[1]
    tile = 256
    firsts = range(0, hidden_units, tile)
    if stage == 0:
        far_matrices = matrices
        *refs, gate_held, up_held, rows_ref, copy_sems = refs
        matrices = [gate_held, up_held]
        copies = [
            pltpu.make_async_copy(
                source.at[:, first : first + tile],
                target.at[:, first : first + tile],
                copy_sems.at[which, number],
            )
            for number, first in enumerate(firsts)
            for which, (source, target) in enumerate(zip(far_matrices, matrices))
        ]
        for copy in copies:
            copy.start()
        turned_ref, *refs = refs
    elif stage == 3:
        sums_ref, *downs = refs[:3]
        earlier, refs = refs[3:6], refs[6:]
        *refs, terms_ref, rows_ref = refs
    else:
        *refs, rows_ref = refs
    gates_ref, *outs = refs
    expert = lax.axis_index("exp")
    first = 0
    for piece in pieces:
        rows_ref[first : first + piece.shape[0], :] = piece[...]
        first += piece.shape[0]
    size = first // len(owners)
    logits = lax.dot_general(
        rows_ref[...], router_ref[...], across, preferred_element_type=jnp.float32
    )
    weights = jnp.exp(logits)
    gates = weights / jnp.sum(weights, axis=1, keepdims=True)
    gates_ref[...] = gates
    lane = lax.broadcasted_iota(jnp.int32, gates.shape, 1)
    if stage == 0:
        weights = jnp.exp(
            lax.dot_general(
                router_ref[...], rows_ref[...], across, preferred_element_type=jnp.float32
            )
        )
        turned_ref[...] = weights / jnp.sum(weights, axis=0, keepdims=True)

    totals = []
    for place, which in enumerate(sets):
        gate_ref, up_ref = matrices[2 * place : 2 * place + 2]
        if stage == 3:
            slope_ref, silu_ref, act_ref = outs[3 * place : 3 * place + 3]
        else:
            slope_ref, silu_ref, act_ref, part_ref = outs
        own = jnp.sum(jnp.where(lane == expert ^ which, gates, 0.0), axis=1, keepdims=True)
        low = own.astype(jnp.bfloat16).astype(jnp.float32)
        parts = []
        for number, first in enumerate(firsts):
            columns = slice(first, first + tile)
            if stage == 0:
                copies[2 * number].wait()
                copies[2 * number + 1].wait()
            rows = rows_ref[...]
            pre_gate = jnp.dot(rows, gate_ref[:, columns], preferred_element_type=jnp.float32)
            pre_up = jnp.dot(rows, up_ref[:, columns], preferred_element_type=jnp.float32)
            silu_gate, slope = gate_parts(pre_gate)
            activation = (silu_gate * pre_up).astype(jnp.bfloat16)
            slope_ref[:, columns] = slope * pre_up
            silu_ref[:, columns] = silu_gate
            act_ref[:, columns] = activation
            weighted = activation.astype(jnp.float32) * low
            found = {
                owner: jnp.sum(weighted[index * size : (index + 1) * size], axis=0, keepdims=True)
                for index, owner in enumerate(owners)
            }
            nothing = jnp.zeros_like(weighted[:1])
            parts.append(
                jnp.concatenate([found.get(owner, nothing) for owner in range(8)], axis=0)
            )
        totals.append(jnp.concatenate(parts, axis=1))
    if stage < 3:
        part_ref[...] = totals[0]
        return
    own_first, own_second, other_first = earlier
    totals[0] = totals[0] + (own_first[...] + own_second[...])
    totals[1] = totals[1] + other_first[...]
    terms = exact_dot(totals[0], downs[0][...], forward) + exact_dot(
        totals[1], downs[1][...], forward
    )
    row = lax.broadcasted_iota(jnp.int32, terms.shape, 0)
    terms_ref[...] = (terms + jnp.where(row == 0, sums_ref[...], 0.0))[:4]


def front(stage, owners, sets, pieces, router_rows, matrices, more=()):
    model_width, hidden_units = matrices[0].shape
    row_total = sum(piece.shape[0] for piece in pieces)
    outs = [kept((row_total, 8), jnp.float32)]
    if stage == 0:
        outs.insert(0, kept((8, row_total), jnp.float32))
    for which in sets:
        outs += [
            kept((row_total, hidden_units), jnp.float32),
            kept((row_total, hidden_units), jnp.float32),
            kept((row_total, hidden_units), jnp.bfloat16),
        ]
    outs.append(
        kept((4, model_width), jnp.float32) if stage == 3 else kept((8, hidden_units), jnp.float32)
    )
    scratch = [pltpu.VMEM((row_total, model_width), jnp.bfloat16)]
    far = ()
    if stage == 0:
        far = (1, 2)
        outs += [kept(matrix.shape, jnp.bfloat16) for matrix in matrices]
        scratch.append(pltpu.SemaphoreType.DMA((2, hidden_units // 256)))
    else:
        matrices = [pinned(matrix) for matrix in matrices]
    if stage == 3:
        more = [pinned(array) for array in more]
    return kernel_call(
        functools.partial(front_kernel, stage, owners, sets, len(pieces)),
        "front",
        outs,
        [pinned(router_rows), *matrices, *(pinned(piece) for piece in pieces), *more],
        far,
        scratch,
    )


def near_kernel(
    own_ref, x_ref, y_ref, far_ref, head_ref, down_ref, other_down_ref,
    near_ref, other_near_ref, unit_ref, score_ref, own_score_ref, *, token_count,
):
    pooled = (
        (own_ref[...] + other_order(x_ref[...], 1))
        + (other_order(y_ref[...], 2) + other_order(far_ref[...], 3))
    ) / token_count
    pooled = jnp.concatenate([pooled, jnp.zeros_like(pooled)], axis=0)
    head = head_ref[...]
    scale = rms_scale(pooled)
    along = jnp.sum(pooled * head, axis=1, keepdims=True)
    own_score = (scale * along)[:1]
    own_score_ref[...] = own_score
    score_ref[...] = jnp.broadcast_to(own_score, score_ref.shape)
    unit = (
        scale * head - scale * scale * scale * (along / pooled.shape[1]) * pooled
    ) / token_count
    unit_ref[...] = unit[:1]
    near_ref[...] = exact_dot(unit, down_ref[...], forward)
    other_near_ref[...] = exact_dot(unit, other_down_ref[...], forward)


def back_kernel(passages, gate_count, saved_count, near_ref, other_near_ref, *refs):
    gates_refs, refs = refs[:gate_count], refs[gate_count:]
    saved, refs = refs[: 3 * saved_count], refs[3 * saved_count :]
    matrices, refs = refs[:4], refs[4:]
    *out_refs, d_gate_ref, d_up_ref, other_d_gate_ref, other_d_up_ref = refs
    expert = lax.axis_index("exp")
    size = out_refs[0].shape[1]
    model_width = matrices[0].shape[1]
    lane = lax.broadcasted_iota(jnp.int32, (size, 8), 1)
    line = lax.broadcasted_iota(jnp.int32, (16, size), 0)
    experts = (
        (near_ref, d_gate_ref, d_up_ref), (other_near_ref, other_d_gate_ref, other_d_up_ref)
    )
    sides = (d_gate_ref, d_up_ref, other_d_gate_ref, other_d_up_ref)
    for index, (owner, gates_place, saved_places, windows, unused) in enumerate(passages):
        rows = slice(index * size, (index + 1) * size)
        lines = jnp.zeros((16, size), jnp.float32)
        gates = gates_refs[gates_place[0]][gates_place[1] : gates_place[1] + size, :]
        for which, (table_ref, d_gate_out, d_up_out) in enumerate(experts):
            number, first = saved_places[which]
            slope_ref, silu_ref, act_ref = saved[3 * number : 3 * number + 3]
            held = slice(first, first + size)
            near = table_ref[owner : owner + 1, :]
            own = jnp.sum(
                jnp.where(lane == expert ^ which, gates, 0.0), axis=1, keepdims=True
            )
            d_act = own.astype(jnp.bfloat16).astype(jnp.float32) * near
            d_gate_out[rows, :] = (d_act * slope_ref[held, :]).astype(jnp.bfloat16)
            d_up_out[rows, :] = (d_act * silu_ref[held, :]).astype(jnp.bfloat16)
            if windows[-1][1] == model_width:
                gate_grad = exact_dot(table_ref[...], act_ref[held, :], across)
                lines = jnp.where(line == expert ^ which, gate_grad[owner : owner + 1], lines)
        for start, stop in windows:
            out_ref, *out_refs = out_refs
            used = stop - start
            if stop == model_width:
                out_ref[used : used + 16, :] = lines.astype(jnp.bfloat16)
                used += 16
            if out_ref.shape[0] > used:
                out_ref[used:, :] = jnp.zeros((out_ref.shape[0] - used, size), jnp.bfloat16)
            for first in range(start, stop, 256):
                pick_grad = None
                for side_ref, matrix in zip(sides, matrices):
                    term = jnp.dot(
                        side_ref[rows, :],
                        matrix[:, first : first + 256],
                        preferred_element_type=jnp.float32,
                    )
                    pick_grad = term if pick_grad is None else pick_grad + term
                out_ref[first - start : first - start + 256, :] = pick_grad.T.astype(jnp.bfloat16)


def back(passages, near, other_near, gates, saved, matrices, size):
    hidden_units, model_width = matrices[0].shape
    heights = [
        max(least, stop - start + (16 if stop == model_width else 0))
        for passage in passages
        for (start, stop), least in zip(*passage[3:])
    ]
    arrays = [array for group in saved for array in group]
    return kernel_call(
        functools.partial(back_kernel, passages, len(gates), len(saved)),
        "back",
        [kept((height, size), jnp.bfloat16) for height in heights],
        [pinned(array) for array in (near, other_near, *gates, *arrays, *matrices)],
        (),
        [pltpu.VMEM((len(passages) * size, hidden_units), jnp.bfloat16)] * 4,
    )


def add_kernel(x_ref, y_ref, high_ref, low_ref, x_out, y_out):
    for own_ref, other_ref, out_ref in ((x_ref, high_ref, x_out), (y_ref, low_ref, y_out)):
        out_ref[...] = (
            own_ref[...].astype(jnp.float32)
            + other_ref[: own_ref.shape[0], :].astype(jnp.float32)
        ).astype(jnp.bfloat16)


def turn_kernel(*refs):
    count = len(refs) // 2
    for source_ref, target_ref in zip(refs[:count], refs[count:]):
        for first in range(0, source_ref.shape[0], 256):
            rows = slice(first, first + 256)
            target_ref[:, rows] = source_ref[rows, :].T


def turn(matrices):
    return kernel_call(
        turn_kernel,
        "turn",
        [kept(matrix.shape[::-1], jnp.bfloat16) for matrix in matrices],
        [pinned(matrix) for matrix in matrices],
    )


def half_kernel(part, rows_ref, out_ref):
    half = out_ref.shape[0]
    out_ref[...] = rows_ref[part * half : (part + 1) * half, :]


def half_of(rows, part):
    total, wide = rows.shape
    (out,) = kernel_call(
        functools.partial(half_kernel, part), "half", [kept((total // 2, wide), rows.dtype)], [rows]
    )
    return out


def pack_kernel(first_ref, second_ref, out_ref):
    out_ref[:1, :] = first_ref[:1, :]
    out_ref[1:, :] = second_ref[:1, :]


def pack(first, second):
    return kernel_call(
        pack_kernel, "pack", [kept((2, first.shape[1]), first.dtype)], [pinned(first), second]
    )[0]


def pairs_of(passages):
    row = lax.broadcasted_iota(jnp.int32, (8, 128), 0)
    lane = lax.broadcasted_iota(jnp.int32, (8, 128), 1)
    return row, lane, jnp.logical_and(row < passages, lane < passages)


def spread(index, values):
    total = jnp.zeros((8, 128), jnp.float32)
    for number, value in values:
        total = jnp.where(index == number, value, total)
    return total


def whole_sum(values):
    return jnp.sum(jnp.sum(values, axis=1, keepdims=True), axis=0, keepdims=True)


def pair_kernel(
    grades_far, ranks_far, down_far, swap_gain_ref, down_ref, grades_ref, ranks_ref, copy_sems
):
    down_copy = pltpu.make_async_copy(down_far, down_ref, copy_sems.at[2])
    down_copy.start()
    copies = [
        pltpu.make_async_copy(grades_far, grades_ref, copy_sems.at[0]),
        pltpu.make_async_copy(ranks_far, ranks_ref, copy_sems.at[1]),
    ]
    for copy in copies:
        copy.start()
    for copy in copies:
        copy.wait()
    passages = grades_ref.shape[1]
    row, lane, pair = pairs_of(passages)
    grade_list = [(number, grades_ref[0, number].astype(jnp.float32)) for number in range(passages)]
    rank_list = [(number, ranks_ref[0, number].astype(jnp.float32)) for number in range(passages)]
    grade_row, grade_lane = spread(row, grade_list), spread(lane, grade_list)
    worth_row, worth_lane = jnp.exp2(grade_row), jnp.exp2(grade_lane)
    discount_row = 1.0 / jnp.log2(2.0 + spread(row, rank_list))
    discount_lane = 1.0 / jnp.log2(2.0 + spread(lane, rank_list))
    ahead = jnp.logical_or(
        grade_lane > grade_row, jnp.logical_and(grade_lane == grade_row, lane < row)
    )
    ideal_rank = jnp.sum(
        jnp.where(jnp.logical_and(pair, ahead), 1.0, 0.0), axis=1, keepdims=True
    )
    ideal_terms = (worth_row - 1.0) / jnp.log2(2.0 + ideal_rank)
    one_lane = jnp.logical_and(pair, lane == 0)
    ideal_gain = whole_sum(jnp.where(one_lane, ideal_terms, 0.0))
    swap_gain = (
        jnp.abs((worth_row - worth_lane) * (discount_row - discount_lane)) / ideal_gain
    )
    swap_gain_ref[...] = jnp.where(
        jnp.logical_and(pair, grade_row > grade_lane), swap_gain, 0.0
    )
    down_copy.wait()


def rank_kernel(swap_gain_ref, near_scores_ref, far_scores_ref, loss_ref, factor_ref):
    passages = 2 * near_scores_ref.shape[0]
    place = lax.axis_index("psg")
    row, lane, unused = pairs_of(passages)
    score_list = [
        (place ^ (base + number), jnp.broadcast_to(ref[number : number + 1, :], (8, 128)))
        for base, ref in ((0, near_scores_ref), (passages // 2, far_scores_ref))
        for number in range(passages // 2)
    ]
    swap_gain = swap_gain_ref[...]
    margin = spread(row, score_list) - spread(lane, score_list)
    softplus = jnp.maximum(-margin, 0.0) + jnp.log1p(jnp.exp(-jnp.abs(margin)))
    loss_ref[...] = whole_sum(swap_gain * softplus)
    pull = swap_gain * jax.nn.sigmoid(-margin)
    gradient = whole_sum(jnp.where(lane == place, pull, 0.0) - jnp.where(row == place, pull, 0.0))
    factor_ref[...] = jnp.broadcast_to(gradient * loss_scale, factor_ref.shape)


def first_end_kernel(own_ref, x_low_ref, y_high_ref, total_ref, lines_ref):
    model_width = total_ref.shape[1]
    cut = model_width // 2
    for first in range(0, model_width, 256):
        rows = slice(first, first + 256)
        if first < cut:
            term = x_low_ref[rows, :]
        else:
            term = y_high_ref[first - cut : first - cut + 256, :]
        total = own_ref[rows, :].astype(jnp.float32) + term.astype(jnp.float32)
        total_ref[:, rows] = total.T
    end = slice(model_width, model_width + 8)
    end_high = slice(model_width - cut, model_width - cut + 8)
    lines_ref[...] = own_ref[end, :].astype(jnp.float32) + y_high_ref[end_high, :].astype(
        jnp.float32
    )


def end_kernel(
    factor_ref, total_ref, lines_ref, x_high_ref, y_low_ref,
    hidden_ref, gain_ref, gates_ref, router_ref, unit_ref,
    grad_far, turned_ref, grad_ref, copy_sems,
):
    token_count, model_width = hidden_ref.shape
    cut = y_low_ref.shape[0]
    end_high = slice(model_width - cut, model_width - cut + 8)
    slot_grad = lines_ref[...] + x_high_ref[end_high, :].astype(jnp.float32)
    gates = gates_ref[...]
    d_logit = gates * (slot_grad - jnp.sum(gates * slot_grad, axis=0, keepdims=True))
    d_logit = jnp.concatenate([d_logit, jnp.zeros((120, token_count), jnp.float32)], axis=0).T
    d_logit = jnp.concatenate(split_low(d_logit[:, :8]), axis=1)
    router_rows = jnp.concatenate([router_ref[...]] * 3, axis=0)
    for first in range(0, model_width, 256):
        columns = slice(first, first + 256)
        if first < cut:
            term = y_low_ref[columns, :]
        else:
            term = x_high_ref[first - cut : first - cut + 256, :]
        turned_ref[:, columns] = (
            total_ref[:, columns]
            + term.astype(jnp.float32).T
            + jnp.dot(d_logit, router_rows[:, columns], preferred_element_type=jnp.float32)
        )
    gain = gain_ref[...]
    factor = factor_ref[:, :1]
    size = 16
    copies = []
    for first in range(0, token_count, size):
        rows = slice(first, first + size)
        flat_rows = hidden_ref[rows, :].astype(jnp.float32)
        grad = norm_back(flat_rows, rms_scale(flat_rows), gain, turned_ref[rows, :])
        grad_ref[rows, :] = ((grad + unit_ref[...]) * factor).astype(jnp.bfloat16)
        copies.append(
            pltpu.make_async_copy(
                grad_ref.at[rows, :], grad_far.at[rows, :], copy_sems.at[first // size]
            )
        )
        copies[-1].start()
    for copy in copies:
        copy.wait()


def every_expert(
    hidden,
    norm_gain,
    router,
    gate_proj,
    up_proj,
    down_proj,
    final_gain,
    score_vector,
    expert_ids,
    grades,
    passage_ranks,
):
    unused_query, unused_passage, token_count, model_width = hidden.shape
    passages = grades.shape[1]
    flat = hidden.reshape(token_count, model_width)
    gate_matrix, up_matrix, down_matrix = gate_proj[0], up_proj[0], down_proj[0]
    mine = [gate_matrix, up_matrix, down_matrix]
    flat, gain, router_rows, normed, token_sums, head = kernel_call(
        norm_kernel,
        "norm",
        [
            kept(flat.shape, jnp.bfloat16),
            kept((1, model_width), jnp.float32),
            kept((8, model_width), jnp.bfloat16),
            kept(flat.shape, jnp.bfloat16),
            kept((1, model_width), jnp.float32),
            kept((1, model_width), jnp.float32),
        ],
        [
            flat,
            norm_gain.reshape(1, model_width),
            router.T,
            final_gain.reshape(1, model_width),
            score_vector.reshape(model_width // 128, 128),
        ],
        range(5),
        [
            pltpu.VMEM((1, model_width), jnp.float32),
            pltpu.VMEM((model_width // 128, 128), jnp.bfloat16),
            pltpu.SemaphoreType.DMA((5,)),
        ],
    )
    others = [swap(matrix, CORE) for matrix in mine]
    x_rows, y_rows = swap(normed, ACROSS_X), swap(normed, ACROSS_Y)
    turned_gates, own_gates, *own_saved, own_part, mine[0], mine[1] = front(
        0, (0,), (0,), [normed], router_rows, mine[:2]
    )
    swap_gain, mine[2] = kernel_call(
        pair_kernel,
        "pairs",
        [kept((8, 128), jnp.float32), kept(down_matrix.shape, jnp.bfloat16)],
        [grades, after(passage_ranks, own_part), down_matrix],
        (0, 1, 2),
        [
            pltpu.SMEM(grades.shape, jnp.int32),
            pltpu.SMEM(grades.shape, jnp.int32),
            pltpu.SemaphoreType.DMA((3,)),
        ],
    )
    *mine_turned, down_turned = turn(mine)
    x_rows, y_rows = after(x_rows, mine_turned[0]), after(y_rows, mine_turned[0])
    far_low = swap(half_of(x_rows, 0), ACROSS_Y)
    far_high = swap(half_of(y_rows, 1), ACROSS_X)
    side_gates, *side_saved, side_part = front(
        1, (1, 2), (0,), [x_rows, y_rows], router_rows, mine[:2]
    )
    others[0] = after(others[0], side_part)
    unused, *other_saved, other_part = front(
        2, (0, 1, 2), (1,), [normed, x_rows, y_rows], router_rows, others[:2]
    )
    far_low, far_high = after(far_low, other_part), after(far_high, other_part)
    far_gates, *far_saved, terms = front(
        3, (3,), (0, 1), [far_low, far_high], router_rows, mine[:2] + others[:2],
        (token_sums, mine[2], others[2], own_part, side_part, other_part),
    )

    *others_turned, other_down_turned = turn([after(others[0], terms), *others[1:]])
    head = after(head, others_turned[0])
    near, other_near, unit_vector, travelling, own_score = kernel_call(
        functools.partial(near_kernel, token_count=token_count),
        "near",
        [
            kept((8, down_matrix.shape[0]), jnp.float32),
            kept((8, down_matrix.shape[0]), jnp.float32),
            kept((1, model_width), jnp.float32),
            kept((1, 128), jnp.float32),
            shape_of((1, 1), jnp.float32),
        ],
        [
            pinned(terms),
            swap(terms, ACROSS_X),
            swap(terms, ACROSS_Y),
            swap(terms, ACROSS_X | ACROSS_Y),
            pinned(head),
            pinned(down_turned),
            pinned(other_down_turned),
        ],
    )
    matrices = [*mine_turned, *others_turned]
    middle = model_width // 2
    lower, upper, early, earlier = (0, middle), (middle, model_width), middle + 32, middle + 64
    far_low, far_high = back(
        ((3, (0, 0), ((0, 0), (1, 0)), (lower, upper), (earlier, earlier)),),
        near, other_near, [far_gates], [far_saved[:3], far_saved[3:]], matrices, token_count,
    )
    far_sent = far_low
    far_low, far_high = swap(far_low, ACROSS_X), swap(far_high, ACROSS_Y)

    def sides_back(x_window, y_window, least, *earlier):
        return back(
            (
                (1, (0, 0), ((0, 0), (1, token_count)), (x_window,), (least,)),
                (2, (0, token_count), ((0, token_count), (1, 2 * token_count)), (y_window,), (least,)),
            ),
            after(near, *earlier), other_near, [side_gates], [side_saved, other_saved], matrices,
            token_count,
        )

    x_low, y_high = sides_back(lower, upper, early, far_sent)
    first_sent = x_low
    x_low, y_high = swap(x_low, ACROSS_X), swap(y_high, ACROSS_Y)
    x_high, y_low = sides_back(upper, lower, 0, first_sent)
    travelling = after(travelling, first_sent)
    met = lax.ppermute(travelling, "psg", [(index, index ^ 1) for index in range(passages)])
    near_scores = pack(travelling, met)
    far_high = after(far_high, near_scores)
    x_high, y_low = kernel_call(
        add_kernel,
        "add",
        [kept(x_high.shape, jnp.bfloat16), kept(y_low.shape, jnp.bfloat16)],
        [pinned(x_high), pinned(y_low), far_high, far_low],
    )
    x_high, y_low, near_scores, other_near = lax.optimization_barrier(
        (x_high, y_low, near_scores, other_near)
    )
    x_high, y_low = swap(x_high, ACROSS_X), swap(y_low, ACROSS_Y)
    (own_sums,) = back(
        ((0, (0, 0), ((0, 0), (1, 0)), ((0, model_width),), (0,)),),
        near, other_near, [own_gates], [own_saved, other_saved], matrices, token_count,
    )
    far_scores = lax.ppermute(near_scores, "psg", [(index, index ^ 2) for index in range(passages)])
    loss, factor = kernel_call(
        rank_kernel,
        "rank",
        [shape_of((1, 1), jnp.float32), kept((1, 128), jnp.float32)],
        [pinned(swap_gain), pinned(near_scores), far_scores],
    )
    total, lines = kernel_call(
        first_end_kernel,
        "first_end",
        [
            kept((token_count, model_width), jnp.float32),
            kept((8, token_count), jnp.float32),
        ],
        [pinned(own_sums), after(x_low, factor), y_high],
    )
    (grad,) = kernel_call(
        end_kernel,
        "end",
        [shape_of((token_count, model_width), jnp.bfloat16)],
        [
            pinned(factor), pinned(total), pinned(lines), x_high, y_low, pinned(flat), pinned(gain),
            pinned(turned_gates), pinned(router_rows), pinned(unit_vector),
        ],
        scratch=[
            pltpu.VMEM((token_count, model_width), jnp.float32),
            pltpu.VMEM((token_count, model_width), jnp.bfloat16),
            pltpu.SemaphoreType.DMA((token_count // 16,)),
        ],
        result=pl.ANY,
    )
    return (loss.reshape(1), own_score, grad.reshape(hidden.shape))


def block(*arrays):
    hidden, router, expert_ids, grades = arrays[0], arrays[2], arrays[8], arrays[9]
    each_expert = router.shape[1] == expert_ids.shape[3] == 8
    if hidden.shape[1] == 1 and each_expert and grades.shape[1] == 4:
        return every_expert(*arrays)
    return local(*arrays)


def solution(mesh):
    placed = (
        P("exp", "psg", None, None),
        P(),
        P(),
        P("exp", None, None),
        P("exp", None, None),
        P("exp", None, None),
        P(),
        P(),
        P("exp", "psg", None, None),
        P("exp", None),
        P("exp", None),
    )
    return jax.shard_map(
        block,
        mesh=mesh,
        in_specs=placed,
        out_specs=(P("exp"), P("exp", "psg"), P("exp", "psg", None, None)),
        check_vma=False,
    )
```

```python
import functools
import math

import jax
import jax.numpy as jnp
from jax import lax
from jax.experimental import pallas as pl
from jax.experimental.pallas import tpu as pltpu
from jax.sharding import PartitionSpec as P

epsilon = 1e-06
loss_scale = 256.0
highest = lax.Precision.HIGHEST


def rms_scale(values):
    return lax.rsqrt(jnp.mean(values * values, axis=-1, keepdims=True) + epsilon)


def head_score(pooled, final_gain, score_vector):
    scaled = pooled * rms_scale(pooled) * final_gain
    return jnp.dot(scaled, score_vector.astype(jnp.float32), precision=highest)


def rank_loss(scores, grades, passage_ranks):
    grade_value = grades.astype(jnp.float32)
    worth_gain = jnp.exp2(grade_value)
    discount = 1.0 / jnp.log2(2.0 + passage_ranks.astype(jnp.float32))
    better_than = grades[None, :] > grades[:, None]
    equal_grade = grades[None, :] == grades[:, None]
    position = jnp.arange(grades.shape[0], dtype=jnp.int32)
    earlier = position[None, :] < position[:, None]
    ideal_rank = jnp.sum(
        jnp.logical_or(better_than, jnp.logical_and(equal_grade, earlier)).astype(jnp.float32),
        axis=1,
    )
    ideal_gain = jnp.sum((worth_gain - 1.0) / jnp.log2(2.0 + ideal_rank))
    ordered = (grades[:, None] > grades[None, :]).astype(jnp.float32)
    swap_gain = (
        jnp.abs(
            (worth_gain[:, None] - worth_gain[None, :]) * (discount[:, None] - discount[None, :])
        )
        / ideal_gain
    )
    margin = scores[:, None] - scores[None, :]
    return jnp.sum(ordered * swap_gain * jax.nn.softplus(-margin))


def pick_gates(normed, router, picked_ids):
    expert_total = router.shape[1]
    logits = jnp.dot(normed, router, preferred_element_type=jnp.float32)
    onehot = (
        picked_ids[:, :, None] == jnp.arange(expert_total, dtype=jnp.int32)[None, None, :]
    ).astype(jnp.float32)
    chosen = jnp.einsum("nke,ne->nk", onehot, logits, precision=highest)
    weights = jnp.exp(chosen)
    return (weights / jnp.sum(weights, axis=1, keepdims=True), onehot)


def gate_parts(pre_gate):
    sigmoid_gate = jax.nn.sigmoid(pre_gate)
    return (pre_gate * sigmoid_gate, sigmoid_gate * (1.0 + pre_gate * (1.0 - sigmoid_gate)))


def norm_back(flat_rows, inverse, norm_gain, d_normed):
    scaled = d_normed * norm_gain
    return inverse * scaled - flat_rows * inverse * inverse * inverse * jnp.mean(
        flat_rows * scaled, axis=-1, keepdims=True
    )


def unpack_front(front_out, buffer_rows):
    pre_gate, pre_up, received = front_out
    hidden_units = pre_gate.shape[2]
    pre_gate = pre_gate.reshape(buffer_rows, hidden_units)
    pre_up = pre_up.reshape(buffer_rows, hidden_units)
    silu_gate, slope = gate_parts(pre_gate)
    activation = (silu_gate * pre_up).astype(jnp.bfloat16)
    return (pre_up, received, silu_gate, slope, activation)


def local(
    hidden,
    norm_gain,
    router,
    gate_proj,
    up_proj,
    down_proj,
    final_gain,
    score_vector,
    expert_ids,
    grades,
    passage_ranks,
):
    unused_query, local_passages, local_positions, model_width = hidden.shape
    top_count = expert_ids.shape[3]
    expert_count = lax.axis_size("exp")
    token_count = local_passages * local_positions
    slot_count = token_count * top_count
    capacity = min(token_count, 9 * token_count * top_count // (8 * expert_count))
    buffer_rows = expert_count * capacity
    flat_rows = hidden.reshape(token_count, model_width).astype(jnp.float32)
    inverse = rms_scale(flat_rows)
    normed = (flat_rows * inverse * norm_gain).astype(jnp.bfloat16)
    picked_ids = expert_ids.reshape(token_count, top_count)
    gate_values, onehot = pick_gates(normed, router, picked_ids)
    slot_hits = onehot.reshape(slot_count, expert_count).astype(jnp.int32)
    slot_rank = jnp.sum((jnp.cumsum(slot_hits, axis=0) - slot_hits) * slot_hits, axis=1)
    target = picked_ids.reshape(slot_count) * capacity + slot_rank
    source_token = jnp.arange(slot_count, dtype=jnp.int32) // top_count
    passage_onehot = (
        source_token[:, None] // local_positions
        == jnp.arange(local_passages, dtype=jnp.int32)[None, :]
    ).astype(jnp.float32)
    weighted = (passage_onehot * gate_values.reshape(slot_count, 1)).astype(jnp.bfloat16)
    send_rows = (
        jnp.zeros((buffer_rows, model_width), jnp.bfloat16).at[target].set(normed[source_token])
    )
    send_weights = jnp.zeros((buffer_rows, local_passages), jnp.bfloat16).at[target].set(weighted)
    outgoing = (
        send_rows.reshape(expert_count, capacity, model_width),
        send_weights.reshape(expert_count, capacity, local_passages),
    )
    gate_matrix = gate_proj[0]
    up_matrix = up_proj[0]
    down_matrix = down_proj[0]
    rows_in = lax.all_to_all(outgoing[0], "exp", split_axis=0, concat_axis=0, tiled=True)
    weights_in = lax.all_to_all(outgoing[1], "exp", split_axis=0, concat_axis=0, tiled=True)
    pre_gate = jnp.einsum("end,df->enf", rows_in, gate_matrix, preferred_element_type=jnp.float32)
    pre_up = jnp.einsum("end,df->enf", rows_in, up_matrix, preferred_element_type=jnp.float32)
    front_out = (pre_gate, pre_up, weights_in)
    pre_up, received, silu_gate, slope, activation = unpack_front(front_out, buffer_rows)
    hidden_units = activation.shape[1]
    passage_part = jnp.einsum(
        "scp,scf->spf",
        received,
        activation.reshape(expert_count, capacity, hidden_units),
        preferred_element_type=jnp.float32,
    )
    down_wide = down_matrix.astype(jnp.float32)
    expert_terms = jnp.einsum("spf,fd->spd", passage_part, down_wide, precision=highest)
    came_back = lax.all_to_all(expert_terms, "exp", split_axis=0, concat_axis=0, tiled=True)
    token_sums = jnp.sum(flat_rows.reshape(local_passages, local_positions, model_width), axis=1)
    pooled = (token_sums + jnp.sum(came_back, axis=0)) / local_positions
    first_row = lax.axis_index("psg") * local_passages
    own_score = head_score(pooled, final_gain, score_vector)
    every_score = lax.all_gather(own_score, "psg", axis=0, tiled=True)
    loss_value, loss_grad = jax.value_and_grad(rank_loss)(every_score, grades[0], passage_ranks[0])
    d_own = lax.dynamic_slice_in_dim(loss_grad, first_row, local_passages, 0) * loss_scale
    unused_score, head_back = jax.vjp(
        lambda values: head_score(values, final_gain, score_vector), pooled
    )
    d_vector = head_back(d_own)[0] / local_positions
    every_vector = lax.all_gather(d_vector[None], "exp", axis=0, tiled=True)
    near_table = jnp.einsum("spd,fd->spf", every_vector, down_wide, precision=highest)
    present = (received != 0).astype(jnp.float32)
    near_rows = jnp.einsum("scp,spf->scf", present, near_table, precision=highest).reshape(
        buffer_rows, hidden_units
    )
    gate_weight = jnp.sum(received.astype(jnp.float32), axis=2).reshape(buffer_rows, 1)
    d_act = gate_weight * near_rows
    d_gate = (d_act * pre_up * slope).astype(jnp.bfloat16)
    d_up = (d_act * silu_gate).astype(jnp.bfloat16)
    contract = (((1,), (1,)), ((), ()))
    pick_grad = lax.dot_general(d_gate, gate_matrix, contract, preferred_element_type=jnp.float32)
    pick_grad = (
        pick_grad + lax.dot_general(d_up, up_matrix, contract, preferred_element_type=jnp.float32)
    ).astype(jnp.bfloat16)
    gate_grad = jnp.sum(activation.astype(jnp.float32) * near_rows, axis=1).astype(jnp.bfloat16)
    back_rows, back_gate = (
        lax.all_to_all(
            pick_grad.reshape(expert_count, capacity, model_width),
            "exp",
            split_axis=0,
            concat_axis=0,
            tiled=True,
        ),
        lax.all_to_all(
            gate_grad.reshape(expert_count, capacity),
            "exp",
            split_axis=0,
            concat_axis=0,
            tiled=True,
        ),
    )
    picked_rows = back_rows.reshape(buffer_rows, model_width)[target]
    d_normed = jnp.sum(
        picked_rows.reshape(token_count, top_count, model_width).astype(jnp.float32), axis=1
    )
    picked_gate = (
        back_gate.reshape(buffer_rows)[target].astype(jnp.float32).reshape(token_count, top_count)
    )
    d_logit = gate_values * (
        picked_gate - jnp.sum(gate_values * picked_gate, axis=1, keepdims=True)
    )
    dense_logit = jnp.einsum("nk,nke->ne", d_logit, onehot, precision=highest)
    d_normed = d_normed + jnp.einsum(
        "ne,de->nd", dense_logit, router.astype(jnp.float32), precision=highest
    )
    grad_flat = norm_back(flat_rows, inverse, norm_gain, d_normed)
    grad_hidden = (
        grad_flat.reshape(1, local_passages, local_positions, model_width)
        + d_vector[None, :, None, :]
    )
    return (
        loss_value.reshape(1),
        own_score.reshape(1, local_passages),
        grad_hidden.astype(jnp.bfloat16),
    )


CORE, ACROSS_X, ACROSS_Y = 1, 2, 4
forward = (((1,), (0,)), ((), ()))
across = (((1,), (1,)), ((), ()))
MIB = 1 << 20


def swap(value, bit, size=8):
    return lax.ppermute(value, "exp", [(index, index ^ bit) for index in range(size)])


def shape_of(shape, dtype):
    return jax.ShapeDtypeStruct(shape, dtype)


def after(value, *others):
    return lax.optimization_barrier((value, *others))[0]


def kept(shape, dtype):
    return pltpu.VMEM(shape, dtype)


def pinned(array):
    return pltpu.with_memory_space_constraint(array, pltpu.VMEM)


def kernel_call(body, name, outs, ins, far=(), scratch=(), result=pltpu.VMEM, earlier=()):
    aliases = {len(ins) + index: index for index in range(len(earlier))}
    ins = [*ins, *(pinned(array) for array in earlier)]
    spaces = [pltpu.VMEM] * len(ins)
    for index in far:
        spaces[index] = pl.ANY
        ins[index] = pltpu.with_memory_space_constraint(ins[index], pltpu.HBM)
    return pl.pallas_call(
        body,
        name=name,
        out_shape=outs,
        in_specs=[pl.BlockSpec(memory_space=space) for space in spaces],
        out_specs=[pl.BlockSpec(memory_space=result)] * len(outs),
        scratch_shapes=scratch,
        input_output_aliases=aliases,
        compiler_params=pltpu.CompilerParams(vmem_limit_bytes=8 * MIB),
        cost_estimate=pl.CostEstimate(flops=1, bytes_accessed=1, transcendentals=0),
    )(*ins)


def split_low(values):
    high = values.astype(jnp.bfloat16)
    rest = values - high.astype(jnp.float32)
    middle = rest.astype(jnp.bfloat16)
    low = (rest - middle.astype(jnp.float32)).astype(jnp.bfloat16)
    return high, middle, low


def exact_dot(values, low_matrix, contract):
    parts = lax.dot_general(
        jnp.concatenate(split_low(values), axis=0),
        low_matrix,
        contract,
        preferred_element_type=jnp.float32,
    )
    return parts[0:8] + parts[8:16] + parts[16:24]


def other_order(values, bits):
    return jnp.concatenate([values[row ^ bits : (row ^ bits) + 1] for row in range(4)], axis=0)


def norm_kernel(
    hidden_far, gain_far, router_far, final_far, vector_far,
    hidden_ref, gain_ref, router_ref, normed_ref, sums_ref, head_ref,
    final_ref, vector_ref, copy_sems,
):
    pairs = (
        (hidden_far, hidden_ref), (gain_far, gain_ref), (router_far, router_ref),
        (final_far, final_ref), (vector_far, vector_ref),
    )
    copies = [
        pltpu.make_async_copy(source, target, copy_sems.at[index])
        for index, (source, target) in enumerate(pairs)
    ]
    for copy in copies:
        copy.start()
    for copy in copies:
        copy.wait()
    vector = vector_ref[...].astype(jnp.float32)
    vector = jnp.concatenate([vector[row : row + 1] for row in range(vector.shape[0])], axis=1)
    head_ref[...] = final_ref[...] * vector
    rows = hidden_ref[...].astype(jnp.float32)
    normed_ref[...] = (rows * rms_scale(rows) * gain_ref[...]).astype(jnp.bfloat16)
    sums_ref[...] = jnp.sum(rows, axis=0, keepdims=True)


def on_side(side, body, held, far_count, *refs):
    refs = refs[:far_count] + refs[far_count + held :]

    @pl.when(lax.rem(lax.axis_index("exp"), 2) == side)
    def run():
        body(*refs)


def front_kernel(stage, owners, sets, count, router_ref, *refs):
    matrices, refs = refs[: 2 * len(sets)], refs[2 * len(sets) :]
    pieces, refs = refs[:count], refs[count:]
    matrices = list(matrices)
    hidden_units = matrices[0].shape[1]
    tile = 256
    firsts = range(0, hidden_units, tile)
    if stage == 0:
        far_matrices = matrices
        *refs, gate_held, up_held, rows_ref, copy_sems = refs
        matrices = [gate_held, up_held]
        copies = [
            pltpu.make_async_copy(
                source.at[:, first : first + tile],
                target.at[:, first : first + tile],
                copy_sems.at[which, number],
            )
            for number, first in enumerate(firsts)
            for which, (source, target) in enumerate(zip(far_matrices, matrices))
        ]
        for copy in copies:
            copy.start()
        turned_ref, *refs = refs
    elif stage == 3:
        sums_ref, *downs = refs[:3]
        earlier, refs = refs[3:6], refs[6:]
        *refs, terms_ref, rows_ref = refs
    else:
        *refs, rows_ref = refs
    gates_ref, *outs = refs
    expert = lax.axis_index("exp")
    first = 0
    for piece in pieces:
        rows_ref[first : first + piece.shape[0], :] = piece[...]
        first += piece.shape[0]
    size = first // len(owners)
    logits = lax.dot_general(
        rows_ref[...], router_ref[...], across, preferred_element_type=jnp.float32
    )
    weights = jnp.exp(logits)
    gates = weights / jnp.sum(weights, axis=1, keepdims=True)
    gates_ref[...] = gates
    lane = lax.broadcasted_iota(jnp.int32, gates.shape, 1)
    if stage == 0:
        weights = jnp.exp(
            lax.dot_general(
                router_ref[...], rows_ref[...], across, preferred_element_type=jnp.float32
            )
        )
        turned_ref[...] = weights / jnp.sum(weights, axis=0, keepdims=True)

    totals = []
    for place, which in enumerate(sets):
        gate_ref, up_ref = matrices[2 * place : 2 * place + 2]
        if stage == 3:
            slope_ref, silu_ref, act_ref = outs[3 * place : 3 * place + 3]
        else:
            slope_ref, silu_ref, act_ref, part_ref = outs
        own = jnp.sum(jnp.where(lane == expert ^ which, gates, 0.0), axis=1, keepdims=True)
        low = own.astype(jnp.bfloat16).astype(jnp.float32)
        parts = []
        for number, first in enumerate(firsts):
            columns = slice(first, first + tile)
            if stage == 0:
                copies[2 * number].wait()
                copies[2 * number + 1].wait()
            rows = rows_ref[...]
            pre_gate = jnp.dot(rows, gate_ref[:, columns], preferred_element_type=jnp.float32)
            pre_up = jnp.dot(rows, up_ref[:, columns], preferred_element_type=jnp.float32)
            silu_gate, slope = gate_parts(pre_gate)
            activation = (silu_gate * pre_up).astype(jnp.bfloat16)
            slope_ref[:, columns] = slope * pre_up
            silu_ref[:, columns] = silu_gate
            act_ref[:, columns] = activation
            weighted = activation.astype(jnp.float32) * low
            found = {
                owner: jnp.sum(weighted[index * size : (index + 1) * size], axis=0, keepdims=True)
                for index, owner in enumerate(owners)
            }
            nothing = jnp.zeros_like(weighted[:1])
            parts.append(
                jnp.concatenate([found.get(owner, nothing) for owner in range(8)], axis=0)
            )
        totals.append(jnp.concatenate(parts, axis=1))
    if stage < 3:
        part_ref[...] = totals[0]
        return
    own_first, own_second, other_first = earlier
    totals[0] = totals[0] + (own_first[...] + own_second[...])
    totals[1] = totals[1] + other_first[...]
    terms = exact_dot(totals[0], downs[0][...], forward) + exact_dot(
        totals[1], downs[1][...], forward
    )
    row = lax.broadcasted_iota(jnp.int32, terms.shape, 0)
    terms_ref[...] = (terms + jnp.where(row == 0, sums_ref[...], 0.0))[:4]


def front(stage, owners, sets, pieces, router_rows, matrices, more=(), side=None, earlier=()):
    model_width, hidden_units = matrices[0].shape
    row_total = sum(piece.shape[0] for piece in pieces)
    outs = [kept((row_total, 8), jnp.float32)]
    if stage == 0:
        outs.insert(0, kept((8, row_total), jnp.float32))
    for which in sets:
        outs += [
            kept((row_total, hidden_units), jnp.float32),
            kept((row_total, hidden_units), jnp.float32),
            kept((row_total, hidden_units), jnp.bfloat16),
        ]
    outs.append(
        kept((4, model_width), jnp.float32) if stage == 3 else kept((8, hidden_units), jnp.float32)
    )
    scratch = [pltpu.VMEM((row_total, model_width), jnp.bfloat16)]
    far = ()
    if stage == 0:
        far = (1, 2)
        outs += [kept(matrix.shape, jnp.bfloat16) for matrix in matrices]
        scratch.append(pltpu.SemaphoreType.DMA((2, hidden_units // 256)))
    else:
        matrices = [pinned(matrix) for matrix in matrices]
    if stage == 3:
        more = [pinned(array) for array in more]
    body = functools.partial(front_kernel, stage, owners, sets, len(pieces))
    ins = [pinned(router_rows), *matrices, *(pinned(piece) for piece in pieces), *more]
    if side is not None:
        body = functools.partial(on_side, side, body, len(earlier), len(ins))
    return kernel_call(body, "front", outs, ins, far, scratch, earlier=earlier)


def near_kernel(
    own_ref, x_ref, y_ref, far_ref, head_ref, down_ref, other_down_ref,
    near_ref, other_near_ref, unit_ref, score_ref, own_score_ref, *, token_count,
):
    pooled = (
        (own_ref[...] + other_order(x_ref[...], 1))
        + (other_order(y_ref[...], 2) + other_order(far_ref[...], 3))
    ) / token_count
    pooled = jnp.concatenate([pooled, jnp.zeros_like(pooled)], axis=0)
    head = head_ref[...]
    scale = rms_scale(pooled)
    along = jnp.sum(pooled * head, axis=1, keepdims=True)
    own_score = (scale * along)[:1]
    own_score_ref[...] = own_score
    score_ref[...] = jnp.broadcast_to(own_score, score_ref.shape)
    unit = (
        scale * head - scale * scale * scale * (along / pooled.shape[1]) * pooled
    ) / token_count
    unit_ref[...] = unit[:1]
    near_ref[...] = exact_dot(unit, down_ref[...], forward)
    other_near_ref[...] = exact_dot(unit, other_down_ref[...], forward)


def back_kernel(passages, gate_count, saved_count, near_ref, other_near_ref, *refs):
    gates_refs, refs = refs[:gate_count], refs[gate_count:]
    saved, refs = refs[: 3 * saved_count], refs[3 * saved_count :]
    matrices, refs = refs[:4], refs[4:]
    *out_refs, d_gate_ref, d_up_ref, other_d_gate_ref, other_d_up_ref = refs
    expert = lax.axis_index("exp")
    size = out_refs[0].shape[1]
    model_width = matrices[0].shape[1]
    lane = lax.broadcasted_iota(jnp.int32, (size, 8), 1)
    line = lax.broadcasted_iota(jnp.int32, (16, size), 0)
    experts = (
        (near_ref, d_gate_ref, d_up_ref), (other_near_ref, other_d_gate_ref, other_d_up_ref)
    )
    sides = (d_gate_ref, d_up_ref, other_d_gate_ref, other_d_up_ref)
    for index, (owner, gates_place, saved_places, windows, unused) in enumerate(passages):
        rows = slice(index * size, (index + 1) * size)
        lines = jnp.zeros((16, size), jnp.float32)
        gates = gates_refs[gates_place[0]][gates_place[1] : gates_place[1] + size, :]
        for which, (table_ref, d_gate_out, d_up_out) in enumerate(experts):
            number, first = saved_places[which]
            slope_ref, silu_ref, act_ref = saved[3 * number : 3 * number + 3]
            held = slice(first, first + size)
            near = table_ref[owner : owner + 1, :]
            own = jnp.sum(
                jnp.where(lane == expert ^ which, gates, 0.0), axis=1, keepdims=True
            )
            d_act = own.astype(jnp.bfloat16).astype(jnp.float32) * near
            d_gate_out[rows, :] = (d_act * slope_ref[held, :]).astype(jnp.bfloat16)
            d_up_out[rows, :] = (d_act * silu_ref[held, :]).astype(jnp.bfloat16)
            if windows[-1][1] == model_width:
                gate_grad = exact_dot(table_ref[...], act_ref[held, :], across)
                lines = jnp.where(line == expert ^ which, gate_grad[owner : owner + 1], lines)
        for start, stop in windows:
            out_ref, *out_refs = out_refs
            used = stop - start
            if stop == model_width:
                out_ref[used : used + 16, :] = lines.astype(jnp.bfloat16)
                used += 16
            if out_ref.shape[0] > used:
                out_ref[used:, :] = jnp.zeros((out_ref.shape[0] - used, size), jnp.bfloat16)
            for first in range(start, stop, 256):
                pick_grad = None
                for side_ref, matrix in zip(sides, matrices):
                    term = jnp.dot(
                        side_ref[rows, :],
                        matrix[:, first : first + 256],
                        preferred_element_type=jnp.float32,
                    )
                    pick_grad = term if pick_grad is None else pick_grad + term
                out_ref[first - start : first - start + 256, :] = pick_grad.T.astype(jnp.bfloat16)


def back(passages, near, other_near, gates, saved, matrices, size):
    hidden_units, model_width = matrices[0].shape
    heights = [
        max(least, stop - start + (16 if stop == model_width else 0))
        for passage in passages
        for (start, stop), least in zip(*passage[3:])
    ]
    arrays = [array for group in saved for array in group]
    return kernel_call(
        functools.partial(back_kernel, passages, len(gates), len(saved)),
        "back",
        [kept((height, size), jnp.bfloat16) for height in heights],
        [pinned(array) for array in (near, other_near, *gates, *arrays, *matrices)],
        (),
        [pltpu.VMEM((len(passages) * size, hidden_units), jnp.bfloat16)] * 4,
    )


def add_kernel(x_ref, y_ref, high_ref, low_ref, x_out, y_out):
    for own_ref, other_ref, out_ref in ((x_ref, high_ref, x_out), (y_ref, low_ref, y_out)):
        out_ref[...] = (
            own_ref[...].astype(jnp.float32)
            + other_ref[: own_ref.shape[0], :].astype(jnp.float32)
        ).astype(jnp.bfloat16)


def turn_kernel(*refs):
    count = len(refs) // 2
    for source_ref, target_ref in zip(refs[:count], refs[count:]):
        for first in range(0, source_ref.shape[0], 256):
            rows = slice(first, first + 256)
            target_ref[:, rows] = source_ref[rows, :].T


def turn(matrices):
    return kernel_call(
        turn_kernel,
        "turn",
        [kept(matrix.shape[::-1], jnp.bfloat16) for matrix in matrices],
        [pinned(matrix) for matrix in matrices],
    )


def half_kernel(part, rows_ref, out_ref):
    half = out_ref.shape[0]
    out_ref[...] = rows_ref[part * half : (part + 1) * half, :]


def half_of(rows, part):
    total, wide = rows.shape
    (out,) = kernel_call(
        functools.partial(half_kernel, part), "half", [kept((total // 2, wide), rows.dtype)], [rows]
    )
    return out


def pack_kernel(first_ref, second_ref, out_ref):
    out_ref[:1, :] = first_ref[:1, :]
    out_ref[1:, :] = second_ref[:1, :]


def pack(first, second):
    return kernel_call(
        pack_kernel, "pack", [kept((2, first.shape[1]), first.dtype)], [pinned(first), second]
    )[0]


def pairs_of(passages):
    row = lax.broadcasted_iota(jnp.int32, (8, 128), 0)
    lane = lax.broadcasted_iota(jnp.int32, (8, 128), 1)
    return row, lane, jnp.logical_and(row < passages, lane < passages)


def spread(index, values):
    total = jnp.zeros((8, 128), jnp.float32)
    for number, value in values:
        total = jnp.where(index == number, value, total)
    return total


def whole_sum(values):
    return jnp.sum(jnp.sum(values, axis=1, keepdims=True), axis=0, keepdims=True)


def pair_kernel(
    grades_far, ranks_far, down_far, swap_gain_ref, down_ref, grades_ref, ranks_ref, copy_sems
):
    down_copy = pltpu.make_async_copy(down_far, down_ref, copy_sems.at[2])
    down_copy.start()
    copies = [
        pltpu.make_async_copy(grades_far, grades_ref, copy_sems.at[0]),
        pltpu.make_async_copy(ranks_far, ranks_ref, copy_sems.at[1]),
    ]
    for copy in copies:
        copy.start()
    for copy in copies:
        copy.wait()
    passages = grades_ref.shape[1]
    row, lane, pair = pairs_of(passages)
    grade_list = [(number, grades_ref[0, number].astype(jnp.float32)) for number in range(passages)]
    rank_list = [(number, ranks_ref[0, number].astype(jnp.float32)) for number in range(passages)]
    grade_row, grade_lane = spread(row, grade_list), spread(lane, grade_list)
    worth_row, worth_lane = jnp.exp2(grade_row), jnp.exp2(grade_lane)
    discount_row = 1.0 / jnp.log2(2.0 + spread(row, rank_list))
    discount_lane = 1.0 / jnp.log2(2.0 + spread(lane, rank_list))
    ahead = jnp.logical_or(
        grade_lane > grade_row, jnp.logical_and(grade_lane == grade_row, lane < row)
    )
    ideal_rank = jnp.sum(
        jnp.where(jnp.logical_and(pair, ahead), 1.0, 0.0), axis=1, keepdims=True
    )
    ideal_terms = (worth_row - 1.0) / jnp.log2(2.0 + ideal_rank)
    one_lane = jnp.logical_and(pair, lane == 0)
    ideal_gain = whole_sum(jnp.where(one_lane, ideal_terms, 0.0))
    swap_gain = (
        jnp.abs((worth_row - worth_lane) * (discount_row - discount_lane)) / ideal_gain
    )
    swap_gain_ref[...] = jnp.where(
        jnp.logical_and(pair, grade_row > grade_lane), swap_gain, 0.0
    )
    down_copy.wait()


def rank_kernel(swap_gain_ref, near_scores_ref, far_scores_ref, loss_ref, factor_ref):
    passages = 2 * near_scores_ref.shape[0]
    place = lax.axis_index("psg")
    row, lane, unused = pairs_of(passages)
    score_list = [
        (place ^ (base + number), jnp.broadcast_to(ref[number : number + 1, :], (8, 128)))
        for base, ref in ((0, near_scores_ref), (passages // 2, far_scores_ref))
        for number in range(passages // 2)
    ]
    swap_gain = swap_gain_ref[...]
    margin = spread(row, score_list) - spread(lane, score_list)
    softplus = jnp.maximum(-margin, 0.0) + jnp.log1p(jnp.exp(-jnp.abs(margin)))
    loss_ref[...] = whole_sum(swap_gain * softplus)
    pull = swap_gain * jax.nn.sigmoid(-margin)
    gradient = whole_sum(jnp.where(lane == place, pull, 0.0) - jnp.where(row == place, pull, 0.0))
    factor_ref[...] = jnp.broadcast_to(gradient * loss_scale, factor_ref.shape)


def first_end_kernel(own_ref, x_low_ref, y_high_ref, total_ref, lines_ref):
    model_width = total_ref.shape[1]
    cut = model_width // 2
    for first in range(0, model_width, 256):
        rows = slice(first, first + 256)
        if first < cut:
            term = x_low_ref[rows, :]
        else:
            term = y_high_ref[first - cut : first - cut + 256, :]
        total = own_ref[rows, :].astype(jnp.float32) + term.astype(jnp.float32)
        total_ref[:, rows] = total.T
    end = slice(model_width, model_width + 8)
    end_high = slice(model_width - cut, model_width - cut + 8)
    lines_ref[...] = own_ref[end, :].astype(jnp.float32) + y_high_ref[end_high, :].astype(
        jnp.float32
    )


def end_kernel(
    factor_ref, total_ref, lines_ref, x_high_ref, y_low_ref,
    hidden_ref, gain_ref, gates_ref, router_ref, unit_ref,
    grad_far, turned_ref, grad_ref, copy_sems,
):
    token_count, model_width = hidden_ref.shape
    cut = y_low_ref.shape[0]
    end_high = slice(model_width - cut, model_width - cut + 8)
    slot_grad = lines_ref[...] + x_high_ref[end_high, :].astype(jnp.float32)
    gates = gates_ref[...]
    d_logit = gates * (slot_grad - jnp.sum(gates * slot_grad, axis=0, keepdims=True))
    d_logit = jnp.concatenate([d_logit, jnp.zeros((120, token_count), jnp.float32)], axis=0).T
    d_logit = jnp.concatenate(split_low(d_logit[:, :8]), axis=1)
    router_rows = jnp.concatenate([router_ref[...]] * 3, axis=0)
    for first in range(0, model_width, 256):
        columns = slice(first, first + 256)
        if first < cut:
            term = y_low_ref[columns, :]
        else:
            term = x_high_ref[first - cut : first - cut + 256, :]
        turned_ref[:, columns] = (
            total_ref[:, columns]
            + term.astype(jnp.float32).T
            + jnp.dot(d_logit, router_rows[:, columns], preferred_element_type=jnp.float32)
        )
    gain = gain_ref[...]
    factor = factor_ref[:, :1]
    size = 16
    copies = []
    for first in range(0, token_count, size):
        rows = slice(first, first + size)
        flat_rows = hidden_ref[rows, :].astype(jnp.float32)
        grad = norm_back(flat_rows, rms_scale(flat_rows), gain, turned_ref[rows, :])
        grad_ref[rows, :] = ((grad + unit_ref[...]) * factor).astype(jnp.bfloat16)
        copies.append(
            pltpu.make_async_copy(
                grad_ref.at[rows, :], grad_far.at[rows, :], copy_sems.at[first // size]
            )
        )
        copies[-1].start()
    for copy in copies:
        copy.wait()


def every_expert(
    hidden,
    norm_gain,
    router,
    gate_proj,
    up_proj,
    down_proj,
    final_gain,
    score_vector,
    expert_ids,
    grades,
    passage_ranks,
):
    unused_query, unused_passage, token_count, model_width = hidden.shape
    passages = grades.shape[1]
    flat = hidden.reshape(token_count, model_width)
    gate_matrix, up_matrix, down_matrix = gate_proj[0], up_proj[0], down_proj[0]
    mine = [gate_matrix, up_matrix, down_matrix]
    flat, gain, router_rows, normed, token_sums, head = kernel_call(
        norm_kernel,
        "norm",
        [
            kept(flat.shape, jnp.bfloat16),
            kept((1, model_width), jnp.float32),
            kept((8, model_width), jnp.bfloat16),
            kept(flat.shape, jnp.bfloat16),
            kept((1, model_width), jnp.float32),
            kept((1, model_width), jnp.float32),
        ],
        [
            flat,
            norm_gain.reshape(1, model_width),
            router.T,
            final_gain.reshape(1, model_width),
            score_vector.reshape(model_width // 128, 128),
        ],
        range(5),
        [
            pltpu.VMEM((1, model_width), jnp.float32),
            pltpu.VMEM((model_width // 128, 128), jnp.bfloat16),
            pltpu.SemaphoreType.DMA((5,)),
        ],
    )
    others = [swap(matrix, CORE) for matrix in mine]
    def own_front(side, *earlier):
        arrays = front(
            0, (0,), (0,), [normed], router_rows, [gate_matrix, up_matrix], (), side, earlier[:8]
        )
        ins = [grades, passage_ranks, down_matrix]
        body = functools.partial(on_side, side, pair_kernel, len(earlier[8:]), len(ins))
        pairs = kernel_call(
            body,
            "pairs",
            [kept((8, 128), jnp.float32), kept(down_matrix.shape, jnp.bfloat16)],
            ins,
            (0, 1, 2),
            [
                pltpu.SMEM(grades.shape, jnp.int32),
                pltpu.SMEM(grades.shape, jnp.int32),
                pltpu.SemaphoreType.DMA((3,)),
            ],
            earlier=earlier[8:],
        )
        return [*arrays, *pairs]

    arrays = own_front(1)
    normed, *arrays = lax.optimization_barrier((normed, *arrays))
    x_rows, y_rows = swap(normed, ACROSS_X), swap(normed, ACROSS_Y)
    arrays = own_front(0, *arrays)
    turned_gates, own_gates, *own_saved, own_part, mine[0], mine[1], swap_gain, mine[2] = arrays
    *mine_turned, down_turned = turn(mine)
    x_rows, y_rows = after(x_rows, mine_turned[0]), after(y_rows, mine_turned[0])
    far_low = swap(half_of(x_rows, 0), ACROSS_Y)
    far_high = swap(half_of(y_rows, 1), ACROSS_X)
    side_gates, *side_saved, side_part = front(
        1, (1, 2), (0,), [x_rows, y_rows], router_rows, mine[:2]
    )
    others[0] = after(others[0], side_part)
    unused, *other_saved, other_part = front(
        2, (0, 1, 2), (1,), [normed, x_rows, y_rows], router_rows, others[:2]
    )
    far_low, far_high = after(far_low, other_part), after(far_high, other_part)
    far_gates, *far_saved, terms = front(
        3, (3,), (0, 1), [far_low, far_high], router_rows, mine[:2] + others[:2],
        (token_sums, mine[2], others[2], own_part, side_part, other_part),
    )

    *others_turned, other_down_turned = turn([after(others[0], terms), *others[1:]])
    head = after(head, others_turned[0])
    near, other_near, unit_vector, travelling, own_score = kernel_call(
        functools.partial(near_kernel, token_count=token_count),
        "near",
        [
            kept((8, down_matrix.shape[0]), jnp.float32),
            kept((8, down_matrix.shape[0]), jnp.float32),
            kept((1, model_width), jnp.float32),
            kept((1, 128), jnp.float32),
            shape_of((1, 1), jnp.float32),
        ],
        [
            pinned(terms),
            swap(terms, ACROSS_X),
            swap(terms, ACROSS_Y),
            swap(terms, ACROSS_X | ACROSS_Y),
            pinned(head),
            pinned(down_turned),
            pinned(other_down_turned),
        ],
    )
    matrices = [*mine_turned, *others_turned]
    middle = model_width // 2
    lower, upper, early, earlier = (0, middle), (middle, model_width), middle + 32, middle + 64
    far_low, far_high = back(
        ((3, (0, 0), ((0, 0), (1, 0)), (lower, upper), (earlier, earlier)),),
        near, other_near, [far_gates], [far_saved[:3], far_saved[3:]], matrices, token_count,
    )
    far_sent = far_low
    far_low, far_high = swap(far_low, ACROSS_X), swap(far_high, ACROSS_Y)

    def sides_back(x_window, y_window, least, *earlier):
        return back(
            (
                (1, (0, 0), ((0, 0), (1, token_count)), (x_window,), (least,)),
                (2, (0, token_count), ((0, token_count), (1, 2 * token_count)), (y_window,), (least,)),
            ),
            after(near, *earlier), other_near, [side_gates], [side_saved, other_saved], matrices,
            token_count,
        )

    x_low, y_high = sides_back(lower, upper, early, far_sent)
    first_sent = x_low
    x_low, y_high = swap(x_low, ACROSS_X), swap(y_high, ACROSS_Y)
    x_high, y_low = sides_back(upper, lower, 0, first_sent)
    travelling = after(travelling, first_sent)
    met = lax.ppermute(travelling, "psg", [(index, index ^ 1) for index in range(passages)])
    near_scores = pack(travelling, met)
    far_high = after(far_high, near_scores)
    x_high, y_low = kernel_call(
        add_kernel,
        "add",
        [kept(x_high.shape, jnp.bfloat16), kept(y_low.shape, jnp.bfloat16)],
        [pinned(x_high), pinned(y_low), far_high, far_low],
    )
    x_high, y_low, near_scores, other_near = lax.optimization_barrier(
        (x_high, y_low, near_scores, other_near)
    )
    x_high, y_low = swap(x_high, ACROSS_X), swap(y_low, ACROSS_Y)
    (own_sums,) = back(
        ((0, (0, 0), ((0, 0), (1, 0)), ((0, model_width),), (0,)),),
        near, other_near, [own_gates], [own_saved, other_saved], matrices, token_count,
    )
    far_scores = lax.ppermute(near_scores, "psg", [(index, index ^ 2) for index in range(passages)])
    loss, factor = kernel_call(
        rank_kernel,
        "rank",
        [shape_of((1, 1), jnp.float32), kept((1, 128), jnp.float32)],
        [pinned(swap_gain), pinned(near_scores), far_scores],
    )
    total, lines = kernel_call(
        first_end_kernel,
        "first_end",
        [
            kept((token_count, model_width), jnp.float32),
            kept((8, token_count), jnp.float32),
        ],
        [pinned(own_sums), after(x_low, factor), y_high],
    )
    (grad,) = kernel_call(
        end_kernel,
        "end",
        [shape_of((token_count, model_width), jnp.bfloat16)],
        [
            pinned(factor), pinned(total), pinned(lines), x_high, y_low, pinned(flat), pinned(gain),
            pinned(turned_gates), pinned(router_rows), pinned(unit_vector),
        ],
        scratch=[
            pltpu.VMEM((token_count, model_width), jnp.float32),
            pltpu.VMEM((token_count, model_width), jnp.bfloat16),
            pltpu.SemaphoreType.DMA((token_count // 16,)),
        ],
        result=pl.ANY,
    )
    return (loss.reshape(1), own_score, grad.reshape(hidden.shape))


def block(*arrays):
    hidden, router, expert_ids, grades = arrays[0], arrays[2], arrays[8], arrays[9]
    each_expert = router.shape[1] == expert_ids.shape[3] == 8
    if hidden.shape[1] == 1 and each_expert and grades.shape[1] == 4:
        return every_expert(*arrays)
    return local(*arrays)


def solution(mesh):
    placed = (
        P("exp", "psg", None, None),
        P(),
        P(),
        P("exp", None, None),
        P("exp", None, None),
        P("exp", None, None),
        P(),
        P(),
        P("exp", "psg", None, None),
        P("exp", None),
        P("exp", None),
    )
    return jax.shard_map(
        block,
        mesh=mesh,
        in_specs=placed,
        out_specs=(P("exp"), P("exp", "psg"), P("exp", "psg", None, None)),
        check_vma=False,
    )
```

```python
import functools
import math

import jax
import jax.numpy as jnp
from jax import lax
from jax.experimental import pallas as pl
from jax.experimental.pallas import tpu as pltpu
from jax.sharding import PartitionSpec as P

epsilon = 1e-06
loss_scale = 256.0
highest = lax.Precision.HIGHEST


def rms_scale(values):
    return lax.rsqrt(jnp.mean(values * values, axis=-1, keepdims=True) + epsilon)


def head_score(pooled, final_gain, score_vector):
    scaled = pooled * rms_scale(pooled) * final_gain
    return jnp.dot(scaled, score_vector.astype(jnp.float32), precision=highest)


def rank_loss(scores, grades, passage_ranks):
    grade_value = grades.astype(jnp.float32)
    worth_gain = jnp.exp2(grade_value)
    discount = 1.0 / jnp.log2(2.0 + passage_ranks.astype(jnp.float32))
    better_than = grades[None, :] > grades[:, None]
    equal_grade = grades[None, :] == grades[:, None]
    position = jnp.arange(grades.shape[0], dtype=jnp.int32)
    earlier = position[None, :] < position[:, None]
    ideal_rank = jnp.sum(
        jnp.logical_or(better_than, jnp.logical_and(equal_grade, earlier)).astype(jnp.float32),
        axis=1,
    )
    ideal_gain = jnp.sum((worth_gain - 1.0) / jnp.log2(2.0 + ideal_rank))
    ordered = (grades[:, None] > grades[None, :]).astype(jnp.float32)
    swap_gain = (
        jnp.abs(
            (worth_gain[:, None] - worth_gain[None, :]) * (discount[:, None] - discount[None, :])
        )
        / ideal_gain
    )
    margin = scores[:, None] - scores[None, :]
    return jnp.sum(ordered * swap_gain * jax.nn.softplus(-margin))


def pick_gates(normed, router, picked_ids):
    expert_total = router.shape[1]
    logits = jnp.dot(normed, router, preferred_element_type=jnp.float32)
    onehot = (
        picked_ids[:, :, None] == jnp.arange(expert_total, dtype=jnp.int32)[None, None, :]
    ).astype(jnp.float32)
    chosen = jnp.einsum("nke,ne->nk", onehot, logits, precision=highest)
    weights = jnp.exp(chosen)
    return (weights / jnp.sum(weights, axis=1, keepdims=True), onehot)


def gate_parts(pre_gate):
    sigmoid_gate = jax.nn.sigmoid(pre_gate)
    return (pre_gate * sigmoid_gate, sigmoid_gate * (1.0 + pre_gate * (1.0 - sigmoid_gate)))


def norm_back(flat_rows, inverse, norm_gain, d_normed):
    scaled = d_normed * norm_gain
    return inverse * scaled - flat_rows * inverse * inverse * inverse * jnp.mean(
        flat_rows * scaled, axis=-1, keepdims=True
    )


def unpack_front(front_out, buffer_rows):
    pre_gate, pre_up, received = front_out
    hidden_units = pre_gate.shape[2]
    pre_gate = pre_gate.reshape(buffer_rows, hidden_units)
    pre_up = pre_up.reshape(buffer_rows, hidden_units)
    silu_gate, slope = gate_parts(pre_gate)
    activation = (silu_gate * pre_up).astype(jnp.bfloat16)
    return (pre_up, received, silu_gate, slope, activation)


def local(
    hidden,
    norm_gain,
    router,
    gate_proj,
    up_proj,
    down_proj,
    final_gain,
    score_vector,
    expert_ids,
    grades,
    passage_ranks,
):
    unused_query, local_passages, local_positions, model_width = hidden.shape
    top_count = expert_ids.shape[3]
    expert_count = lax.axis_size("exp")
    token_count = local_passages * local_positions
    slot_count = token_count * top_count
    capacity = min(token_count, 9 * token_count * top_count // (8 * expert_count))
    buffer_rows = expert_count * capacity
    flat_rows = hidden.reshape(token_count, model_width).astype(jnp.float32)
    inverse = rms_scale(flat_rows)
    normed = (flat_rows * inverse * norm_gain).astype(jnp.bfloat16)
    picked_ids = expert_ids.reshape(token_count, top_count)
    gate_values, onehot = pick_gates(normed, router, picked_ids)
    slot_hits = onehot.reshape(slot_count, expert_count).astype(jnp.int32)
    slot_rank = jnp.sum((jnp.cumsum(slot_hits, axis=0) - slot_hits) * slot_hits, axis=1)
    target = picked_ids.reshape(slot_count) * capacity + slot_rank
    source_token = jnp.arange(slot_count, dtype=jnp.int32) // top_count
    passage_onehot = (
        source_token[:, None] // local_positions
        == jnp.arange(local_passages, dtype=jnp.int32)[None, :]
    ).astype(jnp.float32)
    weighted = (passage_onehot * gate_values.reshape(slot_count, 1)).astype(jnp.bfloat16)
    send_rows = (
        jnp.zeros((buffer_rows, model_width), jnp.bfloat16).at[target].set(normed[source_token])
    )
    send_weights = jnp.zeros((buffer_rows, local_passages), jnp.bfloat16).at[target].set(weighted)
    outgoing = (
        send_rows.reshape(expert_count, capacity, model_width),
        send_weights.reshape(expert_count, capacity, local_passages),
    )
    gate_matrix = gate_proj[0]
    up_matrix = up_proj[0]
    down_matrix = down_proj[0]
    rows_in = lax.all_to_all(outgoing[0], "exp", split_axis=0, concat_axis=0, tiled=True)
    weights_in = lax.all_to_all(outgoing[1], "exp", split_axis=0, concat_axis=0, tiled=True)
    pre_gate = jnp.einsum("end,df->enf", rows_in, gate_matrix, preferred_element_type=jnp.float32)
    pre_up = jnp.einsum("end,df->enf", rows_in, up_matrix, preferred_element_type=jnp.float32)
    front_out = (pre_gate, pre_up, weights_in)
    pre_up, received, silu_gate, slope, activation = unpack_front(front_out, buffer_rows)
    hidden_units = activation.shape[1]
    passage_part = jnp.einsum(
        "scp,scf->spf",
        received,
        activation.reshape(expert_count, capacity, hidden_units),
        preferred_element_type=jnp.float32,
    )
    down_wide = down_matrix.astype(jnp.float32)
    expert_terms = jnp.einsum("spf,fd->spd", passage_part, down_wide, precision=highest)
    came_back = lax.all_to_all(expert_terms, "exp", split_axis=0, concat_axis=0, tiled=True)
    token_sums = jnp.sum(flat_rows.reshape(local_passages, local_positions, model_width), axis=1)
    pooled = (token_sums + jnp.sum(came_back, axis=0)) / local_positions
    first_row = lax.axis_index("psg") * local_passages
    own_score = head_score(pooled, final_gain, score_vector)
    every_score = lax.all_gather(own_score, "psg", axis=0, tiled=True)
    loss_value, loss_grad = jax.value_and_grad(rank_loss)(every_score, grades[0], passage_ranks[0])
    d_own = lax.dynamic_slice_in_dim(loss_grad, first_row, local_passages, 0) * loss_scale
    unused_score, head_back = jax.vjp(
        lambda values: head_score(values, final_gain, score_vector), pooled
    )
    d_vector = head_back(d_own)[0] / local_positions
    every_vector = lax.all_gather(d_vector[None], "exp", axis=0, tiled=True)
    near_table = jnp.einsum("spd,fd->spf", every_vector, down_wide, precision=highest)
    present = (received != 0).astype(jnp.float32)
    near_rows = jnp.einsum("scp,spf->scf", present, near_table, precision=highest).reshape(
        buffer_rows, hidden_units
    )
    gate_weight = jnp.sum(received.astype(jnp.float32), axis=2).reshape(buffer_rows, 1)
    d_act = gate_weight * near_rows
    d_gate = (d_act * pre_up * slope).astype(jnp.bfloat16)
    d_up = (d_act * silu_gate).astype(jnp.bfloat16)
    contract = (((1,), (1,)), ((), ()))
    pick_grad = lax.dot_general(d_gate, gate_matrix, contract, preferred_element_type=jnp.float32)
    pick_grad = (
        pick_grad + lax.dot_general(d_up, up_matrix, contract, preferred_element_type=jnp.float32)
    ).astype(jnp.bfloat16)
    gate_grad = jnp.sum(activation.astype(jnp.float32) * near_rows, axis=1).astype(jnp.bfloat16)
    back_rows, back_gate = (
        lax.all_to_all(
            pick_grad.reshape(expert_count, capacity, model_width),
            "exp",
            split_axis=0,
            concat_axis=0,
            tiled=True,
        ),
        lax.all_to_all(
            gate_grad.reshape(expert_count, capacity),
            "exp",
            split_axis=0,
            concat_axis=0,
            tiled=True,
        ),
    )
    picked_rows = back_rows.reshape(buffer_rows, model_width)[target]
    d_normed = jnp.sum(
        picked_rows.reshape(token_count, top_count, model_width).astype(jnp.float32), axis=1
    )
    picked_gate = (
        back_gate.reshape(buffer_rows)[target].astype(jnp.float32).reshape(token_count, top_count)
    )
    d_logit = gate_values * (
        picked_gate - jnp.sum(gate_values * picked_gate, axis=1, keepdims=True)
    )
    dense_logit = jnp.einsum("nk,nke->ne", d_logit, onehot, precision=highest)
    d_normed = d_normed + jnp.einsum(
        "ne,de->nd", dense_logit, router.astype(jnp.float32), precision=highest
    )
    grad_flat = norm_back(flat_rows, inverse, norm_gain, d_normed)
    grad_hidden = (
        grad_flat.reshape(1, local_passages, local_positions, model_width)
        + d_vector[None, :, None, :]
    )
    return (
        loss_value.reshape(1),
        own_score.reshape(1, local_passages),
        grad_hidden.astype(jnp.bfloat16),
    )


CORE, ACROSS_X, ACROSS_Y = 1, 2, 4
forward = (((1,), (0,)), ((), ()))
across = (((1,), (1,)), ((), ()))
MIB = 1 << 20


def swap(value, bit, size=8):
    return lax.ppermute(value, "exp", [(index, index ^ bit) for index in range(size)])


def shape_of(shape, dtype):
    return jax.ShapeDtypeStruct(shape, dtype)


def after(value, *others):
    return lax.optimization_barrier((value, *others))[0]


def kept(shape, dtype):
    return pltpu.VMEM(shape, dtype)


def pinned(array):
    return pltpu.with_memory_space_constraint(array, pltpu.VMEM)


def kernel_call(body, name, outs, ins, far=(), scratch=(), result=pltpu.VMEM, earlier=()):
    aliases = {len(ins) + index: index for index in range(len(earlier))}
    ins = [*ins, *(pinned(array) for array in earlier)]
    spaces = [pltpu.VMEM] * len(ins)
    for index in far:
        spaces[index] = pl.ANY
        ins[index] = pltpu.with_memory_space_constraint(ins[index], pltpu.HBM)
    return pl.pallas_call(
        body,
        name=name,
        out_shape=outs,
        in_specs=[pl.BlockSpec(memory_space=space) for space in spaces],
        out_specs=[pl.BlockSpec(memory_space=result)] * len(outs),
        scratch_shapes=scratch,
        input_output_aliases=aliases,
        compiler_params=pltpu.CompilerParams(vmem_limit_bytes=8 * MIB),
        cost_estimate=pl.CostEstimate(flops=1, bytes_accessed=1, transcendentals=0),
    )(*ins)


def split_low(values):
    high = values.astype(jnp.bfloat16)
    rest = values - high.astype(jnp.float32)
    middle = rest.astype(jnp.bfloat16)
    low = (rest - middle.astype(jnp.float32)).astype(jnp.bfloat16)
    return high, middle, low


def exact_dot(values, low_matrix, contract):
    parts = lax.dot_general(
        jnp.concatenate(split_low(values), axis=0),
        low_matrix,
        contract,
        preferred_element_type=jnp.float32,
    )
    return parts[0:8] + parts[8:16] + parts[16:24]


def other_order(values, bits):
    return jnp.concatenate([values[row ^ bits : (row ^ bits) + 1] for row in range(4)], axis=0)


def norm_kernel(
    hidden_far, gain_far, router_far, final_far, vector_far,
    hidden_ref, gain_ref, router_ref, normed_ref, sums_ref, head_ref,
    final_ref, vector_ref, copy_sems,
):
    pairs = (
        (hidden_far, hidden_ref), (gain_far, gain_ref), (router_far, router_ref),
        (final_far, final_ref), (vector_far, vector_ref),
    )
    copies = [
        pltpu.make_async_copy(source, target, copy_sems.at[index])
        for index, (source, target) in enumerate(pairs)
    ]
    for copy in copies:
        copy.start()
    for copy in copies:
        copy.wait()
    vector = vector_ref[...].astype(jnp.float32)
    vector = jnp.concatenate([vector[row : row + 1] for row in range(vector.shape[0])], axis=1)
    head_ref[...] = final_ref[...] * vector
    rows = hidden_ref[...].astype(jnp.float32)
    normed_ref[...] = (rows * rms_scale(rows) * gain_ref[...]).astype(jnp.bfloat16)
    sums_ref[...] = jnp.sum(rows, axis=0, keepdims=True)


def on_side(side, body, held, far_count, *refs):
    refs = refs[:far_count] + refs[far_count + held :]

    @pl.when(lax.rem(lax.axis_index("exp"), 2) == side)
    def run():
        body(*refs)


def front_kernel(stage, owners, sets, count, router_ref, *refs):
    matrices, refs = refs[: 2 * len(sets)], refs[2 * len(sets) :]
    pieces, refs = refs[:count], refs[count:]
    matrices = list(matrices)
    hidden_units = matrices[0].shape[1]
    tile = 256
    firsts = range(0, hidden_units, tile)
    if stage == 3:
        sums_ref, *downs = refs[:3]
        earlier, refs = refs[3:6], refs[6:]
        *refs, terms_ref, rows_ref = refs
    else:
        *refs, rows_ref = refs
    gates_ref, *outs = refs
    expert = lax.axis_index("exp")
    first = 0
    for piece in pieces:
        rows_ref[first : first + piece.shape[0], :] = piece[...]
        first += piece.shape[0]
    size = first // len(owners)
    logits = lax.dot_general(
        rows_ref[...], router_ref[...], across, preferred_element_type=jnp.float32
    )
    weights = jnp.exp(logits)
    gates = weights / jnp.sum(weights, axis=1, keepdims=True)
    gates_ref[...] = gates
    lane = lax.broadcasted_iota(jnp.int32, gates.shape, 1)

    totals = []
    for place, which in enumerate(sets):
        gate_ref, up_ref = matrices[2 * place : 2 * place + 2]
        if stage == 3:
            slope_ref, silu_ref, act_ref = outs[3 * place : 3 * place + 3]
        else:
            slope_ref, silu_ref, act_ref, part_ref = outs
        own = jnp.sum(jnp.where(lane == expert ^ which, gates, 0.0), axis=1, keepdims=True)
        low = own.astype(jnp.bfloat16).astype(jnp.float32)
        parts = []
        for first in firsts:
            columns = slice(first, first + tile)
            rows = rows_ref[...]
            pre_gate = jnp.dot(rows, gate_ref[:, columns], preferred_element_type=jnp.float32)
            pre_up = jnp.dot(rows, up_ref[:, columns], preferred_element_type=jnp.float32)
            silu_gate, slope = gate_parts(pre_gate)
            activation = (silu_gate * pre_up).astype(jnp.bfloat16)
            slope_ref[:, columns] = slope * pre_up
            silu_ref[:, columns] = silu_gate
            act_ref[:, columns] = activation
            weighted = activation.astype(jnp.float32) * low
            found = {
                owner: jnp.sum(weighted[index * size : (index + 1) * size], axis=0, keepdims=True)
                for index, owner in enumerate(owners)
            }
            nothing = jnp.zeros_like(weighted[:1])
            parts.append(
                jnp.concatenate([found.get(owner, nothing) for owner in range(8)], axis=0)
            )
        totals.append(jnp.concatenate(parts, axis=1))
    if stage < 3:
        part_ref[...] = totals[0]
        return
    own_first, own_second, other_first = earlier
    totals[0] = totals[0] + (own_first[...] + own_second[...])
    totals[1] = totals[1] + other_first[...]
    terms = exact_dot(totals[0], downs[0][...], forward) + exact_dot(
        totals[1], downs[1][...], forward
    )
    row = lax.broadcasted_iota(jnp.int32, terms.shape, 0)
    terms_ref[...] = (terms + jnp.where(row == 0, sums_ref[...], 0.0))[:4]


def front(stage, owners, sets, pieces, router_rows, matrices, more=()):
    model_width, hidden_units = matrices[0].shape
    row_total = sum(piece.shape[0] for piece in pieces)
    outs = [kept((row_total, 8), jnp.float32)]
    for which in sets:
        outs += [
            kept((row_total, hidden_units), jnp.float32),
            kept((row_total, hidden_units), jnp.float32),
            kept((row_total, hidden_units), jnp.bfloat16),
        ]
    outs.append(
        kept((4, model_width), jnp.float32) if stage == 3 else kept((8, hidden_units), jnp.float32)
    )
    scratch = [pltpu.VMEM((row_total, model_width), jnp.bfloat16)]
    matrices = [pinned(matrix) for matrix in matrices]
    if stage == 3:
        more = [pinned(array) for array in more]
    return kernel_call(
        functools.partial(front_kernel, stage, owners, sets, len(pieces)),
        "front",
        outs,
        [pinned(router_rows), *matrices, *(pinned(piece) for piece in pieces), *more],
        (),
        scratch,
    )


def turn_block(source_ref, target_ref, rows, columns):
    target_ref[columns, rows] = source_ref[rows, columns].T


def own_kernel(
    grades_far, ranks_far, gate_far, up_far, down_far, router_ref, rows_ref,
    turned_ref, gates_ref, slope_ref, silu_ref, act_ref, part_ref, swap_gain_ref,
    gate_ref, up_ref, down_ref, gate_turned_ref, up_turned_ref, down_turned_ref,
    grades_ref, ranks_ref, copy_sems,
):
    hidden_units = gate_ref.shape[1]
    model_width = gate_ref.shape[0]
    tile = 256
    pairs = [(grades_far, grades_ref), (ranks_far, ranks_ref)]
    for first in range(0, hidden_units, tile):
        columns = slice(first, first + tile)
        pairs += [
            (gate_far.at[:, columns], gate_ref.at[:, columns]),
            (up_far.at[:, columns], up_ref.at[:, columns]),
        ]
    pairs.append((down_far, down_ref))
    copies = [
        pltpu.make_async_copy(source, target, copy_sems.at[index])
        for index, (source, target) in enumerate(pairs)
    ]
    for copy in copies:
        copy.start()
    rows = rows_ref[...]
    weights = jnp.exp(
        lax.dot_general(rows, router_ref[...], across, preferred_element_type=jnp.float32)
    )
    gates = weights / jnp.sum(weights, axis=1, keepdims=True)
    gates_ref[...] = gates
    weights = jnp.exp(
        lax.dot_general(router_ref[...], rows, across, preferred_element_type=jnp.float32)
    )
    turned_ref[...] = weights / jnp.sum(weights, axis=0, keepdims=True)
    lane = lax.broadcasted_iota(jnp.int32, gates.shape, 1)
    own = jnp.sum(
        jnp.where(lane == lax.axis_index("exp"), gates, 0.0), axis=1, keepdims=True
    )
    low = own.astype(jnp.bfloat16).astype(jnp.float32)
    copies[0].wait()
    copies[1].wait()
    swap_gain_ref[...] = swap_gains(grades_ref, ranks_ref)
    for number, first in enumerate(range(0, hidden_units, tile)):
        columns = slice(first, first + tile)
        copies[2 + 2 * number].wait()
        copies[3 + 2 * number].wait()
        pre_gate = jnp.dot(rows, gate_ref[:, columns], preferred_element_type=jnp.float32)
        pre_up = jnp.dot(rows, up_ref[:, columns], preferred_element_type=jnp.float32)
        silu_gate, slope = gate_parts(pre_gate)
        activation = (silu_gate * pre_up).astype(jnp.bfloat16)
        slope_ref[:, columns] = slope * pre_up
        silu_ref[:, columns] = silu_gate
        act_ref[:, columns] = activation
        total = jnp.sum(activation.astype(jnp.float32) * low, axis=0, keepdims=True)
        part_ref[:, columns] = jnp.concatenate([total, jnp.zeros((7, tile), jnp.float32)], axis=0)
        for start in range(0, model_width, tile):
            block = slice(start, start + tile)
            turn_block(gate_ref, gate_turned_ref, block, columns)
            turn_block(up_ref, up_turned_ref, block, columns)
    copies[-1].wait()
    for first in range(0, hidden_units, tile):
        for start in range(0, model_width, tile):
            turn_block(
                down_ref, down_turned_ref, slice(first, first + tile), slice(start, start + tile)
            )


def own_front(side, normed, router_rows, matrices, grades, passage_ranks, earlier=()):
    model_width, hidden_units = matrices[0].shape
    token_count = normed.shape[0]
    ins = [grades, passage_ranks, *matrices, pinned(router_rows), pinned(normed)]
    return kernel_call(
        functools.partial(on_side, side, own_kernel, len(earlier), len(ins)),
        "own",
        [
            kept((8, token_count), jnp.float32),
            kept((token_count, 8), jnp.float32),
            kept((token_count, hidden_units), jnp.float32),
            kept((token_count, hidden_units), jnp.float32),
            kept((token_count, hidden_units), jnp.bfloat16),
            kept((8, hidden_units), jnp.float32),
            kept((8, 128), jnp.float32),
            *(kept(matrix.shape, jnp.bfloat16) for matrix in matrices),
            *(kept(matrix.shape[::-1], jnp.bfloat16) for matrix in matrices),
        ],
        ins,
        range(5),
        [
            pltpu.SMEM(grades.shape, jnp.int32),
            pltpu.SMEM(grades.shape, jnp.int32),
            pltpu.SemaphoreType.DMA((3 + 2 * (hidden_units // 256),)),
        ],
        earlier=earlier,
    )


def near_kernel(
    own_ref, x_ref, y_ref, far_ref, head_ref, down_ref, other_down_ref,
    near_ref, other_near_ref, unit_ref, score_ref, own_score_ref, *, token_count,
):
    pooled = (
        (own_ref[...] + other_order(x_ref[...], 1))
        + (other_order(y_ref[...], 2) + other_order(far_ref[...], 3))
    ) / token_count
    pooled = jnp.concatenate([pooled, jnp.zeros_like(pooled)], axis=0)
    head = head_ref[...]
    scale = rms_scale(pooled)
    along = jnp.sum(pooled * head, axis=1, keepdims=True)
    own_score = (scale * along)[:1]
    own_score_ref[...] = own_score
    score_ref[...] = jnp.broadcast_to(own_score, score_ref.shape)
    unit = (
        scale * head - scale * scale * scale * (along / pooled.shape[1]) * pooled
    ) / token_count
    unit_ref[...] = unit[:1]
    near_ref[...] = exact_dot(unit, down_ref[...], forward)
    other_near_ref[...] = exact_dot(unit, other_down_ref[...], forward)


def back_kernel(passages, gate_count, saved_count, near_ref, other_near_ref, *refs):
    gates_refs, refs = refs[:gate_count], refs[gate_count:]
    saved, refs = refs[: 3 * saved_count], refs[3 * saved_count :]
    matrices, refs = refs[:4], refs[4:]
    *out_refs, d_gate_ref, d_up_ref, other_d_gate_ref, other_d_up_ref = refs
    expert = lax.axis_index("exp")
    size = out_refs[0].shape[1]
    model_width = matrices[0].shape[1]
    lane = lax.broadcasted_iota(jnp.int32, (size, 8), 1)
    line = lax.broadcasted_iota(jnp.int32, (16, size), 0)
    experts = (
        (near_ref, d_gate_ref, d_up_ref), (other_near_ref, other_d_gate_ref, other_d_up_ref)
    )
    sides = (d_gate_ref, d_up_ref, other_d_gate_ref, other_d_up_ref)
    for index, (owner, gates_place, saved_places, windows, unused) in enumerate(passages):
        rows = slice(index * size, (index + 1) * size)
        lines = jnp.zeros((16, size), jnp.float32)
        gates = gates_refs[gates_place[0]][gates_place[1] : gates_place[1] + size, :]
        for which, (table_ref, d_gate_out, d_up_out) in enumerate(experts):
            number, first = saved_places[which]
            slope_ref, silu_ref, act_ref = saved[3 * number : 3 * number + 3]
            held = slice(first, first + size)
            near = table_ref[owner : owner + 1, :]
            own = jnp.sum(
                jnp.where(lane == expert ^ which, gates, 0.0), axis=1, keepdims=True
            )
            d_act = own.astype(jnp.bfloat16).astype(jnp.float32) * near
            d_gate_out[rows, :] = (d_act * slope_ref[held, :]).astype(jnp.bfloat16)
            d_up_out[rows, :] = (d_act * silu_ref[held, :]).astype(jnp.bfloat16)
            if windows[-1][1] == model_width:
                gate_grad = exact_dot(table_ref[...], act_ref[held, :], across)
                lines = jnp.where(line == expert ^ which, gate_grad[owner : owner + 1], lines)
        for start, stop in windows:
            out_ref, *out_refs = out_refs
            used = stop - start
            if stop == model_width:
                out_ref[used : used + 16, :] = lines.astype(jnp.bfloat16)
                used += 16
            if out_ref.shape[0] > used:
                out_ref[used:, :] = jnp.zeros((out_ref.shape[0] - used, size), jnp.bfloat16)
            for first in range(start, stop, 256):
                pick_grad = None
                for side_ref, matrix in zip(sides, matrices):
                    term = jnp.dot(
                        side_ref[rows, :],
                        matrix[:, first : first + 256],
                        preferred_element_type=jnp.float32,
                    )
                    pick_grad = term if pick_grad is None else pick_grad + term
                out_ref[first - start : first - start + 256, :] = pick_grad.T.astype(jnp.bfloat16)


def back(passages, near, other_near, gates, saved, matrices, size):
    hidden_units, model_width = matrices[0].shape
    heights = [
        max(least, stop - start + (16 if stop == model_width else 0))
        for passage in passages
        for (start, stop), least in zip(*passage[3:])
    ]
    arrays = [array for group in saved for array in group]
    return kernel_call(
        functools.partial(back_kernel, passages, len(gates), len(saved)),
        "back",
        [kept((height, size), jnp.bfloat16) for height in heights],
        [pinned(array) for array in (near, other_near, *gates, *arrays, *matrices)],
        (),
        [pltpu.VMEM((len(passages) * size, hidden_units), jnp.bfloat16)] * 4,
    )


def add_kernel(x_ref, y_ref, high_ref, low_ref, x_out, y_out):
    for own_ref, other_ref, out_ref in ((x_ref, high_ref, x_out), (y_ref, low_ref, y_out)):
        out_ref[...] = (
            own_ref[...].astype(jnp.float32)
            + other_ref[: own_ref.shape[0], :].astype(jnp.float32)
        ).astype(jnp.bfloat16)


def turn_kernel(*refs):
    count = len(refs) // 2
    for source_ref, target_ref in zip(refs[:count], refs[count:]):
        for first in range(0, source_ref.shape[0], 256):
            rows = slice(first, first + 256)
            target_ref[:, rows] = source_ref[rows, :].T


def turn(matrices):
    return kernel_call(
        turn_kernel,
        "turn",
        [kept(matrix.shape[::-1], jnp.bfloat16) for matrix in matrices],
        [pinned(matrix) for matrix in matrices],
    )


def half_kernel(part, rows_ref, out_ref):
    half = out_ref.shape[0]
    out_ref[...] = rows_ref[part * half : (part + 1) * half, :]


def half_of(rows, part):
    total, wide = rows.shape
    (out,) = kernel_call(
        functools.partial(half_kernel, part), "half", [kept((total // 2, wide), rows.dtype)], [rows]
    )
    return out


def pack_kernel(first_ref, second_ref, out_ref):
    out_ref[:1, :] = first_ref[:1, :]
    out_ref[1:, :] = second_ref[:1, :]


def pack(first, second):
    return kernel_call(
        pack_kernel, "pack", [kept((2, first.shape[1]), first.dtype)], [pinned(first), second]
    )[0]


def pairs_of(passages):
    row = lax.broadcasted_iota(jnp.int32, (8, 128), 0)
    lane = lax.broadcasted_iota(jnp.int32, (8, 128), 1)
    return row, lane, jnp.logical_and(row < passages, lane < passages)


def spread(index, values):
    total = jnp.zeros((8, 128), jnp.float32)
    for number, value in values:
        total = jnp.where(index == number, value, total)
    return total


def whole_sum(values):
    return jnp.sum(jnp.sum(values, axis=1, keepdims=True), axis=0, keepdims=True)


def swap_gains(grades_ref, ranks_ref):
    passages = grades_ref.shape[1]
    row, lane, pair = pairs_of(passages)
    grade_list = [(number, grades_ref[0, number].astype(jnp.float32)) for number in range(passages)]
    rank_list = [(number, ranks_ref[0, number].astype(jnp.float32)) for number in range(passages)]
    grade_row, grade_lane = spread(row, grade_list), spread(lane, grade_list)
    worth_row, worth_lane = jnp.exp2(grade_row), jnp.exp2(grade_lane)
    discount_row = 1.0 / jnp.log2(2.0 + spread(row, rank_list))
    discount_lane = 1.0 / jnp.log2(2.0 + spread(lane, rank_list))
    ahead = jnp.logical_or(
        grade_lane > grade_row, jnp.logical_and(grade_lane == grade_row, lane < row)
    )
    ideal_rank = jnp.sum(
        jnp.where(jnp.logical_and(pair, ahead), 1.0, 0.0), axis=1, keepdims=True
    )
    ideal_terms = (worth_row - 1.0) / jnp.log2(2.0 + ideal_rank)
    one_lane = jnp.logical_and(pair, lane == 0)
    ideal_gain = whole_sum(jnp.where(one_lane, ideal_terms, 0.0))
    swap_gain = (
        jnp.abs((worth_row - worth_lane) * (discount_row - discount_lane)) / ideal_gain
    )
    return jnp.where(jnp.logical_and(pair, grade_row > grade_lane), swap_gain, 0.0)


def rank_kernel(swap_gain_ref, near_scores_ref, far_scores_ref, loss_ref, factor_ref):
    passages = 2 * near_scores_ref.shape[0]
    place = lax.axis_index("psg")
    row, lane, unused = pairs_of(passages)
    score_list = [
        (place ^ (base + number), jnp.broadcast_to(ref[number : number + 1, :], (8, 128)))
        for base, ref in ((0, near_scores_ref), (passages // 2, far_scores_ref))
        for number in range(passages // 2)
    ]
    swap_gain = swap_gain_ref[...]
    margin = spread(row, score_list) - spread(lane, score_list)
    softplus = jnp.maximum(-margin, 0.0) + jnp.log1p(jnp.exp(-jnp.abs(margin)))
    loss_ref[...] = whole_sum(swap_gain * softplus)
    pull = swap_gain * jax.nn.sigmoid(-margin)
    gradient = whole_sum(jnp.where(lane == place, pull, 0.0) - jnp.where(row == place, pull, 0.0))
    factor_ref[...] = jnp.broadcast_to(gradient * loss_scale, factor_ref.shape)


def first_end_kernel(own_ref, x_low_ref, y_high_ref, total_ref, lines_ref):
    model_width = total_ref.shape[1]
    cut = model_width // 2
    for first in range(0, model_width, 256):
        rows = slice(first, first + 256)
        if first < cut:
            term = x_low_ref[rows, :]
        else:
            term = y_high_ref[first - cut : first - cut + 256, :]
        total = own_ref[rows, :].astype(jnp.float32) + term.astype(jnp.float32)
        total_ref[:, rows] = total.T
    end = slice(model_width, model_width + 8)
    end_high = slice(model_width - cut, model_width - cut + 8)
    lines_ref[...] = own_ref[end, :].astype(jnp.float32) + y_high_ref[end_high, :].astype(
        jnp.float32
    )


def end_kernel(
    factor_ref, total_ref, lines_ref, x_high_ref, y_low_ref,
    hidden_ref, gain_ref, gates_ref, router_ref, unit_ref,
    grad_far, turned_ref, grad_ref, copy_sems,
):
    token_count, model_width = hidden_ref.shape
    cut = y_low_ref.shape[0]
    end_high = slice(model_width - cut, model_width - cut + 8)
    slot_grad = lines_ref[...] + x_high_ref[end_high, :].astype(jnp.float32)
    gates = gates_ref[...]
    d_logit = gates * (slot_grad - jnp.sum(gates * slot_grad, axis=0, keepdims=True))
    d_logit = jnp.concatenate([d_logit, jnp.zeros((120, token_count), jnp.float32)], axis=0).T
    d_logit = jnp.concatenate(split_low(d_logit[:, :8]), axis=1)
    router_rows = jnp.concatenate([router_ref[...]] * 3, axis=0)
    for first in range(0, model_width, 256):
        columns = slice(first, first + 256)
        if first < cut:
            term = y_low_ref[columns, :]
        else:
            term = x_high_ref[first - cut : first - cut + 256, :]
        turned_ref[:, columns] = (
            total_ref[:, columns]
            + term.astype(jnp.float32).T
            + jnp.dot(d_logit, router_rows[:, columns], preferred_element_type=jnp.float32)
        )
    gain = gain_ref[...]
    factor = factor_ref[:, :1]
    size = 16
    copies = []
    for first in range(0, token_count, size):
        rows = slice(first, first + size)
        flat_rows = hidden_ref[rows, :].astype(jnp.float32)
        grad = norm_back(flat_rows, rms_scale(flat_rows), gain, turned_ref[rows, :])
        grad_ref[rows, :] = ((grad + unit_ref[...]) * factor).astype(jnp.bfloat16)
        copies.append(
            pltpu.make_async_copy(
                grad_ref.at[rows, :], grad_far.at[rows, :], copy_sems.at[first // size]
            )
        )
        copies[-1].start()
    for copy in copies:
        copy.wait()


def every_expert(
    hidden,
    norm_gain,
    router,
    gate_proj,
    up_proj,
    down_proj,
    final_gain,
    score_vector,
    expert_ids,
    grades,
    passage_ranks,
):
    unused_query, unused_passage, token_count, model_width = hidden.shape
    passages = grades.shape[1]
    flat = hidden.reshape(token_count, model_width)
    gate_matrix, up_matrix, down_matrix = gate_proj[0], up_proj[0], down_proj[0]
    mine = [gate_matrix, up_matrix, down_matrix]
    flat, gain, router_rows, normed, token_sums, head = kernel_call(
        norm_kernel,
        "norm",
        [
            kept(flat.shape, jnp.bfloat16),
            kept((1, model_width), jnp.float32),
            kept((8, model_width), jnp.bfloat16),
            kept(flat.shape, jnp.bfloat16),
            kept((1, model_width), jnp.float32),
            kept((1, model_width), jnp.float32),
        ],
        [
            flat,
            norm_gain.reshape(1, model_width),
            router.T,
            final_gain.reshape(1, model_width),
            score_vector.reshape(model_width // 128, 128),
        ],
        range(5),
        [
            pltpu.VMEM((1, model_width), jnp.float32),
            pltpu.VMEM((model_width // 128, 128), jnp.bfloat16),
            pltpu.SemaphoreType.DMA((5,)),
        ],
    )
    others = [swap(matrix, CORE) for matrix in mine]
    arrays = own_front(1, normed, router_rows, mine, grades, passage_ranks)
    normed, *arrays = lax.optimization_barrier((normed, *arrays))
    x_rows, y_rows = swap(normed, ACROSS_X), swap(normed, ACROSS_Y)
    arrays = own_front(0, normed, router_rows, mine, grades, passage_ranks, arrays)
    turned_gates, own_gates, *own_saved, own_part, swap_gain = arrays[:7]
    mine, (*mine_turned, down_turned) = list(arrays[7:10]), arrays[10:]
    x_rows, y_rows = after(x_rows, mine_turned[0]), after(y_rows, mine_turned[0])
    far_low = swap(half_of(x_rows, 0), ACROSS_Y)
    far_high = swap(half_of(y_rows, 1), ACROSS_X)
    side_gates, *side_saved, side_part = front(
        1, (1, 2), (0,), [x_rows, y_rows], router_rows, mine[:2]
    )
    others[0] = after(others[0], side_part)
    unused, *other_saved, other_part = front(
        2, (0, 1, 2), (1,), [normed, x_rows, y_rows], router_rows, others[:2]
    )
    far_low, far_high = after(far_low, other_part), after(far_high, other_part)
    far_gates, *far_saved, terms = front(
        3, (3,), (0, 1), [far_low, far_high], router_rows, mine[:2] + others[:2],
        (token_sums, mine[2], others[2], own_part, side_part, other_part),
    )

    *others_turned, other_down_turned = turn([after(others[0], terms), *others[1:]])
    head = after(head, others_turned[0])
    near, other_near, unit_vector, travelling, own_score = kernel_call(
        functools.partial(near_kernel, token_count=token_count),
        "near",
        [
            kept((8, down_matrix.shape[0]), jnp.float32),
            kept((8, down_matrix.shape[0]), jnp.float32),
            kept((1, model_width), jnp.float32),
            kept((1, 128), jnp.float32),
            shape_of((1, 1), jnp.float32),
        ],
        [
            pinned(terms),
            swap(terms, ACROSS_X),
            swap(terms, ACROSS_Y),
            swap(terms, ACROSS_X | ACROSS_Y),
            pinned(head),
            pinned(down_turned),
            pinned(other_down_turned),
        ],
    )
    matrices = [*mine_turned, *others_turned]
    middle = model_width // 2
    lower, upper, early, earlier = (0, middle), (middle, model_width), middle + 32, middle + 48
    far_low, far_high = back(
        ((3, (0, 0), ((0, 0), (1, 0)), (lower, upper), (earlier, earlier)),),
        near, other_near, [far_gates], [far_saved[:3], far_saved[3:]], matrices, token_count,
    )
    far_sent = far_low
    far_low, far_high = swap(far_low, ACROSS_X), swap(far_high, ACROSS_Y)

    def sides_back(x_window, y_window, least, *earlier):
        return back(
            (
                (1, (0, 0), ((0, 0), (1, token_count)), (x_window,), (least,)),
                (2, (0, token_count), ((0, token_count), (1, 2 * token_count)), (y_window,), (least,)),
            ),
            after(near, *earlier), other_near, [side_gates], [side_saved, other_saved], matrices,
            token_count,
        )

    x_low, y_high = sides_back(lower, upper, early, far_sent)
    first_sent = x_low
    x_low, y_high = swap(x_low, ACROSS_X), swap(y_high, ACROSS_Y)
    x_high, y_low = sides_back(upper, lower, 0, first_sent)
    travelling = after(travelling, first_sent)
    met = lax.ppermute(travelling, "psg", [(index, index ^ 1) for index in range(passages)])
    near_scores = pack(travelling, met)
    far_high = after(far_high, near_scores)
    x_high, y_low = kernel_call(
        add_kernel,
        "add",
        [kept(x_high.shape, jnp.bfloat16), kept(y_low.shape, jnp.bfloat16)],
        [pinned(x_high), pinned(y_low), far_high, far_low],
    )
    x_high, y_low, near_scores, other_near = lax.optimization_barrier(
        (x_high, y_low, near_scores, other_near)
    )
    x_high, y_low = swap(x_high, ACROSS_X), swap(y_low, ACROSS_Y)
    (own_sums,) = back(
        ((0, (0, 0), ((0, 0), (1, 0)), ((0, model_width),), (0,)),),
        near, other_near, [own_gates], [own_saved, other_saved], matrices, token_count,
    )
    far_scores = lax.ppermute(near_scores, "psg", [(index, index ^ 2) for index in range(passages)])
    loss, factor = kernel_call(
        rank_kernel,
        "rank",
        [shape_of((1, 1), jnp.float32), kept((1, 128), jnp.float32)],
        [pinned(swap_gain), pinned(near_scores), far_scores],
    )
    total, lines = kernel_call(
        first_end_kernel,
        "first_end",
        [
            kept((token_count, model_width), jnp.float32),
            kept((8, token_count), jnp.float32),
        ],
        [pinned(own_sums), after(x_low, factor), y_high],
    )
    (grad,) = kernel_call(
        end_kernel,
        "end",
        [shape_of((token_count, model_width), jnp.bfloat16)],
        [
            pinned(factor), pinned(total), pinned(lines), x_high, y_low, pinned(flat), pinned(gain),
            pinned(turned_gates), pinned(router_rows), pinned(unit_vector),
        ],
        scratch=[
            pltpu.VMEM((token_count, model_width), jnp.float32),
            pltpu.VMEM((token_count, model_width), jnp.bfloat16),
            pltpu.SemaphoreType.DMA((token_count // 16,)),
        ],
        result=pl.ANY,
    )
    return (loss.reshape(1), own_score, grad.reshape(hidden.shape))


def block(*arrays):
    hidden, router, expert_ids, grades = arrays[0], arrays[2], arrays[8], arrays[9]
    each_expert = router.shape[1] == expert_ids.shape[3] == 8
    if hidden.shape[1] == 1 and each_expert and grades.shape[1] == 4:
        return every_expert(*arrays)
    return local(*arrays)


def solution(mesh):
    placed = (
        P("exp", "psg", None, None),
        P(),
        P(),
        P("exp", None, None),
        P("exp", None, None),
        P("exp", None, None),
        P(),
        P(),
        P("exp", "psg", None, None),
        P("exp", None),
        P("exp", None),
    )
    return jax.shard_map(
        block,
        mesh=mesh,
        in_specs=placed,
        out_specs=(P("exp"), P("exp", "psg"), P("exp", "psg", None, None)),
        check_vma=False,
    )
```

```python
import functools
import math

import jax
import jax.numpy as jnp
from jax import lax
from jax.experimental import pallas as pl
from jax.experimental.pallas import tpu as pltpu
from jax.sharding import PartitionSpec as P

epsilon = 1e-06
loss_scale = 256.0
highest = lax.Precision.HIGHEST


def rms_scale(values):
    return lax.rsqrt(jnp.mean(values * values, axis=-1, keepdims=True) + epsilon)


def head_score(pooled, final_gain, score_vector):
    scaled = pooled * rms_scale(pooled) * final_gain
    return jnp.dot(scaled, score_vector.astype(jnp.float32), precision=highest)


def rank_loss(scores, grades, passage_ranks):
    grade_value = grades.astype(jnp.float32)
    worth_gain = jnp.exp2(grade_value)
    discount = 1.0 / jnp.log2(2.0 + passage_ranks.astype(jnp.float32))
    better_than = grades[None, :] > grades[:, None]
    equal_grade = grades[None, :] == grades[:, None]
    position = jnp.arange(grades.shape[0], dtype=jnp.int32)
    earlier = position[None, :] < position[:, None]
    ideal_rank = jnp.sum(
        jnp.logical_or(better_than, jnp.logical_and(equal_grade, earlier)).astype(jnp.float32),
        axis=1,
    )
    ideal_gain = jnp.sum((worth_gain - 1.0) / jnp.log2(2.0 + ideal_rank))
    ordered = (grades[:, None] > grades[None, :]).astype(jnp.float32)
    swap_gain = (
        jnp.abs(
            (worth_gain[:, None] - worth_gain[None, :]) * (discount[:, None] - discount[None, :])
        )
        / ideal_gain
    )
    margin = scores[:, None] - scores[None, :]
    return jnp.sum(ordered * swap_gain * jax.nn.softplus(-margin))


def pick_gates(normed, router, picked_ids):
    expert_total = router.shape[1]
    logits = jnp.dot(normed, router, preferred_element_type=jnp.float32)
    onehot = (
        picked_ids[:, :, None] == jnp.arange(expert_total, dtype=jnp.int32)[None, None, :]
    ).astype(jnp.float32)
    chosen = jnp.einsum("nke,ne->nk", onehot, logits, precision=highest)
    weights = jnp.exp(chosen)
    return (weights / jnp.sum(weights, axis=1, keepdims=True), onehot)


def gate_parts(pre_gate):
    sigmoid_gate = jax.nn.sigmoid(pre_gate)
    return (pre_gate * sigmoid_gate, sigmoid_gate * (1.0 + pre_gate * (1.0 - sigmoid_gate)))


def norm_back(flat_rows, inverse, norm_gain, d_normed):
    scaled = d_normed * norm_gain
    return inverse * scaled - flat_rows * inverse * inverse * inverse * jnp.mean(
        flat_rows * scaled, axis=-1, keepdims=True
    )


def unpack_front(front_out, buffer_rows):
    pre_gate, pre_up, received = front_out
    hidden_units = pre_gate.shape[2]
    pre_gate = pre_gate.reshape(buffer_rows, hidden_units)
    pre_up = pre_up.reshape(buffer_rows, hidden_units)
    silu_gate, slope = gate_parts(pre_gate)
    activation = (silu_gate * pre_up).astype(jnp.bfloat16)
    return (pre_up, received, silu_gate, slope, activation)


def local(
    hidden,
    norm_gain,
    router,
    gate_proj,
    up_proj,
    down_proj,
    final_gain,
    score_vector,
    expert_ids,
    grades,
    passage_ranks,
):
    unused_query, local_passages, local_positions, model_width = hidden.shape
    top_count = expert_ids.shape[3]
    expert_count = lax.axis_size("exp")
    token_count = local_passages * local_positions
    slot_count = token_count * top_count
    capacity = min(token_count, 9 * token_count * top_count // (8 * expert_count))
    buffer_rows = expert_count * capacity
    flat_rows = hidden.reshape(token_count, model_width).astype(jnp.float32)
    inverse = rms_scale(flat_rows)
    normed = (flat_rows * inverse * norm_gain).astype(jnp.bfloat16)
    picked_ids = expert_ids.reshape(token_count, top_count)
    gate_values, onehot = pick_gates(normed, router, picked_ids)
    slot_hits = onehot.reshape(slot_count, expert_count).astype(jnp.int32)
    slot_rank = jnp.sum((jnp.cumsum(slot_hits, axis=0) - slot_hits) * slot_hits, axis=1)
    target = picked_ids.reshape(slot_count) * capacity + slot_rank
    source_token = jnp.arange(slot_count, dtype=jnp.int32) // top_count
    passage_onehot = (
        source_token[:, None] // local_positions
        == jnp.arange(local_passages, dtype=jnp.int32)[None, :]
    ).astype(jnp.float32)
    weighted = (passage_onehot * gate_values.reshape(slot_count, 1)).astype(jnp.bfloat16)
    send_rows = (
        jnp.zeros((buffer_rows, model_width), jnp.bfloat16).at[target].set(normed[source_token])
    )
    send_weights = jnp.zeros((buffer_rows, local_passages), jnp.bfloat16).at[target].set(weighted)
    outgoing = (
        send_rows.reshape(expert_count, capacity, model_width),
        send_weights.reshape(expert_count, capacity, local_passages),
    )
    gate_matrix = gate_proj[0]
    up_matrix = up_proj[0]
    down_matrix = down_proj[0]
    rows_in = lax.all_to_all(outgoing[0], "exp", split_axis=0, concat_axis=0, tiled=True)
    weights_in = lax.all_to_all(outgoing[1], "exp", split_axis=0, concat_axis=0, tiled=True)
    pre_gate = jnp.einsum("end,df->enf", rows_in, gate_matrix, preferred_element_type=jnp.float32)
    pre_up = jnp.einsum("end,df->enf", rows_in, up_matrix, preferred_element_type=jnp.float32)
    front_out = (pre_gate, pre_up, weights_in)
    pre_up, received, silu_gate, slope, activation = unpack_front(front_out, buffer_rows)
    hidden_units = activation.shape[1]
    passage_part = jnp.einsum(
        "scp,scf->spf",
        received,
        activation.reshape(expert_count, capacity, hidden_units),
        preferred_element_type=jnp.float32,
    )
    down_wide = down_matrix.astype(jnp.float32)
    expert_terms = jnp.einsum("spf,fd->spd", passage_part, down_wide, precision=highest)
    came_back = lax.all_to_all(expert_terms, "exp", split_axis=0, concat_axis=0, tiled=True)
    token_sums = jnp.sum(flat_rows.reshape(local_passages, local_positions, model_width), axis=1)
    pooled = (token_sums + jnp.sum(came_back, axis=0)) / local_positions
    first_row = lax.axis_index("psg") * local_passages
    own_score = head_score(pooled, final_gain, score_vector)
    every_score = lax.all_gather(own_score, "psg", axis=0, tiled=True)
    loss_value, loss_grad = jax.value_and_grad(rank_loss)(every_score, grades[0], passage_ranks[0])
    d_own = lax.dynamic_slice_in_dim(loss_grad, first_row, local_passages, 0) * loss_scale
    unused_score, head_back = jax.vjp(
        lambda values: head_score(values, final_gain, score_vector), pooled
    )
    d_vector = head_back(d_own)[0] / local_positions
    every_vector = lax.all_gather(d_vector[None], "exp", axis=0, tiled=True)
    near_table = jnp.einsum("spd,fd->spf", every_vector, down_wide, precision=highest)
    present = (received != 0).astype(jnp.float32)
    near_rows = jnp.einsum("scp,spf->scf", present, near_table, precision=highest).reshape(
        buffer_rows, hidden_units
    )
    gate_weight = jnp.sum(received.astype(jnp.float32), axis=2).reshape(buffer_rows, 1)
    d_act = gate_weight * near_rows
    d_gate = (d_act * pre_up * slope).astype(jnp.bfloat16)
    d_up = (d_act * silu_gate).astype(jnp.bfloat16)
    contract = (((1,), (1,)), ((), ()))
    pick_grad = lax.dot_general(d_gate, gate_matrix, contract, preferred_element_type=jnp.float32)
    pick_grad = (
        pick_grad + lax.dot_general(d_up, up_matrix, contract, preferred_element_type=jnp.float32)
    ).astype(jnp.bfloat16)
    gate_grad = jnp.sum(activation.astype(jnp.float32) * near_rows, axis=1).astype(jnp.bfloat16)
    back_rows, back_gate = (
        lax.all_to_all(
            pick_grad.reshape(expert_count, capacity, model_width),
            "exp",
            split_axis=0,
            concat_axis=0,
            tiled=True,
        ),
        lax.all_to_all(
            gate_grad.reshape(expert_count, capacity),
            "exp",
            split_axis=0,
            concat_axis=0,
            tiled=True,
        ),
    )
    picked_rows = back_rows.reshape(buffer_rows, model_width)[target]
    d_normed = jnp.sum(
        picked_rows.reshape(token_count, top_count, model_width).astype(jnp.float32), axis=1
    )
    picked_gate = (
        back_gate.reshape(buffer_rows)[target].astype(jnp.float32).reshape(token_count, top_count)
    )
    d_logit = gate_values * (
        picked_gate - jnp.sum(gate_values * picked_gate, axis=1, keepdims=True)
    )
    dense_logit = jnp.einsum("nk,nke->ne", d_logit, onehot, precision=highest)
    d_normed = d_normed + jnp.einsum(
        "ne,de->nd", dense_logit, router.astype(jnp.float32), precision=highest
    )
    grad_flat = norm_back(flat_rows, inverse, norm_gain, d_normed)
    grad_hidden = (
        grad_flat.reshape(1, local_passages, local_positions, model_width)
        + d_vector[None, :, None, :]
    )
    return (
        loss_value.reshape(1),
        own_score.reshape(1, local_passages),
        grad_hidden.astype(jnp.bfloat16),
    )


CORE, ACROSS_X, ACROSS_Y = 1, 2, 4
forward = (((1,), (0,)), ((), ()))
across = (((1,), (1,)), ((), ()))
MIB = 1 << 20


def swap(value, bit, size=8):
    return lax.ppermute(value, "exp", [(index, index ^ bit) for index in range(size)])


def shape_of(shape, dtype):
    return jax.ShapeDtypeStruct(shape, dtype)


def after(value, *others):
    return lax.optimization_barrier((value, *others))[0]


def kept(shape, dtype):
    return pltpu.VMEM(shape, dtype)


def pinned(array):
    return pltpu.with_memory_space_constraint(array, pltpu.VMEM)


def kernel_call(body, name, outs, ins, far=(), scratch=(), result=pltpu.VMEM, earlier=()):
    aliases = {len(ins) + index: index for index in range(len(earlier))}
    ins = [*ins, *(pinned(array) for array in earlier)]
    spaces = [pltpu.VMEM] * len(ins)
    for index in far:
        spaces[index] = pl.ANY
        ins[index] = pltpu.with_memory_space_constraint(ins[index], pltpu.HBM)
    return pl.pallas_call(
        body,
        name=name,
        out_shape=outs,
        in_specs=[pl.BlockSpec(memory_space=space) for space in spaces],
        out_specs=[pl.BlockSpec(memory_space=result)] * len(outs),
        scratch_shapes=scratch,
        input_output_aliases=aliases,
        compiler_params=pltpu.CompilerParams(vmem_limit_bytes=8 * MIB),
        cost_estimate=pl.CostEstimate(flops=1, bytes_accessed=1, transcendentals=0),
    )(*ins)


def split_low(values):
    high = values.astype(jnp.bfloat16)
    rest = values - high.astype(jnp.float32)
    middle = rest.astype(jnp.bfloat16)
    low = (rest - middle.astype(jnp.float32)).astype(jnp.bfloat16)
    return high, middle, low


def exact_dot(values, low_matrix, contract):
    parts = lax.dot_general(
        jnp.concatenate(split_low(values), axis=0),
        low_matrix,
        contract,
        preferred_element_type=jnp.float32,
    )
    return parts[0:8] + parts[8:16] + parts[16:24]


def other_order(values, bits):
    return jnp.concatenate([values[row ^ bits : (row ^ bits) + 1] for row in range(4)], axis=0)


def norm_kernel(
    hidden_far, gain_far, router_far, final_far, vector_far,
    hidden_ref, gain_ref, router_ref, normed_ref, sums_ref, head_ref,
    final_ref, vector_ref, copy_sems,
):
    pairs = (
        (hidden_far, hidden_ref), (gain_far, gain_ref), (router_far, router_ref),
        (final_far, final_ref), (vector_far, vector_ref),
    )
    copies = [
        pltpu.make_async_copy(source, target, copy_sems.at[index])
        for index, (source, target) in enumerate(pairs)
    ]
    for copy in copies:
        copy.start()
    for copy in copies:
        copy.wait()
    vector = vector_ref[...].astype(jnp.float32)
    vector = jnp.concatenate([vector[row : row + 1] for row in range(vector.shape[0])], axis=1)
    head_ref[...] = final_ref[...] * vector
    rows = hidden_ref[...].astype(jnp.float32)
    normed_ref[...] = (rows * rms_scale(rows) * gain_ref[...]).astype(jnp.bfloat16)
    sums_ref[...] = jnp.sum(rows, axis=0, keepdims=True)


def on_side(side, body, held, far_count, *refs):
    refs = refs[:far_count] + refs[far_count + held :]

    @pl.when(lax.rem(lax.axis_index("exp"), 2) == side)
    def run():
        body(*refs)


def front_kernel(stage, owners, sets, count, router_ref, *refs):
    matrices, refs = refs[: 2 * len(sets)], refs[2 * len(sets) :]
    pieces, refs = refs[:count], refs[count:]
    matrices = list(matrices)
    hidden_units = matrices[0].shape[1]
    tile = 256
    firsts = range(0, hidden_units, tile)
    if stage == 3:
        sums_ref, *downs = refs[:3]
        earlier, refs = refs[3:6], refs[6:]
        *refs, terms_ref, rows_ref = refs
    else:
        *refs, rows_ref = refs
    gates_ref, *outs = refs
    expert = lax.axis_index("exp")
    first = 0
    for piece in pieces:
        rows_ref[first : first + piece.shape[0], :] = piece[...]
        first += piece.shape[0]
    size = first // len(owners)
    logits = lax.dot_general(
        rows_ref[...], router_ref[...], across, preferred_element_type=jnp.float32
    )
    weights = jnp.exp(logits)
    gates = weights / jnp.sum(weights, axis=1, keepdims=True)
    gates_ref[...] = gates
    lane = lax.broadcasted_iota(jnp.int32, gates.shape, 1)

    totals = []
    for place, which in enumerate(sets):
        gate_ref, up_ref = matrices[2 * place : 2 * place + 2]
        if stage == 3:
            slope_ref, silu_ref, act_ref = outs[3 * place : 3 * place + 3]
        else:
            slope_ref, silu_ref, act_ref, part_ref = outs
        own = jnp.sum(jnp.where(lane == expert ^ which, gates, 0.0), axis=1, keepdims=True)
        low = own.astype(jnp.bfloat16).astype(jnp.float32)
        parts = []
        for first in firsts:
            columns = slice(first, first + tile)
            rows = rows_ref[...]
            pre_gate = jnp.dot(rows, gate_ref[:, columns], preferred_element_type=jnp.float32)
            pre_up = jnp.dot(rows, up_ref[:, columns], preferred_element_type=jnp.float32)
            silu_gate, slope = gate_parts(pre_gate)
            activation = (silu_gate * pre_up).astype(jnp.bfloat16)
            slope_ref[:, columns] = slope * pre_up
            silu_ref[:, columns] = silu_gate
            act_ref[:, columns] = activation
            weighted = activation.astype(jnp.float32) * low
            found = {
                owner: jnp.sum(weighted[index * size : (index + 1) * size], axis=0, keepdims=True)
                for index, owner in enumerate(owners)
            }
            nothing = jnp.zeros_like(weighted[:1])
            parts.append(
                jnp.concatenate([found.get(owner, nothing) for owner in range(8)], axis=0)
            )
        totals.append(jnp.concatenate(parts, axis=1))
    if stage < 3:
        part_ref[...] = totals[0]
        return
    own_first, own_second, other_first = earlier
    totals[0] = totals[0] + (own_first[...] + own_second[...])
    totals[1] = totals[1] + other_first[...]
    terms = exact_dot(totals[0], downs[0][...], forward) + exact_dot(
        totals[1], downs[1][...], forward
    )
    row = lax.broadcasted_iota(jnp.int32, terms.shape, 0)
    terms_ref[...] = (terms + jnp.where(row == 0, sums_ref[...], 0.0))[:4]


def front(stage, owners, sets, pieces, router_rows, matrices, more=()):
    model_width, hidden_units = matrices[0].shape
    row_total = sum(piece.shape[0] for piece in pieces)
    outs = [kept((row_total, 8), jnp.float32)]
    for which in sets:
        outs += [
            kept((row_total, hidden_units), jnp.float32),
            kept((row_total, hidden_units), jnp.float32),
            kept((row_total, hidden_units), jnp.bfloat16),
        ]
    outs.append(
        kept((4, model_width), jnp.float32) if stage == 3 else kept((8, hidden_units), jnp.float32)
    )
    scratch = [pltpu.VMEM((row_total, model_width), jnp.bfloat16)]
    matrices = [pinned(matrix) for matrix in matrices]
    if stage == 3:
        more = [pinned(array) for array in more]
    return kernel_call(
        functools.partial(front_kernel, stage, owners, sets, len(pieces)),
        "front",
        outs,
        [pinned(router_rows), *matrices, *(pinned(piece) for piece in pieces), *more],
        (),
        scratch,
    )


def own_kernel(
    gate_far, up_far, router_ref, rows_ref,
    turned_ref, gates_ref, slope_ref, silu_ref, act_ref, part_ref, gate_ref, up_ref, copy_sems,
):
    hidden_units = gate_ref.shape[1]
    tile = 256
    pairs = []
    for first in range(0, hidden_units, tile):
        columns = slice(first, first + tile)
        pairs += [
            (gate_far.at[:, columns], gate_ref.at[:, columns]),
            (up_far.at[:, columns], up_ref.at[:, columns]),
        ]
    copies = [
        pltpu.make_async_copy(source, target, copy_sems.at[index])
        for index, (source, target) in enumerate(pairs)
    ]
    for copy in copies:
        copy.start()
    rows = rows_ref[...]
    weights = jnp.exp(
        lax.dot_general(rows, router_ref[...], across, preferred_element_type=jnp.float32)
    )
    gates = weights / jnp.sum(weights, axis=1, keepdims=True)
    gates_ref[...] = gates
    weights = jnp.exp(
        lax.dot_general(router_ref[...], rows, across, preferred_element_type=jnp.float32)
    )
    turned_ref[...] = weights / jnp.sum(weights, axis=0, keepdims=True)
    lane = lax.broadcasted_iota(jnp.int32, gates.shape, 1)
    own = jnp.sum(
        jnp.where(lane == lax.axis_index("exp"), gates, 0.0), axis=1, keepdims=True
    )
    low = own.astype(jnp.bfloat16).astype(jnp.float32)
    for number, first in enumerate(range(0, hidden_units, tile)):
        columns = slice(first, first + tile)
        copies[2 * number].wait()
        copies[2 * number + 1].wait()
        pre_gate = jnp.dot(rows, gate_ref[:, columns], preferred_element_type=jnp.float32)
        pre_up = jnp.dot(rows, up_ref[:, columns], preferred_element_type=jnp.float32)
        silu_gate, slope = gate_parts(pre_gate)
        activation = (silu_gate * pre_up).astype(jnp.bfloat16)
        slope_ref[:, columns] = slope * pre_up
        silu_ref[:, columns] = silu_gate
        act_ref[:, columns] = activation
        total = jnp.sum(activation.astype(jnp.float32) * low, axis=0, keepdims=True)
        part_ref[:, columns] = jnp.concatenate([total, jnp.zeros((7, tile), jnp.float32)], axis=0)


def own_front(side, normed, router_rows, matrices, earlier=()):
    hidden_units = matrices[0].shape[1]
    token_count = normed.shape[0]
    ins = [*matrices, pinned(router_rows), pinned(normed)]
    return kernel_call(
        functools.partial(on_side, side, own_kernel, len(earlier), len(ins)),
        "own",
        [
            kept((8, token_count), jnp.float32),
            kept((token_count, 8), jnp.float32),
            kept((token_count, hidden_units), jnp.float32),
            kept((token_count, hidden_units), jnp.float32),
            kept((token_count, hidden_units), jnp.bfloat16),
            kept((8, hidden_units), jnp.float32),
            *(kept(matrix.shape, jnp.bfloat16) for matrix in matrices),
        ],
        ins,
        range(2),
        [pltpu.SemaphoreType.DMA((2 * (hidden_units // 256),))],
        earlier=earlier,
    )


def ready_kernel(
    grades_far, ranks_far, down_far, gate_ref, up_ref,
    swap_gain_ref, down_ref, gate_turned_ref, up_turned_ref, down_turned_ref,
    grades_ref, ranks_ref, copy_sems,
):
    pairs = ((grades_far, grades_ref), (ranks_far, ranks_ref), (down_far, down_ref))
    copies = [
        pltpu.make_async_copy(source, target, copy_sems.at[index])
        for index, (source, target) in enumerate(pairs)
    ]
    for copy in copies:
        copy.start()
    turn_kernel(gate_ref, up_ref, gate_turned_ref, up_turned_ref)
    copies[0].wait()
    copies[1].wait()
    swap_gain_ref[...] = swap_gains(grades_ref, ranks_ref)
    copies[2].wait()
    turn_kernel(down_ref, down_turned_ref)


def get_ready(grades, passage_ranks, down_matrix, matrices):
    return kernel_call(
        ready_kernel,
        "ready",
        [
            kept((8, 128), jnp.float32),
            kept(down_matrix.shape, jnp.bfloat16),
            *(kept(matrix.shape[::-1], jnp.bfloat16) for matrix in (*matrices, down_matrix)),
        ],
        [grades, passage_ranks, down_matrix, *(pinned(matrix) for matrix in matrices)],
        range(3),
        [
            pltpu.SMEM(grades.shape, jnp.int32),
            pltpu.SMEM(grades.shape, jnp.int32),
            pltpu.SemaphoreType.DMA((3,)),
        ],
    )


def near_kernel(
    own_ref, x_ref, y_ref, far_ref, head_ref, down_ref, other_down_ref,
    near_ref, other_near_ref, unit_ref, score_ref, own_score_ref, *, token_count,
):
    pooled = (
        (own_ref[...] + other_order(x_ref[...], 1))
        + (other_order(y_ref[...], 2) + other_order(far_ref[...], 3))
    ) / token_count
    pooled = jnp.concatenate([pooled, jnp.zeros_like(pooled)], axis=0)
    head = head_ref[...]
    scale = rms_scale(pooled)
    along = jnp.sum(pooled * head, axis=1, keepdims=True)
    own_score = (scale * along)[:1]
    own_score_ref[...] = own_score
    score_ref[...] = jnp.broadcast_to(own_score, score_ref.shape)
    unit = (
        scale * head - scale * scale * scale * (along / pooled.shape[1]) * pooled
    ) / token_count
    unit_ref[...] = unit[:1]
    near_ref[...] = exact_dot(unit, down_ref[...], forward)
    other_near_ref[...] = exact_dot(unit, other_down_ref[...], forward)


def back_kernel(passages, gate_count, saved_count, near_ref, other_near_ref, *refs):
    gates_refs, refs = refs[:gate_count], refs[gate_count:]
    saved, refs = refs[: 3 * saved_count], refs[3 * saved_count :]
    matrices, refs = refs[:4], refs[4:]
    *out_refs, d_gate_ref, d_up_ref, other_d_gate_ref, other_d_up_ref = refs
    expert = lax.axis_index("exp")
    size = out_refs[0].shape[1]
    model_width = matrices[0].shape[1]
    lane = lax.broadcasted_iota(jnp.int32, (size, 8), 1)
    line = lax.broadcasted_iota(jnp.int32, (16, size), 0)
    experts = (
        (near_ref, d_gate_ref, d_up_ref), (other_near_ref, other_d_gate_ref, other_d_up_ref)
    )
    sides = (d_gate_ref, d_up_ref, other_d_gate_ref, other_d_up_ref)
    for index, (owner, gates_place, saved_places, windows, unused) in enumerate(passages):
        rows = slice(index * size, (index + 1) * size)
        lines = jnp.zeros((16, size), jnp.float32)
        gates = gates_refs[gates_place[0]][gates_place[1] : gates_place[1] + size, :]
        for which, (table_ref, d_gate_out, d_up_out) in enumerate(experts):
            number, first = saved_places[which]
            slope_ref, silu_ref, act_ref = saved[3 * number : 3 * number + 3]
            held = slice(first, first + size)
            near = table_ref[owner : owner + 1, :]
            own = jnp.sum(
                jnp.where(lane == expert ^ which, gates, 0.0), axis=1, keepdims=True
            )
            d_act = own.astype(jnp.bfloat16).astype(jnp.float32) * near
            d_gate_out[rows, :] = (d_act * slope_ref[held, :]).astype(jnp.bfloat16)
            d_up_out[rows, :] = (d_act * silu_ref[held, :]).astype(jnp.bfloat16)
            if windows[-1][1] == model_width:
                gate_grad = exact_dot(table_ref[...], act_ref[held, :], across)
                lines = jnp.where(line == expert ^ which, gate_grad[owner : owner + 1], lines)
        for start, stop in windows:
            out_ref, *out_refs = out_refs
            used = stop - start
            if stop == model_width:
                out_ref[used : used + 16, :] = lines.astype(jnp.bfloat16)
                used += 16
            if out_ref.shape[0] > used:
                out_ref[used:, :] = jnp.zeros((out_ref.shape[0] - used, size), jnp.bfloat16)
            for first in range(start, stop, 256):
                pick_grad = None
                for side_ref, matrix in zip(sides, matrices):
                    term = jnp.dot(
                        side_ref[rows, :],
                        matrix[:, first : first + 256],
                        preferred_element_type=jnp.float32,
                    )
                    pick_grad = term if pick_grad is None else pick_grad + term
                out_ref[first - start : first - start + 256, :] = pick_grad.T.astype(jnp.bfloat16)


def back(passages, near, other_near, gates, saved, matrices, size):
    hidden_units, model_width = matrices[0].shape
    heights = [
        max(least, stop - start + (16 if stop == model_width else 0))
        for passage in passages
        for (start, stop), least in zip(*passage[3:])
    ]
    arrays = [array for group in saved for array in group]
    return kernel_call(
        functools.partial(back_kernel, passages, len(gates), len(saved)),
        "back",
        [kept((height, size), jnp.bfloat16) for height in heights],
        [pinned(array) for array in (near, other_near, *gates, *arrays, *matrices)],
        (),
        [pltpu.VMEM((len(passages) * size, hidden_units), jnp.bfloat16)] * 4,
    )


def add_kernel(x_ref, y_ref, high_ref, low_ref, x_out, y_out):
    for own_ref, other_ref, out_ref in ((x_ref, high_ref, x_out), (y_ref, low_ref, y_out)):
        out_ref[...] = (
            own_ref[...].astype(jnp.float32)
            + other_ref[: own_ref.shape[0], :].astype(jnp.float32)
        ).astype(jnp.bfloat16)


def turn_kernel(*refs):
    count = len(refs) // 2
    for source_ref, target_ref in zip(refs[:count], refs[count:]):
        for first in range(0, source_ref.shape[0], 256):
            rows = slice(first, first + 256)
            target_ref[:, rows] = source_ref[rows, :].T


def turn(matrices):
    return kernel_call(
        turn_kernel,
        "turn",
        [kept(matrix.shape[::-1], jnp.bfloat16) for matrix in matrices],
        [pinned(matrix) for matrix in matrices],
    )


def half_kernel(part, rows_ref, out_ref):
    half = out_ref.shape[0]
    out_ref[...] = rows_ref[part * half : (part + 1) * half, :]


def half_of(rows, part):
    total, wide = rows.shape
    (out,) = kernel_call(
        functools.partial(half_kernel, part), "half", [kept((total // 2, wide), rows.dtype)], [rows]
    )
    return out


def pack_kernel(first_ref, second_ref, out_ref):
    out_ref[:1, :] = first_ref[:1, :]
    out_ref[1:, :] = second_ref[:1, :]


def pack(first, second):
    return kernel_call(
        pack_kernel, "pack", [kept((2, first.shape[1]), first.dtype)], [pinned(first), second]
    )[0]


def pairs_of(passages):
    row = lax.broadcasted_iota(jnp.int32, (8, 128), 0)
    lane = lax.broadcasted_iota(jnp.int32, (8, 128), 1)
    return row, lane, jnp.logical_and(row < passages, lane < passages)


def spread(index, values):
    total = jnp.zeros((8, 128), jnp.float32)
    for number, value in values:
        total = jnp.where(index == number, value, total)
    return total


def whole_sum(values):
    return jnp.sum(jnp.sum(values, axis=1, keepdims=True), axis=0, keepdims=True)


def swap_gains(grades_ref, ranks_ref):
    passages = grades_ref.shape[1]
    row, lane, pair = pairs_of(passages)
    grade_list = [(number, grades_ref[0, number].astype(jnp.float32)) for number in range(passages)]
    rank_list = [(number, ranks_ref[0, number].astype(jnp.float32)) for number in range(passages)]
    grade_row, grade_lane = spread(row, grade_list), spread(lane, grade_list)
    worth_row, worth_lane = jnp.exp2(grade_row), jnp.exp2(grade_lane)
    discount_row = 1.0 / jnp.log2(2.0 + spread(row, rank_list))
    discount_lane = 1.0 / jnp.log2(2.0 + spread(lane, rank_list))
    ahead = jnp.logical_or(
        grade_lane > grade_row, jnp.logical_and(grade_lane == grade_row, lane < row)
    )
    ideal_rank = jnp.sum(
        jnp.where(jnp.logical_and(pair, ahead), 1.0, 0.0), axis=1, keepdims=True
    )
    ideal_terms = (worth_row - 1.0) / jnp.log2(2.0 + ideal_rank)
    one_lane = jnp.logical_and(pair, lane == 0)
    ideal_gain = whole_sum(jnp.where(one_lane, ideal_terms, 0.0))
    swap_gain = (
        jnp.abs((worth_row - worth_lane) * (discount_row - discount_lane)) / ideal_gain
    )
    return jnp.where(jnp.logical_and(pair, grade_row > grade_lane), swap_gain, 0.0)


def rank_kernel(swap_gain_ref, near_scores_ref, far_scores_ref, loss_ref, factor_ref):
    passages = 2 * near_scores_ref.shape[0]
    place = lax.axis_index("psg")
    row, lane, unused = pairs_of(passages)
    score_list = [
        (place ^ (base + number), jnp.broadcast_to(ref[number : number + 1, :], (8, 128)))
        for base, ref in ((0, near_scores_ref), (passages // 2, far_scores_ref))
        for number in range(passages // 2)
    ]
    swap_gain = swap_gain_ref[...]
    margin = spread(row, score_list) - spread(lane, score_list)
    softplus = jnp.maximum(-margin, 0.0) + jnp.log1p(jnp.exp(-jnp.abs(margin)))
    loss_ref[...] = whole_sum(swap_gain * softplus)
    pull = swap_gain * jax.nn.sigmoid(-margin)
    gradient = whole_sum(jnp.where(lane == place, pull, 0.0) - jnp.where(row == place, pull, 0.0))
    factor_ref[...] = jnp.broadcast_to(gradient * loss_scale, factor_ref.shape)


def first_end_kernel(own_ref, x_low_ref, y_high_ref, total_ref, lines_ref):
    model_width = total_ref.shape[1]
    cut = model_width // 2
    for first in range(0, model_width, 256):
        rows = slice(first, first + 256)
        if first < cut:
            term = x_low_ref[rows, :]
        else:
            term = y_high_ref[first - cut : first - cut + 256, :]
        total = own_ref[rows, :].astype(jnp.float32) + term.astype(jnp.float32)
        total_ref[:, rows] = total.T
    end = slice(model_width, model_width + 8)
    end_high = slice(model_width - cut, model_width - cut + 8)
    lines_ref[...] = own_ref[end, :].astype(jnp.float32) + y_high_ref[end_high, :].astype(
        jnp.float32
    )


def end_kernel(
    factor_ref, total_ref, lines_ref, x_high_ref, y_low_ref,
    hidden_ref, gain_ref, gates_ref, router_ref, unit_ref,
    grad_far, turned_ref, grad_ref, copy_sems,
):
    token_count, model_width = hidden_ref.shape
    cut = y_low_ref.shape[0]
    end_high = slice(model_width - cut, model_width - cut + 8)
    slot_grad = lines_ref[...] + x_high_ref[end_high, :].astype(jnp.float32)
    gates = gates_ref[...]
    d_logit = gates * (slot_grad - jnp.sum(gates * slot_grad, axis=0, keepdims=True))
    d_logit = jnp.concatenate([d_logit, jnp.zeros((120, token_count), jnp.float32)], axis=0).T
    d_logit = jnp.concatenate(split_low(d_logit[:, :8]), axis=1)
    router_rows = jnp.concatenate([router_ref[...]] * 3, axis=0)
    for first in range(0, model_width, 256):
        columns = slice(first, first + 256)
        if first < cut:
            term = y_low_ref[columns, :]
        else:
            term = x_high_ref[first - cut : first - cut + 256, :]
        turned_ref[:, columns] = (
            total_ref[:, columns]
            + term.astype(jnp.float32).T
            + jnp.dot(d_logit, router_rows[:, columns], preferred_element_type=jnp.float32)
        )
    gain = gain_ref[...]
    factor = factor_ref[:, :1]
    size = 16
    copies = []
    for first in range(0, token_count, size):
        rows = slice(first, first + size)
        flat_rows = hidden_ref[rows, :].astype(jnp.float32)
        grad = norm_back(flat_rows, rms_scale(flat_rows), gain, turned_ref[rows, :])
        grad_ref[rows, :] = ((grad + unit_ref[...]) * factor).astype(jnp.bfloat16)
        copies.append(
            pltpu.make_async_copy(
                grad_ref.at[rows, :], grad_far.at[rows, :], copy_sems.at[first // size]
            )
        )
        copies[-1].start()
    for copy in copies:
        copy.wait()


def every_expert(
    hidden,
    norm_gain,
    router,
    gate_proj,
    up_proj,
    down_proj,
    final_gain,
    score_vector,
    expert_ids,
    grades,
    passage_ranks,
):
    unused_query, unused_passage, token_count, model_width = hidden.shape
    passages = grades.shape[1]
    flat = hidden.reshape(token_count, model_width)
    gate_matrix, up_matrix, down_matrix = gate_proj[0], up_proj[0], down_proj[0]
    mine = [gate_matrix, up_matrix, down_matrix]
    flat, gain, router_rows, normed, token_sums, head = kernel_call(
        norm_kernel,
        "norm",
        [
            kept(flat.shape, jnp.bfloat16),
            kept((1, model_width), jnp.float32),
            kept((8, model_width), jnp.bfloat16),
            kept(flat.shape, jnp.bfloat16),
            kept((1, model_width), jnp.float32),
            kept((1, model_width), jnp.float32),
        ],
        [
            flat,
            norm_gain.reshape(1, model_width),
            router.T,
            final_gain.reshape(1, model_width),
            score_vector.reshape(model_width // 128, 128),
        ],
        range(5),
        [
            pltpu.VMEM((1, model_width), jnp.float32),
            pltpu.VMEM((model_width // 128, 128), jnp.bfloat16),
            pltpu.SemaphoreType.DMA((5,)),
        ],
    )
    others = [swap(matrix, CORE) for matrix in mine]
    arrays = own_front(1, normed, router_rows, mine[:2])
    normed, *arrays = lax.optimization_barrier((normed, *arrays))
    x_rows, y_rows = swap(normed, ACROSS_X), swap(normed, ACROSS_Y)
    arrays = own_front(0, normed, router_rows, mine[:2], arrays)
    turned_gates, own_gates, *own_saved, own_part = arrays[:6]
    mine[:2] = arrays[6:]
    swap_gain, mine[2], *mine_turned, down_turned = get_ready(
        grades, passage_ranks, down_matrix, mine[:2]
    )
    x_rows, y_rows = after(x_rows, mine_turned[0]), after(y_rows, mine_turned[0])
    far_low = swap(half_of(x_rows, 0), ACROSS_Y)
    far_high = swap(half_of(y_rows, 1), ACROSS_X)
    side_gates, *side_saved, side_part = front(
        1, (1, 2), (0,), [x_rows, y_rows], router_rows, mine[:2]
    )
    others[0] = after(others[0], side_part)
    unused, *other_saved, other_part = front(
        2, (0, 1, 2), (1,), [normed, x_rows, y_rows], router_rows, others[:2]
    )
    far_low, far_high = after(far_low, other_part), after(far_high, other_part)
    far_gates, *far_saved, terms = front(
        3, (3,), (0, 1), [far_low, far_high], router_rows, mine[:2] + others[:2],
        (token_sums, mine[2], others[2], own_part, side_part, other_part),
    )

    *others_turned, other_down_turned = turn([after(others[0], terms), *others[1:]])
    head = after(head, others_turned[0])
    near, other_near, unit_vector, travelling, own_score = kernel_call(
        functools.partial(near_kernel, token_count=token_count),
        "near",
        [
            kept((8, down_matrix.shape[0]), jnp.float32),
            kept((8, down_matrix.shape[0]), jnp.float32),
            kept((1, model_width), jnp.float32),
            kept((1, 128), jnp.float32),
            shape_of((1, 1), jnp.float32),
        ],
        [
            pinned(terms),
            swap(terms, ACROSS_X),
            swap(terms, ACROSS_Y),
            swap(terms, ACROSS_X | ACROSS_Y),
            pinned(head),
            pinned(down_turned),
            pinned(other_down_turned),
        ],
    )
    matrices = [*mine_turned, *others_turned]
    middle = model_width // 2
    lower, upper, early, earlier = (0, middle), (middle, model_width), middle + 32, middle + 48
    far_low, far_high = back(
        ((3, (0, 0), ((0, 0), (1, 0)), (lower, upper), (earlier, earlier)),),
        near, other_near, [far_gates], [far_saved[:3], far_saved[3:]], matrices, token_count,
    )
    far_sent = far_low
    far_low, far_high = swap(far_low, ACROSS_X), swap(far_high, ACROSS_Y)

    def sides_back(x_window, y_window, least, *earlier):
        return back(
            (
                (1, (0, 0), ((0, 0), (1, token_count)), (x_window,), (least,)),
                (2, (0, token_count), ((0, token_count), (1, 2 * token_count)), (y_window,), (least,)),
            ),
            after(near, *earlier), other_near, [side_gates], [side_saved, other_saved], matrices,
            token_count,
        )

    x_low, y_high = sides_back(lower, upper, early, far_sent)
    first_sent = x_low
    x_low, y_high = swap(x_low, ACROSS_X), swap(y_high, ACROSS_Y)
    x_high, y_low = sides_back(upper, lower, 0, first_sent)
    travelling = after(travelling, first_sent)
    met = lax.ppermute(travelling, "psg", [(index, index ^ 1) for index in range(passages)])
    near_scores = pack(travelling, met)
    far_high = after(far_high, near_scores)
    x_high, y_low = kernel_call(
        add_kernel,
        "add",
        [kept(x_high.shape, jnp.bfloat16), kept(y_low.shape, jnp.bfloat16)],
        [pinned(x_high), pinned(y_low), far_high, far_low],
    )
    x_high, y_low, near_scores, other_near = lax.optimization_barrier(
        (x_high, y_low, near_scores, other_near)
    )
    x_high, y_low = swap(x_high, ACROSS_X), swap(y_low, ACROSS_Y)
    (own_sums,) = back(
        ((0, (0, 0), ((0, 0), (1, 0)), ((0, model_width),), (0,)),),
        near, other_near, [own_gates], [own_saved, other_saved], matrices, token_count,
    )
    far_scores = lax.ppermute(near_scores, "psg", [(index, index ^ 2) for index in range(passages)])
    loss, factor = kernel_call(
        rank_kernel,
        "rank",
        [shape_of((1, 1), jnp.float32), kept((1, 128), jnp.float32)],
        [pinned(swap_gain), pinned(near_scores), far_scores],
    )
    total, lines = kernel_call(
        first_end_kernel,
        "first_end",
        [
            kept((token_count, model_width), jnp.float32),
            kept((8, token_count), jnp.float32),
        ],
        [pinned(own_sums), after(x_low, factor), y_high],
    )
    (grad,) = kernel_call(
        end_kernel,
        "end",
        [shape_of((token_count, model_width), jnp.bfloat16)],
        [
            pinned(factor), pinned(total), pinned(lines), x_high, y_low, pinned(flat), pinned(gain),
            pinned(turned_gates), pinned(router_rows), pinned(unit_vector),
        ],
        scratch=[
            pltpu.VMEM((token_count, model_width), jnp.float32),
            pltpu.VMEM((token_count, model_width), jnp.bfloat16),
            pltpu.SemaphoreType.DMA((token_count // 16,)),
        ],
        result=pl.ANY,
    )
    return (loss.reshape(1), own_score, grad.reshape(hidden.shape))


def block(*arrays):
    hidden, router, expert_ids, grades = arrays[0], arrays[2], arrays[8], arrays[9]
    each_expert = router.shape[1] == expert_ids.shape[3] == 8
    if hidden.shape[1] == 1 and each_expert and grades.shape[1] == 4:
        return every_expert(*arrays)
    return local(*arrays)


def solution(mesh):
    placed = (
        P("exp", "psg", None, None),
        P(),
        P(),
        P("exp", None, None),
        P("exp", None, None),
        P("exp", None, None),
        P(),
        P(),
        P("exp", "psg", None, None),
        P("exp", None),
        P("exp", None),
    )
    return jax.shard_map(
        block,
        mesh=mesh,
        in_specs=placed,
        out_specs=(P("exp"), P("exp", "psg"), P("exp", "psg", None, None)),
        check_vma=False,
    )
```

```python
import functools
import math

import jax
import jax.numpy as jnp
from jax import lax
from jax.experimental import pallas as pl
from jax.experimental.pallas import tpu as pltpu
from jax.sharding import PartitionSpec as P

epsilon = 1e-06
loss_scale = 256.0
highest = lax.Precision.HIGHEST


def rms_scale(values):
    return lax.rsqrt(jnp.mean(values * values, axis=-1, keepdims=True) + epsilon)


def head_score(pooled, final_gain, score_vector):
    scaled = pooled * rms_scale(pooled) * final_gain
    return jnp.dot(scaled, score_vector.astype(jnp.float32), precision=highest)


def rank_loss(scores, grades, passage_ranks):
    grade_value = grades.astype(jnp.float32)
    worth_gain = jnp.exp2(grade_value)
    discount = 1.0 / jnp.log2(2.0 + passage_ranks.astype(jnp.float32))
    better_than = grades[None, :] > grades[:, None]
    equal_grade = grades[None, :] == grades[:, None]
    position = jnp.arange(grades.shape[0], dtype=jnp.int32)
    earlier = position[None, :] < position[:, None]
    ideal_rank = jnp.sum(
        jnp.logical_or(better_than, jnp.logical_and(equal_grade, earlier)).astype(jnp.float32),
        axis=1,
    )
    ideal_gain = jnp.sum((worth_gain - 1.0) / jnp.log2(2.0 + ideal_rank))
    ordered = (grades[:, None] > grades[None, :]).astype(jnp.float32)
    swap_gain = (
        jnp.abs(
            (worth_gain[:, None] - worth_gain[None, :]) * (discount[:, None] - discount[None, :])
        )
        / ideal_gain
    )
    margin = scores[:, None] - scores[None, :]
    return jnp.sum(ordered * swap_gain * jax.nn.softplus(-margin))


def pick_gates(normed, router, picked_ids):
    expert_total = router.shape[1]
    logits = jnp.dot(normed, router, preferred_element_type=jnp.float32)
    onehot = (
        picked_ids[:, :, None] == jnp.arange(expert_total, dtype=jnp.int32)[None, None, :]
    ).astype(jnp.float32)
    chosen = jnp.einsum("nke,ne->nk", onehot, logits, precision=highest)
    weights = jnp.exp(chosen)
    return (weights / jnp.sum(weights, axis=1, keepdims=True), onehot)


def gate_parts(pre_gate):
    sigmoid_gate = jax.nn.sigmoid(pre_gate)
    return (pre_gate * sigmoid_gate, sigmoid_gate * (1.0 + pre_gate * (1.0 - sigmoid_gate)))


def norm_back(flat_rows, inverse, norm_gain, d_normed):
    scaled = d_normed * norm_gain
    return inverse * scaled - flat_rows * inverse * inverse * inverse * jnp.mean(
        flat_rows * scaled, axis=-1, keepdims=True
    )


def unpack_front(front_out, buffer_rows):
    pre_gate, pre_up, received = front_out
    hidden_units = pre_gate.shape[2]
    pre_gate = pre_gate.reshape(buffer_rows, hidden_units)
    pre_up = pre_up.reshape(buffer_rows, hidden_units)
    silu_gate, slope = gate_parts(pre_gate)
    activation = (silu_gate * pre_up).astype(jnp.bfloat16)
    return (pre_up, received, silu_gate, slope, activation)


def local(
    hidden,
    norm_gain,
    router,
    gate_proj,
    up_proj,
    down_proj,
    final_gain,
    score_vector,
    expert_ids,
    grades,
    passage_ranks,
):
    unused_query, local_passages, local_positions, model_width = hidden.shape
    top_count = expert_ids.shape[3]
    expert_count = lax.axis_size("exp")
    token_count = local_passages * local_positions
    slot_count = token_count * top_count
    capacity = min(token_count, 9 * token_count * top_count // (8 * expert_count))
    buffer_rows = expert_count * capacity
    flat_rows = hidden.reshape(token_count, model_width).astype(jnp.float32)
    inverse = rms_scale(flat_rows)
    normed = (flat_rows * inverse * norm_gain).astype(jnp.bfloat16)
    picked_ids = expert_ids.reshape(token_count, top_count)
    gate_values, onehot = pick_gates(normed, router, picked_ids)
    slot_hits = onehot.reshape(slot_count, expert_count).astype(jnp.int32)
    slot_rank = jnp.sum((jnp.cumsum(slot_hits, axis=0) - slot_hits) * slot_hits, axis=1)
    target = picked_ids.reshape(slot_count) * capacity + slot_rank
    source_token = jnp.arange(slot_count, dtype=jnp.int32) // top_count
    passage_onehot = (
        source_token[:, None] // local_positions
        == jnp.arange(local_passages, dtype=jnp.int32)[None, :]
    ).astype(jnp.float32)
    weighted = (passage_onehot * gate_values.reshape(slot_count, 1)).astype(jnp.bfloat16)
    send_rows = (
        jnp.zeros((buffer_rows, model_width), jnp.bfloat16).at[target].set(normed[source_token])
    )
    send_weights = jnp.zeros((buffer_rows, local_passages), jnp.bfloat16).at[target].set(weighted)
    outgoing = (
        send_rows.reshape(expert_count, capacity, model_width),
        send_weights.reshape(expert_count, capacity, local_passages),
    )
    gate_matrix = gate_proj[0]
    up_matrix = up_proj[0]
    down_matrix = down_proj[0]
    rows_in = lax.all_to_all(outgoing[0], "exp", split_axis=0, concat_axis=0, tiled=True)
    weights_in = lax.all_to_all(outgoing[1], "exp", split_axis=0, concat_axis=0, tiled=True)
    pre_gate = jnp.einsum("end,df->enf", rows_in, gate_matrix, preferred_element_type=jnp.float32)
    pre_up = jnp.einsum("end,df->enf", rows_in, up_matrix, preferred_element_type=jnp.float32)
    front_out = (pre_gate, pre_up, weights_in)
    pre_up, received, silu_gate, slope, activation = unpack_front(front_out, buffer_rows)
    hidden_units = activation.shape[1]
    passage_part = jnp.einsum(
        "scp,scf->spf",
        received,
        activation.reshape(expert_count, capacity, hidden_units),
        preferred_element_type=jnp.float32,
    )
    down_wide = down_matrix.astype(jnp.float32)
    expert_terms = jnp.einsum("spf,fd->spd", passage_part, down_wide, precision=highest)
    came_back = lax.all_to_all(expert_terms, "exp", split_axis=0, concat_axis=0, tiled=True)
    token_sums = jnp.sum(flat_rows.reshape(local_passages, local_positions, model_width), axis=1)
    pooled = (token_sums + jnp.sum(came_back, axis=0)) / local_positions
    first_row = lax.axis_index("psg") * local_passages
    own_score = head_score(pooled, final_gain, score_vector)
    every_score = lax.all_gather(own_score, "psg", axis=0, tiled=True)
    loss_value, loss_grad = jax.value_and_grad(rank_loss)(every_score, grades[0], passage_ranks[0])
    d_own = lax.dynamic_slice_in_dim(loss_grad, first_row, local_passages, 0) * loss_scale
    unused_score, head_back = jax.vjp(
        lambda values: head_score(values, final_gain, score_vector), pooled
    )
    d_vector = head_back(d_own)[0] / local_positions
    every_vector = lax.all_gather(d_vector[None], "exp", axis=0, tiled=True)
    near_table = jnp.einsum("spd,fd->spf", every_vector, down_wide, precision=highest)
    present = (received != 0).astype(jnp.float32)
    near_rows = jnp.einsum("scp,spf->scf", present, near_table, precision=highest).reshape(
        buffer_rows, hidden_units
    )
    gate_weight = jnp.sum(received.astype(jnp.float32), axis=2).reshape(buffer_rows, 1)
    d_act = gate_weight * near_rows
    d_gate = (d_act * pre_up * slope).astype(jnp.bfloat16)
    d_up = (d_act * silu_gate).astype(jnp.bfloat16)
    contract = (((1,), (1,)), ((), ()))
    pick_grad = lax.dot_general(d_gate, gate_matrix, contract, preferred_element_type=jnp.float32)
    pick_grad = (
        pick_grad + lax.dot_general(d_up, up_matrix, contract, preferred_element_type=jnp.float32)
    ).astype(jnp.bfloat16)
    gate_grad = jnp.sum(activation.astype(jnp.float32) * near_rows, axis=1).astype(jnp.bfloat16)
    back_rows, back_gate = (
        lax.all_to_all(
            pick_grad.reshape(expert_count, capacity, model_width),
            "exp",
            split_axis=0,
            concat_axis=0,
            tiled=True,
        ),
        lax.all_to_all(
            gate_grad.reshape(expert_count, capacity),
            "exp",
            split_axis=0,
            concat_axis=0,
            tiled=True,
        ),
    )
    picked_rows = back_rows.reshape(buffer_rows, model_width)[target]
    d_normed = jnp.sum(
        picked_rows.reshape(token_count, top_count, model_width).astype(jnp.float32), axis=1
    )
    picked_gate = (
        back_gate.reshape(buffer_rows)[target].astype(jnp.float32).reshape(token_count, top_count)
    )
    d_logit = gate_values * (
        picked_gate - jnp.sum(gate_values * picked_gate, axis=1, keepdims=True)
    )
    dense_logit = jnp.einsum("nk,nke->ne", d_logit, onehot, precision=highest)
    d_normed = d_normed + jnp.einsum(
        "ne,de->nd", dense_logit, router.astype(jnp.float32), precision=highest
    )
    grad_flat = norm_back(flat_rows, inverse, norm_gain, d_normed)
    grad_hidden = (
        grad_flat.reshape(1, local_passages, local_positions, model_width)
        + d_vector[None, :, None, :]
    )
    return (
        loss_value.reshape(1),
        own_score.reshape(1, local_passages),
        grad_hidden.astype(jnp.bfloat16),
    )


CORE, ACROSS_X, ACROSS_Y = 1, 2, 4
forward = (((1,), (0,)), ((), ()))
across = (((1,), (1,)), ((), ()))
MIB = 1 << 20


def swap(value, bit, size=8):
    return lax.ppermute(value, "exp", [(index, index ^ bit) for index in range(size)])


def shape_of(shape, dtype):
    return jax.ShapeDtypeStruct(shape, dtype)


def after(value, *others):
    return lax.optimization_barrier((value, *others))[0]


def kept(shape, dtype):
    return pltpu.VMEM(shape, dtype)


def pinned(array):
    return pltpu.with_memory_space_constraint(array, pltpu.VMEM)


def kernel_call(body, name, outs, ins, far=(), scratch=(), result=pltpu.VMEM, earlier=()):
    aliases = {len(ins) + index: index for index in range(len(earlier))}
    ins = [*ins, *(pinned(array) for array in earlier)]
    spaces = [pltpu.VMEM] * len(ins)
    for index in far:
        spaces[index] = pl.ANY
        ins[index] = pltpu.with_memory_space_constraint(ins[index], pltpu.HBM)
    return pl.pallas_call(
        body,
        name=name,
        out_shape=outs,
        in_specs=[pl.BlockSpec(memory_space=space) for space in spaces],
        out_specs=[pl.BlockSpec(memory_space=result)] * len(outs),
        scratch_shapes=scratch,
        input_output_aliases=aliases,
        compiler_params=pltpu.CompilerParams(vmem_limit_bytes=8 * MIB),
        cost_estimate=pl.CostEstimate(flops=1, bytes_accessed=1, transcendentals=0),
    )(*ins)


def split_low(values):
    high = values.astype(jnp.bfloat16)
    rest = values - high.astype(jnp.float32)
    middle = rest.astype(jnp.bfloat16)
    low = (rest - middle.astype(jnp.float32)).astype(jnp.bfloat16)
    return high, middle, low


def exact_dot(values, low_matrix, contract):
    parts = lax.dot_general(
        jnp.concatenate(split_low(values), axis=0),
        low_matrix,
        contract,
        preferred_element_type=jnp.float32,
    )
    return parts[0:8] + parts[8:16] + parts[16:24]


def other_order(values, bits):
    return jnp.concatenate([values[row ^ bits : (row ^ bits) + 1] for row in range(4)], axis=0)


def norm_kernel(
    hidden_far, gain_far, router_far, final_far, vector_far,
    hidden_ref, gain_ref, router_ref, normed_ref, sums_ref, head_ref,
    final_ref, vector_ref, copy_sems,
):
    pairs = (
        (hidden_far, hidden_ref), (gain_far, gain_ref), (router_far, router_ref),
        (final_far, final_ref), (vector_far, vector_ref),
    )
    copies = [
        pltpu.make_async_copy(source, target, copy_sems.at[index])
        for index, (source, target) in enumerate(pairs)
    ]
    for copy in copies:
        copy.start()
    for copy in copies:
        copy.wait()
    vector = vector_ref[...].astype(jnp.float32)
    vector = jnp.concatenate([vector[row : row + 1] for row in range(vector.shape[0])], axis=1)
    head_ref[...] = final_ref[...] * vector
    rows = hidden_ref[...].astype(jnp.float32)
    normed_ref[...] = (rows * rms_scale(rows) * gain_ref[...]).astype(jnp.bfloat16)
    sums_ref[...] = jnp.sum(rows, axis=0, keepdims=True)


def on_side(side, body, held, far_count, *refs):
    refs = refs[:far_count] + refs[far_count + held :]

    @pl.when(lax.rem(lax.axis_index("exp"), 2) == side)
    def run():
        body(*refs)


def front_kernel(stage, owners, sets, count, router_ref, *refs):
    matrices, refs = refs[: 2 * len(sets)], refs[2 * len(sets) :]
    pieces, refs = refs[:count], refs[count:]
    matrices = list(matrices)
    hidden_units = matrices[0].shape[1]
    tile = 256
    firsts = range(0, hidden_units, tile)
    if stage == 3:
        sums_ref, *downs = refs[:3]
        earlier, refs = (refs[3:5], refs[5:7]), refs[7:]
        *refs, terms_ref, rows_ref = refs
    else:
        *refs, rows_ref = refs
    gates_ref, *outs = refs
    expert = lax.axis_index("exp")
    first = 0
    for piece in pieces:
        rows_ref[first : first + piece.shape[0], :] = piece[...]
        first += piece.shape[0]
    size = first // len(owners)
    logits = lax.dot_general(
        rows_ref[...], router_ref[...], across, preferred_element_type=jnp.float32
    )
    weights = jnp.exp(logits)
    gates = weights / jnp.sum(weights, axis=1, keepdims=True)
    gates_ref[...] = gates
    lane = lax.broadcasted_iota(jnp.int32, gates.shape, 1)

    totals = []
    for place, which in enumerate(sets):
        gate_ref, up_ref = matrices[2 * place : 2 * place + 2]
        if stage == 3:
            slope_ref, silu_ref, act_ref = outs[3 * place : 3 * place + 3]
        else:
            slope_ref, silu_ref, act_ref, part_ref = outs
        own = jnp.sum(jnp.where(lane == expert ^ which, gates, 0.0), axis=1, keepdims=True)
        low = own.astype(jnp.bfloat16).astype(jnp.float32)
        parts = []
        for first in firsts:
            columns = slice(first, first + tile)
            rows = rows_ref[...]
            pre_gate = jnp.dot(rows, gate_ref[:, columns], preferred_element_type=jnp.float32)
            pre_up = jnp.dot(rows, up_ref[:, columns], preferred_element_type=jnp.float32)
            silu_gate, slope = gate_parts(pre_gate)
            activation = (silu_gate * pre_up).astype(jnp.bfloat16)
            slope_ref[:, columns] = slope * pre_up
            silu_ref[:, columns] = silu_gate
            act_ref[:, columns] = activation
            weighted = activation.astype(jnp.float32) * low
            found = {
                owner: jnp.sum(weighted[index * size : (index + 1) * size], axis=0, keepdims=True)
                for index, owner in enumerate(owners)
            }
            nothing = jnp.zeros_like(weighted[:1])
            parts.append(
                jnp.concatenate([found.get(owner, nothing) for owner in range(8)], axis=0)
            )
        totals.append(jnp.concatenate(parts, axis=1))
    if stage < 3:
        part_ref[...] = totals[0]
        return
    totals = [
        total + (first_ref[...] + second_ref[...])
        for total, (first_ref, second_ref) in zip(totals, earlier)
    ]
    terms = exact_dot(totals[0], downs[0][...], forward) + exact_dot(
        totals[1], downs[1][...], forward
    )
    row = lax.broadcasted_iota(jnp.int32, terms.shape, 0)
    terms_ref[...] = (terms + jnp.where(row == 0, sums_ref[...], 0.0))[:4]


def front(stage, owners, sets, pieces, router_rows, matrices, more=()):
    model_width, hidden_units = matrices[0].shape
    row_total = sum(piece.shape[0] for piece in pieces)
    outs = [kept((row_total, 8), jnp.float32)]
    for which in sets:
        outs += [
            kept((row_total, hidden_units), jnp.float32),
            kept((row_total, hidden_units), jnp.float32),
            kept((row_total, hidden_units), jnp.bfloat16),
        ]
    outs.append(
        kept((4, model_width), jnp.float32) if stage == 3 else kept((8, hidden_units), jnp.float32)
    )
    scratch = [pltpu.VMEM((row_total, model_width), jnp.bfloat16)]
    matrices = [pinned(matrix) for matrix in matrices]
    if stage == 3:
        more = [pinned(array) for array in more]
    return kernel_call(
        functools.partial(front_kernel, stage, owners, sets, len(pieces)),
        "front",
        outs,
        [pinned(router_rows), *matrices, *(pinned(piece) for piece in pieces), *more],
        (),
        scratch,
    )


def turn_block(source_ref, target_ref, rows, columns):
    target_ref[columns, rows] = source_ref[rows, columns].T


def own_kernel(
    grades_far, ranks_far, gate_far, up_far, down_far, router_ref, rows_ref,
    turned_ref, gates_ref, slope_ref, silu_ref, act_ref, part_ref, swap_gain_ref,
    gate_ref, up_ref, down_ref, gate_turned_ref, up_turned_ref, down_turned_ref,
    grades_ref, ranks_ref, copy_sems,
):
    hidden_units = gate_ref.shape[1]
    model_width = gate_ref.shape[0]
    tile = 256
    pairs = [(grades_far, grades_ref), (ranks_far, ranks_ref)]
    for first in range(0, hidden_units, tile):
        columns = slice(first, first + tile)
        pairs += [
            (gate_far.at[:, columns], gate_ref.at[:, columns]),
            (up_far.at[:, columns], up_ref.at[:, columns]),
        ]
    pairs.append((down_far, down_ref))
    copies = [
        pltpu.make_async_copy(source, target, copy_sems.at[index])
        for index, (source, target) in enumerate(pairs)
    ]
    for copy in copies:
        copy.start()
    rows = rows_ref[...]
    weights = jnp.exp(
        lax.dot_general(rows, router_ref[...], across, preferred_element_type=jnp.float32)
    )
    gates = weights / jnp.sum(weights, axis=1, keepdims=True)
    gates_ref[...] = gates
    weights = jnp.exp(
        lax.dot_general(router_ref[...], rows, across, preferred_element_type=jnp.float32)
    )
    turned_ref[...] = weights / jnp.sum(weights, axis=0, keepdims=True)
    lane = lax.broadcasted_iota(jnp.int32, gates.shape, 1)
    own = jnp.sum(
        jnp.where(lane == lax.axis_index("exp"), gates, 0.0), axis=1, keepdims=True
    )
    low = own.astype(jnp.bfloat16).astype(jnp.float32)
    copies[0].wait()
    copies[1].wait()
    swap_gain_ref[...] = swap_gains(grades_ref, ranks_ref)
    for number, first in enumerate(range(0, hidden_units, tile)):
        columns = slice(first, first + tile)
        copies[2 + 2 * number].wait()
        copies[3 + 2 * number].wait()
        pre_gate = jnp.dot(rows, gate_ref[:, columns], preferred_element_type=jnp.float32)
        pre_up = jnp.dot(rows, up_ref[:, columns], preferred_element_type=jnp.float32)
        silu_gate, slope = gate_parts(pre_gate)
        activation = (silu_gate * pre_up).astype(jnp.bfloat16)
        slope_ref[:, columns] = slope * pre_up
        silu_ref[:, columns] = silu_gate
        act_ref[:, columns] = activation
        total = jnp.sum(activation.astype(jnp.float32) * low, axis=0, keepdims=True)
        part_ref[:, columns] = jnp.concatenate([total, jnp.zeros((7, tile), jnp.float32)], axis=0)
        for start in range(0, model_width, tile):
            block = slice(start, start + tile)
            turn_block(gate_ref, gate_turned_ref, block, columns)
            turn_block(up_ref, up_turned_ref, block, columns)
    copies[-1].wait()
    for first in range(0, hidden_units, tile):
        for start in range(0, model_width, tile):
            turn_block(
                down_ref, down_turned_ref, slice(first, first + tile), slice(start, start + tile)
            )


def own_front(side, normed, router_rows, matrices, grades, passage_ranks, earlier=()):
    model_width, hidden_units = matrices[0].shape
    token_count = normed.shape[0]
    ins = [grades, passage_ranks, *matrices, pinned(router_rows), pinned(normed)]
    return kernel_call(
        functools.partial(on_side, side, own_kernel, len(earlier), len(ins)),
        "own",
        [
            kept((8, token_count), jnp.float32),
            kept((token_count, 8), jnp.float32),
            kept((token_count, hidden_units), jnp.float32),
            kept((token_count, hidden_units), jnp.float32),
            kept((token_count, hidden_units), jnp.bfloat16),
            kept((8, hidden_units), jnp.float32),
            kept((8, 128), jnp.float32),
            *(kept(matrix.shape, jnp.bfloat16) for matrix in matrices),
            *(kept(matrix.shape[::-1], jnp.bfloat16) for matrix in matrices),
        ],
        ins,
        range(5),
        [
            pltpu.SMEM(grades.shape, jnp.int32),
            pltpu.SMEM(grades.shape, jnp.int32),
            pltpu.SemaphoreType.DMA((3 + 2 * (hidden_units // 256),)),
        ],
        earlier=earlier,
    )


def near_kernel(
    own_ref, x_ref, y_ref, far_ref, head_ref, down_ref, other_down_ref,
    near_ref, other_near_ref, unit_ref, score_ref, own_score_ref, *, token_count,
):
    pooled = (
        (own_ref[...] + other_order(x_ref[...], 1))
        + (other_order(y_ref[...], 2) + other_order(far_ref[...], 3))
    ) / token_count
    pooled = jnp.concatenate([pooled, jnp.zeros_like(pooled)], axis=0)
    head = head_ref[...]
    scale = rms_scale(pooled)
    along = jnp.sum(pooled * head, axis=1, keepdims=True)
    own_score = (scale * along)[:1]
    own_score_ref[...] = own_score
    score_ref[...] = jnp.broadcast_to(own_score, score_ref.shape)
    unit = (
        scale * head - scale * scale * scale * (along / pooled.shape[1]) * pooled
    ) / token_count
    unit_ref[...] = unit[:1]
    near_ref[...] = exact_dot(unit, down_ref[...], forward)
    other_near_ref[...] = exact_dot(unit, other_down_ref[...], forward)


def back_kernel(passages, gate_count, saved_count, near_ref, other_near_ref, *refs):
    gates_refs, refs = refs[:gate_count], refs[gate_count:]
    saved, refs = refs[: 3 * saved_count], refs[3 * saved_count :]
    matrices, refs = refs[:4], refs[4:]
    *out_refs, d_gate_ref, d_up_ref, other_d_gate_ref, other_d_up_ref = refs
    expert = lax.axis_index("exp")
    size = out_refs[0].shape[1]
    model_width = matrices[0].shape[1]
    lane = lax.broadcasted_iota(jnp.int32, (size, 8), 1)
    line = lax.broadcasted_iota(jnp.int32, (16, size), 0)
    experts = (
        (near_ref, d_gate_ref, d_up_ref), (other_near_ref, other_d_gate_ref, other_d_up_ref)
    )
    sides = (d_gate_ref, d_up_ref, other_d_gate_ref, other_d_up_ref)
    for index, (owner, gates_place, saved_places, windows, unused) in enumerate(passages):
        rows = slice(index * size, (index + 1) * size)
        lines = jnp.zeros((16, size), jnp.float32)
        gates = gates_refs[gates_place[0]][gates_place[1] : gates_place[1] + size, :]
        for which, (table_ref, d_gate_out, d_up_out) in enumerate(experts):
            number, first = saved_places[which]
            slope_ref, silu_ref, act_ref = saved[3 * number : 3 * number + 3]
            held = slice(first, first + size)
            near = table_ref[owner : owner + 1, :]
            own = jnp.sum(
                jnp.where(lane == expert ^ which, gates, 0.0), axis=1, keepdims=True
            )
            d_act = own.astype(jnp.bfloat16).astype(jnp.float32) * near
            d_gate_out[rows, :] = (d_act * slope_ref[held, :]).astype(jnp.bfloat16)
            d_up_out[rows, :] = (d_act * silu_ref[held, :]).astype(jnp.bfloat16)
            if windows[-1][1] == model_width:
                gate_grad = exact_dot(table_ref[...], act_ref[held, :], across)
                lines = jnp.where(line == expert ^ which, gate_grad[owner : owner + 1], lines)
        for start, stop in windows:
            out_ref, *out_refs = out_refs
            used = stop - start
            if stop == model_width:
                out_ref[used : used + 16, :] = lines.astype(jnp.bfloat16)
                used += 16
            if out_ref.shape[0] > used:
                out_ref[used:, :] = jnp.zeros((out_ref.shape[0] - used, size), jnp.bfloat16)
            for first in range(start, stop, 256):
                pick_grad = None
                for side_ref, matrix in zip(sides, matrices):
                    term = jnp.dot(
                        side_ref[rows, :],
                        matrix[:, first : first + 256],
                        preferred_element_type=jnp.float32,
                    )
                    pick_grad = term if pick_grad is None else pick_grad + term
                out_ref[first - start : first - start + 256, :] = pick_grad.T.astype(jnp.bfloat16)


def back(passages, near, other_near, gates, saved, matrices, size):
    hidden_units, model_width = matrices[0].shape
    heights = [
        max(least, stop - start + (16 if stop == model_width else 0))
        for passage in passages
        for (start, stop), least in zip(*passage[3:])
    ]
    arrays = [array for group in saved for array in group]
    return kernel_call(
        functools.partial(back_kernel, passages, len(gates), len(saved)),
        "back",
        [kept((height, size), jnp.bfloat16) for height in heights],
        [pinned(array) for array in (near, other_near, *gates, *arrays, *matrices)],
        (),
        [pltpu.VMEM((len(passages) * size, hidden_units), jnp.bfloat16)] * 4,
    )


def add_kernel(x_ref, y_ref, high_ref, low_ref, x_out, y_out):
    for own_ref, other_ref, out_ref in ((x_ref, high_ref, x_out), (y_ref, low_ref, y_out)):
        out_ref[...] = (
            own_ref[...].astype(jnp.float32)
            + other_ref[: own_ref.shape[0], :].astype(jnp.float32)
        ).astype(jnp.bfloat16)


def turn_kernel(*refs):
    count = len(refs) // 2
    for source_ref, target_ref in zip(refs[:count], refs[count:]):
        for first in range(0, source_ref.shape[0], 256):
            rows = slice(first, first + 256)
            target_ref[:, rows] = source_ref[rows, :].T


def turn(matrices):
    return kernel_call(
        turn_kernel,
        "turn",
        [kept(matrix.shape[::-1], jnp.bfloat16) for matrix in matrices],
        [pinned(matrix) for matrix in matrices],
    )


def half_kernel(part, rows_ref, out_ref):
    half = out_ref.shape[0]
    out_ref[...] = rows_ref[part * half : (part + 1) * half, :]


def half_of(rows, part):
    total, wide = rows.shape
    (out,) = kernel_call(
        functools.partial(half_kernel, part), "half", [kept((total // 2, wide), rows.dtype)], [rows]
    )
    return out


def pack_kernel(first_ref, second_ref, out_ref):
    out_ref[:1, :] = first_ref[:1, :]
    out_ref[1:, :] = second_ref[:1, :]


def pack(first, second):
    return kernel_call(
        pack_kernel, "pack", [kept((2, first.shape[1]), first.dtype)], [pinned(first), second]
    )[0]


def pairs_of(passages):
    row = lax.broadcasted_iota(jnp.int32, (8, 128), 0)
    lane = lax.broadcasted_iota(jnp.int32, (8, 128), 1)
    return row, lane, jnp.logical_and(row < passages, lane < passages)


def spread(index, values):
    total = jnp.zeros((8, 128), jnp.float32)
    for number, value in values:
        total = jnp.where(index == number, value, total)
    return total


def whole_sum(values):
    return jnp.sum(jnp.sum(values, axis=1, keepdims=True), axis=0, keepdims=True)


def swap_gains(grades_ref, ranks_ref):
    passages = grades_ref.shape[1]
    row, lane, pair = pairs_of(passages)
    grade_list = [(number, grades_ref[0, number].astype(jnp.float32)) for number in range(passages)]
    rank_list = [(number, ranks_ref[0, number].astype(jnp.float32)) for number in range(passages)]
    grade_row, grade_lane = spread(row, grade_list), spread(lane, grade_list)
    worth_row, worth_lane = jnp.exp2(grade_row), jnp.exp2(grade_lane)
    discount_row = 1.0 / jnp.log2(2.0 + spread(row, rank_list))
    discount_lane = 1.0 / jnp.log2(2.0 + spread(lane, rank_list))
    ahead = jnp.logical_or(
        grade_lane > grade_row, jnp.logical_and(grade_lane == grade_row, lane < row)
    )
    ideal_rank = jnp.sum(
        jnp.where(jnp.logical_and(pair, ahead), 1.0, 0.0), axis=1, keepdims=True
    )
    ideal_terms = (worth_row - 1.0) / jnp.log2(2.0 + ideal_rank)
    one_lane = jnp.logical_and(pair, lane == 0)
    ideal_gain = whole_sum(jnp.where(one_lane, ideal_terms, 0.0))
    swap_gain = (
        jnp.abs((worth_row - worth_lane) * (discount_row - discount_lane)) / ideal_gain
    )
    return jnp.where(jnp.logical_and(pair, grade_row > grade_lane), swap_gain, 0.0)


def rank_kernel(swap_gain_ref, near_scores_ref, far_scores_ref, loss_ref, factor_ref):
    passages = 2 * near_scores_ref.shape[0]
    place = lax.axis_index("psg")
    row, lane, unused = pairs_of(passages)
    score_list = [
        (place ^ (base + number), jnp.broadcast_to(ref[number : number + 1, :], (8, 128)))
        for base, ref in ((0, near_scores_ref), (passages // 2, far_scores_ref))
        for number in range(passages // 2)
    ]
    swap_gain = swap_gain_ref[...]
    margin = spread(row, score_list) - spread(lane, score_list)
    softplus = jnp.maximum(-margin, 0.0) + jnp.log1p(jnp.exp(-jnp.abs(margin)))
    loss_ref[...] = whole_sum(swap_gain * softplus)
    pull = swap_gain * jax.nn.sigmoid(-margin)
    gradient = whole_sum(jnp.where(lane == place, pull, 0.0) - jnp.where(row == place, pull, 0.0))
    factor_ref[...] = jnp.broadcast_to(gradient * loss_scale, factor_ref.shape)


def first_end_kernel(own_ref, x_low_ref, y_high_ref, total_ref, lines_ref):
    model_width = total_ref.shape[1]
    cut = model_width // 2
    for first in range(0, model_width, 256):
        rows = slice(first, first + 256)
        if first < cut:
            term = x_low_ref[rows, :]
        else:
            term = y_high_ref[first - cut : first - cut + 256, :]
        total = own_ref[rows, :].astype(jnp.float32) + term.astype(jnp.float32)
        total_ref[:, rows] = total.T
    end = slice(model_width, model_width + 8)
    end_high = slice(model_width - cut, model_width - cut + 8)
    lines_ref[...] = own_ref[end, :].astype(jnp.float32) + y_high_ref[end_high, :].astype(
        jnp.float32
    )


def end_kernel(
    factor_ref, total_ref, lines_ref, x_high_ref, y_low_ref,
    hidden_ref, gain_ref, gates_ref, router_ref, unit_ref,
    grad_far, turned_ref, grad_ref, copy_sems,
):
    token_count, model_width = hidden_ref.shape
    cut = y_low_ref.shape[0]
    end_high = slice(model_width - cut, model_width - cut + 8)
    slot_grad = lines_ref[...] + x_high_ref[end_high, :].astype(jnp.float32)
    gates = gates_ref[...]
    d_logit = gates * (slot_grad - jnp.sum(gates * slot_grad, axis=0, keepdims=True))
    d_logit = jnp.concatenate([d_logit, jnp.zeros((120, token_count), jnp.float32)], axis=0).T
    d_logit = jnp.concatenate(split_low(d_logit[:, :8]), axis=1)
    router_rows = jnp.concatenate([router_ref[...]] * 3, axis=0)
    for first in range(0, model_width, 256):
        columns = slice(first, first + 256)
        if first < cut:
            term = y_low_ref[columns, :]
        else:
            term = x_high_ref[first - cut : first - cut + 256, :]
        turned_ref[:, columns] = (
            total_ref[:, columns]
            + term.astype(jnp.float32).T
            + jnp.dot(d_logit, router_rows[:, columns], preferred_element_type=jnp.float32)
        )
    gain = gain_ref[...]
    factor = factor_ref[:, :1]
    size = 16
    copies = []
    for first in range(0, token_count, size):
        rows = slice(first, first + size)
        flat_rows = hidden_ref[rows, :].astype(jnp.float32)
        grad = norm_back(flat_rows, rms_scale(flat_rows), gain, turned_ref[rows, :])
        grad_ref[rows, :] = ((grad + unit_ref[...]) * factor).astype(jnp.bfloat16)
        copies.append(
            pltpu.make_async_copy(
                grad_ref.at[rows, :], grad_far.at[rows, :], copy_sems.at[first // size]
            )
        )
        copies[-1].start()
    for copy in copies:
        copy.wait()


def every_expert(
    hidden,
    norm_gain,
    router,
    gate_proj,
    up_proj,
    down_proj,
    final_gain,
    score_vector,
    expert_ids,
    grades,
    passage_ranks,
):
    unused_query, unused_passage, token_count, model_width = hidden.shape
    passages = grades.shape[1]
    flat = hidden.reshape(token_count, model_width)
    gate_matrix, up_matrix, down_matrix = gate_proj[0], up_proj[0], down_proj[0]
    mine = [gate_matrix, up_matrix, down_matrix]
    flat, gain, router_rows, normed, token_sums, head = kernel_call(
        norm_kernel,
        "norm",
        [
            kept(flat.shape, jnp.bfloat16),
            kept((1, model_width), jnp.float32),
            kept((8, model_width), jnp.bfloat16),
            kept(flat.shape, jnp.bfloat16),
            kept((1, model_width), jnp.float32),
            kept((1, model_width), jnp.float32),
        ],
        [
            flat,
            norm_gain.reshape(1, model_width),
            router.T,
            final_gain.reshape(1, model_width),
            score_vector.reshape(model_width // 128, 128),
        ],
        range(5),
        [
            pltpu.VMEM((1, model_width), jnp.float32),
            pltpu.VMEM((model_width // 128, 128), jnp.bfloat16),
            pltpu.SemaphoreType.DMA((5,)),
        ],
    )
    others = [swap(matrix, CORE) for matrix in mine[:2]]
    arrays = own_front(1, normed, router_rows, mine, grades, passage_ranks)
    normed, *arrays = lax.optimization_barrier((normed, *arrays))
    x_rows, y_rows = swap(normed, ACROSS_X), swap(normed, ACROSS_Y)
    arrays = own_front(0, normed, router_rows, mine, grades, passage_ranks, arrays)
    turned_gates, own_gates, *own_saved, own_part, swap_gain = arrays[:7]
    mine, (*mine_turned, down_turned) = list(arrays[7:10]), arrays[10:]
    unused, *other_own_saved, other_own_part = front(
        2, (0,), (1,), [after(normed, mine_turned[0])], router_rows, others[:2]
    )
    x_rows, y_rows = after(x_rows, other_own_part), after(y_rows, other_own_part)
    others.append(swap(after(mine[2], x_rows, y_rows), CORE))
    far_low = swap(half_of(x_rows, 0), ACROSS_Y)
    far_high = swap(half_of(y_rows, 1), ACROSS_X)
    side_gates, *side_saved, side_part = front(
        1, (1, 2), (0,), [x_rows, y_rows], router_rows, mine[:2]
    )
    others[0] = after(others[0], side_part)
    unused, *other_saved, other_part = front(
        2, (1, 2), (1,), [x_rows, y_rows], router_rows, others[:2]
    )
    far_low, far_high = after(far_low, other_part), after(far_high, other_part)
    far_gates, *far_saved, terms = front(
        3, (3,), (0, 1), [far_low, far_high], router_rows, mine[:2] + others[:2],
        (
            token_sums, mine[2], others[2],
            own_part, side_part, other_own_part, other_part,
        ),
    )

    *others_turned, other_down_turned = turn([after(others[0], terms), *others[1:]])
    head = after(head, others_turned[0])
    near, other_near, unit_vector, travelling, own_score = kernel_call(
        functools.partial(near_kernel, token_count=token_count),
        "near",
        [
            kept((8, down_matrix.shape[0]), jnp.float32),
            kept((8, down_matrix.shape[0]), jnp.float32),
            kept((1, model_width), jnp.float32),
            kept((1, 128), jnp.float32),
            shape_of((1, 1), jnp.float32),
        ],
        [
            pinned(terms),
            swap(terms, ACROSS_X),
            swap(terms, ACROSS_Y),
            swap(terms, ACROSS_X | ACROSS_Y),
            pinned(head),
            pinned(down_turned),
            pinned(other_down_turned),
        ],
    )
    matrices = [*mine_turned, *others_turned]
    middle = model_width // 2
    lower, upper, early, earlier = (0, middle), (middle, model_width), middle + 32, middle + 48
    far_low, far_high = back(
        ((3, (0, 0), ((0, 0), (1, 0)), (lower, upper), (earlier, earlier)),),
        near, other_near, [far_gates], [far_saved[:3], far_saved[3:]], matrices, token_count,
    )
    far_sent = far_low
    far_low, far_high = swap(far_low, ACROSS_X), swap(far_high, ACROSS_Y)

    def sides_back(x_window, y_window, least, *earlier):
        return back(
            (
                (1, (0, 0), ((0, 0), (1, 0)), (x_window,), (least,)),
                (2, (0, token_count), ((0, token_count), (1, token_count)), (y_window,), (least,)),
            ),
            after(near, *earlier), other_near, [side_gates], [side_saved, other_saved], matrices,
            token_count,
        )

    x_low, y_high = sides_back(lower, upper, early, far_sent)
    first_sent = x_low
    x_low, y_high = swap(x_low, ACROSS_X), swap(y_high, ACROSS_Y)
    x_high, y_low = sides_back(upper, lower, 0, first_sent)
    travelling = after(travelling, first_sent)
    met = lax.ppermute(travelling, "psg", [(index, index ^ 1) for index in range(passages)])
    near_scores = pack(travelling, met)
    far_high = after(far_high, near_scores)
    x_high, y_low = kernel_call(
        add_kernel,
        "add",
        [kept(x_high.shape, jnp.bfloat16), kept(y_low.shape, jnp.bfloat16)],
        [pinned(x_high), pinned(y_low), far_high, far_low],
    )
    x_high, y_low, near_scores, other_near = lax.optimization_barrier(
        (x_high, y_low, near_scores, other_near)
    )
    x_high, y_low = swap(x_high, ACROSS_X), swap(y_low, ACROSS_Y)
    (own_sums,) = back(
        ((0, (0, 0), ((0, 0), (1, 0)), ((0, model_width),), (0,)),),
        near, other_near, [own_gates], [own_saved, other_own_saved], matrices, token_count,
    )
    far_scores = lax.ppermute(near_scores, "psg", [(index, index ^ 2) for index in range(passages)])
    loss, factor = kernel_call(
        rank_kernel,
        "rank",
        [shape_of((1, 1), jnp.float32), kept((1, 128), jnp.float32)],
        [pinned(swap_gain), pinned(near_scores), far_scores],
    )
    total, lines = kernel_call(
        first_end_kernel,
        "first_end",
        [
            kept((token_count, model_width), jnp.float32),
            kept((8, token_count), jnp.float32),
        ],
        [pinned(own_sums), after(x_low, factor), y_high],
    )
    (grad,) = kernel_call(
        end_kernel,
        "end",
        [shape_of((token_count, model_width), jnp.bfloat16)],
        [
            pinned(factor), pinned(total), pinned(lines), x_high, y_low, pinned(flat), pinned(gain),
            pinned(turned_gates), pinned(router_rows), pinned(unit_vector),
        ],
        scratch=[
            pltpu.VMEM((token_count, model_width), jnp.float32),
            pltpu.VMEM((token_count, model_width), jnp.bfloat16),
            pltpu.SemaphoreType.DMA((token_count // 16,)),
        ],
        result=pl.ANY,
    )
    return (loss.reshape(1), own_score, grad.reshape(hidden.shape))


def block(*arrays):
    hidden, router, expert_ids, grades = arrays[0], arrays[2], arrays[8], arrays[9]
    each_expert = router.shape[1] == expert_ids.shape[3] == 8
    if hidden.shape[1] == 1 and each_expert and grades.shape[1] == 4:
        return every_expert(*arrays)
    return local(*arrays)


def solution(mesh):
    placed = (
        P("exp", "psg", None, None),
        P(),
        P(),
        P("exp", None, None),
        P("exp", None, None),
        P("exp", None, None),
        P(),
        P(),
        P("exp", "psg", None, None),
        P("exp", None),
        P("exp", None),
    )
    return jax.shard_map(
        block,
        mesh=mesh,
        in_specs=placed,
        out_specs=(P("exp"), P("exp", "psg"), P("exp", "psg", None, None)),
        check_vma=False,
    )
```

```python
import functools
import math

import jax
import jax.numpy as jnp
from jax import lax
from jax.experimental import pallas as pl
from jax.experimental.pallas import tpu as pltpu
from jax.sharding import PartitionSpec as P

epsilon = 1e-06
loss_scale = 256.0
highest = lax.Precision.HIGHEST


def rms_scale(values):
    return lax.rsqrt(jnp.mean(values * values, axis=-1, keepdims=True) + epsilon)


def head_score(pooled, final_gain, score_vector):
    scaled = pooled * rms_scale(pooled) * final_gain
    return jnp.dot(scaled, score_vector.astype(jnp.float32), precision=highest)


def rank_loss(scores, grades, passage_ranks):
    grade_value = grades.astype(jnp.float32)
    worth_gain = jnp.exp2(grade_value)
    discount = 1.0 / jnp.log2(2.0 + passage_ranks.astype(jnp.float32))
    better_than = grades[None, :] > grades[:, None]
    equal_grade = grades[None, :] == grades[:, None]
    position = jnp.arange(grades.shape[0], dtype=jnp.int32)
    earlier = position[None, :] < position[:, None]
    ideal_rank = jnp.sum(
        jnp.logical_or(better_than, jnp.logical_and(equal_grade, earlier)).astype(jnp.float32),
        axis=1,
    )
    ideal_gain = jnp.sum((worth_gain - 1.0) / jnp.log2(2.0 + ideal_rank))
    ordered = (grades[:, None] > grades[None, :]).astype(jnp.float32)
    swap_gain = (
        jnp.abs(
            (worth_gain[:, None] - worth_gain[None, :]) * (discount[:, None] - discount[None, :])
        )
        / ideal_gain
    )
    margin = scores[:, None] - scores[None, :]
    return jnp.sum(ordered * swap_gain * jax.nn.softplus(-margin))


def pick_gates(normed, router, picked_ids):
    expert_total = router.shape[1]
    logits = jnp.dot(normed, router, preferred_element_type=jnp.float32)
    onehot = (
        picked_ids[:, :, None] == jnp.arange(expert_total, dtype=jnp.int32)[None, None, :]
    ).astype(jnp.float32)
    chosen = jnp.einsum("nke,ne->nk", onehot, logits, precision=highest)
    weights = jnp.exp(chosen)
    return (weights / jnp.sum(weights, axis=1, keepdims=True), onehot)


def gate_parts(pre_gate):
    sigmoid_gate = jax.nn.sigmoid(pre_gate)
    return (pre_gate * sigmoid_gate, sigmoid_gate * (1.0 + pre_gate * (1.0 - sigmoid_gate)))


def norm_back(flat_rows, inverse, norm_gain, d_normed):
    scaled = d_normed * norm_gain
    return inverse * scaled - flat_rows * inverse * inverse * inverse * jnp.mean(
        flat_rows * scaled, axis=-1, keepdims=True
    )


def unpack_front(front_out, buffer_rows):
    pre_gate, pre_up, received = front_out
    hidden_units = pre_gate.shape[2]
    pre_gate = pre_gate.reshape(buffer_rows, hidden_units)
    pre_up = pre_up.reshape(buffer_rows, hidden_units)
    silu_gate, slope = gate_parts(pre_gate)
    activation = (silu_gate * pre_up).astype(jnp.bfloat16)
    return (pre_up, received, silu_gate, slope, activation)


def local(
    hidden,
    norm_gain,
    router,
    gate_proj,
    up_proj,
    down_proj,
    final_gain,
    score_vector,
    expert_ids,
    grades,
    passage_ranks,
):
    unused_query, local_passages, local_positions, model_width = hidden.shape
    top_count = expert_ids.shape[3]
    expert_count = lax.axis_size("exp")
    token_count = local_passages * local_positions
    slot_count = token_count * top_count
    capacity = min(token_count, 9 * token_count * top_count // (8 * expert_count))
    buffer_rows = expert_count * capacity
    flat_rows = hidden.reshape(token_count, model_width).astype(jnp.float32)
    inverse = rms_scale(flat_rows)
    normed = (flat_rows * inverse * norm_gain).astype(jnp.bfloat16)
    picked_ids = expert_ids.reshape(token_count, top_count)
    gate_values, onehot = pick_gates(normed, router, picked_ids)
    slot_hits = onehot.reshape(slot_count, expert_count).astype(jnp.int32)
    slot_rank = jnp.sum((jnp.cumsum(slot_hits, axis=0) - slot_hits) * slot_hits, axis=1)
    target = picked_ids.reshape(slot_count) * capacity + slot_rank
    source_token = jnp.arange(slot_count, dtype=jnp.int32) // top_count
    passage_onehot = (
        source_token[:, None] // local_positions
        == jnp.arange(local_passages, dtype=jnp.int32)[None, :]
    ).astype(jnp.float32)
    weighted = (passage_onehot * gate_values.reshape(slot_count, 1)).astype(jnp.bfloat16)
    send_rows = (
        jnp.zeros((buffer_rows, model_width), jnp.bfloat16).at[target].set(normed[source_token])
    )
    send_weights = jnp.zeros((buffer_rows, local_passages), jnp.bfloat16).at[target].set(weighted)
    outgoing = (
        send_rows.reshape(expert_count, capacity, model_width),
        send_weights.reshape(expert_count, capacity, local_passages),
    )
    gate_matrix = gate_proj[0]
    up_matrix = up_proj[0]
    down_matrix = down_proj[0]
    rows_in = lax.all_to_all(outgoing[0], "exp", split_axis=0, concat_axis=0, tiled=True)
    weights_in = lax.all_to_all(outgoing[1], "exp", split_axis=0, concat_axis=0, tiled=True)
    pre_gate = jnp.einsum("end,df->enf", rows_in, gate_matrix, preferred_element_type=jnp.float32)
    pre_up = jnp.einsum("end,df->enf", rows_in, up_matrix, preferred_element_type=jnp.float32)
    front_out = (pre_gate, pre_up, weights_in)
    pre_up, received, silu_gate, slope, activation = unpack_front(front_out, buffer_rows)
    hidden_units = activation.shape[1]
    passage_part = jnp.einsum(
        "scp,scf->spf",
        received,
        activation.reshape(expert_count, capacity, hidden_units),
        preferred_element_type=jnp.float32,
    )
    down_wide = down_matrix.astype(jnp.float32)
    expert_terms = jnp.einsum("spf,fd->spd", passage_part, down_wide, precision=highest)
    came_back = lax.all_to_all(expert_terms, "exp", split_axis=0, concat_axis=0, tiled=True)
    token_sums = jnp.sum(flat_rows.reshape(local_passages, local_positions, model_width), axis=1)
    pooled = (token_sums + jnp.sum(came_back, axis=0)) / local_positions
    first_row = lax.axis_index("psg") * local_passages
    own_score = head_score(pooled, final_gain, score_vector)
    every_score = lax.all_gather(own_score, "psg", axis=0, tiled=True)
    loss_value, loss_grad = jax.value_and_grad(rank_loss)(every_score, grades[0], passage_ranks[0])
    d_own = lax.dynamic_slice_in_dim(loss_grad, first_row, local_passages, 0) * loss_scale
    unused_score, head_back = jax.vjp(
        lambda values: head_score(values, final_gain, score_vector), pooled
    )
    d_vector = head_back(d_own)[0] / local_positions
    every_vector = lax.all_gather(d_vector[None], "exp", axis=0, tiled=True)
    near_table = jnp.einsum("spd,fd->spf", every_vector, down_wide, precision=highest)
    present = (received != 0).astype(jnp.float32)
    near_rows = jnp.einsum("scp,spf->scf", present, near_table, precision=highest).reshape(
        buffer_rows, hidden_units
    )
    gate_weight = jnp.sum(received.astype(jnp.float32), axis=2).reshape(buffer_rows, 1)
    d_act = gate_weight * near_rows
    d_gate = (d_act * pre_up * slope).astype(jnp.bfloat16)
    d_up = (d_act * silu_gate).astype(jnp.bfloat16)
    contract = (((1,), (1,)), ((), ()))
    pick_grad = lax.dot_general(d_gate, gate_matrix, contract, preferred_element_type=jnp.float32)
    pick_grad = (
        pick_grad + lax.dot_general(d_up, up_matrix, contract, preferred_element_type=jnp.float32)
    ).astype(jnp.bfloat16)
    gate_grad = jnp.sum(activation.astype(jnp.float32) * near_rows, axis=1).astype(jnp.bfloat16)
    back_rows, back_gate = (
        lax.all_to_all(
            pick_grad.reshape(expert_count, capacity, model_width),
            "exp",
            split_axis=0,
            concat_axis=0,
            tiled=True,
        ),
        lax.all_to_all(
            gate_grad.reshape(expert_count, capacity),
            "exp",
            split_axis=0,
            concat_axis=0,
            tiled=True,
        ),
    )
    picked_rows = back_rows.reshape(buffer_rows, model_width)[target]
    d_normed = jnp.sum(
        picked_rows.reshape(token_count, top_count, model_width).astype(jnp.float32), axis=1
    )
    picked_gate = (
        back_gate.reshape(buffer_rows)[target].astype(jnp.float32).reshape(token_count, top_count)
    )
    d_logit = gate_values * (
        picked_gate - jnp.sum(gate_values * picked_gate, axis=1, keepdims=True)
    )
    dense_logit = jnp.einsum("nk,nke->ne", d_logit, onehot, precision=highest)
    d_normed = d_normed + jnp.einsum(
        "ne,de->nd", dense_logit, router.astype(jnp.float32), precision=highest
    )
    grad_flat = norm_back(flat_rows, inverse, norm_gain, d_normed)
    grad_hidden = (
        grad_flat.reshape(1, local_passages, local_positions, model_width)
        + d_vector[None, :, None, :]
    )
    return (
        loss_value.reshape(1),
        own_score.reshape(1, local_passages),
        grad_hidden.astype(jnp.bfloat16),
    )


CORE, ACROSS_X, ACROSS_Y = 1, 2, 4
forward = (((1,), (0,)), ((), ()))
across = (((1,), (1,)), ((), ()))
MIB = 1 << 20


def swap(value, bit, size=8):
    return lax.ppermute(value, "exp", [(index, index ^ bit) for index in range(size)])


def shape_of(shape, dtype):
    return jax.ShapeDtypeStruct(shape, dtype)


def after(value, *others):
    return lax.optimization_barrier((value, *others))[0]


def kept(shape, dtype):
    return pltpu.VMEM(shape, dtype)


def pinned(array):
    return pltpu.with_memory_space_constraint(array, pltpu.VMEM)


def kernel_call(body, name, outs, ins, far=(), scratch=(), result=pltpu.VMEM, earlier=()):
    aliases = {len(ins) + index: index for index in range(len(earlier))}
    ins = [*ins, *(pinned(array) for array in earlier)]
    spaces = [pltpu.VMEM] * len(ins)
    for index in far:
        spaces[index] = pl.ANY
        ins[index] = pltpu.with_memory_space_constraint(ins[index], pltpu.HBM)
    return pl.pallas_call(
        body,
        name=name,
        out_shape=outs,
        in_specs=[pl.BlockSpec(memory_space=space) for space in spaces],
        out_specs=[pl.BlockSpec(memory_space=result)] * len(outs),
        scratch_shapes=scratch,
        input_output_aliases=aliases,
        compiler_params=pltpu.CompilerParams(vmem_limit_bytes=8 * MIB),
        cost_estimate=pl.CostEstimate(flops=1, bytes_accessed=1, transcendentals=0),
    )(*ins)


def split_low(values):
    high = values.astype(jnp.bfloat16)
    rest = values - high.astype(jnp.float32)
    middle = rest.astype(jnp.bfloat16)
    low = (rest - middle.astype(jnp.float32)).astype(jnp.bfloat16)
    return high, middle, low


def exact_dot(values, low_matrix, contract):
    parts = lax.dot_general(
        jnp.concatenate(split_low(values), axis=0),
        low_matrix,
        contract,
        preferred_element_type=jnp.float32,
    )
    return parts[0:8] + parts[8:16] + parts[16:24]


def other_order(values, bits):
    return jnp.concatenate([values[row ^ bits : (row ^ bits) + 1] for row in range(4)], axis=0)


def norm_kernel(
    hidden_far, gain_far, router_far, final_far, vector_far,
    hidden_ref, gain_ref, router_ref, normed_ref, sums_ref, head_ref,
    final_ref, vector_ref, copy_sems,
):
    pairs = (
        (hidden_far, hidden_ref), (gain_far, gain_ref), (router_far, router_ref),
        (final_far, final_ref), (vector_far, vector_ref),
    )
    copies = [
        pltpu.make_async_copy(source, target, copy_sems.at[index])
        for index, (source, target) in enumerate(pairs)
    ]
    for copy in copies:
        copy.start()
    for copy in copies:
        copy.wait()
    vector = vector_ref[...].astype(jnp.float32)
    vector = jnp.concatenate([vector[row : row + 1] for row in range(vector.shape[0])], axis=1)
    head_ref[...] = final_ref[...] * vector
    rows = hidden_ref[...].astype(jnp.float32)
    normed_ref[...] = (rows * rms_scale(rows) * gain_ref[...]).astype(jnp.bfloat16)
    sums_ref[...] = jnp.sum(rows, axis=0, keepdims=True)


def on_side(side, body, held, far_count, *refs):
    refs = refs[:far_count] + refs[far_count + held :]

    @pl.when(lax.rem(lax.axis_index("exp"), 2) == side)
    def run():
        body(*refs)


def front_kernel(stage, owners, sets, count, router_ref, *refs):
    matrices, refs = refs[: 2 * len(sets)], refs[2 * len(sets) :]
    pieces, refs = refs[:count], refs[count:]
    matrices = list(matrices)
    hidden_units = matrices[0].shape[1]
    tile = 256
    firsts = range(0, hidden_units, tile)
    if stage == 3:
        sums_ref, *downs = refs[:3]
        earlier, refs = refs[3:6], refs[6:]
        *refs, terms_ref, rows_ref = refs
    else:
        *refs, rows_ref = refs
    gates_ref, *outs = refs
    expert = lax.axis_index("exp")
    first = 0
    for piece in pieces:
        rows_ref[first : first + piece.shape[0], :] = piece[...]
        first += piece.shape[0]
    size = first // len(owners)
    logits = lax.dot_general(
        rows_ref[...], router_ref[...], across, preferred_element_type=jnp.float32
    )
    weights = jnp.exp(logits)
    gates = weights / jnp.sum(weights, axis=1, keepdims=True)
    gates_ref[...] = gates
    lane = lax.broadcasted_iota(jnp.int32, gates.shape, 1)

    totals = []
    for place, which in enumerate(sets):
        gate_ref, up_ref = matrices[2 * place : 2 * place + 2]
        if stage == 3:
            slope_ref, silu_ref, act_ref = outs[3 * place : 3 * place + 3]
        else:
            slope_ref, silu_ref, act_ref, part_ref = outs
        own = jnp.sum(jnp.where(lane == expert ^ which, gates, 0.0), axis=1, keepdims=True)
        low = own.astype(jnp.bfloat16).astype(jnp.float32)
        parts = []
        for first in firsts:
            columns = slice(first, first + tile)
            rows = rows_ref[...]
            pre_gate = jnp.dot(rows, gate_ref[:, columns], preferred_element_type=jnp.float32)
            pre_up = jnp.dot(rows, up_ref[:, columns], preferred_element_type=jnp.float32)
            silu_gate, slope = gate_parts(pre_gate)
            activation = (silu_gate * pre_up).astype(jnp.bfloat16)
            slope_ref[:, columns] = slope * pre_up
            silu_ref[:, columns] = silu_gate
            act_ref[:, columns] = activation
            weighted = activation.astype(jnp.float32) * low
            found = {
                owner: jnp.sum(weighted[index * size : (index + 1) * size], axis=0, keepdims=True)
                for index, owner in enumerate(owners)
            }
            nothing = jnp.zeros_like(weighted[:1])
            parts.append(
                jnp.concatenate([found.get(owner, nothing) for owner in range(8)], axis=0)
            )
        totals.append(jnp.concatenate(parts, axis=1))
    if stage < 3:
        part_ref[...] = totals[0]
        return
    own_first, own_second, other_first = earlier
    totals[0] = totals[0] + (own_first[...] + own_second[...])
    totals[1] = totals[1] + other_first[...]
    terms = exact_dot(totals[0], downs[0][...], forward) + exact_dot(
        totals[1], downs[1][...], forward
    )
    row = lax.broadcasted_iota(jnp.int32, terms.shape, 0)
    terms_ref[...] = (terms + jnp.where(row == 0, sums_ref[...], 0.0))[:4]


def front(stage, owners, sets, pieces, router_rows, matrices, more=()):
    model_width, hidden_units = matrices[0].shape
    row_total = sum(piece.shape[0] for piece in pieces)
    outs = [kept((row_total, 8), jnp.float32)]
    for which in sets:
        outs += [
            kept((row_total, hidden_units), jnp.float32),
            kept((row_total, hidden_units), jnp.float32),
            kept((row_total, hidden_units), jnp.bfloat16),
        ]
    outs.append(
        kept((4, model_width), jnp.float32) if stage == 3 else kept((8, hidden_units), jnp.float32)
    )
    scratch = [pltpu.VMEM((row_total, model_width), jnp.bfloat16)]
    matrices = [pinned(matrix) for matrix in matrices]
    if stage == 3:
        more = [pinned(array) for array in more]
    return kernel_call(
        functools.partial(front_kernel, stage, owners, sets, len(pieces)),
        "front",
        outs,
        [pinned(router_rows), *matrices, *(pinned(piece) for piece in pieces), *more],
        (),
        scratch,
    )


def own_kernel(
    gate_far, up_far, router_ref, rows_ref,
    turned_ref, gates_ref, slope_ref, silu_ref, act_ref, part_ref, gate_ref, up_ref, copy_sems,
):
    hidden_units = gate_ref.shape[1]
    tile = 256
    pairs = []
    for first in range(0, hidden_units, tile):
        columns = slice(first, first + tile)
        pairs += [
            (gate_far.at[:, columns], gate_ref.at[:, columns]),
            (up_far.at[:, columns], up_ref.at[:, columns]),
        ]
    copies = [
        pltpu.make_async_copy(source, target, copy_sems.at[index])
        for index, (source, target) in enumerate(pairs)
    ]
    for copy in copies:
        copy.start()
    rows = rows_ref[...]
    weights = jnp.exp(
        lax.dot_general(rows, router_ref[...], across, preferred_element_type=jnp.float32)
    )
    gates = weights / jnp.sum(weights, axis=1, keepdims=True)
    gates_ref[...] = gates
    weights = jnp.exp(
        lax.dot_general(router_ref[...], rows, across, preferred_element_type=jnp.float32)
    )
    turned_ref[...] = weights / jnp.sum(weights, axis=0, keepdims=True)
    lane = lax.broadcasted_iota(jnp.int32, gates.shape, 1)
    own = jnp.sum(
        jnp.where(lane == lax.axis_index("exp"), gates, 0.0), axis=1, keepdims=True
    )
    low = own.astype(jnp.bfloat16).astype(jnp.float32)
    for number, first in enumerate(range(0, hidden_units, tile)):
        columns = slice(first, first + tile)
        copies[2 * number].wait()
        copies[2 * number + 1].wait()
        pre_gate = jnp.dot(rows, gate_ref[:, columns], preferred_element_type=jnp.float32)
        pre_up = jnp.dot(rows, up_ref[:, columns], preferred_element_type=jnp.float32)
        silu_gate, slope = gate_parts(pre_gate)
        activation = (silu_gate * pre_up).astype(jnp.bfloat16)
        slope_ref[:, columns] = slope * pre_up
        silu_ref[:, columns] = silu_gate
        act_ref[:, columns] = activation
        total = jnp.sum(activation.astype(jnp.float32) * low, axis=0, keepdims=True)
        part_ref[:, columns] = jnp.concatenate([total, jnp.zeros((7, tile), jnp.float32)], axis=0)


def own_front(side, normed, router_rows, matrices, earlier=()):
    hidden_units = matrices[0].shape[1]
    token_count = normed.shape[0]
    ins = [*matrices, pinned(router_rows), pinned(normed)]
    return kernel_call(
        functools.partial(on_side, side, own_kernel, len(earlier), len(ins)),
        "own",
        [
            kept((8, token_count), jnp.float32),
            kept((token_count, 8), jnp.float32),
            kept((token_count, hidden_units), jnp.float32),
            kept((token_count, hidden_units), jnp.float32),
            kept((token_count, hidden_units), jnp.bfloat16),
            kept((8, hidden_units), jnp.float32),
            *(kept(matrix.shape, jnp.bfloat16) for matrix in matrices),
        ],
        ins,
        range(2),
        [pltpu.SemaphoreType.DMA((2 * (hidden_units // 256),))],
        earlier=earlier,
    )


def ready_kernel(
    grades_far, ranks_far, down_far, gate_ref, up_ref,
    swap_gain_ref, down_ref, gate_turned_ref, up_turned_ref, down_turned_ref,
    grades_ref, ranks_ref, copy_sems,
):
    pairs = ((grades_far, grades_ref), (ranks_far, ranks_ref), (down_far, down_ref))
    copies = [
        pltpu.make_async_copy(source, target, copy_sems.at[index])
        for index, (source, target) in enumerate(pairs)
    ]
    for copy in copies:
        copy.start()
    turn_kernel(gate_ref, up_ref, gate_turned_ref, up_turned_ref)
    copies[0].wait()
    copies[1].wait()
    swap_gain_ref[...] = swap_gains(grades_ref, ranks_ref)
    copies[2].wait()
    turn_kernel(down_ref, down_turned_ref)


def get_ready(side, grades, passage_ranks, down_matrix, matrices, earlier=()):
    return kernel_call(
        functools.partial(on_side, side, ready_kernel, len(earlier), 5),
        "ready",
        [
            kept((8, 128), jnp.float32),
            kept(down_matrix.shape, jnp.bfloat16),
            *(kept(matrix.shape[::-1], jnp.bfloat16) for matrix in (*matrices, down_matrix)),
        ],
        [grades, passage_ranks, down_matrix, *(pinned(matrix) for matrix in matrices)],
        range(3),
        [
            pltpu.SMEM(grades.shape, jnp.int32),
            pltpu.SMEM(grades.shape, jnp.int32),
            pltpu.SemaphoreType.DMA((3,)),
        ],
        earlier=earlier,
    )


def near_kernel(
    own_ref, x_ref, y_ref, far_ref, head_ref, down_ref, other_down_ref,
    near_ref, other_near_ref, unit_ref, score_ref, own_score_ref, *, token_count,
):
    pooled = (
        (own_ref[...] + other_order(x_ref[...], 1))
        + (other_order(y_ref[...], 2) + other_order(far_ref[...], 3))
    ) / token_count
    pooled = jnp.concatenate([pooled, jnp.zeros_like(pooled)], axis=0)
    head = head_ref[...]
    scale = rms_scale(pooled)
    along = jnp.sum(pooled * head, axis=1, keepdims=True)
    own_score = (scale * along)[:1]
    own_score_ref[...] = own_score
    score_ref[...] = jnp.broadcast_to(own_score, score_ref.shape)
    unit = (
        scale * head - scale * scale * scale * (along / pooled.shape[1]) * pooled
    ) / token_count
    unit_ref[...] = unit[:1]
    near_ref[...] = exact_dot(unit, down_ref[...], forward)
    other_near_ref[...] = exact_dot(unit, other_down_ref[...], forward)


def back_kernel(passages, gate_count, saved_count, near_ref, other_near_ref, *refs):
    gates_refs, refs = refs[:gate_count], refs[gate_count:]
    saved, refs = refs[: 3 * saved_count], refs[3 * saved_count :]
    matrices, refs = refs[:4], refs[4:]
    *out_refs, d_gate_ref, d_up_ref, other_d_gate_ref, other_d_up_ref = refs
    expert = lax.axis_index("exp")
    size = out_refs[0].shape[1]
    model_width = matrices[0].shape[1]
    lane = lax.broadcasted_iota(jnp.int32, (size, 8), 1)
    line = lax.broadcasted_iota(jnp.int32, (16, size), 0)
    experts = (
        (near_ref, d_gate_ref, d_up_ref), (other_near_ref, other_d_gate_ref, other_d_up_ref)
    )
    sides = (d_gate_ref, d_up_ref, other_d_gate_ref, other_d_up_ref)
    for index, (owner, gates_place, saved_places, windows, unused) in enumerate(passages):
        rows = slice(index * size, (index + 1) * size)
        lines = jnp.zeros((16, size), jnp.float32)
        gates = gates_refs[gates_place[0]][gates_place[1] : gates_place[1] + size, :]
        for which, (table_ref, d_gate_out, d_up_out) in enumerate(experts):
            number, first = saved_places[which]
            slope_ref, silu_ref, act_ref = saved[3 * number : 3 * number + 3]
            held = slice(first, first + size)
            near = table_ref[owner : owner + 1, :]
            own = jnp.sum(
                jnp.where(lane == expert ^ which, gates, 0.0), axis=1, keepdims=True
            )
            d_act = own.astype(jnp.bfloat16).astype(jnp.float32) * near
            d_gate_out[rows, :] = (d_act * slope_ref[held, :]).astype(jnp.bfloat16)
            d_up_out[rows, :] = (d_act * silu_ref[held, :]).astype(jnp.bfloat16)
            if windows[-1][1] == model_width:
                gate_grad = exact_dot(table_ref[...], act_ref[held, :], across)
                lines = jnp.where(line == expert ^ which, gate_grad[owner : owner + 1], lines)
        for start, stop in windows:
            out_ref, *out_refs = out_refs
            used = stop - start
            if stop == model_width:
                out_ref[used : used + 16, :] = lines.astype(jnp.bfloat16)
                used += 16
            if out_ref.shape[0] > used:
                out_ref[used:, :] = jnp.zeros((out_ref.shape[0] - used, size), jnp.bfloat16)
            for first in range(start, stop, 256):
                pick_grad = None
                for side_ref, matrix in zip(sides, matrices):
                    term = jnp.dot(
                        side_ref[rows, :],
                        matrix[:, first : first + 256],
                        preferred_element_type=jnp.float32,
                    )
                    pick_grad = term if pick_grad is None else pick_grad + term
                out_ref[first - start : first - start + 256, :] = pick_grad.T.astype(jnp.bfloat16)


def back(passages, near, other_near, gates, saved, matrices, size):
    hidden_units, model_width = matrices[0].shape
    heights = [
        max(least, stop - start + (16 if stop == model_width else 0))
        for passage in passages
        for (start, stop), least in zip(*passage[3:])
    ]
    arrays = [array for group in saved for array in group]
    return kernel_call(
        functools.partial(back_kernel, passages, len(gates), len(saved)),
        "back",
        [kept((height, size), jnp.bfloat16) for height in heights],
        [pinned(array) for array in (near, other_near, *gates, *arrays, *matrices)],
        (),
        [pltpu.VMEM((len(passages) * size, hidden_units), jnp.bfloat16)] * 4,
    )


def add_kernel(x_ref, y_ref, high_ref, low_ref, x_out, y_out):
    for own_ref, other_ref, out_ref in ((x_ref, high_ref, x_out), (y_ref, low_ref, y_out)):
        out_ref[...] = (
            own_ref[...].astype(jnp.float32)
            + other_ref[: own_ref.shape[0], :].astype(jnp.float32)
        ).astype(jnp.bfloat16)


def turn_kernel(*refs):
    count = len(refs) // 2
    for source_ref, target_ref in zip(refs[:count], refs[count:]):
        for first in range(0, source_ref.shape[0], 256):
            rows = slice(first, first + 256)
            target_ref[:, rows] = source_ref[rows, :].T


def turn(matrices):
    return kernel_call(
        turn_kernel,
        "turn",
        [kept(matrix.shape[::-1], jnp.bfloat16) for matrix in matrices],
        [pinned(matrix) for matrix in matrices],
    )


def half_kernel(part, rows_ref, out_ref):
    half = out_ref.shape[0]
    out_ref[...] = rows_ref[part * half : (part + 1) * half, :]


def half_of(rows, part):
    total, wide = rows.shape
    (out,) = kernel_call(
        functools.partial(half_kernel, part), "half", [kept((total // 2, wide), rows.dtype)], [rows]
    )
    return out


def pack_kernel(first_ref, second_ref, out_ref):
    out_ref[:1, :] = first_ref[:1, :]
    out_ref[1:, :] = second_ref[:1, :]


def pack(first, second):
    return kernel_call(
        pack_kernel, "pack", [kept((2, first.shape[1]), first.dtype)], [pinned(first), second]
    )[0]


def pairs_of(passages):
    row = lax.broadcasted_iota(jnp.int32, (8, 128), 0)
    lane = lax.broadcasted_iota(jnp.int32, (8, 128), 1)
    return row, lane, jnp.logical_and(row < passages, lane < passages)


def spread(index, values):
    total = jnp.zeros((8, 128), jnp.float32)
    for number, value in values:
        total = jnp.where(index == number, value, total)
    return total


def whole_sum(values):
    return jnp.sum(jnp.sum(values, axis=1, keepdims=True), axis=0, keepdims=True)


def swap_gains(grades_ref, ranks_ref):
    passages = grades_ref.shape[1]
    row, lane, pair = pairs_of(passages)
    grade_list = [(number, grades_ref[0, number].astype(jnp.float32)) for number in range(passages)]
    rank_list = [(number, ranks_ref[0, number].astype(jnp.float32)) for number in range(passages)]
    grade_row, grade_lane = spread(row, grade_list), spread(lane, grade_list)
    worth_row, worth_lane = jnp.exp2(grade_row), jnp.exp2(grade_lane)
    discount_row = 1.0 / jnp.log2(2.0 + spread(row, rank_list))
    discount_lane = 1.0 / jnp.log2(2.0 + spread(lane, rank_list))
    ahead = jnp.logical_or(
        grade_lane > grade_row, jnp.logical_and(grade_lane == grade_row, lane < row)
    )
    ideal_rank = jnp.sum(
        jnp.where(jnp.logical_and(pair, ahead), 1.0, 0.0), axis=1, keepdims=True
    )
    ideal_terms = (worth_row - 1.0) / jnp.log2(2.0 + ideal_rank)
    one_lane = jnp.logical_and(pair, lane == 0)
    ideal_gain = whole_sum(jnp.where(one_lane, ideal_terms, 0.0))
    swap_gain = (
        jnp.abs((worth_row - worth_lane) * (discount_row - discount_lane)) / ideal_gain
    )
    return jnp.where(jnp.logical_and(pair, grade_row > grade_lane), swap_gain, 0.0)


def rank_kernel(swap_gain_ref, near_scores_ref, far_scores_ref, loss_ref, factor_ref):
    passages = 2 * near_scores_ref.shape[0]
    place = lax.axis_index("psg")
    row, lane, unused = pairs_of(passages)
    score_list = [
        (place ^ (base + number), jnp.broadcast_to(ref[number : number + 1, :], (8, 128)))
        for base, ref in ((0, near_scores_ref), (passages // 2, far_scores_ref))
        for number in range(passages // 2)
    ]
    swap_gain = swap_gain_ref[...]
    margin = spread(row, score_list) - spread(lane, score_list)
    softplus = jnp.maximum(-margin, 0.0) + jnp.log1p(jnp.exp(-jnp.abs(margin)))
    loss_ref[...] = whole_sum(swap_gain * softplus)
    pull = swap_gain * jax.nn.sigmoid(-margin)
    gradient = whole_sum(jnp.where(lane == place, pull, 0.0) - jnp.where(row == place, pull, 0.0))
    factor_ref[...] = jnp.broadcast_to(gradient * loss_scale, factor_ref.shape)


def first_end_kernel(own_ref, x_low_ref, y_high_ref, total_ref, lines_ref):
    model_width = total_ref.shape[1]
    cut = model_width // 2
    for first in range(0, model_width, 256):
        rows = slice(first, first + 256)
        if first < cut:
            term = x_low_ref[rows, :]
        else:
            term = y_high_ref[first - cut : first - cut + 256, :]
        total = own_ref[rows, :].astype(jnp.float32) + term.astype(jnp.float32)
        total_ref[:, rows] = total.T
    end = slice(model_width, model_width + 8)
    end_high = slice(model_width - cut, model_width - cut + 8)
    lines_ref[...] = own_ref[end, :].astype(jnp.float32) + y_high_ref[end_high, :].astype(
        jnp.float32
    )


def end_kernel(
    factor_ref, total_ref, lines_ref, x_high_ref, y_low_ref,
    hidden_ref, gain_ref, gates_ref, router_ref, unit_ref,
    grad_far, turned_ref, grad_ref, copy_sems,
):
    token_count, model_width = hidden_ref.shape
    cut = y_low_ref.shape[0]
    end_high = slice(model_width - cut, model_width - cut + 8)
    slot_grad = lines_ref[...] + x_high_ref[end_high, :].astype(jnp.float32)
    gates = gates_ref[...]
    d_logit = gates * (slot_grad - jnp.sum(gates * slot_grad, axis=0, keepdims=True))
    d_logit = jnp.concatenate([d_logit, jnp.zeros((120, token_count), jnp.float32)], axis=0).T
    d_logit = jnp.concatenate(split_low(d_logit[:, :8]), axis=1)
    router_rows = jnp.concatenate([router_ref[...]] * 3, axis=0)
    for first in range(0, model_width, 256):
        columns = slice(first, first + 256)
        if first < cut:
            term = y_low_ref[columns, :]
        else:
            term = x_high_ref[first - cut : first - cut + 256, :]
        turned_ref[:, columns] = (
            total_ref[:, columns]
            + term.astype(jnp.float32).T
            + jnp.dot(d_logit, router_rows[:, columns], preferred_element_type=jnp.float32)
        )
    gain = gain_ref[...]
    factor = factor_ref[:, :1]
    size = 16
    copies = []
    for first in range(0, token_count, size):
        rows = slice(first, first + size)
        flat_rows = hidden_ref[rows, :].astype(jnp.float32)
        grad = norm_back(flat_rows, rms_scale(flat_rows), gain, turned_ref[rows, :])
        grad_ref[rows, :] = ((grad + unit_ref[...]) * factor).astype(jnp.bfloat16)
        copies.append(
            pltpu.make_async_copy(
                grad_ref.at[rows, :], grad_far.at[rows, :], copy_sems.at[first // size]
            )
        )
        copies[-1].start()
    for copy in copies:
        copy.wait()


def every_expert(
    hidden,
    norm_gain,
    router,
    gate_proj,
    up_proj,
    down_proj,
    final_gain,
    score_vector,
    expert_ids,
    grades,
    passage_ranks,
):
    unused_query, unused_passage, token_count, model_width = hidden.shape
    passages = grades.shape[1]
    flat = hidden.reshape(token_count, model_width)
    gate_matrix, up_matrix, down_matrix = gate_proj[0], up_proj[0], down_proj[0]
    mine = [gate_matrix, up_matrix, down_matrix]
    flat, gain, router_rows, normed, token_sums, head = kernel_call(
        norm_kernel,
        "norm",
        [
            kept(flat.shape, jnp.bfloat16),
            kept((1, model_width), jnp.float32),
            kept((8, model_width), jnp.bfloat16),
            kept(flat.shape, jnp.bfloat16),
            kept((1, model_width), jnp.float32),
            kept((1, model_width), jnp.float32),
        ],
        [
            flat,
            norm_gain.reshape(1, model_width),
            router.T,
            final_gain.reshape(1, model_width),
            score_vector.reshape(model_width // 128, 128),
        ],
        range(5),
        [
            pltpu.VMEM((1, model_width), jnp.float32),
            pltpu.VMEM((model_width // 128, 128), jnp.bfloat16),
            pltpu.SemaphoreType.DMA((5,)),
        ],
    )
    others = [swap(matrix, CORE) for matrix in mine]
    arrays = own_front(1, normed, router_rows, mine[:2])
    ready = get_ready(1, grades, passage_ranks, down_matrix, arrays[6:])
    normed, arrays, ready = lax.optimization_barrier((normed, arrays, ready))
    x_rows, y_rows = swap(normed, ACROSS_X), swap(normed, ACROSS_Y)
    arrays = own_front(0, normed, router_rows, mine[:2], arrays)
    turned_gates, own_gates, *own_saved, own_part = arrays[:6]
    mine[:2] = arrays[6:]
    swap_gain, mine[2], *mine_turned, down_turned = get_ready(
        0, grades, passage_ranks, down_matrix, mine[:2], ready
    )
    x_rows, y_rows = after(x_rows, mine_turned[0]), after(y_rows, mine_turned[0])
    far_low = swap(half_of(x_rows, 0), ACROSS_Y)
    far_high = swap(half_of(y_rows, 1), ACROSS_X)
    side_gates, *side_saved, side_part = front(
        1, (1, 2), (0,), [x_rows, y_rows], router_rows, mine[:2]
    )
    others[0] = after(others[0], side_part)
    unused, *other_saved, other_part = front(
        2, (0, 1, 2), (1,), [normed, x_rows, y_rows], router_rows, others[:2]
    )
    far_low, far_high = after(far_low, other_part), after(far_high, other_part)
    far_gates, *far_saved, terms = front(
        3, (3,), (0, 1), [far_low, far_high], router_rows, mine[:2] + others[:2],
        (token_sums, mine[2], others[2], own_part, side_part, other_part),
    )

    *others_turned, other_down_turned = turn([after(others[0], terms), *others[1:]])
    head = after(head, others_turned[0])
    near, other_near, unit_vector, travelling, own_score = kernel_call(
        functools.partial(near_kernel, token_count=token_count),
        "near",
        [
            kept((8, down_matrix.shape[0]), jnp.float32),
            kept((8, down_matrix.shape[0]), jnp.float32),
            kept((1, model_width), jnp.float32),
            kept((1, 128), jnp.float32),
            shape_of((1, 1), jnp.float32),
        ],
        [
            pinned(terms),
            swap(terms, ACROSS_X),
            swap(terms, ACROSS_Y),
            swap(terms, ACROSS_X | ACROSS_Y),
            pinned(head),
            pinned(down_turned),
            pinned(other_down_turned),
        ],
    )
    matrices = [*mine_turned, *others_turned]
    middle = model_width // 2
    lower, upper, early, earlier = (0, middle), (middle, model_width), middle + 32, middle + 48
    far_low, far_high = back(
        ((3, (0, 0), ((0, 0), (1, 0)), (lower, upper), (earlier, earlier)),),
        near, other_near, [far_gates], [far_saved[:3], far_saved[3:]], matrices, token_count,
    )
    far_sent = far_low
    far_low, far_high = swap(far_low, ACROSS_X), swap(far_high, ACROSS_Y)

    def sides_back(x_window, y_window, least, *earlier):
        return back(
            (
                (1, (0, 0), ((0, 0), (1, token_count)), (x_window,), (least,)),
                (2, (0, token_count), ((0, token_count), (1, 2 * token_count)), (y_window,), (least,)),
            ),
            after(near, *earlier), other_near, [side_gates], [side_saved, other_saved], matrices,
            token_count,
        )

    x_low, y_high = sides_back(lower, upper, early, far_sent)
    first_sent = x_low
    x_low, y_high = swap(x_low, ACROSS_X), swap(y_high, ACROSS_Y)
    x_high, y_low = sides_back(upper, lower, 0, first_sent)
    travelling = after(travelling, first_sent)
    met = lax.ppermute(travelling, "psg", [(index, index ^ 1) for index in range(passages)])
    near_scores = pack(travelling, met)
    far_high = after(far_high, near_scores)
    x_high, y_low = kernel_call(
        add_kernel,
        "add",
        [kept(x_high.shape, jnp.bfloat16), kept(y_low.shape, jnp.bfloat16)],
        [pinned(x_high), pinned(y_low), far_high, far_low],
    )
    x_high, y_low, near_scores, other_near = lax.optimization_barrier(
        (x_high, y_low, near_scores, other_near)
    )
    x_high, y_low = swap(x_high, ACROSS_X), swap(y_low, ACROSS_Y)
    (own_sums,) = back(
        ((0, (0, 0), ((0, 0), (1, 0)), ((0, model_width),), (0,)),),
        near, other_near, [own_gates], [own_saved, other_saved], matrices, token_count,
    )
    far_scores = lax.ppermute(near_scores, "psg", [(index, index ^ 2) for index in range(passages)])
    loss, factor = kernel_call(
        rank_kernel,
        "rank",
        [shape_of((1, 1), jnp.float32), kept((1, 128), jnp.float32)],
        [pinned(swap_gain), pinned(near_scores), far_scores],
    )
    total, lines = kernel_call(
        first_end_kernel,
        "first_end",
        [
            kept((token_count, model_width), jnp.float32),
            kept((8, token_count), jnp.float32),
        ],
        [pinned(own_sums), after(x_low, factor), y_high],
    )
    (grad,) = kernel_call(
        end_kernel,
        "end",
        [shape_of((token_count, model_width), jnp.bfloat16)],
        [
            pinned(factor), pinned(total), pinned(lines), x_high, y_low, pinned(flat), pinned(gain),
            pinned(turned_gates), pinned(router_rows), pinned(unit_vector),
        ],
        scratch=[
            pltpu.VMEM((token_count, model_width), jnp.float32),
            pltpu.VMEM((token_count, model_width), jnp.bfloat16),
            pltpu.SemaphoreType.DMA((token_count // 16,)),
        ],
        result=pl.ANY,
    )
    return (loss.reshape(1), own_score, grad.reshape(hidden.shape))


def block(*arrays):
    hidden, router, expert_ids, grades = arrays[0], arrays[2], arrays[8], arrays[9]
    each_expert = router.shape[1] == expert_ids.shape[3] == 8
    if hidden.shape[1] == 1 and each_expert and grades.shape[1] == 4:
        return every_expert(*arrays)
    return local(*arrays)


def solution(mesh):
    placed = (
        P("exp", "psg", None, None),
        P(),
        P(),
        P("exp", None, None),
        P("exp", None, None),
        P("exp", None, None),
        P(),
        P(),
        P("exp", "psg", None, None),
        P("exp", None),
        P("exp", None),
    )
    return jax.shard_map(
        block,
        mesh=mesh,
        in_specs=placed,
        out_specs=(P("exp"), P("exp", "psg"), P("exp", "psg", None, None)),
        check_vma=False,
    )
```
